32 devices in a mesh: seq: 8 (over z, y), tp: 4 (over x, core).
Axes of the slice: x: 2, y: 2, z: 4, core: 2. Of those that a mesh axis runs over, the one named last changes fastest.
Arguments:
- tokens: bfloat16 [2, 4096, 512], P(None, ('seq', 'tp')), may hold values from -6 to 6
- cotangent: bfloat16 [2, 4096, 512], P(None, ('seq', 'tp')), may hold values from -6 to 6
- valid_lengths: int32 [2], replicated, may hold values from 1024 to 4096, as said below
- norm1_gain: float32 [512], replicated, may hold values from 0.25 to 1.75
- ema_rate: float32 [512, 16], replicated, may hold values from 0.00012207031 to 0.035
- ema_beta: float32 [512, 16], replicated, may hold values from -4 to 4
- ema_eta: float32 [512, 16], replicated, may hold values from -1.5 to 1.5
- ema_skip: float32 [512], replicated, may hold values from -4 to 4
- w_shared: bfloat16 [512, 128], replicated, may hold values from -0.25 to 0.25
- query_gain: float32 [128], replicated, may hold values from -2.5 to 2.5
- key_gain: float32 [128], replicated, may hold values from -2.5 to 2.5
- rel_bias: float32 [128], replicated, may hold values from -4 to 4
- w_value: bfloat16 [512, 1024], P(None, 'tp'), may hold values from -0.25 to 0.25
- w_reset: bfloat16 [512, 1024], P(None, 'tp'), may hold values from -0.25 to 0.25
- w_update: bfloat16 [512, 512], P('tp'), may hold values from -0.25 to 0.25
- w_hidden: bfloat16 [512, 512], P('tp'), may hold values from -0.25 to 0.25
- u_hidden: bfloat16 [1024, 512], P('tp'), may hold values from -0.5 to 0.5
- norm2_gain: float32 [512], replicated, may hold values from 0.25 to 1.75
- w_in: bfloat16 [512, 1024], P(None, 'tp'), may hold values from -0.25 to 0.25
- w_out: bfloat16 [1024, 512], P('tp'), may hold values from -0.1875 to 0.1875
Outputs:
- output: bfloat16 [2, 4096, 512], P(None, ('seq', 'tp'))
- grad_tokens: bfloat16 [2, 4096, 512], P(None, ('seq', 'tp'))
- grad_norm1_gain: float32 [512], replicated
- grad_ema_rate: float32 [512, 16], replicated
- grad_ema_beta: float32 [512, 16], replicated
- grad_ema_eta: float32 [512, 16], replicated
- grad_ema_skip: float32 [512], replicated
- grad_w_shared: float32 [512, 128], replicated
- grad_query_gain: float32 [128], replicated
- grad_key_gain: float32 [128], replicated
- grad_rel_bias: float32 [128], replicated
- grad_w_value: float32 [512, 1024], P(None, 'tp')
- grad_w_reset: float32 [512, 1024], P(None, 'tp')
- grad_w_update: float32 [512, 512], P('tp')
- grad_w_hidden: float32 [512, 512], P('tp')
- grad_u_hidden: float32 [1024, 512], P('tp')
- grad_norm2_gain: float32 [512], replicated
- grad_w_in: float32 [512, 1024], P(None, 'tp')
- grad_w_out: float32 [1024, 512], P('tp')
The draws below stay inside these ranges and needn't reach their ends.
Inputs may be any that keep to these rules, and one draw needn't show every extreme that they name: `valid_lengths`: one length per sequence; at least one sequence, drawn from the seed, has all 4096 positions valid.
All inputs are finite; a program needn't handle non-finite values.
Results may differ from the reference program's by a relative error of at most 0.018.
The reference program's roundings to bfloat16 on the way count: a program that leaves them out, or rounds other values in their place, can miss the bound.
Values may be sent and summed in bfloat16 or wider, within the bound.
No kernel may reach another device: no remote copies, remote signals or barrier semaphores. Data moves between devices by JAX's collectives and lax.ppermute only.
A program may use at most 320 MiB of HBM per device.

```python
import math
import jax
import jax.numpy as jnp
from jax import lax

D = 512
Z = 128
V = 1024
NDIM = 16
FF = 1024
CH = 128
SEQS = 2
SEQ_LEN = 4096


def draw_valid_lengths(key, part):
    key = jax.random.fold_in(key, 7)
    first_key, second_key = jax.random.split(key)
    lengths = jax.random.randint(first_key, (SEQS,), SEQ_LEN // 4, SEQ_LEN + 1)
    chosen = jax.random.randint(second_key, (), 0, SEQS)
    lengths = jnp.where(jnp.arange(SEQS) == chosen, SEQ_LEN, lengths)
    return lengths.astype(jnp.int32)


def shard_levels(own_key, dims, cuts, least, largest):
    def one(axis_at, shards_of):
        steps = jax.random.uniform(jax.random.fold_in(jax.random.fold_in(own_key, 6), axis_at), (shards_of,), jnp.float32, least / len(cuts), largest / len(cuts))
        return jnp.repeat(jnp.exp(steps), dims[axis_at] // shards_of).reshape((-1,) + (1,) * (len(dims) - axis_at - 1))

    loudness = one(*cuts[0])
    for cut in cuts[1:]:
        loudness = loudness * one(*cut)
    return loudness


def noise(key, extent, width, most, cuts=(), kind=jnp.bfloat16):
    values = width * jax.random.normal(key, extent, jnp.float32)
    if cuts:
        values = values * shard_levels(key, extent, cuts, -0.22, 0.18)
    return jnp.clip(values, -most, most).astype(kind)


def setup_inputs(seed: int = 0) -> dict:
    splits = jax.random.split(jax.random.key(seed), 21)
    return {
        "tokens": noise(splits[0], (SEQS, SEQ_LEN, D), 1.0, 6.0, ((1, 32),)),
        "cotangent": noise(splits[1], (SEQS, SEQ_LEN, D), 1.0, 6.0, ((1, 32),)),
        "valid_lengths": draw_valid_lengths(jax.random.fold_in(splits[20], 71), 0),
        "norm1_gain": jnp.clip(1.0 + 0.15 * jax.random.normal(splits[3], (D,), jnp.float32), 0.25, 1.75),
        "ema_rate": jnp.clip(jnp.exp(jax.random.uniform(splits[4], (D, NDIM), jnp.float32, math.log(0.00012207031), math.log(0.035))), 0.00012207031, 0.035),
        "ema_beta": noise(splits[5], (D, NDIM), 1.0, 4.0, (), jnp.float32),
        "ema_eta": noise(splits[6], (D, NDIM), NDIM ** -0.5, 1.5, (), jnp.float32),
        "ema_skip": noise(splits[7], (D,), 1.0, 4.0, (), jnp.float32),
        "w_shared": noise(splits[8], (D, Z), D ** -0.5, 0.25),
        "query_gain": noise(splits[9], (Z,), 1.0, 2.5, (), jnp.float32),
        "key_gain": noise(splits[10], (Z,), 1.0, 2.5, (), jnp.float32),
        "rel_bias": noise(splits[11], (CH,), 1.0, 4.0, (), jnp.float32),
        "w_value": noise(splits[12], (D, V), D ** -0.5, 0.25, ((1, 4),)),
        "w_reset": noise(splits[13], (D, V), D ** -0.5, 0.25, ((1, 4),)),
        "w_update": noise(splits[14], (D, D), D ** -0.5, 0.25, ((0, 4),)),
        "w_hidden": noise(splits[15], (D, D), D ** -0.5, 0.25, ((0, 4),)),
        "u_hidden": noise(splits[16], (V, D), (V // 8) ** -0.5, 0.5, ((0, 4),)),
        "norm2_gain": jnp.clip(1.0 + 0.15 * jax.random.normal(splits[17], (D,), jnp.float32), 0.25, 1.75),
        "w_in": noise(splits[18], (D, FF), D ** -0.5, 0.25, ((1, 4),)),
        "w_out": noise(splits[19], (FF, D), FF ** -0.5, 0.1875, ((0, 4),)),
    }


@jax.custom_vjp
def low(v):
    return lax.optimization_barrier(v.astype(jnp.bfloat16)).astype(jnp.float32)

@jax.custom_vjp
def low_back(v):
    return v

def low_keep(v):
    return (low(v), None)

def low_pass(kept, grad):
    return (grad,)

def back_keep(v):
    return (v, None)

def back_low(kept, grad):
    return (low(grad),)
low.defvjp(low_keep, low_pass)
low_back.defvjp(back_keep, back_low)
highest = lax.Precision.HIGHEST
epsilon = 1e-05

def product(left, right):
    return jnp.dot(left, right, precision=highest)

def layer_norm(rows, gain):
    center = rows - lax.optimization_barrier(jnp.mean(rows, axis=-1, keepdims=True))
    spread = lax.optimization_barrier(jnp.mean(center * center, axis=-1, keepdims=True))
    return center * lax.rsqrt(spread + epsilon) * gain

def ema_sequence(values, rate, beta, eta):
    decay = 1.0 - rate
    inflow = jnp.sqrt(rate * (2.0 - rate)) * beta

    def stretch_pass(state, block):

        def one_step(state, row):
            state = decay * state + inflow * row[:, None]
            return (state, lax.optimization_barrier(jnp.sum(eta * state, axis=1)))
        return lax.scan(one_step, state, block)
    blocks = values.reshape(-1, CH, D)
    start = jnp.zeros((D, NDIM), jnp.float32)
    _, smooth = lax.scan(jax.checkpoint(stretch_pass), start, blocks)
    return smooth.reshape(-1, D)

def attend(query, keys, values, rel_bias, length):
    count = query.shape[0] // CH
    query_c = query.reshape(count, CH, Z)
    keys_c = keys.reshape(count, CH, Z)
    values_c = values.reshape(count, CH, -1)
    raw = jnp.einsum('ntz,nsz->nts', query_c, keys_c, precision=highest) * Z ** (-0.5)
    offset = jnp.arange(CH)[:, None] - jnp.arange(CH)[None, :]
    scores = low_back(raw + rel_bias[jnp.clip(offset, 0, CH - 1)][None])
    position = jnp.arange(count * CH).reshape(count, CH)
    allowed = (offset >= 0)[None] & ((position[:, None, :] < length) | (offset == 0)[None])
    masked = jnp.where(allowed, scores, -1e+30)
    top = lax.optimization_barrier(jnp.max(masked, axis=-1, keepdims=True))
    weights = jnp.where(allowed, jnp.exp(masked - top), 0.0)
    prob = weights / lax.optimization_barrier(jnp.sum(weights, axis=-1, keepdims=True))
    result = jnp.einsum('nts,nsv->ntv', low(prob), values_c, precision=highest)
    return result.reshape(count * CH, -1)

def forward_one(params, rows, length):
    norm1_gain, ema_rate, ema_beta, ema_eta, ema_skip, w_shared, query_gain, key_gain, rel_bias, w_value, w_reset, w_update, w_hidden, u_hidden, norm2_gain, w_in, w_out = params
    normed = low(layer_norm(rows, norm1_gain))
    smooth = ema_sequence(normed, ema_rate, ema_beta, ema_eta)
    mixed = low(jax.nn.silu(smooth + ema_skip * normed))
    shared = jax.nn.silu(low_back(product(mixed, w_shared)))
    query = low(shared * query_gain)
    keys = low(shared * key_gain)
    values = low(jax.nn.silu(low_back(product(normed, w_value))))
    attended = low_back(attend(query, keys, values, rel_bias, length))
    reset_pre = low_back(product(mixed, w_reset))
    gated = low(jax.nn.silu(reset_pre) * attended)
    hidden_pre = low_back(product(mixed, w_hidden) + product(gated, u_hidden))
    update_pre = low_back(product(mixed, w_update))
    update = jax.nn.sigmoid(update_pre)
    middle = rows + update * (jax.nn.silu(hidden_pre) - rows)
    normed2 = low(layer_norm(middle, norm2_gain))
    inner = low(jax.nn.silu(low_back(product(normed2, w_in))))
    return middle + product(inner, w_out)

def reference(tokens, cotangent, valid_lengths, norm1_gain, ema_rate, ema_beta, ema_eta, ema_skip, w_shared, query_gain, key_gain, rel_bias, w_value, w_reset, w_update, w_hidden, u_hidden, norm2_gain, w_in, w_out):
    params = tuple((item.astype(jnp.float32) for item in (norm1_gain, ema_rate, ema_beta, ema_eta, ema_skip, w_shared, query_gain, key_gain, rel_bias, w_value, w_reset, w_update, w_hidden, u_hidden, norm2_gain, w_in, w_out)))
    rows = tokens.astype(jnp.float32)
    live = jnp.arange(SEQ_LEN)[None, :] < valid_lengths[:, None]
    live_grad = jnp.where(live[:, :, None], cotangent.astype(jnp.float32), 0.0)

    def whole(params, rows):
        return lax.map(lambda item: forward_one(params, item[0], item[1]), (rows, valid_lengths))
    output, pull = jax.vjp(whole, params, rows)
    grads, grad_rows = pull(live_grad)
    grad_norm1_gain, grad_ema_rate, grad_ema_beta, grad_ema_eta, grad_ema_skip, grad_w_shared, grad_query_gain, grad_key_gain, grad_rel_bias, grad_w_value, grad_w_reset, grad_w_update, grad_w_hidden, grad_u_hidden, grad_norm2_gain, grad_w_in, grad_w_out = grads
    return (output.astype(jnp.bfloat16), grad_rows.astype(jnp.bfloat16), grad_norm1_gain, grad_ema_rate, grad_ema_beta, grad_ema_eta, grad_ema_skip, grad_w_shared, grad_query_gain, grad_key_gain, grad_rel_bias, grad_w_value, grad_w_reset, grad_w_update, grad_w_hidden, grad_u_hidden, grad_norm2_gain, grad_w_in, grad_w_out)
```

```python
import functools

import jax
import jax.numpy as jnp
from jax import lax
from jax.experimental import pallas as pl
from jax.experimental.pallas import tpu as pltpu
from jax.sharding import PartitionSpec as P

D = 512
Z = 128
NDIM = 16
CH = 128
PIECE = 16
PIECES = CH // PIECE
LANES = 128
BLOCKS = D // LANES
EPS = 1e-05
F32 = jnp.float32
BF16 = jnp.bfloat16
SMALL_ROWS = 64

VMEM = pl.BlockSpec(memory_space=pltpu.VMEM)
SMEM = pl.BlockSpec(memory_space=pltpu.SMEM)
ANY = pl.BlockSpec(memory_space=pl.ANY)


def sigmoid(v):
    return 0.5 * jnp.tanh(0.5 * v) + 0.5


def silu(v):
    return v * sigmoid(v)


def silu_slope(v):
    s = sigmoid(v)
    return s * (1.0 + v * (1.0 - s))


def mm(a, b):
    return jnp.dot(a, b, preferred_element_type=F32)


def mm_nt(a, b):
    return lax.dot_general(a, b, (((1,), (1,)), ((), ())), preferred_element_type=F32)


def mm_tn(a, b):
    return lax.dot_general(a, b, (((0,), (0,)), ((), ())), preferred_element_type=F32)


def normalized(v):
    center = v - jnp.mean(v, axis=-1, keepdims=True)
    scale = lax.rsqrt(jnp.mean(center * center, axis=-1, keepdims=True) + EPS)
    return center * scale, scale


def norm_back(grad, xhat, scale, gain):
    full = grad * gain
    return scale * (
        full
        - jnp.mean(full, axis=-1, keepdims=True)
        - xhat * jnp.mean(full * xhat, axis=-1, keepdims=True)
    )


def rows_of(s):
    return pl.ds(s * CH, CH)


def lanes_of(i):
    return pl.ds(pl.multiple_of((i % BLOCKS) * LANES, LANES), LANES)


def spread(row):
    return jnp.broadcast_to(row, (PIECES, LANES))


def piece_rows(s, t):
    return pl.ds(s * CH + t, PIECES, stride=PIECE)


def put_rows(ref, rows, value):
    for b in range(BLOCKS):
        ref[b, rows, :] = value[:, b * LANES : (b + 1) * LANES]


def get_rows(ref, rows):
    return jnp.concatenate([ref[b, rows, :] for b in range(BLOCKS)], axis=1)


def call(body, out, scratch, operands, specs, name, flops=0, moved=0):
    return pl.pallas_call(
        body,
        out_shape=out,
        in_specs=specs,
        out_specs=jax.tree.map(lambda _: VMEM, out),
        scratch_shapes=scratch,
        name=name,
        cost_estimate=pl.CostEstimate(flops=flops, bytes_accessed=moved, transcendentals=0),
        compiler_params=pltpu.CompilerParams(vmem_limit_bytes=48 * 1024 * 1024),
    )(*operands)


def shape(dims, dtype=F32):
    return jax.ShapeDtypeStruct(dims, dtype)


def enter_kernel(seqs, tok, gain, rate, beta, eta, normed, par, before, ends, nf, tab):
    r = rate[...].T
    d = 1.0 - r
    par[0] = d
    par[1] = jnp.log(d)
    par[2] = jnp.sqrt(r * (2.0 - r)) * beta[...].T
    par[3] = eta[...].T
    d2 = d * d
    d4 = d2 * d2
    d8 = d4 * d4
    d15 = d8 * d4 * d2 * d
    q = d8 * d8
    tab[0] = q
    tab[1] = 16.0 * d15
    tab[2] = q * q
    tab[3] = 32.0 * q * d15
    tab[4] = q * q * q * q
    tab[5] = 64.0 * q * q * q * d15
    for s in range(seqs):
        xhat, _ = normalized(tok[s].astype(F32))
        low = (xhat * gain[...]).astype(BF16)
        normed[rows_of(s), :] = low
        put_rows(nf, rows_of(s), low.astype(F32))
    place = lax.broadcasted_iota(jnp.int32, (PIECES, LANES), 0)

    def body(i, carry):
        s = i // BLOCKS
        lane = lanes_of(i)
        xs = [nf[i % BLOCKS, piece_rows(s, t), :] for t in range(PIECE)]
        for j0 in range(0, NDIM, 8):
            ds = [spread(par[0, j0 + j : j0 + j + 1, lane]) for j in range(8)]
            st = [xs[0]] * 8
            ta = [jnp.zeros((PIECES, LANES), F32)] * 8
            for t in range(1, PIECE):
                for j in range(8):
                    ta[j] = ds[j] * ta[j] + st[j]
                    st[j] = ds[j] * st[j] + xs[t]
            for j in range(8):
                a, b = st[j], ta[j]
                for k, step in enumerate((1, 2, 4)):
                    qm = spread(tab[2 * k, j0 + j : j0 + j + 1, lane])
                    rm = spread(tab[2 * k + 1, j0 + j : j0 + j + 1, lane])
                    sa = jnp.where(place >= step, pltpu.roll(a, step, 0), 0.0)
                    sb = jnp.where(place >= step, pltpu.roll(b, step, 0), 0.0)
                    b = b + qm * sb + rm * sa
                    a = a + qm * sa
                before[0, s, j0 + j, :, lane] = jnp.where(place >= 1, pltpu.roll(a, 1, 0), 0.0)
                before[1, s, j0 + j, :, lane] = jnp.where(place >= 1, pltpu.roll(b, 1, 0), 0.0)
                ends[0, s, j0 + j : j0 + j + 1, lane] = a[PIECES - 1 :]
                ends[1, s, j0 + j : j0 + j + 1, lane] = b[PIECES - 1 :]
        return carry

    lax.fori_loop(0, seqs * BLOCKS, body, 0)


def piece_powers(par, pw):
    k = lax.broadcasted_iota(jnp.int32, (PIECES, D), 0).astype(F32) * PIECE
    for j in range(NDIM):
        pw[j] = jnp.exp(k * par[1, j : j + 1, :])


def mix_kernel(
    seqs, tp, levels, first_bit,
    ids, tok, normed, par, before, skip, wsh, qg, kg, rb, *refs,
):
    recvs, refs = refs[:levels], refs[levels:]
    w1s, refs = refs[:tp], refs[tp:]
    w2s, refs = refs[:tp], refs[tp:]
    (
        st_in, skip_pre, mixed, shared_pre, prob, values, value_pre, reset_pre, attended, gated,
        hidden_pre, update_pre, middle,
        w1, whu, uh, nf, sm, pw, sems,
    ) = refs
    vb = values.shape[2]
    nb = D // tp
    me = ids[0]
    place = ids[1]
    copies = []
    for r in range(tp):
        b = jnp.bitwise_xor(me, r)
        row = pl.ds(pl.multiple_of(b * nb, nb), nb)
        copies.append(pltpu.make_async_copy(w1s[r], w1.at[r], sems.at[4 * r]))
        copies.append(
            pltpu.make_async_copy(
                w2s[r].at[pl.ds(0, nb), :], whu.at[row, pl.ds(0, D)], sems.at[4 * r + 1]
            )
        )
        copies.append(
            pltpu.make_async_copy(
                w2s[r].at[pl.ds(nb, nb), :], whu.at[row, pl.ds(D, D)], sems.at[4 * r + 2]
            )
        )
        copies.append(
            pltpu.make_async_copy(w2s[r].at[pl.ds(2 * nb, vb), :], uh.at[r], sems.at[4 * r + 3])
        )
    for c in copies:
        c.start()
    put_rows(nf, slice(None), normed[...].astype(F32))
    piece_powers(par, pw)
    logd = par[1]
    dinv = 1.0 / par[0]
    for s in range(seqs):
        a = jnp.zeros((NDIM, D), F32)
        b = jnp.zeros((NDIM, D), F32)
        for k in range(levels):
            mine = jnp.bitwise_and(place, 1 << k) > 0
            off = jnp.bitwise_and(place, (1 << k) - 1).astype(F32) * float(CH)
            power = jnp.where(mine, jnp.exp(off * logd), 0.0)
            oa = recvs[k][0, s].astype(F32) * power
            b = b + recvs[k][1, s].astype(F32) * power + off * oa * dinv
            a = a + oa
        st_in[0, s] = a
        st_in[1, s] = b

    def ema(i, carry):
        s = i // BLOCKS
        lane = lanes_of(i)
        row = [pl.ds(j, 1) for j in range(NDIM)]
        ds = [spread(par[0, row[j], lane]) for j in range(NDIM)]
        ws = [spread(par[2, row[j], lane] * par[3, row[j], lane]) for j in range(NDIM)]
        st = [
            before[0, s, j, :, lane] + pw[j, :, lane] * st_in[0, s, row[j], lane]
            for j in range(NDIM)
        ]
        for t in range(PIECE):
            x = nf[i % BLOCKS, piece_rows(s, t), :]
            parts = [None, None]
            for j in range(NDIM):
                st[j] = ds[j] * st[j] + x
                term = ws[j] * st[j]
                parts[j % 2] = term if parts[j % 2] is None else parts[j % 2] + term
            sm[i % BLOCKS, piece_rows(s, t), :] = parts[0] + parts[1]
        return carry

    lax.fori_loop(0, seqs * BLOCKS, ema, 0)
    for s in range(seqs):
        pre = get_rows(sm, rows_of(s)) + skip[...] * get_rows(nf, rows_of(s))
        skip_pre[rows_of(s), :] = pre
        mixed[rows_of(s), :] = silu(pre).astype(BF16)
    sp = mm(mixed[...], wsh[...])
    shared_pre[...] = sp
    shared = silu(sp)
    query = (shared * qg[...]).astype(BF16)
    keys = (shared * kg[...]).astype(BF16)
    t_at = lax.broadcasted_iota(jnp.int32, (CH, CH), 0)
    s_at = lax.broadcasted_iota(jnp.int32, (CH, CH), 1)
    bias_t = jnp.broadcast_to(rb[...], (CH, CH))
    for bit in range(7):
        bias_t = jnp.where(
            jnp.bitwise_and(t_at, 1 << bit) > 0, pltpu.roll(bias_t, 1 << bit, 1), bias_t
        )
    bias = bias_t.T
    for s in range(seqs):
        raw = mm_nt(query[s * CH : (s + 1) * CH], keys[s * CH : (s + 1) * CH]) * Z ** (-0.5)
        live = (place * CH + s_at) < ids[2 + s]
        allowed = (s_at <= t_at) & (live | (s_at == t_at))
        masked = jnp.where(allowed, raw + bias, -1e30)
        top = jnp.max(masked, axis=-1, keepdims=True)
        weights = jnp.where(allowed, jnp.exp(masked - top), 0.0)
        prob[s] = weights / jnp.sum(weights, axis=-1, keepdims=True)
    for c in copies:
        c.wait()
    hu = mm(mixed[...], whu[...])
    hidden_pre[...] = hu[:, :D]
    update_pre[...] = hu[:, D:]

    def block(r, carry):
        vp = mm(normed[...], w1[r, :, :vb])
        value_pre[r] = vp
        v = silu(vp).astype(BF16)
        values[r] = v
        rp = mm(mixed[...], w1[r, :, vb:])
        reset_pre[r] = rp
        gate = silu(rp)
        for s in range(seqs):
            att = mm(prob[s].astype(BF16), v[s * CH : (s + 1) * CH])
            attended[r, rows_of(s), :] = att
            gated[r, rows_of(s), :] = (gate[s * CH : (s + 1) * CH] * att).astype(BF16)
        hidden_pre[...] += mm(gated[r], uh[r])
        return carry

    lax.fori_loop(0, tp, block, 0)
    for s in range(seqs):
        x = tok[s].astype(F32)
        middle[rows_of(s), :] = x + sigmoid(update_pre[rows_of(s), :]) * (
            silu(hidden_pre[rows_of(s), :]) - x
        )


def ffn_kernel(seqs, tp, ids, tok, cot, middle, hidden_pre, update_pre, gain2, *refs):
    w3s, refs = refs[:tp], refs[tp:]
    (
        out, keep, send, grad_hu, resid, grad_gain2,
        wi, wo, n2, lg, acc, gn2, sems,
    ) = refs
    vb = wi.shape[2]
    cuts = D // vb
    copies = []
    for r in range(tp):
        copies.append(
            pltpu.make_async_copy(
                w3s[r].at[:, pl.ds(0, vb)], wi.at[r], sems.at[r * (cuts + 1)]
            )
        )
        for k in range(cuts):
            copies.append(
                pltpu.make_async_copy(
                    w3s[r].at[pl.ds(k * vb, vb), pl.ds(vb, vb)],
                    wo.at[r, :, pl.ds(k * vb, vb)],
                    sems.at[r * (cuts + 1) + 1 + k],
                )
            )
    for c in copies:
        c.start()
    place = ids[1]
    xhat, scale = normalized(middle[...])
    n2[...] = (xhat * gain2[...]).astype(BF16)
    at = lax.broadcasted_iota(jnp.int32, (CH, D), 0) + place * CH
    for s in range(seqs):
        lg[rows_of(s), :] = jnp.where(at < ids[2 + s], cot[s].astype(F32), 0.0).astype(BF16)
    acc[...] = jnp.zeros_like(acc)
    gn2[...] = jnp.zeros_like(gn2)
    for c in copies:
        c.wait()

    def block(h, carry):
        for odd in range(2):
            r = 2 * h + odd
            grads = (keep, send)[odd]
            pre = mm(n2[...], wi[r])
            inner = silu(pre).astype(BF16)
            acc[...] += mm(inner, wo[r])
            gip = (mm_nt(lg[...], wo[r]) * silu_slope(pre)).astype(BF16)
            gn2[...] += mm_nt(gip, wi[r])
            grads[h, :, :vb] = mm_tn(n2[...], gip).astype(BF16)
            gwo = mm_tn(inner, lg[...]).astype(BF16)
            for k in range(cuts):
                grads[h, k * vb : (k + 1) * vb, vb:] = gwo[:, k * vb : (k + 1) * vb]
        return carry

    lax.fori_loop(0, tp // 2, block, 0)
    mid = middle[...]
    out[...] = (mid + acc[...]).astype(BF16)
    grad = gn2[...]
    grad_gain2[...] = jnp.sum(grad * xhat, axis=0, keepdims=True)
    gm = lg[...].astype(F32) + norm_back(grad, xhat, scale, gain2[...])
    for s in range(seqs):
        x = tok[s].astype(F32)
        g = gm[s * CH : (s + 1) * CH]
        hp = hidden_pre[rows_of(s), :]
        update = sigmoid(update_pre[rows_of(s), :])
        grad_hu[rows_of(s), :D] = (g * update * silu_slope(hp)).astype(BF16)
        grad_hu[rows_of(s), D:] = (g * (silu(hp) - x) * update * (1.0 - update)).astype(BF16)
        resid[rows_of(s), :] = g * (1.0 - update)


def back_kernel(
    seqs, tp,
    ids, normed, mixed, skip_pre, shared_pre, prob, values, value_pre, reset_pre, attended, gated,
    grad_hu, par, wsh, qg, kg, *refs,
):
    w1s, refs = refs[:tp], refs[tp:]
    w2s, refs = refs[:tp], refs[tp:]
    (
        keep2, send2, keep1, send1, grad_skip, grad_normed, after, ends, grad_wsh, misc,
        w1, whu, uh, ghu, gm, gp, tab, sems,
    ) = refs
    vb = values.shape[2]
    nb = D // tp
    me = ids[0]
    copies = []
    for r in range(tp):
        b = jnp.bitwise_xor(me, r)
        row = pl.ds(pl.multiple_of(b * nb, nb), nb)
        copies.append(pltpu.make_async_copy(w1s[r], w1.at[r], sems.at[4 * r]))
        copies.append(
            pltpu.make_async_copy(
                w2s[r].at[pl.ds(0, nb), :], whu.at[row, pl.ds(0, D)], sems.at[4 * r + 1]
            )
        )
        copies.append(
            pltpu.make_async_copy(
                w2s[r].at[pl.ds(nb, nb), :], whu.at[row, pl.ds(D, D)], sems.at[4 * r + 2]
            )
        )
        copies.append(
            pltpu.make_async_copy(w2s[r].at[pl.ds(2 * nb, vb), :], uh.at[r], sems.at[4 * r + 3])
        )
    for c in copies:
        c.start()
    ghu[...] = mm_tn(mixed[...], grad_hu[...])
    gp[...] = jnp.zeros_like(gp)
    grad_normed[...] = jnp.zeros_like(grad_normed)
    for c in copies:
        c.wait()
    gm[...] = mm_nt(grad_hu[...], whu[...])

    def block(h, carry):
        for odd in range(2):
            r = 2 * h + odd
            g1 = (keep1, send1)[odd]
            g2 = (keep2, send2)[odd]
            row = pl.ds(pl.multiple_of(jnp.bitwise_xor(me, r) * nb, nb), nb)
            g2[h, pl.ds(0, nb), :] = ghu[row, pl.ds(0, D)].astype(BF16)
            g2[h, pl.ds(nb, nb), :] = ghu[row, pl.ds(D, D)].astype(BF16)
            ghp = grad_hu[:, :D]
            g2[h, pl.ds(2 * nb, vb), :] = mm_tn(gated[r], ghp).astype(BF16)
            gg = mm_nt(ghp, uh[r])
            rp = reset_pre[r]
            sig = sigmoid(rp)
            ga = (gg * (rp * sig)).astype(BF16)
            grp = (gg * attended[r] * (sig * (1.0 + rp * (1.0 - sig)))).astype(BF16)
            g1[h, :, vb:] = mm_tn(mixed[...], grp).astype(BF16)
            gm[...] += mm_nt(grp, w1[r, :, vb:])
            gvs = []
            for s in range(seqs):
                part = ga[s * CH : (s + 1) * CH]
                gvs.append(mm_tn(prob[s].astype(BF16), part))
                gp[s] += mm_nt(part, values[r, rows_of(s), :])
            gv = jnp.concatenate(gvs, axis=0) if seqs > 1 else gvs[0]
            gvp = (gv * silu_slope(value_pre[r])).astype(BF16)
            g1[h, :, :vb] = mm_tn(normed[...], gvp).astype(BF16)
            grad_normed[...] += mm_nt(gvp, w1[r, :, :vb])
        return carry

    lax.fori_loop(0, tp // 2, block, 0)
    sp = shared_pre[...]
    shared = silu(sp)
    query = (shared * qg[...]).astype(BF16)
    keys = (shared * kg[...]).astype(BF16)
    total = jnp.zeros((CH, CH), F32)
    gqs = []
    gks = []
    for s in range(seqs):
        pr = prob[s]
        low = (pr * (gp[s] - jnp.sum(pr * gp[s], axis=-1, keepdims=True))).astype(BF16)
        total = total + low.astype(F32)
        gqs.append(mm(low, keys[s * CH : (s + 1) * CH]) * Z ** (-0.5))
        gks.append(mm_tn(low, query[s * CH : (s + 1) * CH]) * Z ** (-0.5))
    gq = jnp.concatenate(gqs, axis=0) if seqs > 1 else gqs[0]
    gk = jnp.concatenate(gks, axis=0) if seqs > 1 else gks[0]
    turned = total.T
    s_at = lax.broadcasted_iota(jnp.int32, (CH, CH), 0)
    for bit in range(7):
        turned = jnp.where(
            jnp.bitwise_and(s_at, 1 << bit) > 0, pltpu.roll(turned, CH - (1 << bit), 1), turned
        )
    misc[...] = jnp.concatenate(
        [
            jnp.sum(gq * shared, axis=0, keepdims=True),
            jnp.sum(gk * shared, axis=0, keepdims=True),
            jnp.sum(turned, axis=0, keepdims=True),
            jnp.zeros((1, D - 3 * Z), F32),
        ],
        axis=1,
    )
    gsp = ((gq * qg[...] + gk * kg[...]) * silu_slope(sp)).astype(BF16)
    grad_wsh[...] = mm_tn(mixed[...], gsp)
    put_rows(
        grad_skip,
        slice(None),
        (gm[...] + mm_nt(gsp, wsh[...])) * silu_slope(skip_pre[...]),
    )
    d = par[0]
    d2 = d * d
    d4 = d2 * d2
    d8 = d4 * d4
    q = d8 * d8
    tab[0] = q
    tab[1] = q * q
    tab[2] = q * q * q * q
    place = lax.broadcasted_iota(jnp.int32, (PIECES, LANES), 0)

    def body(i, carry):
        s = i // BLOCKS
        lane = lanes_of(i)
        ds = [spread(par[0, j : j + 1, lane]) for j in range(NDIM)]
        ad = [grad_skip[i % BLOCKS, piece_rows(s, PIECE - 1), :]] * NDIM
        for t in range(PIECE - 2, -1, -1):
            g = grad_skip[i % BLOCKS, piece_rows(s, t), :]
            for j in range(NDIM):
                ad[j] = ds[j] * ad[j] + g
        for j in range(NDIM):
            a = ad[j]
            for k, step in enumerate((1, 2, 4)):
                qm = spread(tab[k, j : j + 1, lane])
                a = a + qm * jnp.where(place < PIECES - step, pltpu.roll(a, PIECES - step, 0), 0.0)
            after[s, j, :, lane] = jnp.where(
                place < PIECES - 1, pltpu.roll(a, PIECES - 1, 0), 0.0
            )
            ends[s, j : j + 1, lane] = a[:1]
        return carry

    lax.fori_loop(0, seqs * BLOCKS, body, 0)


def sums_kernel(
    seqs,
    tok, normed, grad_skip, grad_normed, par, before, st_in, after, skip, gain2_row, misc,
    local, small, nf, pw,
):
    put_rows(nf, slice(None), normed[...].astype(F32))
    piece_powers(par, pw)
    small[...] = jnp.zeros_like(small)

    def body(i, carry):
        s = i // BLOCKS
        lane = lanes_of(i)
        k16 = lax.broadcasted_iota(jnp.int32, (PIECES, LANES), 0).astype(F32) * PIECE
        for j0 in range(0, NDIM, 8):
            row = [pl.ds(j0 + j, 1) for j in range(8)]
            ds = [spread(par[0, row[j], lane]) for j in range(8)]
            st, ta, q, r = [], [], [], []
            for j in range(8):
                e = pw[j0 + j, :, lane] * st_in[0, s, row[j], lane]
                st.append(before[0, s, j0 + j, :, lane] + e)
                ta.append(
                    before[1, s, j0 + j, :, lane]
                    + pw[j0 + j, :, lane] * st_in[1, s, row[j], lane]
                    + k16 * e / ds[j]
                )
                q.append(jnp.zeros((PIECES, LANES), F32))
                r.append(jnp.zeros((PIECES, LANES), F32))
            for t in range(PIECE):
                x = nf[i % BLOCKS, piece_rows(s, t), :]
                g = grad_skip[i % BLOCKS, piece_rows(s, t), :]
                for j in range(8):
                    ta[j] = ds[j] * ta[j] + st[j]
                    st[j] = ds[j] * st[j] + x
                    q[j] = q[j] + g * st[j]
                    r[j] = r[j] + g * ta[j]
            for j in range(8):
                small[pl.ds(j0 + j, 1), lane] += jnp.sum(q[j], axis=0, keepdims=True)
                small[pl.ds(NDIM + j0 + j, 1), lane] += jnp.sum(r[j], axis=0, keepdims=True)
        ds = [spread(par[0, pl.ds(j, 1), lane]) for j in range(NDIM)]
        ws = [
            spread(par[2, pl.ds(j, 1), lane] * par[3, pl.ds(j, 1), lane]) for j in range(NDIM)
        ]
        ad = [after[s, j, :, lane] for j in range(NDIM)]
        for t in range(PIECE - 1, -1, -1):
            g = grad_skip[i % BLOCKS, piece_rows(s, t), :]
            parts = [None, None]
            for j in range(NDIM):
                ad[j] = ds[j] * ad[j] + g
                term = ws[j] * ad[j]
                parts[j % 2] = term if parts[j % 2] is None else parts[j % 2] + term
            local[i % BLOCKS, piece_rows(s, t), :] = parts[0] + parts[1]
        return carry

    lax.fori_loop(0, seqs * BLOCKS, body, 0)
    gsk = jnp.zeros((1, D), F32)
    gn1 = jnp.zeros((1, D), F32)
    for s in range(seqs):
        xhat, _ = normalized(tok[s].astype(F32))
        g = get_rows(grad_skip, rows_of(s))
        direct = g * skip[...] + grad_normed[rows_of(s), :]
        gsk = gsk + jnp.sum(g * get_rows(nf, rows_of(s)), axis=0, keepdims=True)
        gn1 = gn1 + jnp.sum(direct * xhat, axis=0, keepdims=True)
        put_rows(local, rows_of(s), get_rows(local, rows_of(s)) + direct)
    small[2 * NDIM : 2 * NDIM + 1, :] = gsk
    small[2 * NDIM + 1 : 2 * NDIM + 2, :] = gn1
    small[2 * NDIM + 2 : 2 * NDIM + 3, :] = gain2_row[...]
    small[2 * NDIM + 3 : 2 * NDIM + 4, :] = misc[...]


def leave_kernel(seqs, levels, ids, tok, par, local, resid, gain, *refs):
    recvs, refs = refs[:levels], refs[levels:]
    grad_tokens, ad_in, pw, sm = refs
    place = ids[1]
    logd = par[1]
    w = par[2] * par[3]
    for s in range(seqs):
        a = jnp.zeros((NDIM, D), F32)
        for k in range(levels):
            low = jnp.bitwise_and(place, 1 << k) == 0
            off = jnp.bitwise_and(place, (1 << k) - 1)
            away = ((1 << k) - 1 - off).astype(F32) * float(CH)
            a = a + recvs[k][s].astype(F32) * jnp.where(low, jnp.exp(away * logd), 0.0)
        ad_in[s] = a * w
    k = (PIECES - 1 - lax.broadcasted_iota(jnp.int32, (PIECES, D), 0)).astype(F32) * PIECE
    for j in range(NDIM):
        pw[j] = jnp.exp(k * par[1, j : j + 1, :])

    def body(i, carry):
        s = i // BLOCKS
        lane = lanes_of(i)
        ds = [spread(par[0, pl.ds(j, 1), lane]) for j in range(NDIM)]
        ad = [pw[j, :, lane] * ad_in[s, pl.ds(j, 1), lane] for j in range(NDIM)]
        for t in range(PIECE - 1, -1, -1):
            parts = [None, None]
            for j in range(NDIM):
                ad[j] = ds[j] * ad[j]
                parts[j % 2] = ad[j] if parts[j % 2] is None else parts[j % 2] + ad[j]
            sm[i % BLOCKS, piece_rows(s, t), :] = parts[0] + parts[1]
        return carry

    lax.fori_loop(0, seqs * BLOCKS, body, 0)
    for s in range(seqs):
        xhat, scale = normalized(tok[s].astype(F32))
        grad = get_rows(local, rows_of(s)) + get_rows(sm, rows_of(s))
        grad_tokens[s] = (
            resid[rows_of(s), :] + norm_back(grad, xhat, scale, gain[...])
        ).astype(BF16)


def swap(value, axis, bit):
    count = lax.axis_size(axis)
    return lax.ppermute(value, axis, [(i, i ^ bit) for i in range(count)])


def bits_of(count):
    return [1 << k for k in range(count.bit_length() - 1)]


def has(index, bit):
    return jnp.bitwise_and(index, bit) > 0


def gathered(own, tp):
    pieces = {0: own}
    for bit in reversed(bits_of(tp)):
        for r in list(pieces):
            pieces[r ^ bit] = swap(pieces[r], "tp", bit)
    return [pieces[r] for r in range(tp)]


def add_low(a, b):
    return (a.astype(F32) + b.astype(F32)).astype(BF16)


def half_of(value, upper):
    half = value.shape[0] // 2
    return lax.dynamic_slice_in_dim(value, jnp.where(upper, half, 0), half, 0)


def joined(mine, other, upper):
    return jnp.where(
        upper,
        jnp.concatenate([other, mine], axis=0),
        jnp.concatenate([mine, other], axis=0),
    )


def summed(keep, send, tp, seq, place):
    total = add_low(keep, swap(send, "tp", 1))
    for bit in reversed(bits_of(tp)[1:]):
        half = total.shape[0] // 2
        total = add_low(total[:half], swap(total[half:], "tp", bit))
    total = total[0]
    for bit in bits_of(seq):
        upper = has(place, bit)
        other = swap(half_of(total, ~upper), "seq", bit)
        total = add_low(half_of(total, upper), other)
    for bit in reversed(bits_of(seq)):
        total = joined(total, swap(total, "seq", bit), has(place, bit))
    return total


def per_device(
    tokens,
    cotangent,
    valid_lengths,
    norm1_gain,
    ema_rate,
    ema_beta,
    ema_eta,
    ema_skip,
    w_shared,
    query_gain,
    key_gain,
    rel_bias,
    w_value,
    w_reset,
    w_update,
    w_hidden,
    u_hidden,
    norm2_gain,
    w_in,
    w_out,
):
    part = lax.axis_index("tp")
    place = lax.axis_index("seq")
    tp = lax.axis_size("tp")
    seq = lax.axis_size("seq")
    all_seqs, local_rows, _ = tokens.shape
    vb = w_value.shape[1]
    nb = D // tp
    index = place * tp + part
    traded = local_rows < CH
    lower = part % 2 == 0

    def trade(value):
        if not traded:
            return value
        other = swap(jnp.where(lower, value[1], value[0]), "tp", 1)
        mine = jnp.where(lower, value[0], value[1])
        return joined(mine, other, ~lower)[None]

    def trade_back(value):
        if not traded:
            return value
        first, second = value[0, :local_rows], value[0, local_rows:]
        other = swap(jnp.where(lower, second, first), "tp", 1)
        mine = jnp.where(lower, first, second)
        return jnp.where(lower, jnp.stack([mine, other]), jnp.stack([other, mine]))

    if traded:
        assert all_seqs == 2 and 2 * local_rows == CH
        seqs = 1
        stretch = index // 2
        lengths = jnp.where(lower, valid_lengths[0], valid_lengths[1])[None]
    else:
        assert local_rows == CH
        seqs = all_seqs
        stretch = index
        lengths = valid_lengths
    rows = seqs * CH
    ids = jnp.concatenate([jnp.stack([part, stretch]), lengths]).astype(jnp.int32)
    scan_bits = [("tp", b) for b in bits_of(tp)[int(traded) :]] + [
        ("seq", b) for b in bits_of(seq)
    ]
    levels = len(scan_bits)

    pack1 = jnp.concatenate([w_value, w_reset], axis=1)
    pack2 = jnp.concatenate([w_hidden, w_update, u_hidden], axis=0)
    pack3 = jnp.concatenate(
        [w_in, jnp.concatenate([w_out[:, k * vb : (k + 1) * vb] for k in range(D // vb)], axis=0)],
        axis=1,
    )
    w1 = gathered(pack1, tp)
    w2 = gathered(pack2, tp)
    w3 = gathered(pack3, tp)

    tok = trade(tokens)
    cot = trade(cotangent)
    gain1 = norm1_gain[None]
    gain2 = norm2_gain[None]
    skip = ema_skip[None]
    qg, kg, rb = query_gain[None], key_gain[None], rel_bias[None]

    normed, par, before, ends = call(
        functools.partial(enter_kernel, seqs),
        (
            shape((rows, D), BF16),
            shape((4, NDIM, D)),
            shape((2, seqs, NDIM, PIECES, D)),
            shape((2, seqs, NDIM, D)),
        ),
        [pltpu.VMEM((BLOCKS, rows, LANES), F32), pltpu.VMEM((6, NDIM, D), F32)],
        (tok, gain1, ema_rate, ema_beta, ema_eta),
        [VMEM] * 5,
        "enter",
        flops=20_000_000,
        moved=2_000_000,
    )

    logd = par[1]
    state = ends
    recvs = []
    for k, (axis, bit) in enumerate(scan_bits):
        other = swap(state.astype(BF16), axis, bit)
        recvs.append(other)
        if k + 1 < levels:
            upper = has(stretch, 1 << k)
            other = other.astype(F32)
            early = jnp.where(upper, other, state)
            late = jnp.where(upper, state, other)
            span = float(CH << k)
            power = jnp.exp(span * logd)
            slope = span * jnp.exp((span - 1.0) * logd)
            state = jnp.stack(
                [
                    power * early[0] + late[0],
                    power * early[1] + slope * early[0] + late[1],
                ]
            )

    (
        st_in, skip_pre, mixed, shared_pre, prob, values, value_pre, reset_pre, attended, gated,
        hidden_pre, update_pre, middle,
    ) = call(
        functools.partial(mix_kernel, seqs, tp, levels, 0),
        (
            shape((2, seqs, NDIM, D)),
            shape((rows, D)),
            shape((rows, D), BF16),
            shape((rows, Z)),
            shape((seqs, CH, CH)),
            shape((tp, rows, vb), BF16),
            shape((tp, rows, vb)),
            shape((tp, rows, vb)),
            shape((tp, rows, vb)),
            shape((tp, rows, vb), BF16),
            shape((rows, D)),
            shape((rows, D)),
            shape((rows, D)),
        ),
        [
            pltpu.VMEM((tp, D, 2 * vb), BF16),
            pltpu.VMEM((D, 2 * D), BF16),
            pltpu.VMEM((tp, vb, D), BF16),
            pltpu.VMEM((BLOCKS, rows, LANES), F32),
            pltpu.VMEM((BLOCKS, rows, LANES), F32),
            pltpu.VMEM((NDIM, PIECES, D), F32),
            pltpu.SemaphoreType.DMA((4 * tp,)),
        ],
        (ids, tok, normed, par, before, skip, w_shared, qg, kg, rb, *recvs, *w1, *w2),
        [SMEM] + [VMEM] * (9 + levels) + [ANY] * (2 * tp),
        "mix",
        flops=2 * rows * D * 4 * D * 2,
        moved=12_000_000,
    )

    out, keep3, send3, grad_hu, resid, grad_gain2 = call(
        functools.partial(ffn_kernel, seqs, tp),
        (
            shape((rows, D), BF16),
            shape((tp // 2, D, 2 * vb), BF16),
            shape((tp // 2, D, 2 * vb), BF16),
            shape((rows, 2 * D), BF16),
            shape((rows, D)),
            shape((1, D)),
        ),
        [
            pltpu.VMEM((tp, D, vb), BF16),
            pltpu.VMEM((tp, vb, D), BF16),
            pltpu.VMEM((rows, D), BF16),
            pltpu.VMEM((rows, D), BF16),
            pltpu.VMEM((rows, D), F32),
            pltpu.VMEM((rows, D), F32),
            pltpu.SemaphoreType.DMA((tp * (D // vb + 1),)),
        ],
        (ids, tok, cot, middle, hidden_pre, update_pre, gain2, *w3),
        [SMEM] + [VMEM] * 6 + [ANY] * tp,
        "ffn",
        flops=6 * rows * D * 4 * D,
        moved=8_000_000,
    )

    (
        keep2, send2, keep1, send1, grad_skip, grad_normed, after, back_ends, grad_wsh, misc,
    ) = call(
        functools.partial(back_kernel, seqs, tp),
        (
            shape((tp // 2, 2 * nb + vb, D), BF16),
            shape((tp // 2, 2 * nb + vb, D), BF16),
            shape((tp // 2, D, 2 * vb), BF16),
            shape((tp // 2, D, 2 * vb), BF16),
            shape((BLOCKS, rows, LANES)),
            shape((rows, D)),
            shape((seqs, NDIM, PIECES, D)),
            shape((seqs, NDIM, D)),
            shape((D, Z)),
            shape((1, D)),
        ),
        [
            pltpu.VMEM((tp, D, 2 * vb), BF16),
            pltpu.VMEM((D, 2 * D), BF16),
            pltpu.VMEM((tp, vb, D), BF16),
            pltpu.VMEM((D, 2 * D), F32),
            pltpu.VMEM((rows, D), F32),
            pltpu.VMEM((seqs, CH, CH), F32),
            pltpu.VMEM((3, NDIM, D), F32),
            pltpu.SemaphoreType.DMA((4 * tp,)),
        ],
        (
            ids, normed, mixed, skip_pre, shared_pre, prob, values, value_pre, reset_pre, attended,
            gated, grad_hu, par, w_shared, qg, kg, *w1, *w2,
        ),
        [SMEM] + [VMEM] * 15 + [ANY] * (2 * tp),
        "back",
        flops=4 * rows * D * 8 * D,
        moved=16_000_000,
    )

    local, small = call(
        functools.partial(sums_kernel, seqs),
        (shape((BLOCKS, rows, LANES)), shape((SMALL_ROWS, D))),
        [pltpu.VMEM((BLOCKS, rows, LANES), F32), pltpu.VMEM((NDIM, PIECES, D), F32)],
        (tok, normed, grad_skip, grad_normed, par, before, st_in, after, skip, grad_gain2, misc),
        [VMEM] * 11,
        "sums",
        flops=40_000_000,
        moved=5_000_000,
    )

    wide = grad_wsh.reshape(D // Z, D // (D // Z), Z).transpose(1, 0, 2).reshape(-1, D)
    sums = jnp.concatenate([wide, small], axis=0)
    adjoint = back_ends
    back_recvs = []

    def adjoint_after(k, other):
        upper = has(stretch, 1 << k)
        early = jnp.where(upper, other, adjoint)
        late = jnp.where(upper, adjoint, other)
        return early + jnp.exp(float(CH << k) * logd) * late

    level = 0
    for bit in bits_of(tp):
        upper = has(part, bit)
        send = half_of(sums, ~upper)
        if bit == 1:
            other = swap(send, "tp", bit)
            if not traded:
                got = swap(adjoint, "tp", bit)
                back_recvs.append(got)
                adjoint = adjoint_after(level, got)
                level += 1
        else:
            both = swap(
                jnp.concatenate([adjoint.reshape(-1, D), send], axis=0), "tp", bit
            )
            got = both[: seqs * NDIM].reshape(seqs, NDIM, D)
            other = both[seqs * NDIM :]
            back_recvs.append(got)
            adjoint = adjoint_after(level, got)
            level += 1
        sums = half_of(sums, upper) + other
    for bit in bits_of(seq):
        both = swap(jnp.concatenate([adjoint.reshape(-1, D), sums], axis=0), "seq", bit)
        got = both[: seqs * NDIM].reshape(seqs, NDIM, D)
        back_recvs.append(got)
        adjoint = adjoint_after(level, got)
        level += 1
        sums = sums + both[seqs * NDIM :]

    (grad_tokens,) = call(
        functools.partial(leave_kernel, seqs, levels),
        (shape((seqs, CH, D), BF16),),
        [
            pltpu.VMEM((seqs, NDIM, D), F32),
            pltpu.VMEM((NDIM, PIECES, D), F32),
            pltpu.VMEM((BLOCKS, rows, LANES), F32),
        ],
        (ids, tok, par, local, resid, gain1, *back_recvs),
        [SMEM] + [VMEM] * (5 + levels),
        "leave",
        flops=10_000_000,
        moved=3_000_000,
    )

    for bit in reversed(bits_of(tp)):
        sums = joined(sums, swap(sums, "tp", bit), has(part, bit))
    wide, small = sums[: D * Z // D], sums[D * Z // D :]
    grad_wsh = wide.reshape(-1, D // Z, Z).transpose(1, 0, 2).reshape(D, Z)
    inflow, eta = par[2], par[3]
    q_sum, r_sum = small[:NDIM], small[NDIM : 2 * NDIM]
    tail = small[2 * NDIM : 2 * NDIM + 4]
    root = jnp.sqrt(ema_rate * (2.0 - ema_rate))
    grad_ema_eta = (inflow * q_sum).T
    grad_inflow = (eta * q_sum).T
    grad_decay = (eta * inflow * r_sum).T
    grad_ema_rate = grad_inflow * ema_beta * (1.0 - ema_rate) / root - grad_decay
    grad_ema_beta = grad_inflow * root
    grad_norm1_gain = tail[1] + jnp.sum(inflow * eta * q_sum, axis=0) / norm1_gain

    g3 = summed(keep3, send3, tp, seq, place).astype(F32)
    g2 = summed(keep2, send2, tp, seq, place).astype(F32)
    g1 = summed(keep1, send1, tp, seq, place).astype(F32)
    return (
        trade_back(out.reshape(seqs, CH, D)),
        trade_back(grad_tokens),
        grad_norm1_gain,
        grad_ema_rate,
        grad_ema_beta,
        grad_ema_eta,
        tail[0],
        grad_wsh,
        tail[3, :Z],
        tail[3, Z : 2 * Z],
        tail[3, 2 * Z : 3 * Z],
        g1[:, :vb],
        g1[:, vb:],
        g2[nb : 2 * nb],
        g2[:nb],
        g2[2 * nb :],
        tail[2],
        g3[:, :vb],
        jnp.concatenate([g3[k * vb : (k + 1) * vb, vb:] for k in range(D // vb)], axis=1),
    )


def solution(mesh):
    rows = P(None, ("seq", "tp"), None)
    cols = P(None, "tp")
    tall = P("tp", None)
    whole = P()
    return jax.shard_map(
        per_device,
        mesh=mesh,
        in_specs=(rows, rows) + (whole,) * 10 + (cols, cols, tall, tall, tall, whole, cols, tall),
        out_specs=(rows, rows) + (whole,) * 9 + (cols, cols, tall, tall, tall, whole, cols, tall),
        check_vma=False,
    )
```

```python
import functools

import jax
import jax.numpy as jnp
from jax import lax
from jax.experimental import pallas as pl
from jax.experimental.pallas import tpu as pltpu
from jax.sharding import PartitionSpec as P

D = 512
Z = 128
NDIM = 16
CH = 128
PIECE = 16
PIECES = CH // PIECE
LANES = 128
BLOCKS = D // LANES
EPS = 1e-05
F32 = jnp.float32
BF16 = jnp.bfloat16
SMALL_ROWS = 64

VMEM = pl.BlockSpec(memory_space=pltpu.VMEM)
SMEM = pl.BlockSpec(memory_space=pltpu.SMEM)
ANY = pl.BlockSpec(memory_space=pl.ANY)


def sigmoid(v):
    return 0.5 * jnp.tanh(0.5 * v) + 0.5


def silu(v):
    return v * sigmoid(v)


def silu_slope(v):
    s = sigmoid(v)
    return s * (1.0 + v * (1.0 - s))


def mm(a, b):
    return jnp.dot(a, b, preferred_element_type=F32)


def mm_nt(a, b):
    return lax.dot_general(a, b, (((1,), (1,)), ((), ())), preferred_element_type=F32)


def mm_tn(a, b):
    return lax.dot_general(a, b, (((0,), (0,)), ((), ())), preferred_element_type=F32)


def normalized(v):
    center = v - jnp.mean(v, axis=-1, keepdims=True)
    scale = lax.rsqrt(jnp.mean(center * center, axis=-1, keepdims=True) + EPS)
    return center * scale, scale


def norm_back(grad, xhat, scale, gain):
    full = grad * gain
    return scale * (
        full
        - jnp.mean(full, axis=-1, keepdims=True)
        - xhat * jnp.mean(full * xhat, axis=-1, keepdims=True)
    )


def rows_of(s):
    return pl.ds(s * CH, CH)


def lanes_of(i):
    return pl.ds(pl.multiple_of((i % BLOCKS) * LANES, LANES), LANES)


def spread(row):
    return jnp.broadcast_to(row, (PIECES, LANES))


def piece_rows(s, t):
    return pl.ds(s * CH + t, PIECES, stride=PIECE)


def put_rows(ref, rows, value):
    for b in range(BLOCKS):
        ref[b, rows, :] = value[:, b * LANES : (b + 1) * LANES]


def get_rows(ref, rows):
    return jnp.concatenate([ref[b, rows, :] for b in range(BLOCKS)], axis=1)


def call(body, out, scratch, operands, specs, name, limit=2, outs=None):
    return pl.pallas_call(
        body,
        out_shape=out,
        in_specs=specs,
        out_specs=outs or jax.tree.map(lambda _: VMEM, out),
        scratch_shapes=scratch,
        name=name,
        compiler_params=pltpu.CompilerParams(vmem_limit_bytes=limit * 1024 * 1024),
    )(*operands)


def shape(dims, dtype=F32):
    return jax.ShapeDtypeStruct(dims, dtype)


def enter_kernel(seqs, *refs):
    far, refs = refs[:5], refs[5:]
    w_value, w_reset, w_hidden, w_update, u_hidden, w_in, w_out = refs[:7]
    normed, par, before, ends, low, p1, p2, p3, h1, h2, h3 = refs[7:18]
    tok, gain, rate, beta, eta, nf, tab, sems = refs[18:]
    copies = []

    def add(source, target):
        copies.append(pltpu.make_async_copy(source, target, sems.at[len(copies)]))

    for pair in zip(far, (tok, gain, rate, beta, eta)):
        add(*pair)
    vb, nb, cut = w_value.shape[1], w_hidden.shape[0], D // 2
    at = pl.ds(pl.multiple_of(jnp.bitwise_and(lax.axis_index("seq"), 1) * cut, cut), cut)
    for i, w in enumerate((w_value, w_reset)):
        lane = pl.ds(i * vb, vb)
        add(w.at[at, :], h1.at[:, lane])
        add(w, p1.at[:, lane])
    top = 0
    for w in (w_hidden, w_update, u_hidden):
        row = pl.ds(top, w.shape[0])
        add(w.at[:, at], h2.at[row, :])
        add(w, p2.at[row, :])
        top += w.shape[0]
    add(w_in.at[at, :], h3.at[:, pl.ds(0, vb)])
    add(w_in, p3.at[:, pl.ds(0, vb)])
    for k in range(D // vb):
        row = pl.ds(k * vb, vb)
        add(w_out.at[:, row], p3.at[row, pl.ds(vb, vb)])
        if k < cut // vb:
            first = pl.multiple_of(jnp.bitwise_and(lax.axis_index("seq"), 1) * cut + k * vb, vb)
            add(w_out.at[:, pl.ds(first, vb)], h3.at[row, pl.ds(vb, vb)])
    for c in copies:
        c.start()
    for c in copies[:5]:
        c.wait()
    r = rate[...]
    d = 1.0 - r
    par[0] = d
    par[1] = jnp.log(d)
    par[2] = jnp.sqrt(r * (2.0 - r)) * beta[...]
    par[3] = eta[...]
    d2 = d * d
    d4 = d2 * d2
    d8 = d4 * d4
    d15 = d8 * d4 * d2 * d
    q = d8 * d8
    tab[0] = q
    tab[1] = 16.0 * d15
    tab[2] = q * q
    tab[3] = 32.0 * q * d15
    tab[4] = q * q * q * q
    tab[5] = 64.0 * q * q * q * d15
    for s in range(seqs):
        xhat, _ = normalized(tok[s].astype(F32))
        scaled = (xhat * gain[...]).astype(BF16)
        normed[rows_of(s), :] = scaled
        put_rows(nf, rows_of(s), scaled.astype(F32))
    place = lax.broadcasted_iota(jnp.int32, (PIECES, LANES), 0)

    def body(i, carry):
        s = i // BLOCKS
        lane = lanes_of(i)
        xs = [nf[i % BLOCKS, piece_rows(s, t), :] for t in range(PIECE)]
        for j0 in range(0, NDIM, 8):
            ds = [spread(par[0, j0 + j : j0 + j + 1, lane]) for j in range(8)]
            st = [xs[0]] * 8
            ta = [jnp.zeros((PIECES, LANES), F32)] * 8
            for t in range(1, PIECE):
                for j in range(8):
                    ta[j] = ds[j] * ta[j] + st[j]
                    st[j] = ds[j] * st[j] + xs[t]
            for j in range(8):
                a, b = st[j], ta[j]
                for k, step in enumerate((1, 2, 4)):
                    qm = spread(tab[2 * k, j0 + j : j0 + j + 1, lane])
                    rm = spread(tab[2 * k + 1, j0 + j : j0 + j + 1, lane])
                    sa = jnp.where(place >= step, pltpu.roll(a, step, 0), 0.0)
                    sb = jnp.where(place >= step, pltpu.roll(b, step, 0), 0.0)
                    b = b + qm * sb + rm * sa
                    a = a + qm * sa
                before[0, s, j0 + j, :, lane] = jnp.where(place >= 1, pltpu.roll(a, 1, 0), 0.0)
                before[1, s, j0 + j, :, lane] = jnp.where(place >= 1, pltpu.roll(b, 1, 0), 0.0)
                ends[0, s, j0 + j : j0 + j + 1, lane] = a[PIECES - 1 :]
                ends[1, s, j0 + j : j0 + j + 1, lane] = b[PIECES - 1 :]
        return carry

    lax.fori_loop(0, seqs * BLOCKS, body, 0)
    low[...] = ends[...].astype(BF16)
    for c in copies[5:]:
        c.wait()


def piece_powers(par, pw):
    k = lax.broadcasted_iota(jnp.int32, (PIECES, D), 0).astype(F32) * PIECE
    for j in range(NDIM):
        pw[j] = jnp.exp(k * par[1, j : j + 1, :])


def take_weights(refs, tp, first, second):
    top = tp // 2
    near = [refs[r * first : (r + 1) * first] for r in range(top)]
    refs = refs[top * first :]
    far = [refs[r * second : (r + 1) * second] for r in range(top)]
    return near, far, refs[top * second :]


def gate_copies(tp, ids, near, far, w1, w2, sems):
    top, cut = tp // 2, D // 2
    upper = jnp.bitwise_and(ids[1], 1)
    copies = []

    def add(source, target):
        copies.append(pltpu.make_async_copy(source, target, sems.at[len(copies)]))

    for r in range(top):
        add(near[r][0], w1.at[r])
        add(near[r][1], w2.at[r])
        mine1, other1, mine2, other2 = far[r]
        for part1, part2, at in ((mine1, mine2, upper), (other1, other2, 1 - upper)):
            at = pl.ds(pl.multiple_of(at * cut, cut), cut)
            add(part1, w1.at[top + r, at, :])
            add(part2, w2.at[top + r, :, at])
    for c in copies:
        c.start()
    return copies


def gate_rows(tp, me, w2, whu):
    nb = D // tp
    for r in range(tp):
        row = pl.ds(pl.multiple_of(jnp.bitwise_xor(me, r) * nb, nb), nb)
        whu[row, pl.ds(0, D)] = w2[r, pl.ds(0, nb), :]
        whu[row, pl.ds(D, D)] = w2[r, pl.ds(nb, nb), :]


def look_kernel(
    seqs, hops, ids, normed, par, before, skip, wsh, qg, kg, rb, *refs
):
    recvs, refs = refs[: len(hops)], refs[len(hops) :]
    st_in, skip_pre, mixed, shared_pre, prob, nf, sm, pw = refs
    place = ids[2]
    put_rows(nf, slice(None), normed[...].astype(F32))
    piece_powers(par, pw)
    logd = par[1]
    dinv = 1.0 / par[0]
    for s in range(seqs):
        a = jnp.zeros((NDIM, D), F32)
        b = jnp.zeros((NDIM, D), F32)
        for (shift, k), got in zip(hops, recvs):
            end = jnp.left_shift(jnp.bitwise_xor(jnp.right_shift(place, shift), k) + 1, shift)
            off = (place - end).astype(F32) * float(CH)
            power = jnp.where(place >= end, jnp.exp(jnp.maximum(off, 0.0) * logd), 0.0)
            oa = got[0, s].astype(F32) * power
            b = b + got[1, s].astype(F32) * power + off * oa * dinv
            a = a + oa
        st_in[0, s] = a
        st_in[1, s] = b

    def ema(i, carry):
        s = i // BLOCKS
        lane = lanes_of(i)
        row = [pl.ds(j, 1) for j in range(NDIM)]
        ds = [spread(par[0, row[j], lane]) for j in range(NDIM)]
        ws = [spread(par[2, row[j], lane] * par[3, row[j], lane]) for j in range(NDIM)]
        st = [
            before[0, s, j, :, lane] + pw[j, :, lane] * st_in[0, s, row[j], lane]
            for j in range(NDIM)
        ]
        for t in range(PIECE):
            x = nf[i % BLOCKS, piece_rows(s, t), :]
            parts = [None, None]
            for j in range(NDIM):
                st[j] = ds[j] * st[j] + x
                term = ws[j] * st[j]
                parts[j % 2] = term if parts[j % 2] is None else parts[j % 2] + term
            sm[i % BLOCKS, piece_rows(s, t), :] = parts[0] + parts[1]
        return carry

    lax.fori_loop(0, seqs * BLOCKS, ema, 0)
    for s in range(seqs):
        pre = get_rows(sm, rows_of(s)) + skip[...] * get_rows(nf, rows_of(s))
        skip_pre[rows_of(s), :] = pre
        mixed[rows_of(s), :] = silu(pre).astype(BF16)
    sp = mm(mixed[...], wsh[...])
    shared_pre[...] = sp
    shared = silu(sp)
    query = (shared * qg[...]).astype(BF16)
    keys = (shared * kg[...]).astype(BF16)
    t_at = lax.broadcasted_iota(jnp.int32, (CH, CH), 0)
    s_at = lax.broadcasted_iota(jnp.int32, (CH, CH), 1)
    bias_t = jnp.broadcast_to(rb[...], (CH, CH))
    for bit in range(7):
        bias_t = jnp.where(
            jnp.bitwise_and(t_at, 1 << bit) > 0, pltpu.roll(bias_t, 1 << bit, 1), bias_t
        )
    bias = bias_t.T
    for s in range(seqs):
        raw = mm_nt(query[s * CH : (s + 1) * CH], keys[s * CH : (s + 1) * CH]) * Z ** (-0.5)
        live = (place * CH + s_at) < ids[3 + s]
        allowed = (s_at <= t_at) & (live | (s_at == t_at))
        masked = jnp.where(allowed, raw + bias, -1e30)
        top = jnp.max(masked, axis=-1, keepdims=True)
        weights = jnp.where(allowed, jnp.exp(masked - top), 0.0)
        prob[s] = weights / jnp.sum(weights, axis=-1, keepdims=True)


def mix_kernel(seqs, tp, ids, tok, normed, mixed, prob, *refs):
    near, far, refs = take_weights(refs, tp, 2, 4)
    (
        values, value_pre, reset_pre, attended, gated, hidden_pre, update_pre, middle,
        w1, w2, whu, sems,
    ) = refs
    vb = values.shape[2]
    nb = D // tp
    copies = gate_copies(tp, ids, near, far, w1, w2, sems)
    for c in copies:
        c.wait()
    gate_rows(tp, ids[0], w2, whu)
    hu = mm(mixed[...], whu[...])
    hidden_pre[...] = hu[:, :D]
    update_pre[...] = hu[:, D:]

    def block(r, carry):
        vp = mm(normed[...], w1[r, :, :vb])
        value_pre[r] = vp
        v = silu(vp).astype(BF16)
        values[r] = v
        rp = mm(mixed[...], w1[r, :, vb:])
        reset_pre[r] = rp
        gate = silu(rp)
        for s in range(seqs):
            att = mm(prob[s].astype(BF16), v[s * CH : (s + 1) * CH])
            attended[r, rows_of(s), :] = att
            gated[r, rows_of(s), :] = (gate[s * CH : (s + 1) * CH] * att).astype(BF16)
        hidden_pre[...] += mm(gated[r], w2[r, pl.ds(2 * nb, vb), :])
        return carry

    lax.fori_loop(0, tp, block, 0)
    for s in range(seqs):
        x = tok[s].astype(F32)
        middle[rows_of(s), :] = x + sigmoid(update_pre[rows_of(s), :]) * (
            silu(hidden_pre[rows_of(s), :]) - x
        )


def ffn_kernel(seqs, tp, ids, tok, cot, middle, hidden_pre, update_pre, gain2, *refs):
    near, far, refs = take_weights(refs, tp, 1, 2)
    (
        out, keep, send, grad_hu, resid, grad_gain2,
        w3, n2, lg, acc, gn2, sems,
    ) = refs
    vb = w3.shape[2] // 2
    top, half = tp // 2, D // 2
    cuts = D // vb
    upper = jnp.bitwise_and(ids[1], 1)
    copies = []

    def add(source, target):
        copies.append(pltpu.make_async_copy(source, target, sems.at[len(copies)]))

    for r in range(top):
        add(near[r][0], w3.at[r])
        for part, at in zip(far[r], (upper, 1 - upper)):
            add(part, w3.at[top + r, pl.ds(pl.multiple_of(at * half, half), half), :])
    for c in copies:
        c.start()
    place = ids[2]
    xhat, scale = normalized(middle[...])
    n2[...] = (xhat * gain2[...]).astype(BF16)
    at = lax.broadcasted_iota(jnp.int32, (CH, D), 0) + place * CH
    for s in range(seqs):
        lg[rows_of(s), :] = jnp.where(at < ids[3 + s], cot[s].astype(F32), 0.0).astype(BF16)
    acc[...] = jnp.zeros_like(acc)
    gn2[...] = jnp.zeros_like(gn2)
    for c in copies:
        c.wait()

    def block(h, carry):
        for odd in range(2):
            r = 2 * h + odd
            grads = (keep, send)[odd]
            pre = mm(n2[...], w3[r, :, :vb])
            inner = silu(pre).astype(BF16)
            back = None
            for k in range(cuts):
                cols = slice(k * vb, (k + 1) * vb)
                w_out = w3[r, cols, vb:]
                acc[:, cols] += mm(inner, w_out)
                term = mm_nt(lg[:, cols], w_out)
                back = term if back is None else back + term
            gip = (back * silu_slope(pre)).astype(BF16)
            gn2[...] += mm_nt(gip, w3[r, :, :vb])
            grads[h, :, :vb] = mm_tn(n2[...], gip).astype(BF16)
            gwo = mm_tn(inner, lg[...]).astype(BF16)
            for k in range(cuts):
                grads[h, k * vb : (k + 1) * vb, vb:] = gwo[:, k * vb : (k + 1) * vb]
        return carry

    lax.fori_loop(0, tp // 2, block, 0)
    mid = middle[...]
    out[...] = (mid + acc[...]).astype(BF16)
    grad = gn2[...]
    grad_gain2[...] = jnp.sum(grad * xhat, axis=0, keepdims=True)
    gm = lg[...].astype(F32) + norm_back(grad, xhat, scale, gain2[...])
    for s in range(seqs):
        x = tok[s].astype(F32)
        g = gm[s * CH : (s + 1) * CH]
        hp = hidden_pre[rows_of(s), :]
        update = sigmoid(update_pre[rows_of(s), :])
        grad_hu[rows_of(s), :D] = (g * update * silu_slope(hp)).astype(BF16)
        grad_hu[rows_of(s), D:] = (g * (silu(hp) - x) * update * (1.0 - update)).astype(BF16)
        resid[rows_of(s), :] = g * (1.0 - update)


def gates_kernel(tp, ids, mixed, gated, grad_hu, keep2, send2, ghu):
    nb = D // tp
    vb = gated.shape[2]
    wide = 2 * vb
    me = ids[0]
    ghu[...] = mm_tn(mixed[...], grad_hu[...])

    def block(h, carry):
        for odd in range(2):
            r = 2 * h + odd
            g2 = (keep2, send2)[odd]
            row = pl.ds(pl.multiple_of(jnp.bitwise_xor(me, r) * nb, nb), nb)
            gu = mm_tn(gated[r], grad_hu[:, :D]).astype(BF16)
            for k in range(D // wide):
                top = k * (2 * nb + vb)
                g2[h, pl.ds(top, nb), :] = ghu[row, pl.ds(k * wide, wide)].astype(BF16)
                g2[h, pl.ds(top + nb, nb), :] = ghu[row, pl.ds(D + k * wide, wide)].astype(BF16)
                g2[h, pl.ds(top + 2 * nb, vb), :] = gu[:, k * wide : (k + 1) * wide]
        return carry

    lax.fori_loop(0, tp // 2, block, 0)


def back_kernel(
    seqs, tp,
    ids, normed, mixed, skip_pre, shared_pre, prob, values, value_pre, reset_pre, attended,
    grad_hu, par, wsh, qg, kg, *refs,
):
    near, far, refs = take_weights(refs, tp, 2, 4)
    (
        keep1, send1, grad_skip, grad_normed, after, ends, grad_wsh, misc,
        w1, w2, whu, gm, gp, tab, sems,
    ) = refs
    vb = values.shape[2]
    nb = D // tp
    me = ids[0]
    copies = gate_copies(tp, ids, near, far, w1, w2, sems)
    gp[...] = jnp.zeros_like(gp)
    grad_normed[...] = jnp.zeros_like(grad_normed)
    for c in copies:
        c.wait()
    gate_rows(tp, me, w2, whu)
    gm[...] = mm_nt(grad_hu[...], whu[...])

    def block(h, carry):
        for odd in range(2):
            r = 2 * h + odd
            g1 = (keep1, send1)[odd]
            gg = mm_nt(grad_hu[:, :D], w2[r, pl.ds(2 * nb, vb), :])
            rp = reset_pre[r]
            sig = sigmoid(rp)
            ga = (gg * (rp * sig)).astype(BF16)
            grp = (gg * attended[r] * (sig * (1.0 + rp * (1.0 - sig)))).astype(BF16)
            g1[h, :, vb:] = mm_tn(mixed[...], grp).astype(BF16)
            gm[...] += mm_nt(grp, w1[r, :, vb:])
            gvs = []
            for s in range(seqs):
                part = ga[s * CH : (s + 1) * CH]
                gvs.append(mm_tn(prob[s].astype(BF16), part))
                gp[s] += mm_nt(part, values[r, rows_of(s), :])
            gv = jnp.concatenate(gvs, axis=0) if seqs > 1 else gvs[0]
            gvp = (gv * silu_slope(value_pre[r])).astype(BF16)
            g1[h, :, :vb] = mm_tn(normed[...], gvp).astype(BF16)
            grad_normed[...] += mm_nt(gvp, w1[r, :, :vb])
        return carry

    lax.fori_loop(0, tp // 2, block, 0)
    sp = shared_pre[...]
    shared = silu(sp)
    query = (shared * qg[...]).astype(BF16)
    keys = (shared * kg[...]).astype(BF16)
    total = jnp.zeros((CH, CH), F32)
    gqs = []
    gks = []
    for s in range(seqs):
        pr = prob[s]
        low = (pr * (gp[s] - jnp.sum(pr * gp[s], axis=-1, keepdims=True))).astype(BF16)
        total = total + low.astype(F32)
        gqs.append(mm(low, keys[s * CH : (s + 1) * CH]) * Z ** (-0.5))
        gks.append(mm_tn(low, query[s * CH : (s + 1) * CH]) * Z ** (-0.5))
    gq = jnp.concatenate(gqs, axis=0) if seqs > 1 else gqs[0]
    gk = jnp.concatenate(gks, axis=0) if seqs > 1 else gks[0]
    turned = total.T
    s_at = lax.broadcasted_iota(jnp.int32, (CH, CH), 0)
    for bit in range(7):
        turned = jnp.where(
            jnp.bitwise_and(s_at, 1 << bit) > 0, pltpu.roll(turned, CH - (1 << bit), 1), turned
        )
    misc[...] = jnp.concatenate(
        [
            jnp.sum(gq * shared, axis=0, keepdims=True),
            jnp.sum(gk * shared, axis=0, keepdims=True),
            jnp.sum(turned, axis=0, keepdims=True),
            jnp.zeros((1, D - 3 * Z), F32),
        ],
        axis=1,
    )
    gsp = ((gq * qg[...] + gk * kg[...]) * silu_slope(sp)).astype(BF16)
    grad_wsh[...] = mm_tn(mixed[...], gsp)
    put_rows(
        grad_skip,
        slice(None),
        (gm[...] + mm_nt(gsp, wsh[...])) * silu_slope(skip_pre[...]),
    )
    d = par[0]
    d2 = d * d
    d4 = d2 * d2
    d8 = d4 * d4
    q = d8 * d8
    tab[0] = q
    tab[1] = q * q
    tab[2] = q * q * q * q
    place = lax.broadcasted_iota(jnp.int32, (PIECES, LANES), 0)

    def body(i, carry):
        s = i // BLOCKS
        lane = lanes_of(i)
        ds = [spread(par[0, j : j + 1, lane]) for j in range(NDIM)]
        ad = [grad_skip[i % BLOCKS, piece_rows(s, PIECE - 1), :]] * NDIM
        for t in range(PIECE - 2, -1, -1):
            g = grad_skip[i % BLOCKS, piece_rows(s, t), :]
            for j in range(NDIM):
                ad[j] = ds[j] * ad[j] + g
        for j in range(NDIM):
            a = ad[j]
            for k, step in enumerate((1, 2, 4)):
                qm = spread(tab[k, j : j + 1, lane])
                a = a + qm * jnp.where(place < PIECES - step, pltpu.roll(a, PIECES - step, 0), 0.0)
            after[s, j, :, lane] = jnp.where(
                place < PIECES - 1, pltpu.roll(a, PIECES - 1, 0), 0.0
            )
            ends[s, j : j + 1, lane] = a[:1]
        return carry

    lax.fori_loop(0, seqs * BLOCKS, body, 0)


def sums_kernel(
    seqs,
    ids, tok, normed, grad_skip, grad_normed, par, before, st_in, skip, gain2_row, misc, grad_wsh,
    keep, send, table, nf, pw,
):
    put_rows(nf, slice(None), normed[...].astype(F32))
    piece_powers(par, pw)
    count = D // (D // Z)
    small = table.at[count:, :]
    small[...] = jnp.zeros_like(small)
    for k in range(D // Z):
        table[:count, k * Z : (k + 1) * Z] = grad_wsh[k * count : (k + 1) * count, :]

    def body(i, carry):
        s = i // BLOCKS
        lane = lanes_of(i)
        k16 = lax.broadcasted_iota(jnp.int32, (PIECES, LANES), 0).astype(F32) * PIECE
        for j0 in range(0, NDIM, 8):
            row = [pl.ds(j0 + j, 1) for j in range(8)]
            ds = [spread(par[0, row[j], lane]) for j in range(8)]
            st, ta, q, r = [], [], [], []
            for j in range(8):
                e = pw[j0 + j, :, lane] * st_in[0, s, row[j], lane]
                st.append(before[0, s, j0 + j, :, lane] + e)
                ta.append(
                    before[1, s, j0 + j, :, lane]
                    + pw[j0 + j, :, lane] * st_in[1, s, row[j], lane]
                    + k16 * e / ds[j]
                )
                q.append(jnp.zeros((PIECES, LANES), F32))
                r.append(jnp.zeros((PIECES, LANES), F32))
            for t in range(PIECE):
                x = nf[i % BLOCKS, piece_rows(s, t), :]
                g = grad_skip[i % BLOCKS, piece_rows(s, t), :]
                for j in range(8):
                    ta[j] = ds[j] * ta[j] + st[j]
                    st[j] = ds[j] * st[j] + x
                    q[j] = q[j] + g * st[j]
                    r[j] = r[j] + g * ta[j]
            for j in range(8):
                small[pl.ds(j0 + j, 1), lane] += jnp.sum(q[j], axis=0, keepdims=True)
                small[pl.ds(NDIM + j0 + j, 1), lane] += jnp.sum(r[j], axis=0, keepdims=True)
        return carry

    lax.fori_loop(0, seqs * BLOCKS, body, 0)
    gsk = jnp.zeros((1, D), F32)
    gn1 = jnp.zeros((1, D), F32)
    for s in range(seqs):
        xhat, _ = normalized(tok[s].astype(F32))
        g = get_rows(grad_skip, rows_of(s))
        direct = g * skip[...] + grad_normed[rows_of(s), :]
        gsk = gsk + jnp.sum(g * get_rows(nf, rows_of(s)), axis=0, keepdims=True)
        gn1 = gn1 + jnp.sum(direct * xhat, axis=0, keepdims=True)
    small[2 * NDIM : 2 * NDIM + 1, :] = gsk
    small[2 * NDIM + 1 : 2 * NDIM + 2, :] = gn1
    small[2 * NDIM + 2 : 2 * NDIM + 3, :] = gain2_row[...]
    small[2 * NDIM + 3 : 2 * NDIM + 4, :] = misc[...]
    half = keep.shape[0]
    mine = jnp.bitwise_and(ids[0], 1) * half
    keep[...] = table[pl.ds(pl.multiple_of(mine, 8), half), :]
    send[...] = table[pl.ds(pl.multiple_of(half - mine, 8), half), :]


def pair_kernel(bit, ids, mine, other, out):
    half = mine.shape[0]
    upper = jnp.where(jnp.bitwise_and(ids[0], bit) > 0, half, 0)
    out[pl.ds(pl.multiple_of(upper, 8), half), :] = mine[...]
    out[pl.ds(pl.multiple_of(half - upper, 8), half), :] = other[...]


def finish_kernel(
    ids, par, rate, beta, gain, mine, other,
    grad_gain, grad_rate, grad_beta, grad_eta, grad_skip, grad_wsh, grad_qg, grad_kg, grad_rb,
    grad_gain2, table,
):
    pair_kernel(1, ids, mine, other, table)
    count = D // (D // Z)
    for k in range(D // Z):
        grad_wsh[k * count : (k + 1) * count, :] = table[:count, k * Z : (k + 1) * Z]
    small = table.at[count:, :]
    inflow, eta, r = par[2], par[3], rate[...]
    root = jnp.sqrt(r * (2.0 - r))
    q_sum = small[:NDIM, :]
    grad_inflow = eta * q_sum
    grad_decay = eta * inflow * small[NDIM : 2 * NDIM, :]
    grad_rate[...] = grad_inflow * beta[...] * (1.0 - r) / root - grad_decay
    grad_beta[...] = grad_inflow * root
    grad_eta[...] = inflow * q_sum
    row = [small[2 * NDIM + i : 2 * NDIM + i + 1, :] for i in range(4)]
    grad_skip[...] = row[0]
    grad_gain[...] = row[1] + jnp.sum(inflow * grad_inflow, axis=0, keepdims=True) / gain[...]
    grad_gain2[...] = row[2]
    grad_qg[...] = row[3][:, :Z]
    grad_kg[...] = row[3][:, Z : 2 * Z]
    grad_rb[...] = row[3][:, 2 * Z : 3 * Z]


def leave_kernel(
    seqs, tops, ids, tok, par, grad_skip, grad_normed, behind, resid, gain, skip, *refs
):
    levels = len(tops)
    recvs, refs = refs[:levels], refs[levels:]
    grad_tokens, ad_in, pw, sm = refs
    place = ids[2]
    logd = par[1]
    gots = [get_wide(recvs[k], tops[k], seqs * NDIM) for k in range(levels)]
    for s in range(seqs):
        a = jnp.zeros((NDIM, D), F32)
        for k in range(levels):
            low = jnp.bitwise_and(place, 1 << k) == 0
            off = jnp.bitwise_and(place, (1 << k) - 1)
            away = ((1 << k) - 1 - off).astype(F32) * float(CH)
            got = gots[k][s * NDIM : (s + 1) * NDIM]
            a = a + got * jnp.where(low, jnp.exp(away * logd), 0.0)
        ad_in[s] = a
    k = (PIECES - 1 - lax.broadcasted_iota(jnp.int32, (PIECES, D), 0)).astype(F32) * PIECE
    for j in range(NDIM):
        pw[j] = jnp.exp(k * par[1, j : j + 1, :])

    def body(i, carry):
        s = i // BLOCKS
        lane = lanes_of(i)
        row = [pl.ds(j, 1) for j in range(NDIM)]
        ds = [spread(par[0, row[j], lane]) for j in range(NDIM)]
        ws = [spread(par[2, row[j], lane] * par[3, row[j], lane]) for j in range(NDIM)]
        ad = [
            behind[s, j, :, lane] + pw[j, :, lane] * ad_in[s, row[j], lane] for j in range(NDIM)
        ]
        for t in range(PIECE - 1, -1, -1):
            g = grad_skip[i % BLOCKS, piece_rows(s, t), :]
            parts = [None, None]
            for j in range(NDIM):
                ad[j] = ds[j] * ad[j] + g
                term = ws[j] * ad[j]
                parts[j % 2] = term if parts[j % 2] is None else parts[j % 2] + term
            sm[i % BLOCKS, piece_rows(s, t), :] = parts[0] + parts[1]
        return carry

    lax.fori_loop(0, seqs * BLOCKS, body, 0)
    for s in range(seqs):
        xhat, scale = normalized(tok[s].astype(F32))
        grad = (
            get_rows(sm, rows_of(s))
            + get_rows(grad_skip, rows_of(s)) * skip[...]
            + grad_normed[rows_of(s), :]
        )
        grad_tokens[s] = (
            resid[rows_of(s), :] + norm_back(grad, xhat, scale, gain[...])
        ).astype(BF16)


def hop_kernel(seqs, shift, count, ids, par, state, *refs):
    others, (total, low) = refs[: count - 1], refs[count - 1 :]
    mine = jnp.bitwise_and(jnp.right_shift(ids[2], shift), count - 1)
    logd = par[1]
    sums = [[None, None] for _ in range(seqs)]
    for k in range(count):
        after = (count - 1 - jnp.bitwise_xor(mine, k)).astype(F32) * float(CH << shift)
        power = jnp.exp(after * logd)
        slope = after * jnp.exp((after - 1.0) * logd)
        for s in range(seqs):
            a, b = (state[0, s], state[1, s]) if k == 0 else (
                others[k - 1][0, s].astype(F32), others[k - 1][1, s].astype(F32)
            )
            a, b = power * a, power * b + slope * a
            sums[s] = [a, b] if k == 0 else [sums[s][0] + a, sums[s][1] + b]
    for s in range(seqs):
        for i in range(2):
            total[i, s] = sums[s][i]
            low[i, s] = sums[s][i].astype(BF16)


def put_wide(ref, top, value):
    wide = ref.shape[1]
    count = value.shape[0]
    for k in range(D // wide):
        ref[pl.ds(top + k * count, count), :] = value[:, k * wide : (k + 1) * wide].astype(ref.dtype)


def get_wide(ref, top, count):
    wide = ref.shape[1]
    runs = [ref[pl.ds(top + k * count, count), :].astype(F32) for k in range(D // wide)]
    return jnp.concatenate(runs, axis=1) if len(runs) > 1 else runs[0]


def first_back_hop(seqs, joins, ids, par, own, other, sums, got, out, keep, payload):
    rows = seqs * NDIM
    fold_lanes = D // payload.shape[1]
    if joins:
        join_adjoint(seqs, 0, ids, par, own, other[...], out)
    else:
        out[...] = own[...]
    put_wide(payload, 0, out[...])
    half = keep.shape[0]
    upper = jnp.where(jnp.bitwise_and(ids[0], 2) > 0, half, 0)
    mine = pl.ds(pl.multiple_of(upper, 8), half)
    theirs = pl.ds(pl.multiple_of(half - upper, 8), half)
    keep[...] = sums[mine, :] + got[mine, :]
    put_wide(payload, rows * fold_lanes, sums[theirs, :] + got[theirs, :])


def join_adjoint(seqs, level, ids, par, own, got, out):
    upper = jnp.bitwise_and(ids[2], 1 << level) > 0
    power = jnp.exp(float(CH << level) * par[1])
    for s in range(seqs):
        row = slice(s * NDIM, (s + 1) * NDIM)
        early = jnp.where(upper, got[row], own[row, :])
        late = jnp.where(upper, own[row, :], got[row])
        out[row, :] = early + power * late


def chain_hop(seqs, level, split, halved, top, ids, par, own, kept, sent, other, out, keep, payload, base):
    rows = seqs * NDIM
    lanes = D // other.shape[1]
    if out is not None:
        join_adjoint(seqs, level, ids, par, own, get_wide(other, top, rows), out)
        put_wide(payload, base, out[...])
    half = keep.shape[0]
    if split:
        upper = jnp.bitwise_and(ids[0], split) > 0
        got = get_wide(other, top + rows * lanes, 2 * half)
        first, second = kept[:half, :] + got[:half], kept[half:, :] + got[half:]
        keep[...] = jnp.where(upper, second, first)
        put_wide(payload, base + rows * lanes, jnp.where(upper, first, second))
    else:
        mine = kept[...] if halved else get_wide(sent, top + rows * lanes, half)
        total = mine + get_wide(other, top + rows * lanes, half)
        keep[...] = total
        if payload is not None:
            put_wide(payload, base + rows * lanes, total)


def back_hop(seqs, level, split, halved, ids, par, own, kept, sent, other, out, keep, payload):
    chain_hop(
        seqs, level, split, halved, 0, ids, par, own, kept, sent, other, out, keep, payload, 0
    )


def split_rows(count, cut, place, k):
    shift, bits = cut
    rows = count >> bits
    sub = jnp.bitwise_and(jnp.right_shift(place, shift), (1 << bits) - 1)
    return pl.multiple_of(jnp.bitwise_xor(sub, k) * rows, rows), rows


def add_rows(parts, start, high, out, top, lane, width, at):
    step = min(64, high)

    def body(i, carry):
        row = pl.ds(pl.multiple_of(start + i * step, step), step)
        total = parts[0][row, lane : lane + width].astype(F32)
        for other in parts[1:]:
            total = total + other[row, lane : lane + width].astype(F32)
        out[pl.ds(pl.multiple_of(top + i * step, 16), step), at : at + width] = total.astype(BF16)
        return carry

    lax.fori_loop(0, high // step, body, 0)


def fold_kernel(jobs, inputs, ids, *refs):
    parts, outs = refs[:inputs], refs[inputs:]
    at = 0
    for count, lane, width, cut, targets in jobs:
        own = parts[at : at + count]
        at += count
        blocks, rows, _ = own[0].shape
        for k, (target, block, offset) in enumerate(targets):
            if cut == "tp":
                ranges, start, high = (k,), 0, rows
            elif cut is None:
                ranges, start, high = range(blocks), 0, rows
            else:
                start, high = split_rows(rows, cut, ids[1], k)
                ranges = range(blocks)
            for to, b in enumerate(ranges):
                add_rows(
                    [p.at[b] for p in own], start, high, outs[target].at[block + to], 0, lane,
                    width, offset,
                )


def fold(ids, shapes, jobs):
    arrays = [a for job in jobs for a in job[0]]
    plan = [(len(job[0]),) + tuple(job[1:]) for job in jobs]
    return call(
        functools.partial(fold_kernel, plan, len(arrays)),
        tuple(shape(dims, BF16) for dims in shapes),
        [],
        (ids, *arrays),
        [SMEM] + [VMEM] * len(arrays),
        "fold",
    )


def join_kernel(cut, ids, mine, other, out):
    blocks, rows, _ = mine.shape
    for k, part in enumerate((mine, other)):
        start, _ = split_rows(2 * rows, cut, ids[1], k)
        for b in range(blocks):
            out[b, pl.ds(pl.multiple_of(start, 16), rows), :] = part[b]


def join(ids, mine, other, cut):
    blocks, rows, lanes = mine.shape
    return call(
        functools.partial(join_kernel, cut),
        (shape((blocks, 2 * rows, lanes), BF16),),
        [],
        (ids, mine, other),
        [SMEM, VMEM, VMEM],
        "join",
    )[0]


def ride_kernel(
    seqs, level, split, halved, top, jobs, cut, last, ids, par, own, kept, sent, other, *refs
):
    count = 1 + max(p for job in jobs for p in job[0])
    parts, refs = refs[:count], refs[count:]
    if last:
        keep, kept_out = refs
        out = payload = None
        halves = ((0, keep, None),)
    else:
        keep, kept_out, out, payload = refs
        halves = ((0, keep, cut), (1, payload, cut))
    high = keep.shape[0]
    for picks, width, at in jobs:
        own_parts = [other if p < 0 else parts[p] for p in picks]
        for k, target, where in halves:
            start = 0 if where is None else split_rows(2 * high, where, ids[1], k)[0]
            add_rows(own_parts, start, high, target, 0, 0, width, at)
    chain_hop(
        seqs, level, split, halved, top, ids, par, own, kept, sent, other, out, kept_out, payload,
        high,
    )


def unpack_first(cut, ids, *refs):
    count = 1 << cut[1]
    pieces, refs = refs[:count], refs[count:]
    w_in, w_out = refs[:2]
    outs = refs[2:]
    vb = w_in.shape[1]
    wide = 2 * vb
    each = sum(out.shape[0] for out in outs)
    for k in range(count):
        row, rows = split_rows(D, cut, ids[1], k)
        w_in[pl.ds(row, rows), :] = pieces[k][0, :, :vb].astype(F32)
        for first in range(0, rows, vb):
            w_out[:, pl.ds(pl.multiple_of(row + first, vb), vb)] = pieces[k][
                0, first : first + vb, vb:
            ].astype(F32)
        for b in range(count):

            @pl.when(row == b * rows)
            def _(k=k, b=b, rows=rows):
                for run in range(D // wide):
                    start = run * each
                    for out in outs:
                        end = start + out.shape[0]
                        lo, hi = max(start, b * rows), min(end, (b + 1) * rows)
                        if lo < hi:
                            out[lo - start : hi - start, run * wide : (run + 1) * wide] = pieces[k][
                                1, lo - b * rows : hi - b * rows, :
                            ].astype(F32)
                        start = end


def unpack_sides(cut, ids, *refs):
    count = 1 << cut[1]
    pieces, (left, right) = refs[:count], refs[count:]
    vb = left.shape[1]
    for k in range(count):
        row, rows = split_rows(D, cut, ids[1], k)
        left[pl.ds(row, rows), :] = pieces[k][0, :, :vb].astype(F32)
        right[pl.ds(row, rows), :] = pieces[k][0, :, vb:].astype(F32)


def unpack(body, cut, ids, pieces, dims):
    return call(
        functools.partial(body, cut),
        tuple(shape(d) for d in dims),
        [],
        (ids, *pieces),
        [SMEM] + [VMEM] * len(pieces),
        "unpack",
    )


BOTH = ("seq", "tp")


def swap(value, mask):
    count = lax.axis_size("seq") * lax.axis_size("tp")
    return lax.ppermute(value, BOTH, [(i, i ^ mask) for i in range(count)])


def after(value, *others):
    return lax.optimization_barrier((value, *others))[0]


def bits_of(count):
    return [1 << k for k in range(count.bit_length() - 1)]


def has(index, bit):
    return jnp.bitwise_and(index, bit) > 0


def half_of(value, upper):
    half = value.shape[0] // 2
    return lax.dynamic_slice_in_dim(value, jnp.where(upper, half, 0), half, 0)


def joined(mine, other, upper):
    return jnp.where(
        upper,
        jnp.concatenate([other, mine], axis=0),
        jnp.concatenate([mine, other], axis=0),
    )


def spread_out(own, tp):
    pieces = {0: own}
    for bit in reversed(bits_of(tp // 2)):
        for r in list(pieces):
            pieces[r ^ bit] = [swap(a, bit) for a in pieces[r]]
    return [pieces[r] for r in range(tp // 2)]


def per_device(
    tokens,
    cotangent,
    valid_lengths,
    norm1_gain,
    ema_rate,
    ema_beta,
    ema_eta,
    ema_skip,
    w_shared,
    query_gain,
    key_gain,
    rel_bias,
    w_value,
    w_reset,
    w_update,
    w_hidden,
    u_hidden,
    norm2_gain,
    w_in,
    w_out,
):
    part = lax.axis_index("tp")
    place = lax.axis_index("seq")
    tp = lax.axis_size("tp")
    seq = lax.axis_size("seq")
    all_seqs, local_rows, _ = tokens.shape
    vb = w_value.shape[1]
    nb = D // tp
    index = place * tp + part
    ybits = (seq.bit_length() - 1) // 2
    traded = local_rows < CH
    lower = part % 2 == 0

    def trade(value):
        if not traded:
            return value
        other = swap(jnp.where(lower, value[1], value[0]), 1)
        mine = jnp.where(lower, value[0], value[1])
        return joined(mine, other, ~lower)[None]

    def trade_back(value):
        if not traded:
            return value
        first, second = value[0, :local_rows], value[0, local_rows:]
        other = swap(jnp.where(lower, second, first), 1)
        mine = jnp.where(lower, first, second)
        return jnp.where(lower, jnp.stack([mine, other]), jnp.stack([other, mine]))

    if traded:
        assert all_seqs == 2 and 2 * local_rows == CH
        seqs = 1
        stretch = index // 2
        lengths = jnp.where(lower, valid_lengths[0], valid_lengths[1])[None]
    else:
        assert local_rows == CH
        seqs = all_seqs
        stretch = index
        lengths = valid_lengths
    rows = seqs * CH
    ids = jnp.concatenate([jnp.stack([part, place, stretch]), lengths]).astype(jnp.int32)
    masks = bits_of(tp * seq)[int(traded) :]
    levels = len(masks)
    upper_y = has(place, 1)

    tok = trade(tokens)
    cot = trade(cotangent)
    gain1 = norm1_gain[None]
    gain2 = norm2_gain[None]
    skip = ema_skip[None]
    rate, beta = ema_rate.T, ema_beta.T
    qg, kg, rb = query_gain[None], key_gain[None], rel_bias[None]

    top = tp // 2
    weights = (w_value, w_reset, w_hidden, w_update, u_hidden, w_in, w_out)
    rows2 = 2 * nb + vb
    normed, par, before, ends, low, pack1, pack2, pack3, half1, half2, half3 = call(
        functools.partial(enter_kernel, seqs),
        (
            shape((rows, D), BF16),
            shape((4, NDIM, D)),
            shape((2, seqs, NDIM, PIECES, D)),
            shape((2, seqs, NDIM, D)),
            shape((2, seqs, NDIM, D), BF16),
            shape((D, 2 * vb), BF16),
            shape((rows2, D), BF16),
            shape((D, 2 * vb), BF16),
            shape((D // 2, 2 * vb), BF16),
            shape((rows2, D // 2), BF16),
            shape((D // 2, 2 * vb), BF16),
        ),
        [
            pltpu.VMEM((seqs, CH, D), BF16),
            pltpu.VMEM((1, D), F32),
            pltpu.VMEM((NDIM, D), F32),
            pltpu.VMEM((NDIM, D), F32),
            pltpu.VMEM((NDIM, D), F32),
            pltpu.VMEM((BLOCKS, rows, LANES), F32),
            pltpu.VMEM((6, NDIM, D), F32),
            pltpu.SemaphoreType.DMA((17 + 2 * (D // vb),)),
        ],
        (tok, gain1, rate, beta, ema_eta.T, *weights),
        [ANY] * 12,
        "enter",
        limit=60,
        outs=(pl.BlockSpec(),) * 11,
    )

    start = 1 - int(traded)
    groups = [(0, 1)] * start + [(start, 2)] + [(i, 1) for i in range(start + 2, levels)]
    hops = []
    state = ends
    for i, (shift, bits) in enumerate(groups):
        if i == start:
            mine1 = swap(half1, top)
            near_gates = spread_out([pack1, pack2], tp)
        if i == start + 1:
            low = after(low, mine1)
            mine2 = swap(after(half2, low), top)
            other1 = swap(after(mine1, low), tp)
        if i == start + 2:
            low = after(low, mine2, *near_gates[-1])
            mine3 = swap(after(half3, low), top)
            near_feeds = spread_out([after(pack3, low)], tp)
        got = []
        for k in range(1, 1 << bits):
            got.append(swap(low, k << (shift + int(traded))))
            hops.append((shift, k, got[-1]))
        if i + 1 < len(groups):
            state, low = call(
                functools.partial(hop_kernel, seqs, shift, 1 << bits),
                (shape((2, seqs, NDIM, D)), shape((2, seqs, NDIM, D), BF16)),
                [],
                (ids, par, state, *got),
                [SMEM] + [VMEM] * (2 + len(got)),
                "hop",
            )
    st_in, skip_pre, mixed, shared_pre, prob = call(
        functools.partial(look_kernel, seqs, [h[:2] for h in hops]),
        (
            shape((2, seqs, NDIM, D)),
            shape((rows, D)),
            shape((rows, D), BF16),
            shape((rows, Z)),
            shape((seqs, CH, CH)),
        ),
        [
            pltpu.VMEM((BLOCKS, rows, LANES), F32),
            pltpu.VMEM((BLOCKS, rows, LANES), F32),
            pltpu.VMEM((NDIM, PIECES, D), F32),
        ],
        (
            ids, after(normed, mine3), par, before, skip, w_shared, qg, kg, rb,
            *[h[2] for h in hops],
        ),
        [SMEM] + [VMEM] * (8 + len(hops)),
        "look",
        limit=10,
    )
    other2 = swap(after(mine2, low), tp)
    far_gates = spread_out([mine1, other1, mine2, other2], tp)
    other3 = swap(after(mine3, *got), tp)
    gates = [w for group in near_gates + far_gates for w in group]

    values, value_pre, reset_pre, attended, gated, hidden_pre, update_pre, middle = call(
        functools.partial(mix_kernel, seqs, tp),
        (
            shape((tp, rows, vb), BF16),
            shape((tp, rows, vb)),
            shape((tp, rows, vb)),
            shape((tp, rows, vb)),
            shape((tp, rows, vb), BF16),
            shape((rows, D)),
            shape((rows, D)),
            shape((rows, D)),
        ),
        [
            pltpu.VMEM((tp, D, 2 * vb), BF16),
            pltpu.VMEM((tp, rows2, D), BF16),
            pltpu.VMEM((D, 2 * D), BF16),
            pltpu.SemaphoreType.DMA((3 * tp,)),
        ],
        (ids, tok, normed, mixed, prob, *gates),
        [SMEM] + [VMEM] * 4 + [ANY] * len(gates),
        "mix",
        limit=10,
    )

    far_feeds = spread_out([mine3, after(other3, middle)], tp)
    feeds = [w for group in near_feeds + far_feeds for w in group]
    out, keep3, send3, grad_hu, resid, grad_gain2 = call(
        functools.partial(ffn_kernel, seqs, tp),
        (
            shape((rows, D), BF16),
            shape((tp // 2, D, 2 * vb), BF16),
            shape((tp // 2, D, 2 * vb), BF16),
            shape((rows, 2 * D), BF16),
            shape((rows, D)),
            shape((1, D)),
        ),
        [
            pltpu.VMEM((tp, D, 2 * vb), BF16),
            pltpu.VMEM((rows, D), BF16),
            pltpu.VMEM((rows, D), BF16),
            pltpu.VMEM((rows, D), F32),
            pltpu.VMEM((rows, D), F32),
            pltpu.SemaphoreType.DMA((3 * tp // 2,)),
        ],
        (ids, tok, cot, middle, hidden_pre, update_pre, gain2, *feeds),
        [SMEM] + [VMEM] * 6 + [ANY] * len(feeds),
        "ffn",
        limit=10,
    )

    half = tp // 2
    yn = 1 << ybits
    wide = 2 * vb
    runs = D // wide
    cut_of_y = (0, ybits)
    zcuts = [(shift, 1) for shift in range(ybits, seq.bit_length() - 1)]

    def over_tp(pieces):
        return [pieces[0]] + [swap(p, 2 * k) for k, p in enumerate(pieces) if k]

    def over_y(pieces):
        return [pieces[0]] + [swap(p, tp * k) for k, p in enumerate(pieces) if k]

    def over_z(value, cut):
        return swap(value, tp << cut[0])

    def cut_tp(parts, dims):
        n = dims[0]
        return fold(
            ids,
            [(1,) + dims[1:]] * n,
            [(parts, 0, dims[2], "tp", [(k, 0, 0) for k in range(n)])],
        )

    def cut_y(parts, dims):
        return fold(
            ids,
            [(dims[0], dims[1] // yn, dims[2])] * yn,
            [(parts, 0, dims[2], cut_of_y, [(k, 0, 0) for k in range(yn)])],
        )

    last = [None]

    def now(value):
        return value if last[0] is None else after(value, last[0])

    chunk = (half, D, wide)
    got3 = swap(send3, 1)
    keep2, send2 = call(
        functools.partial(gates_kernel, tp),
        (shape(chunk, BF16), shape(chunk, BF16)),
        [pltpu.VMEM((D, 2 * D), F32)],
        (ids, mixed, gated, grad_hu),
        [SMEM] + [VMEM] * 3,
        "gates",
        limit=10,
    )
    got2 = swap(send2, 1)
    g3 = cut_tp([keep3, got3], chunk)
    g3 = over_tp(g3)
    g2 = cut_y([keep2, after(got2, g3[0])], chunk)
    g2 = over_y(g2)

    (
        keep1, send1, grad_skip, grad_normed, behind, back_ends, grad_wsh, misc,
    ) = call(
        functools.partial(back_kernel, seqs, tp),
        (
            shape((half, D, 2 * vb), BF16),
            shape((half, D, 2 * vb), BF16),
            shape((BLOCKS, rows, LANES)),
            shape((rows, D)),
            shape((seqs, NDIM, PIECES, D)),
            shape((seqs, NDIM, D)),
            shape((D, Z)),
            shape((1, D)),
        ),
        [
            pltpu.VMEM((tp, D, 2 * vb), BF16),
            pltpu.VMEM((tp, rows2, D), BF16),
            pltpu.VMEM((D, 2 * D), BF16),
            pltpu.VMEM((rows, D), F32),
            pltpu.VMEM((seqs, CH, CH), F32),
            pltpu.VMEM((3, NDIM, D), F32),
            pltpu.SemaphoreType.DMA((3 * tp,)),
        ],
        (
            ids, normed, mixed, skip_pre, shared_pre, prob, values, value_pre, reset_pre, attended,
            after(grad_hu, g2[0]), par, w_shared, qg, kg, *gates,
        ),
        [SMEM] + [VMEM] * 14 + [ANY] * len(gates),
        "back",
        limit=10,
    )

    g3 = cut_y([after(g3[0], send1)] + g3[1:], (1, D, wide))
    g2 = cut_tp([after(g2[0], g3[0])] + g2[1:], (half, D // yn, wide))
    keep1, send1, grad_skip, grad_normed, behind, back_ends, grad_wsh, misc, _ = (
        lax.optimization_barrier(
            (keep1, send1, grad_skip, grad_normed, behind, back_ends, grad_wsh, misc, g2[0])
        )
    )
    adjoint = back_ends.reshape(seqs * NDIM, D)
    last[0] = g2[0]
    g3 = over_y(g3)
    g2 = over_tp(g2)
    got1 = swap(send1, 1)
    got_adjoint = adjoint if traded else swap(adjoint, 1)
    done = {}

    def first_chunks():
        high = D // yn >> 1
        keep, send = fold(
            ids,
            [(2, high, wide)] * 2,
            [
                ([now(g3[0])] + g3[1:], 0, wide, zcuts[0], [(0, 0, 0), (1, 0, 0)]),
                (g2, 0, wide, zcuts[0], [(0, 1, 0), (1, 1, 0)]),
            ],
        )
        for cut in zcuts[1:]:
            other = over_z(send, zcuts[zcuts.index(cut) - 1])
            yield keep
            high //= 2
            keep, send = fold(
                ids,
                [(2, high, wide)] * 2,
                [([now(keep), other], 0, wide, cut, [(0, 0, 0), (1, 0, 0)])],
            )
        other = over_z(send, zcuts[-1])
        yield keep
        (total,) = fold(ids, [keep.shape], [([now(keep), other], 0, wide, None, [(0, 0, 0)])])
        for cut in reversed(zcuts):
            other = over_z(total, cut)
            yield total
            total = join(ids, now(total), other, cut)
        pieces = over_y([total] * yn)
        yield total
        done["first"] = unpack(
            unpack_first,
            cut_of_y,
            ids,
            [now(pieces[0])] + pieces[1:],
            [(D, vb), (vb, D), (nb, D), (nb, D), (vb, D)],
        )
        yield done["first"][0]

    def second_chunk():
        parts = fold(
            ids,
            [(1, D, vb)] * half + [(half, D // yn, vb)] * yn,
            [
                ([now(keep1), got1], 0, vb, "tp", [(k, 0, 0) for k in range(half)]),
                ([keep1, got1], vb, vb, cut_of_y, [(half + k, 0, 0) for k in range(yn)]),
            ],
        )
        left, right = over_tp(parts[:half]), over_y(parts[half:])
        yield parts[0]
        count = Z + SMALL_ROWS
        count += -count % (16 * tp)
        sums, send = call(
            functools.partial(sums_kernel, seqs),
            (shape((count // 2, D)), shape((count // 2, D))),
            [
                pltpu.VMEM((count, D), F32),
                pltpu.VMEM((BLOCKS, rows, LANES), F32),
                pltpu.VMEM((NDIM, PIECES, D), F32),
            ],
            (
                ids, tok, normed, now(grad_skip), grad_normed, par, before, st_in, skip, grad_gain2,
                misc, grad_wsh,
            ),
            [SMEM] + [VMEM] * 11,
            "sums",
            limit=10,
        )
        got_sums = swap(send, 1)
        yield sums
        small_high = count // 4
        ad_rows = seqs * NDIM

        def payload_rows():
            return (ad_rows + small_high) * runs

        own, kept, payload = call(
            functools.partial(first_back_hop, seqs, not traded),
            (
                shape((ad_rows, D)),
                shape((small_high, D)),
                shape((payload_rows(), wide), BF16),
            ),
            [],
            (ids, par, now(adjoint), got_adjoint, sums, got_sums),
            [SMEM] + [VMEM] * 5,
            "hop",
        )
        got = [] if traded else [(got_adjoint, 0)]
        level = int(not traded)
        halved = True
        other = swap(payload, masks[level])
        yield payload
        parts = fold(
            ids,
            [(1, D // yn, vb)] * (yn + half),
            [
                ([now(left[0])] + left[1:], 0, vb, cut_of_y, [(k, 0, 0) for k in range(yn)]),
                (right, 0, vb, "tp", [(yn + k, 0, 0) for k in range(half)]),
            ],
        )
        left, right = over_y(parts[:yn]), over_tp(parts[yn:])
        yield parts[0]
        while level + 1 < levels - len(zcuts):
            got.append((other, 0))
            split = 2 * masks[level] if 2 * masks[level] < tp else 0
            small_high = small_high // 2 if split else small_high
            own, kept, payload = call(
                functools.partial(back_hop, seqs, level, split, halved),
                (
                    shape((ad_rows, D)),
                    shape((small_high, D)),
                    shape((payload_rows(), wide), BF16),
                ),
                [],
                (ids, par, now(own), kept, payload, other),
                [SMEM] + [VMEM] * 5,
                "hop",
            )
            halved = bool(split)
            level += 1
            other = swap(payload, masks[level])
            yield payload
        high = D // yn
        top = 0
        flat = [p.reshape(p.shape[1:]) for p in left + right]
        jobs = [
            (tuple(range(len(left))), vb, 0),
            (tuple(range(len(left), len(flat))), vb, vb),
        ]
        for cut in zcuts:
            got.append((other, top))
            high //= 2
            keep, kept, own, payload = call(
                functools.partial(
                    ride_kernel, seqs, level, 0, halved, top, jobs, cut, False
                ),
                (
                    shape((high, wide), BF16),
                    shape((small_high, D)),
                    shape((ad_rows, D)),
                    shape((high + payload_rows(), wide), BF16),
                ),
                [],
                (ids, par, now(own), kept, payload, other, *flat),
                [SMEM] + [VMEM] * (5 + len(flat)),
                "ride",
            )
            halved = False
            level += 1
            top = high
            flat = [keep]
            jobs = [((0, -1), wide, 0)]
            other = swap(payload, masks[level])
            yield keep
        got.append((other, top))
        total, kept = call(
            functools.partial(ride_kernel, seqs, level, 0, False, top, jobs, None, True),
            (shape((high, wide), BF16), shape((small_high, D))),
            [],
            (ids, par, now(own), kept, payload, other, *flat),
            [SMEM] + [VMEM] * (5 + len(flat)),
            "ride",
        )
        bits = list(reversed(bits_of(tp)))
        total = total[None]
        far = swap(kept, bits[0])
        for i, cut in enumerate(reversed(zcuts)):
            other = over_z(total, cut)
            yield total
            total = join(ids, now(total), other, cut)
            if i + 1 < len(bits):
                (kept,) = call(
                    functools.partial(pair_kernel, bits[i]),
                    (shape((2 * kept.shape[0], D)),),
                    [],
                    (ids, after(kept, total), far),
                    [SMEM, VMEM, VMEM],
                    "pair",
                )
                far = swap(kept, bits[i + 1])
        pieces = over_y([total] * yn)
        yield total
        done["small"] = call(
            finish_kernel,
            (
                shape((1, D)),
                shape((NDIM, D)),
                shape((NDIM, D)),
                shape((NDIM, D)),
                shape((1, D)),
                shape((D, Z)),
                shape((1, Z)),
                shape((1, Z)),
                shape((1, Z)),
                shape((1, D)),
            ),
            [pltpu.VMEM((count, D), F32)],
            (ids, par, rate, beta, gain1, now(kept), far),
            [SMEM] + [VMEM] * 6,
            "finish",
        )
        (done["tokens"],) = call(
            functools.partial(leave_kernel, seqs, [at for _, at in got]),
            (shape((seqs, CH, D), BF16),),
            [
                pltpu.VMEM((seqs, NDIM, D), F32),
                pltpu.VMEM((NDIM, PIECES, D), F32),
                pltpu.VMEM((BLOCKS, rows, LANES), F32),
            ],
            (
                ids, tok, par, after(grad_skip, done["small"][0]), grad_normed, behind, resid,
                gain1, skip, *[g for g, _ in got],
            ),
            [SMEM] + [VMEM] * (8 + levels),
            "leave",
            limit=10,
        )
        yield done["tokens"]
        done["second"] = unpack(
            unpack_sides, cut_of_y, ids, [now(pieces[0])] + pieces[1:], [(D, vb), (D, vb)]
        )
        yield done["second"][0]

    walks = {"f": first_chunks(), "s": second_chunk()}
    order = "s s f s s f s f s f s f s s s s f s".replace(" ", "")

    def advance(name):
        try:
            last[0] = next(walks[name])
        except StopIteration:
            del walks[name]

    for name in order:
        if name in walks:
            advance(name)
    while walks:
        for name in list(walks):
            advance(name)

    grad_w_in, grad_w_out, grad_w_hidden, grad_w_update, grad_u_hidden = done["first"]
    grad_w_value, grad_w_reset = done["second"]
    firsts = [
        small.T if small.shape[0] == NDIM else small[0] if small.shape[0] == 1 else small
        for small in done["small"]
    ]
    grad_norm2_gain = firsts.pop()
    return (
        trade_back(out.reshape(seqs, CH, D)),
        trade_back(done["tokens"]),
        *firsts,
        grad_w_value,
        grad_w_reset,
        grad_w_update,
        grad_w_hidden,
        grad_u_hidden,
        grad_norm2_gain,
        grad_w_in,
        grad_w_out,
    )


def solution(mesh):
    rows = P(None, ("seq", "tp"), None)
    cols = P(None, "tp")
    tall = P("tp", None)
    whole = P()
    return jax.shard_map(
        per_device,
        mesh=mesh,
        in_specs=(rows, rows) + (whole,) * 10 + (cols, cols, tall, tall, tall, whole, cols, tall),
        out_specs=(rows, rows) + (whole,) * 9 + (cols, cols, tall, tall, tall, whole, cols, tall),
        check_vma=False,
    )
```

```python
import functools

import jax
import jax.numpy as jnp
from jax import lax
from jax.experimental import pallas as pl
from jax.experimental.pallas import tpu as pltpu
from jax.sharding import PartitionSpec as P

D = 512
Z = 128
NDIM = 16
CH = 128
PIECE = 16
PIECES = CH // PIECE
LANES = 128
BLOCKS = D // LANES
EPS = 1e-05
F32 = jnp.float32
BF16 = jnp.bfloat16
SMALL_ROWS = 64

VMEM = pl.BlockSpec(memory_space=pltpu.VMEM)
SMEM = pl.BlockSpec(memory_space=pltpu.SMEM)
ANY = pl.BlockSpec(memory_space=pl.ANY)


def sigmoid(v):
    return 0.5 * jnp.tanh(0.5 * v) + 0.5


def silu(v):
    return v * sigmoid(v)


def silu_slope(v):
    s = sigmoid(v)
    return s * (1.0 + v * (1.0 - s))


def mm(a, b):
    return jnp.dot(a, b, preferred_element_type=F32)


def mm_nt(a, b):
    return lax.dot_general(a, b, (((1,), (1,)), ((), ())), preferred_element_type=F32)


def mm_tn(a, b):
    return lax.dot_general(a, b, (((0,), (0,)), ((), ())), preferred_element_type=F32)


def normalized(v):
    center = v - jnp.mean(v, axis=-1, keepdims=True)
    scale = lax.rsqrt(jnp.mean(center * center, axis=-1, keepdims=True) + EPS)
    return center * scale, scale


def norm_back(grad, xhat, scale, gain):
    full = grad * gain
    return scale * (
        full
        - jnp.mean(full, axis=-1, keepdims=True)
        - xhat * jnp.mean(full * xhat, axis=-1, keepdims=True)
    )


def rows_of(s):
    return pl.ds(s * CH, CH)


def lanes_of(i):
    return pl.ds(pl.multiple_of((i % BLOCKS) * LANES, LANES), LANES)


def spread(row):
    return jnp.broadcast_to(row, (PIECES, LANES))


def piece_rows(s, t):
    return pl.ds(s * CH + t, PIECES, stride=PIECE)


def put_rows(ref, rows, value):
    for b in range(BLOCKS):
        ref[b, rows, :] = value[:, b * LANES : (b + 1) * LANES]


def get_rows(ref, rows):
    return jnp.concatenate([ref[b, rows, :] for b in range(BLOCKS)], axis=1)


class Here:
    def __init__(self, seqs, lengths):
        self.seqs, self.lengths = seqs, lengths

    def __getitem__(self, i):
        if i == 0:
            return lax.axis_index("tp")
        if i == 1:
            return lax.axis_index("seq")
        if i == 2:
            index = lax.axis_index("seq") * lax.axis_size("tp") + lax.axis_index("tp")
            return index if self.seqs > 1 else jnp.right_shift(index, 1)
        return self.lengths[i - 3 if self.seqs > 1 else jnp.bitwise_and(lax.axis_index("tp"), 1)]


def call(body, out, scratch, operands, specs, name, limit=2, outs=None):
    place = operands[0]
    if isinstance(place, Here):
        kernel = body
        if place.lengths is None:
            operands, specs = operands[1:], specs[1:]
            body = lambda *refs: kernel(place, *refs)
        else:
            operands = (place.lengths, *operands[1:])
            body = lambda lengths, *refs: kernel(Here(place.seqs, lengths), *refs)
    return pl.pallas_call(
        body,
        out_shape=out,
        in_specs=specs,
        out_specs=outs or jax.tree.map(lambda _: VMEM, out),
        scratch_shapes=scratch,
        name=name,
        compiler_params=pltpu.CompilerParams(vmem_limit_bytes=int(limit * 1024 * 1024)),
    )(*operands)


def shape(dims, dtype=F32):
    return jax.ShapeDtypeStruct(dims, dtype)


def enter_kernel(seqs, *refs):
    far, refs = refs[:5], refs[5:]
    normed, par, before, ends, low, tok, gain, rate, beta, eta, nf, tab, sems = refs
    copies = [
        pltpu.make_async_copy(a, b, sems.at[i])
        for i, (a, b) in enumerate(zip(far, (tok, gain, rate, beta, eta)))
    ]
    for c in copies:
        c.start()
    for c in copies:
        c.wait()
    r = rate[...]
    d = 1.0 - r
    par[0] = d
    par[1] = jnp.log(d)
    par[2] = jnp.sqrt(r * (2.0 - r)) * beta[...]
    par[3] = eta[...]
    d2 = d * d
    d4 = d2 * d2
    d8 = d4 * d4
    d15 = d8 * d4 * d2 * d
    q = d8 * d8
    tab[0] = q
    tab[1] = 16.0 * d15
    tab[2] = q * q
    tab[3] = 32.0 * q * d15
    tab[4] = q * q * q * q
    tab[5] = 64.0 * q * q * q * d15
    for s in range(seqs):
        xhat, _ = normalized(tok[s].astype(F32))
        scaled = (xhat * gain[...]).astype(BF16)
        normed[rows_of(s), :] = scaled
        put_rows(nf, rows_of(s), scaled.astype(F32))
    place = lax.broadcasted_iota(jnp.int32, (PIECES, LANES), 0)

    def body(i, carry):
        s = i // BLOCKS
        lane = lanes_of(i)
        xs = [nf[i % BLOCKS, piece_rows(s, t), :] for t in range(PIECE)]
        for j0 in range(0, NDIM, 8):
            ds = [spread(par[0, j0 + j : j0 + j + 1, lane]) for j in range(8)]
            st = [xs[0]] * 8
            ta = [jnp.zeros((PIECES, LANES), F32)] * 8
            for t in range(1, PIECE):
                for j in range(8):
                    ta[j] = ds[j] * ta[j] + st[j]
                    st[j] = ds[j] * st[j] + xs[t]
            for j in range(8):
                a, b = st[j], ta[j]
                for k, step in enumerate((1, 2, 4)):
                    qm = spread(tab[2 * k, j0 + j : j0 + j + 1, lane])
                    rm = spread(tab[2 * k + 1, j0 + j : j0 + j + 1, lane])
                    sa = jnp.where(place >= step, pltpu.roll(a, step, 0), 0.0)
                    sb = jnp.where(place >= step, pltpu.roll(b, step, 0), 0.0)
                    b = b + qm * sb + rm * sa
                    a = a + qm * sa
                before[0, s, j0 + j, :, lane] = jnp.where(place >= 1, pltpu.roll(a, 1, 0), 0.0)
                before[1, s, j0 + j, :, lane] = jnp.where(place >= 1, pltpu.roll(b, 1, 0), 0.0)
                ends[2 * s, j0 + j : j0 + j + 1, lane] = a[PIECES - 1 :]
                ends[2 * s + 1, j0 + j : j0 + j + 1, lane] = b[PIECES - 1 :]
        return carry

    lax.fori_loop(0, seqs * BLOCKS, body, 0)
    low[...] = ends[: 2 * seqs].astype(BF16)
    ends[2 * seqs] = par[1]


def first_half_kernel(w_value, w_reset, h1, sems):
    vb, cut = w_value.shape[1], D // 2
    at = pl.ds(pl.multiple_of(jnp.bitwise_and(lax.axis_index("seq"), 1) * cut, cut), cut)
    copies = [
        pltpu.make_async_copy(w.at[at, :], h1.at[:, pl.ds(i * vb, vb)], sems.at[i])
        for i, w in enumerate((w_value, w_reset))
    ]
    for c in copies:
        c.start()
    for c in copies:
        c.wait()


def pack_kernel(
    w_value, w_reset, w_hidden, w_update, u_hidden, w_in, w_out, p1, p2, p3, h2, h3, sems
):
    copies = []

    def add(source, target):
        copies.append(pltpu.make_async_copy(source, target, sems.at[len(copies)]))

    vb, cut = w_value.shape[1], D // 2
    upper = jnp.bitwise_and(lax.axis_index("seq"), 1) * cut
    at = pl.ds(pl.multiple_of(upper, cut), cut)
    for i, w in enumerate((w_value, w_reset)):
        add(w, p1.at[:, pl.ds(i * vb, vb)])
    far = jnp.bitwise_and(jnp.right_shift(lax.axis_index("seq"), far_shift()), 1) * cut
    top = 0
    for w in (w_hidden, w_update, u_hidden):
        row = pl.ds(top, w.shape[0])
        add(w.at[:, pl.ds(pl.multiple_of(far, cut), cut)], h2.at[row, :])
        add(w, p2.at[row, :])
        top += w.shape[0]
    add(w_in.at[at, :], h3.at[:, pl.ds(0, vb)])
    add(w_in, p3.at[:, pl.ds(0, vb)])
    for k in range(D // vb):
        row = pl.ds(k * vb, vb)
        add(w_out.at[:, row], p3.at[row, pl.ds(vb, vb)])
        if k < cut // vb:
            lane = pl.ds(pl.multiple_of(upper + k * vb, vb), vb)
            add(w_out.at[:, lane], h3.at[row, pl.ds(vb, vb)])
    for c in copies:
        c.start()
    for c in copies:
        c.wait()


def piece_powers(par, pw):
    k = lax.broadcasted_iota(jnp.int32, (PIECES, D), 0).astype(F32) * PIECE
    for j in range(NDIM):
        pw[j] = jnp.exp(k * par[1, j : j + 1, :])


def take_weights(refs, tp, first, second):
    top = tp // 2
    near = [refs[r * first : (r + 1) * first] for r in range(top)]
    refs = refs[top * first :]
    far = [refs[r * second : (r + 1) * second] for r in range(top)]
    return near, far, refs[top * second :]


def far_shift():
    return (lax.axis_size("seq").bit_length() - 1) // 2


def gate_copies(tp, ids, near, far, w1, w2, sems):
    top, cut = tp // 2, D // 2
    first = jnp.bitwise_and(ids[1], 1)
    second = jnp.bitwise_and(jnp.right_shift(ids[1], far_shift()), 1)
    copies = []

    def add(source, target):
        copies.append(pltpu.make_async_copy(source, target, sems.at[len(copies)]))

    for r in range(top):
        add(near[r][0], w1.at[r])
        add(near[r][1], w2.at[r])
        mine1, other1, mine2, other2 = far[r]
        for part, at in ((mine1, first), (other1, 1 - first)):
            add(part, w1.at[top + r, pl.ds(pl.multiple_of(at * cut, cut), cut), :])
        for part, at in ((mine2, second), (other2, 1 - second)):
            add(part, w2.at[top + r, :, pl.ds(pl.multiple_of(at * cut, cut), cut)])
    for c in copies:
        c.start()
    return copies


def gate_rows(tp, me, w2, whu):
    nb = D // tp
    for r in range(tp):
        row = pl.ds(pl.multiple_of(jnp.bitwise_xor(me, r) * nb, nb), nb)
        whu[row, pl.ds(0, D)] = w2[r, pl.ds(0, nb), :]
        whu[row, pl.ds(D, D)] = w2[r, pl.ds(nb, nb), :]


def look_kernel(
    seqs, hops, ids, normed, par, before, skip, wsh, qg, kg, rb, *refs
):
    recvs, refs = refs[: len(hops)], refs[len(hops) :]
    st_in, skip_pre, mixed, shared_pre, prob, nf, sm, pw = refs
    place = ids[2]
    put_rows(nf, slice(None), normed[...].astype(F32))
    piece_powers(par, pw)
    logd = par[1]
    dinv = 1.0 / par[0]
    for s in range(seqs):
        a = jnp.zeros((NDIM, D), F32)
        b = jnp.zeros((NDIM, D), F32)
        for (shift, k), got in zip(hops, recvs):
            end = jnp.left_shift(jnp.bitwise_xor(jnp.right_shift(place, shift), k) + 1, shift)
            off = (place - end).astype(F32) * float(CH)
            power = jnp.where(place >= end, jnp.exp(jnp.maximum(off, 0.0) * logd), 0.0)
            oa = got[2 * s].astype(F32) * power
            b = b + got[2 * s + 1].astype(F32) * power + off * oa * dinv
            a = a + oa
        st_in[0, s] = a
        st_in[1, s] = b

    def ema(i, carry):
        s = i // BLOCKS
        lane = lanes_of(i)
        row = [pl.ds(j, 1) for j in range(NDIM)]
        ds = [spread(par[0, row[j], lane]) for j in range(NDIM)]
        ws = [spread(par[2, row[j], lane] * par[3, row[j], lane]) for j in range(NDIM)]
        st = [
            before[0, s, j, :, lane] + pw[j, :, lane] * st_in[0, s, row[j], lane]
            for j in range(NDIM)
        ]
        for t in range(PIECE):
            x = nf[i % BLOCKS, piece_rows(s, t), :]
            parts = [None, None]
            for j in range(NDIM):
                st[j] = ds[j] * st[j] + x
                term = ws[j] * st[j]
                parts[j % 2] = term if parts[j % 2] is None else parts[j % 2] + term
            sm[i % BLOCKS, piece_rows(s, t), :] = parts[0] + parts[1]
        return carry

    lax.fori_loop(0, seqs * BLOCKS, ema, 0)
    for s in range(seqs):
        pre = get_rows(sm, rows_of(s)) + skip[...] * get_rows(nf, rows_of(s))
        skip_pre[rows_of(s), :] = pre
        mixed[rows_of(s), :] = silu(pre).astype(BF16)
    sp = mm(mixed[...], wsh[...])
    shared_pre[...] = sp
    shared = silu(sp)
    query = (shared * qg[...]).astype(BF16)
    keys = (shared * kg[...]).astype(BF16)
    t_at = lax.broadcasted_iota(jnp.int32, (CH, CH), 0)
    s_at = lax.broadcasted_iota(jnp.int32, (CH, CH), 1)
    bias_t = jnp.broadcast_to(rb[...], (CH, CH))
    for bit in range(7):
        bias_t = jnp.where(
            jnp.bitwise_and(t_at, 1 << bit) > 0, pltpu.roll(bias_t, 1 << bit, 1), bias_t
        )
    bias = bias_t.T
    for s in range(seqs):
        raw = mm_nt(query[s * CH : (s + 1) * CH], keys[s * CH : (s + 1) * CH]) * Z ** (-0.5)
        live = (place * CH + s_at) < ids[3 + s]
        allowed = (s_at <= t_at) & (live | (s_at == t_at))
        masked = jnp.where(allowed, raw + bias, -1e30)
        top = jnp.max(masked, axis=-1, keepdims=True)
        weights = jnp.where(allowed, jnp.exp(masked - top), 0.0)
        prob[s] = weights / jnp.sum(weights, axis=-1, keepdims=True)


def mix_kernel(seqs, tp, ids, tok, normed, mixed, prob, *refs):
    near, far, refs = take_weights(refs, tp, 2, 4)
    (
        values, value_pre, reset_pre, attended, gated, hidden_pre, update_pre, middle,
        w1, w2, whu, sems,
    ) = refs
    vb = values.shape[2]
    nb = D // tp
    copies = gate_copies(tp, ids, near, far, w1, w2, sems)
    for c in copies:
        c.wait()
    gate_rows(tp, ids[0], w2, whu)
    hu = mm(mixed[...], whu[...])
    hidden_pre[...] = hu[:, :D]
    update_pre[...] = hu[:, D:]

    def block(r, carry):
        vp = mm(normed[...], w1[r, :, :vb])
        value_pre[r] = vp
        v = silu(vp).astype(BF16)
        values[r] = v
        rp = mm(mixed[...], w1[r, :, vb:])
        reset_pre[r] = rp
        gate = silu(rp)
        for s in range(seqs):
            att = mm(prob[s].astype(BF16), v[s * CH : (s + 1) * CH])
            attended[r, rows_of(s), :] = att
            gated[r, rows_of(s), :] = (gate[s * CH : (s + 1) * CH] * att).astype(BF16)
        hidden_pre[...] += mm(gated[r], w2[r, pl.ds(2 * nb, vb), :])
        return carry

    lax.fori_loop(0, tp, block, 0)
    for s in range(seqs):
        x = tok[s].astype(F32)
        middle[rows_of(s), :] = x + sigmoid(update_pre[rows_of(s), :]) * (
            silu(hidden_pre[rows_of(s), :]) - x
        )


def ffn_kernel(seqs, tp, ids, tok, cot, middle, hidden_pre, update_pre, gain2, *refs):
    near, far, refs = take_weights(refs, tp, 1, 2)
    (
        out, keep, send, grad_hu, resid, grad_gain2,
        w3, n2, lg, acc, gn2, sems,
    ) = refs
    vb = w3.shape[2] // 2
    top, half = tp // 2, D // 2
    cuts = D // vb
    upper = jnp.bitwise_and(ids[1], 1)
    copies = []

    def add(source, target):
        copies.append(pltpu.make_async_copy(source, target, sems.at[len(copies)]))

    for r in range(top):
        add(near[r][0], w3.at[r])
        for part, at in zip(far[r], (upper, 1 - upper)):
            add(part, w3.at[top + r, pl.ds(pl.multiple_of(at * half, half), half), :])
    for c in copies:
        c.start()
    place = ids[2]
    xhat, scale = normalized(middle[...])
    n2[...] = (xhat * gain2[...]).astype(BF16)
    at = lax.broadcasted_iota(jnp.int32, (CH, D), 0) + place * CH
    for s in range(seqs):
        lg[rows_of(s), :] = jnp.where(at < ids[3 + s], cot[s].astype(F32), 0.0).astype(BF16)
    acc[...] = jnp.zeros_like(acc)
    gn2[...] = jnp.zeros_like(gn2)
    for c in copies:
        c.wait()

    def block(h, carry):
        for odd in range(2):
            r = 2 * h + odd
            grads = (keep, send)[odd]
            pre = mm(n2[...], w3[r, :, :vb])
            inner = silu(pre).astype(BF16)
            back = None
            for k in range(cuts):
                cols = slice(k * vb, (k + 1) * vb)
                w_out = w3[r, cols, vb:]
                acc[:, cols] += mm(inner, w_out)
                term = mm_nt(lg[:, cols], w_out)
                back = term if back is None else back + term
            gip = (back * silu_slope(pre)).astype(BF16)
            gn2[...] += mm_nt(gip, w3[r, :, :vb])
            grads[h, :, :vb] = mm_tn(n2[...], gip).astype(BF16)
            gwo = mm_tn(inner, lg[...]).astype(BF16)
            for k in range(cuts):
                grads[h, k * vb : (k + 1) * vb, vb:] = gwo[:, k * vb : (k + 1) * vb]
        return carry

    lax.fori_loop(0, tp // 2, block, 0)
    mid = middle[...]
    out[...] = (mid + acc[...]).astype(BF16)
    grad = gn2[...]
    grad_gain2[...] = jnp.sum(grad * xhat, axis=0, keepdims=True)
    gm = lg[...].astype(F32) + norm_back(grad, xhat, scale, gain2[...])
    for s in range(seqs):
        x = tok[s].astype(F32)
        g = gm[s * CH : (s + 1) * CH]
        hp = hidden_pre[rows_of(s), :]
        update = sigmoid(update_pre[rows_of(s), :])
        grad_hu[rows_of(s), :D] = (g * update * silu_slope(hp)).astype(BF16)
        grad_hu[rows_of(s), D:] = (g * (silu(hp) - x) * update * (1.0 - update)).astype(BF16)
        resid[rows_of(s), :] = g * (1.0 - update)


def gates_kernel(tp, ids, mixed, gated, grad_hu, keep2, send2, ghu):
    nb = D // tp
    vb = gated.shape[2]
    wide = 2 * vb
    me = ids[0]
    ghu[...] = mm_tn(mixed[...], grad_hu[...])

    def block(h, carry):
        for odd in range(2):
            r = 2 * h + odd
            g2 = (keep2, send2)[odd]
            row = pl.ds(pl.multiple_of(jnp.bitwise_xor(me, r) * nb, nb), nb)
            gu = mm_tn(gated[r], grad_hu[:, :D]).astype(BF16)
            for k in range(D // wide):
                top = k * (2 * nb + vb)
                g2[h, pl.ds(top, nb), :] = ghu[row, pl.ds(k * wide, wide)].astype(BF16)
                g2[h, pl.ds(top + nb, nb), :] = ghu[row, pl.ds(D + k * wide, wide)].astype(BF16)
                g2[h, pl.ds(top + 2 * nb, vb), :] = gu[:, k * wide : (k + 1) * wide]
        return carry

    lax.fori_loop(0, tp // 2, block, 0)


def back_kernel(
    seqs, tp,
    ids, normed, mixed, skip_pre, shared_pre, prob, values, value_pre, reset_pre, attended,
    grad_hu, par, wsh, qg, kg, tok, before, st_in, skip, grad_gain2, *refs,
):
    near, far, refs = take_weights(refs, tp, 2, 4)
    (
        keep1, send1, grad_skip, grad_normed, after, ends, sums_keep, sums_send,
        w1, w2, whu, gm, gp, tab, grad_wsh, misc, table, nf, pw, sems,
    ) = refs
    vb = values.shape[2]
    nb = D // tp
    me = ids[0]
    copies = gate_copies(tp, ids, near, far, w1, w2, sems)
    gp[...] = jnp.zeros_like(gp)
    grad_normed[...] = jnp.zeros_like(grad_normed)
    for c in copies:
        c.wait()
    gate_rows(tp, me, w2, whu)
    gm[...] = mm_nt(grad_hu[...], whu[...])

    def block(h, carry):
        for odd in range(2):
            r = 2 * h + odd
            g1 = (keep1, send1)[odd]
            gg = mm_nt(grad_hu[:, :D], w2[r, pl.ds(2 * nb, vb), :])
            rp = reset_pre[r]
            sig = sigmoid(rp)
            ga = (gg * (rp * sig)).astype(BF16)
            grp = (gg * attended[r] * (sig * (1.0 + rp * (1.0 - sig)))).astype(BF16)
            g1[h, :, vb:] = mm_tn(mixed[...], grp).astype(BF16)
            gm[...] += mm_nt(grp, w1[r, :, vb:])
            gvs = []
            for s in range(seqs):
                part = ga[s * CH : (s + 1) * CH]
                gvs.append(mm_tn(prob[s].astype(BF16), part))
                gp[s] += mm_nt(part, values[r, rows_of(s), :])
            gv = jnp.concatenate(gvs, axis=0) if seqs > 1 else gvs[0]
            gvp = (gv * silu_slope(value_pre[r])).astype(BF16)
            g1[h, :, :vb] = mm_tn(normed[...], gvp).astype(BF16)
            grad_normed[...] += mm_nt(gvp, w1[r, :, :vb])
        return carry

    lax.fori_loop(0, tp // 2, block, 0)
    sp = shared_pre[...]
    shared = silu(sp)
    query = (shared * qg[...]).astype(BF16)
    keys = (shared * kg[...]).astype(BF16)
    total = jnp.zeros((CH, CH), F32)
    gqs = []
    gks = []
    for s in range(seqs):
        pr = prob[s]
        low = (pr * (gp[s] - jnp.sum(pr * gp[s], axis=-1, keepdims=True))).astype(BF16)
        total = total + low.astype(F32)
        gqs.append(mm(low, keys[s * CH : (s + 1) * CH]) * Z ** (-0.5))
        gks.append(mm_tn(low, query[s * CH : (s + 1) * CH]) * Z ** (-0.5))
    gq = jnp.concatenate(gqs, axis=0) if seqs > 1 else gqs[0]
    gk = jnp.concatenate(gks, axis=0) if seqs > 1 else gks[0]
    turned = total.T
    s_at = lax.broadcasted_iota(jnp.int32, (CH, CH), 0)
    for bit in range(7):
        turned = jnp.where(
            jnp.bitwise_and(s_at, 1 << bit) > 0, pltpu.roll(turned, CH - (1 << bit), 1), turned
        )
    misc[...] = jnp.concatenate(
        [
            jnp.sum(gq * shared, axis=0, keepdims=True),
            jnp.sum(gk * shared, axis=0, keepdims=True),
            jnp.sum(turned, axis=0, keepdims=True),
            jnp.zeros((1, D - 3 * Z), F32),
        ],
        axis=1,
    )
    gsp = ((gq * qg[...] + gk * kg[...]) * silu_slope(sp)).astype(BF16)
    grad_wsh[...] = mm_tn(mixed[...], gsp)
    put_rows(
        grad_skip,
        slice(None),
        (gm[...] + mm_nt(gsp, wsh[...])) * silu_slope(skip_pre[...]),
    )
    d = par[0]
    d2 = d * d
    d4 = d2 * d2
    d8 = d4 * d4
    q = d8 * d8
    tab[0] = q
    tab[1] = q * q
    tab[2] = q * q * q * q
    place = lax.broadcasted_iota(jnp.int32, (PIECES, LANES), 0)

    def body(i, carry):
        s = i // BLOCKS
        lane = lanes_of(i)
        ds = [spread(par[0, j : j + 1, lane]) for j in range(NDIM)]
        ad = [grad_skip[i % BLOCKS, piece_rows(s, PIECE - 1), :]] * NDIM
        for t in range(PIECE - 2, -1, -1):
            g = grad_skip[i % BLOCKS, piece_rows(s, t), :]
            for j in range(NDIM):
                ad[j] = ds[j] * ad[j] + g
        for j in range(NDIM):
            a = ad[j]
            for k, step in enumerate((1, 2, 4)):
                qm = spread(tab[k, j : j + 1, lane])
                a = a + qm * jnp.where(place < PIECES - step, pltpu.roll(a, PIECES - step, 0), 0.0)
            after[s, j, :, lane] = jnp.where(
                place < PIECES - 1, pltpu.roll(a, PIECES - 1, 0), 0.0
            )
            ends[s, j : j + 1, lane] = a[:1]
        return carry

    lax.fori_loop(0, seqs * BLOCKS, body, 0)
    small_sums(
        seqs, ids, tok, normed, grad_skip, grad_normed, par, before, st_in, skip, grad_gain2, misc,
        grad_wsh, sums_keep, sums_send, table, nf, pw,
    )


def small_sums(
    seqs, ids, tok, normed, grad_skip, grad_normed, par, before, st_in, skip, gain2_row, misc, grad_wsh,
    keep, send, table, nf, pw,
):
    put_rows(nf, slice(None), normed[...].astype(F32))
    piece_powers(par, pw)
    count = D // (D // Z)
    small = table.at[count:, :]
    small[...] = jnp.zeros_like(small)
    for k in range(D // Z):
        table[:count, k * Z : (k + 1) * Z] = grad_wsh[k * count : (k + 1) * count, :]

    def body(i, carry):
        s = i // BLOCKS
        lane = lanes_of(i)
        k16 = lax.broadcasted_iota(jnp.int32, (PIECES, LANES), 0).astype(F32) * PIECE
        for j0 in range(0, NDIM, 8):
            row = [pl.ds(j0 + j, 1) for j in range(8)]
            ds = [spread(par[0, row[j], lane]) for j in range(8)]
            st, ta, q, r = [], [], [], []
            for j in range(8):
                e = pw[j0 + j, :, lane] * st_in[0, s, row[j], lane]
                st.append(before[0, s, j0 + j, :, lane] + e)
                ta.append(
                    before[1, s, j0 + j, :, lane]
                    + pw[j0 + j, :, lane] * st_in[1, s, row[j], lane]
                    + k16 * e / ds[j]
                )
                q.append(jnp.zeros((PIECES, LANES), F32))
                r.append(jnp.zeros((PIECES, LANES), F32))
            for t in range(PIECE):
                x = nf[i % BLOCKS, piece_rows(s, t), :]
                g = grad_skip[i % BLOCKS, piece_rows(s, t), :]
                for j in range(8):
                    ta[j] = ds[j] * ta[j] + st[j]
                    st[j] = ds[j] * st[j] + x
                    q[j] = q[j] + g * st[j]
                    r[j] = r[j] + g * ta[j]
            for j in range(8):
                small[pl.ds(j0 + j, 1), lane] += jnp.sum(q[j], axis=0, keepdims=True)
                small[pl.ds(NDIM + j0 + j, 1), lane] += jnp.sum(r[j], axis=0, keepdims=True)
        return carry

    lax.fori_loop(0, seqs * BLOCKS, body, 0)
    gsk = jnp.zeros((1, D), F32)
    gn1 = jnp.zeros((1, D), F32)
    for s in range(seqs):
        xhat, _ = normalized(tok[s].astype(F32))
        g = get_rows(grad_skip, rows_of(s))
        direct = g * skip[...] + grad_normed[rows_of(s), :]
        gsk = gsk + jnp.sum(g * get_rows(nf, rows_of(s)), axis=0, keepdims=True)
        gn1 = gn1 + jnp.sum(direct * xhat, axis=0, keepdims=True)
    small[2 * NDIM : 2 * NDIM + 1, :] = gsk
    small[2 * NDIM + 1 : 2 * NDIM + 2, :] = gn1
    small[2 * NDIM + 2 : 2 * NDIM + 3, :] = gain2_row[...]
    small[2 * NDIM + 3 : 2 * NDIM + 4, :] = misc[...]
    half = keep.shape[0]
    mine = jnp.bitwise_and(ids[0], 1) * half
    keep[...] = table[pl.ds(pl.multiple_of(mine, 8), half), :]
    send[...] = table[pl.ds(pl.multiple_of(half - mine, 8), half), :]


def pair_kernel(bit, ids, mine, other, out):
    half = mine.shape[0]
    upper = jnp.where(jnp.bitwise_and(ids[0], bit) > 0, half, 0)
    out[pl.ds(pl.multiple_of(upper, 8), half), :] = mine[...]
    out[pl.ds(pl.multiple_of(half - upper, 8), half), :] = other[...]


def finish_kernel(
    ids, par, rate, beta, gain, mine, other,
    grad_gain, grad_rate, grad_beta, grad_eta, grad_skip, grad_wsh, grad_qg, grad_kg, grad_rb,
    grad_gain2, table,
):
    pair_kernel(1, ids, mine, other, table)
    count = D // (D // Z)
    for k in range(D // Z):
        grad_wsh[k * count : (k + 1) * count, :] = table[:count, k * Z : (k + 1) * Z]
    small = table.at[count:, :]
    inflow, eta, r = par[2], par[3], rate[...]
    root = jnp.sqrt(r * (2.0 - r))
    q_sum = small[:NDIM, :]
    grad_inflow = eta * q_sum
    grad_decay = eta * inflow * small[NDIM : 2 * NDIM, :]
    grad_rate[...] = grad_inflow * beta[...] * (1.0 - r) / root - grad_decay
    grad_beta[...] = grad_inflow * root
    grad_eta[...] = inflow * q_sum
    row = [small[2 * NDIM + i : 2 * NDIM + i + 1, :] for i in range(4)]
    grad_skip[...] = row[0]
    grad_gain[...] = row[1] + jnp.sum(inflow * grad_inflow, axis=0, keepdims=True) / gain[...]
    grad_gain2[...] = row[2]
    grad_qg[...] = row[3][:, :Z]
    grad_kg[...] = row[3][:, Z : 2 * Z]
    grad_rb[...] = row[3][:, 2 * Z : 3 * Z]


def leave_kernel(
    seqs, tops, ids, tok, par, grad_skip, grad_normed, behind, resid, gain, skip, *refs
):
    levels = len(tops)
    recvs, refs = refs[:levels], refs[levels:]
    grad_tokens, ad_in, pw, sm = refs
    place = ids[2]
    logd = par[1]
    gots = [get_wide(recvs[k], tops[k], seqs * NDIM) for k in range(levels)]
    for s in range(seqs):
        a = jnp.zeros((NDIM, D), F32)
        for k in range(levels):
            low = jnp.bitwise_and(place, 1 << k) == 0
            off = jnp.bitwise_and(place, (1 << k) - 1)
            away = ((1 << k) - 1 - off).astype(F32) * float(CH)
            got = gots[k][s * NDIM : (s + 1) * NDIM]
            a = a + got * jnp.where(low, jnp.exp(away * logd), 0.0)
        ad_in[s] = a
    k = (PIECES - 1 - lax.broadcasted_iota(jnp.int32, (PIECES, D), 0)).astype(F32) * PIECE
    for j in range(NDIM):
        pw[j] = jnp.exp(k * par[1, j : j + 1, :])

    def body(i, carry):
        s = i // BLOCKS
        lane = lanes_of(i)
        row = [pl.ds(j, 1) for j in range(NDIM)]
        ds = [spread(par[0, row[j], lane]) for j in range(NDIM)]
        ws = [spread(par[2, row[j], lane] * par[3, row[j], lane]) for j in range(NDIM)]
        ad = [
            behind[s, j, :, lane] + pw[j, :, lane] * ad_in[s, row[j], lane] for j in range(NDIM)
        ]
        for t in range(PIECE - 1, -1, -1):
            g = grad_skip[i % BLOCKS, piece_rows(s, t), :]
            parts = [None, None]
            for j in range(NDIM):
                ad[j] = ds[j] * ad[j] + g
                term = ws[j] * ad[j]
                parts[j % 2] = term if parts[j % 2] is None else parts[j % 2] + term
            sm[i % BLOCKS, piece_rows(s, t), :] = parts[0] + parts[1]
        return carry

    lax.fori_loop(0, seqs * BLOCKS, body, 0)
    for s in range(seqs):
        xhat, scale = normalized(tok[s].astype(F32))
        grad = (
            get_rows(sm, rows_of(s))
            + get_rows(grad_skip, rows_of(s)) * skip[...]
            + grad_normed[rows_of(s), :]
        )
        grad_tokens[s] = (
            resid[rows_of(s), :] + norm_back(grad, xhat, scale, gain[...])
        ).astype(BF16)


def hop_kernel(seqs, shift, count, ids, state, *refs):
    others, (total, low) = refs[: count - 1], refs[count - 1 :]
    mine = jnp.bitwise_and(jnp.right_shift(ids[2], shift), count - 1)
    logd = state[2 * seqs]
    total[2 * seqs] = logd
    sums = [None] * (2 * seqs)
    for k in range(count):
        after = (count - 1 - jnp.bitwise_xor(mine, k)).astype(F32) * float(CH << shift)
        power = jnp.exp(after * logd)
        slope = after * jnp.exp((after - 1.0) * logd)
        for i in range(0, 2 * seqs, 2):
            part = (state if k == 0 else others[k - 1])[i : i + 2].astype(F32)
            a, b = power * part[0], power * part[1] + slope * part[0]
            sums[i : i + 2] = [a, b] if k == 0 else [sums[i] + a, sums[i + 1] + b]
    for i in range(2 * seqs):
        total[i] = sums[i]
        low[i] = sums[i].astype(BF16)


def put_wide(ref, top, value):
    wide = ref.shape[1]
    count = value.shape[0]
    for k in range(D // wide):
        ref[pl.ds(top + k * count, count), :] = value[:, k * wide : (k + 1) * wide].astype(ref.dtype)


def get_wide(ref, top, count):
    wide = ref.shape[1]
    runs = [ref[pl.ds(top + k * count, count), :].astype(F32) for k in range(D // wide)]
    return jnp.concatenate(runs, axis=1) if len(runs) > 1 else runs[0]


def first_back_hop(seqs, joins, ids, par, own, other, sums, got, out, keep, payload):
    rows = seqs * NDIM
    fold_lanes = D // payload.shape[1]
    if joins:
        join_adjoint(seqs, 0, ids, par, own, other[...], out)
    else:
        out[...] = own[...]
    put_wide(payload, 0, out[...])
    half = keep.shape[0]
    upper = jnp.where(jnp.bitwise_and(ids[0], 2) > 0, half, 0)
    mine = pl.ds(pl.multiple_of(upper, 8), half)
    theirs = pl.ds(pl.multiple_of(half - upper, 8), half)
    keep[...] = sums[mine, :] + got[mine, :]
    put_wide(payload, rows * fold_lanes, sums[theirs, :] + got[theirs, :])


def join_adjoint(seqs, level, ids, par, own, got, out):
    upper = jnp.bitwise_and(ids[2], 1 << level) > 0
    power = jnp.exp(float(CH << level) * par[1])
    for s in range(seqs):
        row = slice(s * NDIM, (s + 1) * NDIM)
        early = jnp.where(upper, got[row], own[row, :])
        late = jnp.where(upper, own[row, :], got[row])
        out[row, :] = early + power * late


def chain_hop(seqs, level, split, halved, top, ids, par, own, kept, sent, other, out, keep, payload, base):
    rows = seqs * NDIM
    lanes = D // other.shape[1]
    if out is not None:
        join_adjoint(seqs, level, ids, par, own, get_wide(other, top, rows), out)
        put_wide(payload, base, out[...])
    half = keep.shape[0]
    if split:
        upper = jnp.bitwise_and(ids[0], split) > 0
        got = get_wide(other, top + rows * lanes, 2 * half)
        first, second = kept[:half, :] + got[:half], kept[half:, :] + got[half:]
        keep[...] = jnp.where(upper, second, first)
        put_wide(payload, base + rows * lanes, jnp.where(upper, first, second))
    else:
        mine = kept[...] if halved else get_wide(sent, top + rows * lanes, half)
        total = mine + get_wide(other, top + rows * lanes, half)
        keep[...] = total
        if payload is not None:
            put_wide(payload, base + rows * lanes, total)


def back_hop(seqs, level, split, halved, ids, par, own, kept, sent, other, out, keep, payload):
    chain_hop(
        seqs, level, split, halved, 0, ids, par, own, kept, sent, other, out, keep, payload, 0
    )


def split_rows(count, cut, place, k):
    shift, bits = cut
    rows = count >> bits
    sub = jnp.bitwise_and(jnp.right_shift(place, shift), (1 << bits) - 1)
    return pl.multiple_of(jnp.bitwise_xor(sub, k) * rows, rows), rows


def add_rows(parts, start, high, out, top, lane, width, at):
    step = min(64, high)

    def body(i, carry):
        row = pl.ds(pl.multiple_of(start + i * step, step), step)
        total = parts[0][row, lane : lane + width].astype(F32)
        for other in parts[1:]:
            total = total + other[row, lane : lane + width].astype(F32)
        out[pl.ds(pl.multiple_of(top + i * step, 16), step), at : at + width] = total.astype(BF16)
        return carry

    lax.fori_loop(0, high // step, body, 0)


def fold_kernel(jobs, inputs, ids, *refs):
    parts, outs = refs[:inputs], refs[inputs:]
    at = 0
    for count, lane, width, cut, targets in jobs:
        own = parts[at : at + count]
        at += count
        blocks, rows, _ = own[0].shape
        for k, (target, block, offset) in enumerate(targets):
            if cut == "tp":
                ranges, start, high = (k,), 0, rows
            elif cut is None:
                ranges, start, high = range(blocks), 0, rows
            else:
                start, high = split_rows(rows, cut, ids[1], k)
                ranges = range(blocks)
            for to, b in enumerate(ranges):
                add_rows(
                    [p.at[b] for p in own], start, high, outs[target].at[block + to], 0, lane,
                    width, offset,
                )


def fold(ids, shapes, jobs):
    arrays = [a for job in jobs for a in job[0]]
    plan = [(len(job[0]),) + tuple(job[1:]) for job in jobs]
    return call(
        functools.partial(fold_kernel, plan, len(arrays)),
        tuple(shape(dims, BF16) for dims in shapes),
        [],
        (ids, *arrays),
        [SMEM] + [VMEM] * len(arrays),
        "fold",
    )


def join_kernel(cut, ids, mine, other, out):
    blocks, rows, _ = mine.shape
    for k, part in enumerate((mine, other)):
        start, _ = split_rows(2 * rows, cut, ids[1], k)
        for b in range(blocks):
            out[b, pl.ds(pl.multiple_of(start, 16), rows), :] = part[b]


def join(ids, mine, other, cut):
    blocks, rows, lanes = mine.shape
    return call(
        functools.partial(join_kernel, cut),
        (shape((blocks, 2 * rows, lanes), BF16),),
        [],
        (ids, mine, other),
        [SMEM, VMEM, VMEM],
        "join",
    )[0]


def ride_kernel(
    seqs, level, split, halved, top, jobs, cut, high, last, ids, par, own, kept, sent, other, *refs
):
    count = 1 + max(p for job in jobs for p in job[0])
    parts, refs = refs[:count], refs[count:]
    out = payload = None
    if last:
        keep, kept_out = refs
        halves = ((0, keep),)
    elif cut is None:
        kept_out, out, payload = refs
        halves = ((0, payload),)
    else:
        keep, kept_out, out, payload = refs
        halves = ((0, keep), (1, payload))
    for picks, width, at in jobs:
        chosen = [other if p == -1 else sent if p == -2 else parts[p] for p in picks]
        for k, target in halves:
            start = 0 if cut is None else split_rows(2 * high, cut, ids[1], k)[0]
            add_rows(chosen, start, high, target, 0, 0, width, at)
    chain_hop(
        seqs, level, split, halved, top, ids, par, own, kept, sent, other, out, kept_out, payload,
        high,
    )


def unpack_first(cut, ids, *refs):
    count = 1 << cut[1]
    pieces, refs = refs[:count], refs[count:]
    w_in, w_out = refs[:2]
    outs = refs[2:]
    vb = w_in.shape[1]
    wide = 2 * vb
    each = sum(out.shape[0] for out in outs)
    for k in range(count):
        row, rows = split_rows(D, cut, ids[1], k)
        w_in[pl.ds(row, rows), :] = pieces[k][0, :, :vb].astype(F32)
        for first in range(0, rows, vb):
            w_out[:, pl.ds(pl.multiple_of(row + first, vb), vb)] = pieces[k][
                0, first : first + vb, vb:
            ].astype(F32)
        for b in range(count):

            @pl.when(row == b * rows)
            def _(k=k, b=b, rows=rows):
                for run in range(D // wide):
                    start = run * each
                    for out in outs:
                        end = start + out.shape[0]
                        lo, hi = max(start, b * rows), min(end, (b + 1) * rows)
                        if lo < hi:
                            out[lo - start : hi - start, run * wide : (run + 1) * wide] = pieces[k][
                                1, lo - b * rows : hi - b * rows, :
                            ].astype(F32)
                        start = end


def unpack_sides(cut, ids, *refs):
    count = 1 << cut[1]
    pieces, (left, right) = refs[:count], refs[count:]
    vb = left.shape[1]
    for k in range(count):
        row, rows = split_rows(D, cut, ids[1], k)
        left[pl.ds(row, rows), :] = pieces[k][0, :, :vb].astype(F32)
        right[pl.ds(row, rows), :] = pieces[k][0, :, vb:].astype(F32)


def unpack(body, cut, ids, pieces, dims):
    return call(
        functools.partial(body, cut),
        tuple(shape(d) for d in dims),
        [],
        (ids, *pieces),
        [SMEM] + [VMEM] * len(pieces),
        "unpack",
    )


BOTH = ("seq", "tp")


def swap(value, mask):
    count = lax.axis_size("seq") * lax.axis_size("tp")
    return lax.ppermute(value, BOTH, [(i, i ^ mask) for i in range(count)])


def after(value, *others):
    return lax.optimization_barrier((value, *others))[0]


def bits_of(count):
    return [1 << k for k in range(count.bit_length() - 1)]


def has(index, bit):
    return jnp.bitwise_and(index, bit) > 0


def half_of(value, upper):
    half = value.shape[0] // 2
    return lax.dynamic_slice_in_dim(value, jnp.where(upper, half, 0), half, 0)


def joined(mine, other, upper):
    return jnp.where(
        upper,
        jnp.concatenate([other, mine], axis=0),
        jnp.concatenate([mine, other], axis=0),
    )


def spread_out(own, tp):
    pieces = {0: own}
    for bit in reversed(bits_of(tp // 2)):
        for r in list(pieces):
            pieces[r ^ bit] = [swap(a, bit) for a in pieces[r]]
    return [pieces[r] for r in range(tp // 2)]


def per_device(
    tokens,
    cotangent,
    valid_lengths,
    norm1_gain,
    ema_rate,
    ema_beta,
    ema_eta,
    ema_skip,
    w_shared,
    query_gain,
    key_gain,
    rel_bias,
    w_value,
    w_reset,
    w_update,
    w_hidden,
    u_hidden,
    norm2_gain,
    w_in,
    w_out,
):
    part = lax.axis_index("tp")
    tp = lax.axis_size("tp")
    seq = lax.axis_size("seq")
    all_seqs, local_rows, _ = tokens.shape
    vb = w_value.shape[1]
    nb = D // tp
    ybits = far_shift()
    traded = local_rows < CH
    lower = part % 2 == 0

    def trade(value):
        if not traded:
            return value
        other = swap(jnp.where(lower, value[1], value[0]), 1)
        mine = jnp.where(lower, value[0], value[1])
        return joined(mine, other, ~lower)[None]

    def trade_back(value):
        if not traded:
            return value
        first, second = value[0, :local_rows], value[0, local_rows:]
        other = swap(jnp.where(lower, second, first), 1)
        mine = jnp.where(lower, first, second)
        return jnp.where(lower, jnp.stack([mine, other]), jnp.stack([other, mine]))

    if traded:
        assert all_seqs == 2 and 2 * local_rows == CH
        seqs = 1
    else:
        assert local_rows == CH
        seqs = all_seqs
    rows = seqs * CH
    ids, ids_lengths = Here(seqs, None), Here(seqs, valid_lengths.astype(jnp.int32))
    masks = bits_of(tp * seq)[int(traded) :]
    levels = len(masks)

    tok = trade(tokens)
    cot = trade(cotangent)
    gain1 = norm1_gain[None]
    gain2 = norm2_gain[None]
    skip = ema_skip[None]
    rate, beta = ema_rate.T, ema_beta.T
    qg, kg, rb = query_gain[None], key_gain[None], rel_bias[None]

    top = tp // 2
    weights = (w_value, w_reset, w_hidden, w_update, u_hidden, w_in, w_out)
    rows2 = 2 * nb + vb
    normed, par, before, ends, low = call(
        functools.partial(enter_kernel, seqs),
        (
            shape((rows, D), BF16),
            shape((4, NDIM, D)),
            shape((2, seqs, NDIM, PIECES, D)),
            shape((2 * seqs + 1, NDIM, D)),
            shape((2 * seqs, NDIM, D), BF16),
        ),
        [
            pltpu.VMEM((seqs, CH, D), BF16),
            pltpu.VMEM((1, D), F32),
            pltpu.VMEM((NDIM, D), F32),
            pltpu.VMEM((NDIM, D), F32),
            pltpu.VMEM((NDIM, D), F32),
            pltpu.VMEM((BLOCKS, rows, LANES), F32),
            pltpu.VMEM((6, NDIM, D), F32),
            pltpu.SemaphoreType.DMA((5,)),
        ],
        (tok, gain1, rate, beta, ema_eta.T),
        [ANY] * 5,
        "enter",
        limit=58.96,
    )
    start = 1 - int(traded)
    groups = [(0, 1)] * start + [(start, 2)] + [(i, 1) for i in range(start + 2, levels)]
    hops = []
    (half1,) = call(
        first_half_kernel,
        (shape((D // 2, 2 * vb), BF16),),
        [pltpu.SemaphoreType.DMA((2,))],
        (w_value, w_reset),
        [ANY] * 2,
        "half",
        limit=60,
        outs=(pl.BlockSpec(),),
    )
    mine1 = swap(half1, top)
    state, low = ends, after(low, mine1)
    for i, (shift, bits) in enumerate(groups):
        if i == start:
            pack1, pack2, pack3, half2, half3 = call(
                pack_kernel,
                (
                    shape((D, 2 * vb), BF16),
                    shape((rows2, D), BF16),
                    shape((D, 2 * vb), BF16),
                    shape((rows2, D // 2), BF16),
                    shape((D // 2, 2 * vb), BF16),
                ),
                [pltpu.SemaphoreType.DMA((10 + 3 * D // vb // 2,))],
                lax.optimization_barrier((*weights, low))[:-1],
                [ANY] * 7,
                "pack",
                limit=60,
                outs=(pl.BlockSpec(),) * 5,
            )
        if i == start + 1:
            mine2 = swap(after(half2, low), top)
            other1 = swap(after(mine1, low), tp)
            near_gates = spread_out([after(pack1, low), after(pack2, low)], tp)
        if i == start + 2:
            low = after(low, mine2, other1, *near_gates[-1])
            mine3 = swap(after(half3, low), top)
            other2 = swap(after(mine2, low), tp << ybits)
            near_feeds = spread_out([after(pack3, low)], tp)
        got = []
        for k in range(1, 1 << bits):
            got.append(swap(low, k << (shift + int(traded))))
            hops.append((shift, k, got[-1]))
        if i + 1 < len(groups):
            state, low = call(
                functools.partial(hop_kernel, seqs, shift, 1 << bits),
                (shape((2 * seqs + 1, NDIM, D)), shape((2 * seqs, NDIM, D), BF16)),
                [],
                (ids, state, *got),
                [SMEM] + [VMEM] * (1 + len(got)),
                "hop",
            )
    st_in, skip_pre, mixed, shared_pre, prob = call(
        functools.partial(look_kernel, seqs, [h[:2] for h in hops]),
        (
            shape((2, seqs, NDIM, D)),
            shape((rows, D)),
            shape((rows, D), BF16),
            shape((rows, Z)),
            shape((seqs, CH, CH)),
        ),
        [
            pltpu.VMEM((BLOCKS, rows, LANES), F32),
            pltpu.VMEM((BLOCKS, rows, LANES), F32),
            pltpu.VMEM((NDIM, PIECES, D), F32),
        ],
        (
            ids_lengths, after(normed, mine3), par, before, skip, w_shared, qg, kg, rb,
            *[h[2] for h in hops],
        ),
        [SMEM] + [VMEM] * (8 + len(hops)),
        "look",
        limit=10,
    )
    far_gates = spread_out([mine1, after(other1, prob), mine2, after(other2, prob)], tp)
    other3 = swap(mine3, tp)
    gates = [w for group in near_gates + far_gates for w in group]

    values, value_pre, reset_pre, attended, gated, hidden_pre, update_pre, middle = call(
        functools.partial(mix_kernel, seqs, tp),
        (
            shape((tp, rows, vb), BF16),
            shape((tp, rows, vb)),
            shape((tp, rows, vb)),
            shape((tp, rows, vb)),
            shape((tp, rows, vb), BF16),
            shape((rows, D)),
            shape((rows, D)),
            shape((rows, D)),
        ),
        [
            pltpu.VMEM((tp, D, 2 * vb), BF16),
            pltpu.VMEM((tp, rows2, D), BF16),
            pltpu.VMEM((D, 2 * D), BF16),
            pltpu.SemaphoreType.DMA((3 * tp,)),
        ],
        (ids, tok, normed, after(mixed, other3), prob, *gates),
        [SMEM] + [VMEM] * 4 + [ANY] * len(gates),
        "mix",
        limit=10,
    )

    far_feeds = spread_out([mine3, other3], tp)
    feeds = [w for group in near_feeds + far_feeds for w in group]
    out, keep3, send3, grad_hu, resid, grad_gain2 = call(
        functools.partial(ffn_kernel, seqs, tp),
        (
            shape((rows, D), BF16),
            shape((tp // 2, D, 2 * vb), BF16),
            shape((tp // 2, D, 2 * vb), BF16),
            shape((rows, 2 * D), BF16),
            shape((rows, D)),
            shape((1, D)),
        ),
        [
            pltpu.VMEM((tp, D, 2 * vb), BF16),
            pltpu.VMEM((rows, D), BF16),
            pltpu.VMEM((rows, D), BF16),
            pltpu.VMEM((rows, D), F32),
            pltpu.VMEM((rows, D), F32),
            pltpu.SemaphoreType.DMA((3 * tp // 2,)),
        ],
        (ids_lengths, tok, cot, middle, hidden_pre, update_pre, gain2, *feeds),
        [SMEM] + [VMEM] * 6 + [ANY] * len(feeds),
        "ffn",
        limit=10,
    )

    half = tp // 2
    yn = 1 << ybits
    wide = 2 * vb
    runs = D // wide
    cut_of_y = (0, ybits)
    zcuts = [(shift, 1) for shift in range(ybits, seq.bit_length() - 1)]

    def over_tp(pieces):
        return [pieces[0]] + [swap(p, 2 * k) for k, p in enumerate(pieces) if k]

    def over_y(pieces):
        return [pieces[0]] + [swap(p, tp * k) for k, p in enumerate(pieces) if k]

    def over_z(value, cut):
        return swap(value, tp << cut[0])

    def cut_tp(parts, dims):
        n = dims[0]
        return fold(
            ids,
            [(1,) + dims[1:]] * n,
            [(parts, 0, dims[2], "tp", [(k, 0, 0) for k in range(n)])],
        )

    def cut_y(parts, dims):
        return fold(
            ids,
            [(dims[0], dims[1] // yn, dims[2])] * yn,
            [(parts, 0, dims[2], cut_of_y, [(k, 0, 0) for k in range(yn)])],
        )

    last = [None]

    def now(value):
        return value if last[0] is None else after(value, last[0])

    chunk = (half, D, wide)
    got3 = swap(send3, 1)
    keep2, send2 = call(
        functools.partial(gates_kernel, tp),
        (shape(chunk, BF16), shape(chunk, BF16)),
        [pltpu.VMEM((D, 2 * D), F32)],
        (ids, mixed, gated, grad_hu),
        [SMEM] + [VMEM] * 3,
        "gates",
        limit=10,
    )
    got2 = swap(send2, 1)
    g3 = cut_tp([keep3, got3], chunk)
    g3 = over_tp(g3)
    g2 = cut_y([keep2, after(got2, g3[0])], chunk)
    g2 = over_y(g2)

    count = Z + SMALL_ROWS
    count += -count % (16 * tp)
    (
        keep1, send1, grad_skip, grad_normed, behind, back_ends, sums_keep, sums_send,
    ) = call(
        functools.partial(back_kernel, seqs, tp),
        (
            shape(chunk, BF16),
            shape(chunk, BF16),
            shape((BLOCKS, rows, LANES)),
            shape((rows, D)),
            shape((seqs, NDIM, PIECES, D)),
            shape((seqs, NDIM, D)),
            shape((count // 2, D)),
            shape((count // 2, D)),
        ),
        [
            pltpu.VMEM((tp, D, 2 * vb), BF16),
            pltpu.VMEM((tp, rows2, D), BF16),
            pltpu.VMEM((D, 2 * D), BF16),
            pltpu.VMEM((rows, D), F32),
            pltpu.VMEM((seqs, CH, CH), F32),
            pltpu.VMEM((3, NDIM, D), F32),
            pltpu.VMEM((D, Z), F32),
            pltpu.VMEM((1, D), F32),
            pltpu.VMEM((count, D), F32),
            pltpu.VMEM((BLOCKS, rows, LANES), F32),
            pltpu.VMEM((NDIM, PIECES, D), F32),
            pltpu.SemaphoreType.DMA((3 * tp,)),
        ],
        (
            ids, normed, mixed, skip_pre, shared_pre, prob, values, value_pre, reset_pre, attended,
            after(grad_hu, g2[0]), par, w_shared, qg, kg, tok, before, st_in, skip, grad_gain2,
            *gates,
        ),
        [SMEM] + [VMEM] * 19 + [ANY] * len(gates),
        "back",
        limit=12,
    )

    g3 = cut_y([after(g3[0], send1)] + g3[1:], (1, D, wide))
    g2 = cut_tp([after(g2[0], g3[0])] + g2[1:], (half, D // yn, wide))
    (
        keep1, send1, grad_skip, grad_normed, behind, back_ends, sums_keep, sums_send, _,
    ) = lax.optimization_barrier(
        (keep1, send1, grad_skip, grad_normed, behind, back_ends, sums_keep, sums_send, g2[0])
    )
    adjoint = back_ends.reshape(seqs * NDIM, D)
    last[0] = g2[0]
    g3 = over_y(g3)
    g2 = over_tp(g2)
    got1 = swap(send1, 1)
    got_adjoint = adjoint if traded else swap(adjoint, 1)
    got_sums = swap(sums_send, 1)
    done = {}

    def first_chunks():
        high = D // yn >> 1
        keep, send = fold(
            ids,
            [(2, high, wide)] * 2,
            [
                ([now(g3[0])] + g3[1:], 0, wide, zcuts[0], [(0, 0, 0), (1, 0, 0)]),
                (g2, 0, wide, zcuts[0], [(0, 1, 0), (1, 1, 0)]),
            ],
        )
        for i, cut in enumerate(zcuts[1:-1]):
            other = over_z(send, zcuts[i])
            yield keep
            high //= 2
            keep, send = fold(
                ids,
                [(2, high, wide)] * 2,
                [([now(keep), other], 0, wide, cut, [(0, 0, 0), (1, 0, 0)])],
            )
        other = over_z(send, zcuts[-2])
        yield keep
        total = keep
        for cut in zcuts[-1:] + [None]:
            (total,) = fold(ids, [keep.shape], [([now(total), other], 0, wide, None, [(0, 0, 0)])])
            if cut:
                other = over_z(total, cut)
                yield total
        for cut in reversed(zcuts[:-1]):
            other = over_z(total, cut)
            yield total
            total = join(ids, now(total), other, cut)
        pieces = over_y([total] * yn)
        yield total
        done["first"] = unpack(
            unpack_first,
            cut_of_y,
            ids,
            [now(pieces[0])] + pieces[1:],
            [(D, vb), (vb, D), (nb, D), (nb, D), (vb, D)],
        )
        yield done["first"][0]

    def second_chunk():
        small_high = count // 4
        ad_rows = seqs * NDIM

        def payload_rows():
            return (ad_rows + small_high) * runs

        own, kept, payload = call(
            functools.partial(first_back_hop, seqs, not traded),
            (
                shape((ad_rows, D)),
                shape((small_high, D)),
                shape((payload_rows(), wide), BF16),
            ),
            [],
            (ids, par, now(adjoint), got_adjoint, sums_keep, got_sums),
            [SMEM] + [VMEM] * 5,
            "hop",
        )
        got = [] if traded else [(got_adjoint, 0)]
        level = int(not traded)
        halved = True
        other = swap(payload, masks[level])
        yield payload
        parts = fold(
            ids,
            [(1, D, vb)] * half + [(half, D // yn, vb)] * yn,
            [
                ([now(keep1), got1], 0, vb, "tp", [(k, 0, 0) for k in range(half)]),
                ([keep1, got1], vb, vb, cut_of_y, [(half + k, 0, 0) for k in range(yn)]),
            ],
        )
        left, right = over_tp(parts[:half]), over_y(parts[half:])
        yield parts[0]
        crossed = False
        while level + 1 < levels - len(zcuts):
            got.append((other, 0))
            split = 2 * masks[level] if 2 * masks[level] < tp else 0
            small_high = small_high // 2 if split else small_high
            own, kept, payload = call(
                functools.partial(back_hop, seqs, level, split, halved),
                (
                    shape((ad_rows, D)),
                    shape((small_high, D)),
                    shape((payload_rows(), wide), BF16),
                ),
                [],
                (ids, par, now(own), kept, payload, other),
                [SMEM] + [VMEM] * 5,
                "hop",
            )
            halved = bool(split)
            level += 1
            other = swap(payload, masks[level])
            yield payload
            if crossed:
                continue
            crossed = True
            parts = fold(
                ids,
                [(1, D // yn, vb)] * (yn + half),
                [
                    ([now(left[0])] + left[1:], 0, vb, cut_of_y, [(k, 0, 0) for k in range(yn)]),
                    (right, 0, vb, "tp", [(yn + k, 0, 0) for k in range(half)]),
                ],
            )
            left, right = over_y(parts[:yn]), over_tp(parts[yn:])
            yield parts[0]
        high = D // yn
        top = 0
        flat = [p.reshape(p.shape[1:]) for p in left + right]
        jobs = [
            (tuple(range(len(left))), vb, 0),
            (tuple(range(len(left), len(flat))), vb, vb),
        ]
        for cut in zcuts[:-1] + [None]:
            got.append((other, top))
            high = high // 2 if cut else high
            kept_chunk = [shape((high, wide), BF16)] if cut else []
            *flat, kept, own, payload = call(
                functools.partial(
                    ride_kernel, seqs, level, 0, halved, top, jobs, cut, high, False
                ),
                (
                    *kept_chunk,
                    shape((small_high, D)),
                    shape((ad_rows, D)),
                    shape((high + payload_rows(), wide), BF16),
                ),
                [],
                (ids, par, now(own), kept, payload, other, *flat),
                [SMEM] + [VMEM] * (5 + len(flat)),
                "ride",
            )
            halved = False
            level += 1
            top = high
            jobs = [((0 if cut else -2, -1), wide, 0)]
            other = swap(payload, masks[level])
            yield payload
        got.append((other, top))
        total, kept = call(
            functools.partial(ride_kernel, seqs, level, 0, False, top, jobs, None, high, True),
            (shape((high, wide), BF16), shape((small_high, D))),
            [],
            (ids, par, now(own), kept, payload, other, *flat),
            [SMEM] + [VMEM] * (5 + len(flat)),
            "ride",
        )
        bits = list(reversed(bits_of(tp)))
        total = total[None]
        far = swap(kept, bits[0])
        other = over_z(total, zcuts[-2])
        yield total
        (done["tokens"],) = call(
            functools.partial(leave_kernel, seqs, [at for _, at in got]),
            (shape((seqs, CH, D), BF16),),
            [
                pltpu.VMEM((seqs, NDIM, D), F32),
                pltpu.VMEM((NDIM, PIECES, D), F32),
                pltpu.VMEM((BLOCKS, rows, LANES), F32),
            ],
            (
                ids, tok, par, now(grad_skip), grad_normed, behind, resid, gain1, skip,
                *[g for g, _ in got],
            ),
            [SMEM] + [VMEM] * (8 + levels),
            "leave",
            limit=10,
        )
        yield done["tokens"]
        for i in range(len(zcuts) - 2, -1, -1):
            total = join(ids, now(total), other, zcuts[i])
            if i:
                other = over_z(total, zcuts[i - 1])
                yield total
        pieces = over_y([total] * yn)
        yield total
        for i in range(len(bits) - 1):
            (kept,) = call(
                functools.partial(pair_kernel, bits[i]),
                (shape((2 * kept.shape[0], D)),),
                [],
                (ids, now(kept), far),
                [SMEM, VMEM, VMEM],
                "pair",
            )
            far = swap(kept, bits[i + 1])
            yield kept
        done["small"] = call(
            finish_kernel,
            (
                shape((1, D)),
                shape((NDIM, D)),
                shape((NDIM, D)),
                shape((NDIM, D)),
                shape((1, D)),
                shape((D, Z)),
                shape((1, Z)),
                shape((1, Z)),
                shape((1, Z)),
                shape((1, D)),
            ),
            [pltpu.VMEM((count, D), F32)],
            (ids, par, rate, beta, gain1, now(kept), far),
            [SMEM] + [VMEM] * 6,
            "finish",
        )
        yield done["small"][0]
        done["second"] = unpack(
            unpack_sides, cut_of_y, ids, [now(pieces[0])] + pieces[1:], [(D, vb), (D, vb)]
        )
        yield done["second"][0]

    walks = {"f": first_chunks(), "s": second_chunk()}
    order = "sssfsfsfsfsssssfs"

    def advance(name):
        try:
            last[0] = next(walks[name])
        except StopIteration:
            del walks[name]

    for name in order:
        if name in walks:
            advance(name)
    while walks:
        for name in list(walks):
            advance(name)

    grad_w_in, grad_w_out, grad_w_hidden, grad_w_update, grad_u_hidden = done["first"]
    grad_w_value, grad_w_reset = done["second"]
    firsts = [
        small.T if small.shape[0] == NDIM else small[0] if small.shape[0] == 1 else small
        for small in done["small"]
    ]
    grad_norm2_gain = firsts.pop()
    return (
        trade_back(out.reshape(seqs, CH, D)),
        trade_back(done["tokens"]),
        *firsts,
        grad_w_value,
        grad_w_reset,
        grad_w_update,
        grad_w_hidden,
        grad_u_hidden,
        grad_norm2_gain,
        grad_w_in,
        grad_w_out,
    )


def solution(mesh):
    rows = P(None, ("seq", "tp"), None)
    cols = P(None, "tp")
    tall = P("tp", None)
    whole = P()
    return jax.shard_map(
        per_device,
        mesh=mesh,
        in_specs=(rows, rows) + (whole,) * 10 + (cols, cols, tall, tall, tall, whole, cols, tall),
        out_specs=(rows, rows) + (whole,) * 9 + (cols, cols, tall, tall, tall, whole, cols, tall),
        check_vma=False,
    )
```

```python
import functools

import jax
import jax.numpy as jnp
from jax import lax
from jax.experimental import pallas as pl
from jax.experimental.pallas import tpu as pltpu
from jax.sharding import PartitionSpec as P

D = 512
Z = 128
NDIM = 16
CH = 128
PIECE = 16
PIECES = CH // PIECE
LANES = 128
BLOCKS = D // LANES
EPS = 1e-05
F32 = jnp.float32
BF16 = jnp.bfloat16
SMALL_ROWS = 64

VMEM = pl.BlockSpec(memory_space=pltpu.VMEM)
SMEM = pl.BlockSpec(memory_space=pltpu.SMEM)
ANY = pl.BlockSpec(memory_space=pl.ANY)


def sigmoid(v):
    return 0.5 * jnp.tanh(0.5 * v) + 0.5


def silu(v):
    return v * sigmoid(v)


def silu_slope(v):
    s = sigmoid(v)
    return s * (1.0 + v * (1.0 - s))


def mm(a, b):
    return jnp.dot(a, b, preferred_element_type=F32)


def mm_nt(a, b):
    return lax.dot_general(a, b, (((1,), (1,)), ((), ())), preferred_element_type=F32)


def mm_tn(a, b):
    return lax.dot_general(a, b, (((0,), (0,)), ((), ())), preferred_element_type=F32)


def normalized(v):
    center = v - jnp.mean(v, axis=-1, keepdims=True)
    scale = lax.rsqrt(jnp.mean(center * center, axis=-1, keepdims=True) + EPS)
    return center * scale, scale


def norm_back(grad, xhat, scale, gain):
    full = grad * gain
    return scale * (
        full
        - jnp.mean(full, axis=-1, keepdims=True)
        - xhat * jnp.mean(full * xhat, axis=-1, keepdims=True)
    )


def rows_of(s):
    return pl.ds(s * CH, CH)


def lanes_of(i):
    return pl.ds(pl.multiple_of((i % BLOCKS) * LANES, LANES), LANES)


def spread(row):
    return jnp.broadcast_to(row, (PIECES, LANES))


def piece_rows(s, t):
    return pl.ds(s * CH + t, PIECES, stride=PIECE)


def put_rows(ref, rows, value):
    for b in range(BLOCKS):
        ref[b, rows, :] = value[:, b * LANES : (b + 1) * LANES]


def get_rows(ref, rows):
    return jnp.concatenate([ref[b, rows, :] for b in range(BLOCKS)], axis=1)


class Here:
    def __init__(self, seqs, lengths):
        self.seqs, self.lengths = seqs, lengths

    def __getitem__(self, i):
        if i == 0:
            return lax.axis_index("tp")
        if i == 1:
            return lax.axis_index("seq")
        if i == 2:
            index = lax.axis_index("seq") * lax.axis_size("tp") + lax.axis_index("tp")
            return index if self.seqs > 1 else jnp.right_shift(index, 1)
        return self.lengths[i - 3 if self.seqs > 1 else jnp.bitwise_and(lax.axis_index("tp"), 1)]


def call(body, out, scratch, operands, specs, name, limit=2, outs=None):
    place = operands[0]
    if isinstance(place, Here):
        kernel = body
        if place.lengths is None:
            operands, specs = operands[1:], specs[1:]
            body = lambda *refs: kernel(place, *refs)
        else:
            operands = (place.lengths, *operands[1:])
            body = lambda lengths, *refs: kernel(Here(place.seqs, lengths), *refs)
    return pl.pallas_call(
        body,
        out_shape=out,
        in_specs=specs,
        out_specs=outs or jax.tree.map(lambda _: VMEM, out),
        scratch_shapes=scratch,
        name=name,
        compiler_params=pltpu.CompilerParams(vmem_limit_bytes=int(limit * 1024 * 1024)),
    )(*operands)


def shape(dims, dtype=F32):
    return jax.ShapeDtypeStruct(dims, dtype)


def put_low(low, pairs):
    for i in range(0, len(pairs), 2):
        high = pairs[i].astype(BF16)
        low[3 * i // 2] = high
        low[3 * i // 2 + 1] = (pairs[i] - high.astype(F32)).astype(BF16)
        low[3 * i // 2 + 2] = pairs[i + 1].astype(BF16)


def get_low(low, s):
    high, rest, slope = (low[3 * s + i].astype(F32) for i in range(3))
    return high + rest, slope


def enter_kernel(seqs, *refs):
    far, refs = refs[:5], refs[5:]
    normed, par, before, ends, low, tok, gain, rate, beta, eta, nf, tab, sems = refs
    copies = [
        pltpu.make_async_copy(a, b, sems.at[i])
        for i, (a, b) in enumerate(zip(far, (tok, gain, rate, beta, eta)))
    ]
    for c in copies:
        c.start()
    for c in copies:
        c.wait()
    r = rate[...]
    d = 1.0 - r
    par[0] = d
    par[1] = jnp.log(d)
    par[2] = jnp.sqrt(r * (2.0 - r)) * beta[...]
    par[3] = eta[...]
    d2 = d * d
    d4 = d2 * d2
    d8 = d4 * d4
    d15 = d8 * d4 * d2 * d
    q = d8 * d8
    tab[0] = q
    tab[1] = 16.0 * d15
    tab[2] = q * q
    tab[3] = 32.0 * q * d15
    tab[4] = q * q * q * q
    tab[5] = 64.0 * q * q * q * d15
    for s in range(seqs):
        xhat, _ = normalized(tok[s].astype(F32))
        scaled = (xhat * gain[...]).astype(BF16)
        normed[rows_of(s), :] = scaled
        put_rows(nf, rows_of(s), scaled.astype(F32))
    place = lax.broadcasted_iota(jnp.int32, (PIECES, LANES), 0)

    def body(i, carry):
        s = i // BLOCKS
        lane = lanes_of(i)
        xs = [nf[i % BLOCKS, piece_rows(s, t), :] for t in range(PIECE)]
        for j0 in range(0, NDIM, 8):
            ds = [spread(par[0, j0 + j : j0 + j + 1, lane]) for j in range(8)]
            st = [xs[0]] * 8
            ta = [jnp.zeros((PIECES, LANES), F32)] * 8
            for t in range(1, PIECE):
                for j in range(8):
                    ta[j] = ds[j] * ta[j] + st[j]
                    st[j] = ds[j] * st[j] + xs[t]
            for j in range(8):
                a, b = st[j], ta[j]
                for k, step in enumerate((1, 2, 4)):
                    qm = spread(tab[2 * k, j0 + j : j0 + j + 1, lane])
                    rm = spread(tab[2 * k + 1, j0 + j : j0 + j + 1, lane])
                    sa = jnp.where(place >= step, pltpu.roll(a, step, 0), 0.0)
                    sb = jnp.where(place >= step, pltpu.roll(b, step, 0), 0.0)
                    b = b + qm * sb + rm * sa
                    a = a + qm * sa
                before[0, s, j0 + j, :, lane] = jnp.where(place >= 1, pltpu.roll(a, 1, 0), 0.0)
                before[1, s, j0 + j, :, lane] = jnp.where(place >= 1, pltpu.roll(b, 1, 0), 0.0)
                ends[2 * s, j0 + j : j0 + j + 1, lane] = a[PIECES - 1 :]
                ends[2 * s + 1, j0 + j : j0 + j + 1, lane] = b[PIECES - 1 :]
        return carry

    lax.fori_loop(0, seqs * BLOCKS, body, 0)
    ends[2 * seqs] = par[1]
    put_low(low, [ends[i] for i in range(2 * seqs)])


def first_half_kernel(w_value, w_reset, h1, sems):
    vb, cut = w_value.shape[1], D // 2
    at = pl.ds(pl.multiple_of(jnp.bitwise_and(lax.axis_index("seq"), 1) * cut, cut), cut)
    copies = [
        pltpu.make_async_copy(w.at[at, :], h1.at[:, pl.ds(i * vb, vb)], sems.at[i])
        for i, w in enumerate((w_value, w_reset))
    ]
    for c in copies:
        c.start()
    for c in copies:
        c.wait()


def pack_kernel(
    w_value, w_reset, w_hidden, w_update, u_hidden, w_in, w_out, p1, p2, p3, h2, h3, sems
):
    copies = []

    def add(source, target):
        copies.append(pltpu.make_async_copy(source, target, sems.at[len(copies)]))

    vb, cut = w_value.shape[1], D // 2
    upper = jnp.bitwise_and(lax.axis_index("seq"), 1) * cut
    at = pl.ds(pl.multiple_of(upper, cut), cut)
    for i, w in enumerate((w_value, w_reset)):
        add(w, p1.at[:, pl.ds(i * vb, vb)])
    far = jnp.bitwise_and(jnp.right_shift(lax.axis_index("seq"), far_shift()), 1) * cut
    top = 0
    for w in (w_hidden, w_update, u_hidden):
        row = pl.ds(top, w.shape[0])
        add(w.at[:, pl.ds(pl.multiple_of(far, cut), cut)], h2.at[row, :])
        add(w, p2.at[row, :])
        top += w.shape[0]
    add(w_in.at[at, :], h3.at[:, pl.ds(0, vb)])
    add(w_in, p3.at[:, pl.ds(0, vb)])
    for k in range(D // vb):
        row = pl.ds(k * vb, vb)
        add(w_out.at[:, row], p3.at[row, pl.ds(vb, vb)])
        if k < cut // vb:
            lane = pl.ds(pl.multiple_of(upper + k * vb, vb), vb)
            add(w_out.at[:, lane], h3.at[row, pl.ds(vb, vb)])
    for c in copies:
        c.start()
    for c in copies:
        c.wait()


def piece_powers(par, pw):
    k = lax.broadcasted_iota(jnp.int32, (PIECES, D), 0).astype(F32) * PIECE
    for j in range(NDIM):
        pw[j] = jnp.exp(k * par[1, j : j + 1, :])


def take_weights(refs, tp, first, second):
    top = tp // 2
    near = [refs[r * first : (r + 1) * first] for r in range(top)]
    refs = refs[top * first :]
    far = [refs[r * second : (r + 1) * second] for r in range(top)]
    return near, far, refs[top * second :]


def far_shift():
    return (lax.axis_size("seq").bit_length() - 1) // 2


def gate_copies(tp, ids, near, far, w1, w2, sems):
    top, cut = tp // 2, D // 2
    first = jnp.bitwise_and(ids[1], 1)
    second = jnp.bitwise_and(jnp.right_shift(ids[1], far_shift()), 1)
    copies = []

    def add(source, target):
        copies.append(pltpu.make_async_copy(source, target, sems.at[len(copies)]))

    for r in range(top):
        add(near[r][0], w1.at[r])
        add(near[r][1], w2.at[r])
        mine1, other1, mine2, other2 = far[r]
        for part, at in ((mine1, first), (other1, 1 - first)):
            add(part, w1.at[top + r, pl.ds(pl.multiple_of(at * cut, cut), cut), :])
        for part, at in ((mine2, second), (other2, 1 - second)):
            add(part, w2.at[top + r, :, pl.ds(pl.multiple_of(at * cut, cut), cut)])
    for c in copies:
        c.start()
    return copies


def gate_rows(tp, me, w2, whu):
    nb = D // tp
    for r in range(tp):
        row = pl.ds(pl.multiple_of(jnp.bitwise_xor(me, r) * nb, nb), nb)
        whu[row, pl.ds(0, D)] = w2[r, pl.ds(0, nb), :]
        whu[row, pl.ds(D, D)] = w2[r, pl.ds(nb, nb), :]


def look_kernel(
    seqs, hops, ids, normed, par, before, skip, wsh, qg, kg, rb, *refs
):
    recvs, refs = refs[: len(hops)], refs[len(hops) :]
    st_in, skip_pre, mixed, shared_pre, prob, nf, sm, pw = refs
    place = ids[2]
    put_rows(nf, slice(None), normed[...].astype(F32))
    piece_powers(par, pw)
    logd = par[1]
    dinv = 1.0 / par[0]
    for s in range(seqs):
        a = jnp.zeros((NDIM, D), F32)
        b = jnp.zeros((NDIM, D), F32)
        for (shift, k), got in zip(hops, recvs):
            end = jnp.left_shift(jnp.bitwise_xor(jnp.right_shift(place, shift), k) + 1, shift)
            off = (place - end).astype(F32) * float(CH)
            power = jnp.where(place >= end, jnp.exp(jnp.maximum(off, 0.0) * logd), 0.0)
            oa, ob = (part * power for part in get_low(got, s))
            b = b + ob + off * oa * dinv
            a = a + oa
        st_in[0, s] = a
        st_in[1, s] = b

    def ema(i, carry):
        s = i // BLOCKS
        lane = lanes_of(i)
        row = [pl.ds(j, 1) for j in range(NDIM)]
        ds = [spread(par[0, row[j], lane]) for j in range(NDIM)]
        ws = [spread(par[2, row[j], lane] * par[3, row[j], lane]) for j in range(NDIM)]
        st = [
            before[0, s, j, :, lane] + pw[j, :, lane] * st_in[0, s, row[j], lane]
            for j in range(NDIM)
        ]
        for t in range(PIECE):
            x = nf[i % BLOCKS, piece_rows(s, t), :]
            parts = [None, None]
            for j in range(NDIM):
                st[j] = ds[j] * st[j] + x
                term = ws[j] * st[j]
                parts[j % 2] = term if parts[j % 2] is None else parts[j % 2] + term
            sm[i % BLOCKS, piece_rows(s, t), :] = parts[0] + parts[1]
        return carry

    lax.fori_loop(0, seqs * BLOCKS, ema, 0)
    for s in range(seqs):
        pre = get_rows(sm, rows_of(s)) + skip[...] * get_rows(nf, rows_of(s))
        skip_pre[rows_of(s), :] = pre
        mixed[rows_of(s), :] = silu(pre).astype(BF16)
    sp = mm(mixed[...], wsh[...])
    shared_pre[...] = sp
    shared = silu(sp)
    query = (shared * qg[...]).astype(BF16)
    keys = (shared * kg[...]).astype(BF16)
    t_at = lax.broadcasted_iota(jnp.int32, (CH, CH), 0)
    s_at = lax.broadcasted_iota(jnp.int32, (CH, CH), 1)
    bias_t = jnp.broadcast_to(rb[...], (CH, CH))
    for bit in range(7):
        bias_t = jnp.where(
            jnp.bitwise_and(t_at, 1 << bit) > 0, pltpu.roll(bias_t, 1 << bit, 1), bias_t
        )
    bias = bias_t.T
    for s in range(seqs):
        raw = mm_nt(query[s * CH : (s + 1) * CH], keys[s * CH : (s + 1) * CH]) * Z ** (-0.5)
        live = (place * CH + s_at) < ids[3 + s]
        allowed = (s_at <= t_at) & (live | (s_at == t_at))
        masked = jnp.where(allowed, raw + bias, -1e30)
        top = jnp.max(masked, axis=-1, keepdims=True)
        weights = jnp.where(allowed, jnp.exp(masked - top), 0.0)
        prob[s] = weights / jnp.sum(weights, axis=-1, keepdims=True)


def mix_kernel(seqs, tp, ids, tok, normed, mixed, prob, *refs):
    near, far, refs = take_weights(refs, tp, 2, 4)
    (
        values, value_pre, reset_pre, attended, gated, hidden_pre, update_pre, middle,
        w1, w2, whu, sems,
    ) = refs
    vb = values.shape[2]
    nb = D // tp
    copies = gate_copies(tp, ids, near, far, w1, w2, sems)
    for c in copies:
        c.wait()
    gate_rows(tp, ids[0], w2, whu)
    hu = mm(mixed[...], whu[...])
    hidden_pre[...] = hu[:, :D]
    update_pre[...] = hu[:, D:]

    def block(r, carry):
        vp = mm(normed[...], w1[r, :, :vb])
        value_pre[r] = vp
        v = silu(vp).astype(BF16)
        values[r] = v
        rp = mm(mixed[...], w1[r, :, vb:])
        reset_pre[r] = rp
        gate = silu(rp)
        for s in range(seqs):
            att = mm(prob[s].astype(BF16), v[s * CH : (s + 1) * CH])
            attended[r, rows_of(s), :] = att
            gated[r, rows_of(s), :] = (gate[s * CH : (s + 1) * CH] * att).astype(BF16)
        hidden_pre[...] += mm(gated[r], w2[r, pl.ds(2 * nb, vb), :])
        return carry

    lax.fori_loop(0, tp, block, 0)
    for s in range(seqs):
        x = tok[s].astype(F32)
        middle[rows_of(s), :] = x + sigmoid(update_pre[rows_of(s), :]) * (
            silu(hidden_pre[rows_of(s), :]) - x
        )


def ffn_kernel(seqs, tp, ids, tok, cot, middle, hidden_pre, update_pre, gain2, *refs):
    near, far, refs = take_weights(refs, tp, 1, 2)
    (
        out, keep, send, grad_hu, resid, grad_gain2,
        w3, n2, lg, acc, gn2, sems,
    ) = refs
    vb = w3.shape[2] // 2
    top, half = tp // 2, D // 2
    cuts = D // vb
    upper = jnp.bitwise_and(ids[1], 1)
    copies = []

    def add(source, target):
        copies.append(pltpu.make_async_copy(source, target, sems.at[len(copies)]))

    for r in range(top):
        add(near[r][0], w3.at[r])
        for part, at in zip(far[r], (upper, 1 - upper)):
            add(part, w3.at[top + r, pl.ds(pl.multiple_of(at * half, half), half), :])
    for c in copies:
        c.start()
    place = ids[2]
    xhat, scale = normalized(middle[...])
    n2[...] = (xhat * gain2[...]).astype(BF16)
    at = lax.broadcasted_iota(jnp.int32, (CH, D), 0) + place * CH
    for s in range(seqs):
        lg[rows_of(s), :] = jnp.where(at < ids[3 + s], cot[s].astype(F32), 0.0).astype(BF16)
    acc[...] = jnp.zeros_like(acc)
    gn2[...] = jnp.zeros_like(gn2)
    for c in copies:
        c.wait()

    def block(h, carry):
        for odd in range(2):
            r = 2 * h + odd
            grads = (keep, send)[odd]
            pre = mm(n2[...], w3[r, :, :vb])
            inner = silu(pre).astype(BF16)
            back = None
            for k in range(cuts):
                cols = slice(k * vb, (k + 1) * vb)
                w_out = w3[r, cols, vb:]
                acc[:, cols] += mm(inner, w_out)
                term = mm_nt(lg[:, cols], w_out)
                back = term if back is None else back + term
            gip = (back * silu_slope(pre)).astype(BF16)
            gn2[...] += mm_nt(gip, w3[r, :, :vb])
            grads[h, :, :vb] = mm_tn(n2[...], gip).astype(BF16)
            gwo = mm_tn(inner, lg[...]).astype(BF16)
            for k in range(cuts):
                grads[h, k * vb : (k + 1) * vb, vb:] = gwo[:, k * vb : (k + 1) * vb]
        return carry

    lax.fori_loop(0, tp // 2, block, 0)
    mid = middle[...]
    out[...] = (mid + acc[...]).astype(BF16)
    grad = gn2[...]
    grad_gain2[...] = jnp.sum(grad * xhat, axis=0, keepdims=True)
    gm = lg[...].astype(F32) + norm_back(grad, xhat, scale, gain2[...])
    for s in range(seqs):
        x = tok[s].astype(F32)
        g = gm[s * CH : (s + 1) * CH]
        hp = hidden_pre[rows_of(s), :]
        update = sigmoid(update_pre[rows_of(s), :])
        grad_hu[rows_of(s), :D] = (g * update * silu_slope(hp)).astype(BF16)
        grad_hu[rows_of(s), D:] = (g * (silu(hp) - x) * update * (1.0 - update)).astype(BF16)
        resid[rows_of(s), :] = g * (1.0 - update)


def gates_kernel(tp, ids, mixed, gated, grad_hu, keep2, send2, ghu):
    nb = D // tp
    vb = gated.shape[2]
    wide = 2 * vb
    me = ids[0]
    ghu[...] = mm_tn(mixed[...], grad_hu[...])

    def block(h, carry):
        for odd in range(2):
            r = 2 * h + odd
            g2 = (keep2, send2)[odd]
            row = pl.ds(pl.multiple_of(jnp.bitwise_xor(me, r) * nb, nb), nb)
            gu = mm_tn(gated[r], grad_hu[:, :D]).astype(BF16)
            for k in range(D // wide):
                top = k * (2 * nb + vb)
                g2[h, pl.ds(top, nb), :] = ghu[row, pl.ds(k * wide, wide)].astype(BF16)
                g2[h, pl.ds(top + nb, nb), :] = ghu[row, pl.ds(D + k * wide, wide)].astype(BF16)
                g2[h, pl.ds(top + 2 * nb, vb), :] = gu[:, k * wide : (k + 1) * wide]
        return carry

    lax.fori_loop(0, tp // 2, block, 0)


def back_kernel(
    seqs, tp,
    ids, normed, mixed, skip_pre, shared_pre, prob, values, value_pre, reset_pre, attended,
    grad_hu, par, wsh, qg, kg, tok, before, st_in, skip, grad_gain2, *refs,
):
    near, far, refs = take_weights(refs, tp, 2, 4)
    (
        keep1, send1, grad_skip, grad_normed, after, ends, sums_keep, sums_send,
        w1, w2, whu, gm, gp, tab, grad_wsh, misc, table, nf, pw, sems,
    ) = refs
    vb = values.shape[2]
    nb = D // tp
    me = ids[0]
    copies = gate_copies(tp, ids, near, far, w1, w2, sems)
    gp[...] = jnp.zeros_like(gp)
    grad_normed[...] = jnp.zeros_like(grad_normed)
    for c in copies:
        c.wait()
    gate_rows(tp, me, w2, whu)
    gm[...] = mm_nt(grad_hu[...], whu[...])

    def block(h, carry):
        for odd in range(2):
            r = 2 * h + odd
            g1 = (keep1, send1)[odd]
            gg = mm_nt(grad_hu[:, :D], w2[r, pl.ds(2 * nb, vb), :])
            rp = reset_pre[r]
            sig = sigmoid(rp)
            ga = (gg * (rp * sig)).astype(BF16)
            grp = (gg * attended[r] * (sig * (1.0 + rp * (1.0 - sig)))).astype(BF16)
            g1[h, :, vb:] = mm_tn(mixed[...], grp).astype(BF16)
            gm[...] += mm_nt(grp, w1[r, :, vb:])
            gvs = []
            for s in range(seqs):
                part = ga[s * CH : (s + 1) * CH]
                gvs.append(mm_tn(prob[s].astype(BF16), part))
                gp[s] += mm_nt(part, values[r, rows_of(s), :])
            gv = jnp.concatenate(gvs, axis=0) if seqs > 1 else gvs[0]
            gvp = (gv * silu_slope(value_pre[r])).astype(BF16)
            g1[h, :, :vb] = mm_tn(normed[...], gvp).astype(BF16)
            grad_normed[...] += mm_nt(gvp, w1[r, :, :vb])
        return carry

    lax.fori_loop(0, tp // 2, block, 0)
    sp = shared_pre[...]
    shared = silu(sp)
    query = (shared * qg[...]).astype(BF16)
    keys = (shared * kg[...]).astype(BF16)
    total = jnp.zeros((CH, CH), F32)
    gqs = []
    gks = []
    for s in range(seqs):
        pr = prob[s]
        low = (pr * (gp[s] - jnp.sum(pr * gp[s], axis=-1, keepdims=True))).astype(BF16)
        total = total + low.astype(F32)
        gqs.append(mm(low, keys[s * CH : (s + 1) * CH]) * Z ** (-0.5))
        gks.append(mm_tn(low, query[s * CH : (s + 1) * CH]) * Z ** (-0.5))
    gq = jnp.concatenate(gqs, axis=0) if seqs > 1 else gqs[0]
    gk = jnp.concatenate(gks, axis=0) if seqs > 1 else gks[0]
    turned = total.T
    s_at = lax.broadcasted_iota(jnp.int32, (CH, CH), 0)
    for bit in range(7):
        turned = jnp.where(
            jnp.bitwise_and(s_at, 1 << bit) > 0, pltpu.roll(turned, CH - (1 << bit), 1), turned
        )
    misc[...] = jnp.concatenate(
        [
            jnp.sum(gq * shared, axis=0, keepdims=True),
            jnp.sum(gk * shared, axis=0, keepdims=True),
            jnp.sum(turned, axis=0, keepdims=True),
            jnp.zeros((1, D - 3 * Z), F32),
        ],
        axis=1,
    )
    gsp = ((gq * qg[...] + gk * kg[...]) * silu_slope(sp)).astype(BF16)
    grad_wsh[...] = mm_tn(mixed[...], gsp)
    put_rows(
        grad_skip,
        slice(None),
        (gm[...] + mm_nt(gsp, wsh[...])) * silu_slope(skip_pre[...]),
    )
    d = par[0]
    d2 = d * d
    d4 = d2 * d2
    d8 = d4 * d4
    q = d8 * d8
    tab[0] = q
    tab[1] = q * q
    tab[2] = q * q * q * q
    place = lax.broadcasted_iota(jnp.int32, (PIECES, LANES), 0)

    def body(i, carry):
        s = i // BLOCKS
        lane = lanes_of(i)
        ds = [spread(par[0, j : j + 1, lane]) for j in range(NDIM)]
        ad = [grad_skip[i % BLOCKS, piece_rows(s, PIECE - 1), :]] * NDIM
        for t in range(PIECE - 2, -1, -1):
            g = grad_skip[i % BLOCKS, piece_rows(s, t), :]
            for j in range(NDIM):
                ad[j] = ds[j] * ad[j] + g
        for j in range(NDIM):
            a = ad[j]
            for k, step in enumerate((1, 2, 4)):
                qm = spread(tab[k, j : j + 1, lane])
                a = a + qm * jnp.where(place < PIECES - step, pltpu.roll(a, PIECES - step, 0), 0.0)
            after[s, j, :, lane] = jnp.where(
                place < PIECES - 1, pltpu.roll(a, PIECES - 1, 0), 0.0
            )
            ends[s, j : j + 1, lane] = a[:1]
        return carry

    lax.fori_loop(0, seqs * BLOCKS, body, 0)
    small_sums(
        seqs, ids, tok, normed, grad_skip, grad_normed, par, before, st_in, skip, grad_gain2, misc,
        grad_wsh, sums_keep, sums_send, table, nf, pw,
    )


def small_sums(
    seqs, ids, tok, normed, grad_skip, grad_normed, par, before, st_in, skip, gain2_row, misc, grad_wsh,
    keep, send, table, nf, pw,
):
    put_rows(nf, slice(None), normed[...].astype(F32))
    piece_powers(par, pw)
    count = D // (D // Z)
    small = table.at[count:, :]
    small[...] = jnp.zeros_like(small)
    for k in range(D // Z):
        table[:count, k * Z : (k + 1) * Z] = grad_wsh[k * count : (k + 1) * count, :]

    def body(i, carry):
        s = i // BLOCKS
        lane = lanes_of(i)
        k16 = lax.broadcasted_iota(jnp.int32, (PIECES, LANES), 0).astype(F32) * PIECE
        for j0 in range(0, NDIM, 8):
            row = [pl.ds(j0 + j, 1) for j in range(8)]
            ds = [spread(par[0, row[j], lane]) for j in range(8)]
            st, ta, q, r = [], [], [], []
            for j in range(8):
                e = pw[j0 + j, :, lane] * st_in[0, s, row[j], lane]
                st.append(before[0, s, j0 + j, :, lane] + e)
                ta.append(
                    before[1, s, j0 + j, :, lane]
                    + pw[j0 + j, :, lane] * st_in[1, s, row[j], lane]
                    + k16 * e / ds[j]
                )
                q.append(jnp.zeros((PIECES, LANES), F32))
                r.append(jnp.zeros((PIECES, LANES), F32))
            for t in range(PIECE):
                x = nf[i % BLOCKS, piece_rows(s, t), :]
                g = grad_skip[i % BLOCKS, piece_rows(s, t), :]
                for j in range(8):
                    ta[j] = ds[j] * ta[j] + st[j]
                    st[j] = ds[j] * st[j] + x
                    q[j] = q[j] + g * st[j]
                    r[j] = r[j] + g * ta[j]
            for j in range(8):
                small[pl.ds(j0 + j, 1), lane] += jnp.sum(q[j], axis=0, keepdims=True)
                small[pl.ds(NDIM + j0 + j, 1), lane] += jnp.sum(r[j], axis=0, keepdims=True)
        return carry

    lax.fori_loop(0, seqs * BLOCKS, body, 0)
    gsk = jnp.zeros((1, D), F32)
    gn1 = jnp.zeros((1, D), F32)
    for s in range(seqs):
        xhat, _ = normalized(tok[s].astype(F32))
        g = get_rows(grad_skip, rows_of(s))
        direct = g * skip[...] + grad_normed[rows_of(s), :]
        gsk = gsk + jnp.sum(g * get_rows(nf, rows_of(s)), axis=0, keepdims=True)
        gn1 = gn1 + jnp.sum(direct * xhat, axis=0, keepdims=True)
    small[2 * NDIM : 2 * NDIM + 1, :] = gsk
    small[2 * NDIM + 1 : 2 * NDIM + 2, :] = gn1
    small[2 * NDIM + 2 : 2 * NDIM + 3, :] = gain2_row[...]
    small[2 * NDIM + 3 : 2 * NDIM + 4, :] = misc[...]
    half = keep.shape[0]
    mine = jnp.bitwise_and(ids[0], 1) * half
    keep[...] = table[pl.ds(pl.multiple_of(mine, 8), half), :]
    send[...] = table[pl.ds(pl.multiple_of(half - mine, 8), half), :]


def pair_kernel(bit, ids, mine, other, out):
    half = mine.shape[0]
    upper = jnp.where(jnp.bitwise_and(ids[0], bit) > 0, half, 0)
    out[pl.ds(pl.multiple_of(upper, 8), half), :] = mine[...]
    out[pl.ds(pl.multiple_of(half - upper, 8), half), :] = other[...]


def finish_kernel(
    ids, par, rate, beta, gain, mine, other,
    grad_gain, grad_rate, grad_beta, grad_eta, grad_skip, grad_wsh, grad_qg, grad_kg, grad_rb,
    grad_gain2, table,
):
    pair_kernel(1, ids, mine, other, table)
    count = D // (D // Z)
    for k in range(D // Z):
        grad_wsh[k * count : (k + 1) * count, :] = table[:count, k * Z : (k + 1) * Z]
    small = table.at[count:, :]
    inflow, eta, r = par[2], par[3], rate[...]
    root = jnp.sqrt(r * (2.0 - r))
    q_sum = small[:NDIM, :]
    grad_inflow = eta * q_sum
    grad_decay = eta * inflow * small[NDIM : 2 * NDIM, :]
    grad_rate[...] = grad_inflow * beta[...] * (1.0 - r) / root - grad_decay
    grad_beta[...] = grad_inflow * root
    grad_eta[...] = inflow * q_sum
    row = [small[2 * NDIM + i : 2 * NDIM + i + 1, :] for i in range(4)]
    grad_skip[...] = row[0]
    grad_gain[...] = row[1] + jnp.sum(inflow * grad_inflow, axis=0, keepdims=True) / gain[...]
    grad_gain2[...] = row[2]
    grad_qg[...] = row[3][:, :Z]
    grad_kg[...] = row[3][:, Z : 2 * Z]
    grad_rb[...] = row[3][:, 2 * Z : 3 * Z]


def leave_kernel(
    seqs, tops, ids, tok, par, grad_skip, grad_normed, behind, resid, gain, skip, *refs
):
    levels = len(tops)
    recvs, refs = refs[:levels], refs[levels:]
    grad_tokens, ad_in, pw, sm = refs
    place = ids[2]
    logd = par[1]
    gots = [get_wide(recvs[k], tops[k], seqs * NDIM) for k in range(levels)]
    for s in range(seqs):
        a = jnp.zeros((NDIM, D), F32)
        for k in range(levels):
            low = jnp.bitwise_and(place, 1 << k) == 0
            off = jnp.bitwise_and(place, (1 << k) - 1)
            away = ((1 << k) - 1 - off).astype(F32) * float(CH)
            got = gots[k][s * NDIM : (s + 1) * NDIM]
            a = a + got * jnp.where(low, jnp.exp(away * logd), 0.0)
        ad_in[s] = a
    k = (PIECES - 1 - lax.broadcasted_iota(jnp.int32, (PIECES, D), 0)).astype(F32) * PIECE
    for j in range(NDIM):
        pw[j] = jnp.exp(k * par[1, j : j + 1, :])

    def body(i, carry):
        s = i // BLOCKS
        lane = lanes_of(i)
        row = [pl.ds(j, 1) for j in range(NDIM)]
        ds = [spread(par[0, row[j], lane]) for j in range(NDIM)]
        ws = [spread(par[2, row[j], lane] * par[3, row[j], lane]) for j in range(NDIM)]
        ad = [
            behind[s, j, :, lane] + pw[j, :, lane] * ad_in[s, row[j], lane] for j in range(NDIM)
        ]
        for t in range(PIECE - 1, -1, -1):
            g = grad_skip[i % BLOCKS, piece_rows(s, t), :]
            parts = [None, None]
            for j in range(NDIM):
                ad[j] = ds[j] * ad[j] + g
                term = ws[j] * ad[j]
                parts[j % 2] = term if parts[j % 2] is None else parts[j % 2] + term
            sm[i % BLOCKS, piece_rows(s, t), :] = parts[0] + parts[1]
        return carry

    lax.fori_loop(0, seqs * BLOCKS, body, 0)
    for s in range(seqs):
        xhat, scale = normalized(tok[s].astype(F32))
        grad = (
            get_rows(sm, rows_of(s))
            + get_rows(grad_skip, rows_of(s)) * skip[...]
            + grad_normed[rows_of(s), :]
        )
        grad_tokens[s] = (
            resid[rows_of(s), :] + norm_back(grad, xhat, scale, gain[...])
        ).astype(BF16)


def hop_kernel(seqs, shift, count, ids, state, *refs):
    others, (total, low) = refs[: count - 1], refs[count - 1 :]
    mine = jnp.bitwise_and(jnp.right_shift(ids[2], shift), count - 1)
    logd = state[2 * seqs]
    total[2 * seqs] = logd
    sums = [None] * (2 * seqs)
    for k in range(count):
        after = (count - 1 - jnp.bitwise_xor(mine, k)).astype(F32) * float(CH << shift)
        power = jnp.exp(after * logd)
        slope = after * jnp.exp((after - 1.0) * logd)
        for s in range(seqs):
            part = get_low(others[k - 1], s) if k else (state[2 * s], state[2 * s + 1])
            a, b = power * part[0], power * part[1] + slope * part[0]
            sums[2 * s : 2 * s + 2] = [sums[2 * s] + a, sums[2 * s + 1] + b] if k else [a, b]
    for i in range(2 * seqs):
        total[i] = sums[i]
    put_low(low, sums)


def put_wide(ref, top, value):
    wide = ref.shape[1]
    count = value.shape[0]
    for k in range(D // wide):
        ref[pl.ds(top + k * count, count), :] = value[:, k * wide : (k + 1) * wide].astype(ref.dtype)


def get_wide(ref, top, count):
    wide = ref.shape[1]
    runs = [ref[pl.ds(top + k * count, count), :].astype(F32) for k in range(D // wide)]
    return jnp.concatenate(runs, axis=1) if len(runs) > 1 else runs[0]


def first_back_hop(seqs, joins, ids, par, own, other, sums, got, out, keep, payload):
    rows = seqs * NDIM
    fold_lanes = D // payload.shape[1]
    if joins:
        join_adjoint(seqs, 0, ids, par, own, other[...], out)
    else:
        out[...] = own[...]
    put_wide(payload, 0, out[...])
    half = keep.shape[0]
    upper = jnp.where(jnp.bitwise_and(ids[0], 2) > 0, half, 0)
    mine = pl.ds(pl.multiple_of(upper, 8), half)
    theirs = pl.ds(pl.multiple_of(half - upper, 8), half)
    keep[...] = sums[mine, :] + got[mine, :]
    put_wide(payload, rows * fold_lanes, sums[theirs, :] + got[theirs, :])


def join_adjoint(seqs, level, ids, par, own, got, out):
    upper = jnp.bitwise_and(ids[2], 1 << level) > 0
    power = jnp.exp(float(CH << level) * par[1])
    for s in range(seqs):
        row = slice(s * NDIM, (s + 1) * NDIM)
        early = jnp.where(upper, got[row], own[row, :])
        late = jnp.where(upper, own[row, :], got[row])
        out[row, :] = early + power * late


def chain_hop(seqs, level, split, halved, top, ids, par, own, kept, sent, other, out, keep, payload, base):
    rows = seqs * NDIM
    lanes = D // other.shape[1]
    if out is not None:
        join_adjoint(seqs, level, ids, par, own, get_wide(other, top, rows), out)
        put_wide(payload, base, out[...])
    half = keep.shape[0]
    if split:
        upper = jnp.bitwise_and(ids[0], split) > 0
        got = get_wide(other, top + rows * lanes, 2 * half)
        first, second = kept[:half, :] + got[:half], kept[half:, :] + got[half:]
        keep[...] = jnp.where(upper, second, first)
        put_wide(payload, base + rows * lanes, jnp.where(upper, first, second))
    else:
        mine = kept[...] if halved else get_wide(sent, top + rows * lanes, half)
        total = mine + get_wide(other, top + rows * lanes, half)
        keep[...] = total
        if payload is not None:
            put_wide(payload, base + rows * lanes, total)


def back_hop(seqs, level, split, halved, ids, par, own, kept, sent, other, out, keep, payload):
    chain_hop(
        seqs, level, split, halved, 0, ids, par, own, kept, sent, other, out, keep, payload, 0
    )


def split_rows(count, cut, place, k):
    shift, bits = cut
    rows = count >> bits
    sub = jnp.bitwise_and(jnp.right_shift(place, shift), (1 << bits) - 1)
    return pl.multiple_of(jnp.bitwise_xor(sub, k) * rows, rows), rows


def add_rows(parts, start, high, out, top, lane, width, at):
    step = min(64, high)

    def body(i, carry):
        row = pl.ds(pl.multiple_of(start + i * step, step), step)
        total = parts[0][row, lane : lane + width].astype(F32)
        for other in parts[1:]:
            total = total + other[row, lane : lane + width].astype(F32)
        out[pl.ds(pl.multiple_of(top + i * step, 16), step), at : at + width] = total.astype(BF16)
        return carry

    lax.fori_loop(0, high // step, body, 0)


def fold_kernel(jobs, inputs, ids, *refs):
    parts, outs = refs[:inputs], refs[inputs:]
    at = 0
    for count, lane, width, cut, targets in jobs:
        own = parts[at : at + count]
        at += count
        blocks, rows, _ = own[0].shape
        for k, (target, block, offset) in enumerate(targets):
            if cut == "tp":
                ranges, start, high = (k,), 0, rows
            elif cut is None:
                ranges, start, high = range(blocks), 0, rows
            else:
                start, high = split_rows(rows, cut, ids[1], k)
                ranges = range(blocks)
            for to, b in enumerate(ranges):
                add_rows(
                    [p.at[b] for p in own], start, high, outs[target].at[block + to], 0, lane,
                    width, offset,
                )


def fold(ids, shapes, jobs):
    arrays = [a for job in jobs for a in job[0]]
    plan = [(len(job[0]),) + tuple(job[1:]) for job in jobs]
    return call(
        functools.partial(fold_kernel, plan, len(arrays)),
        tuple(shape(dims, BF16) for dims in shapes),
        [],
        (ids, *arrays),
        [SMEM] + [VMEM] * len(arrays),
        "fold",
    )


def join_kernel(cut, ids, mine, other, out):
    blocks, rows, _ = mine.shape
    for k, part in enumerate((mine, other)):
        start, _ = split_rows(2 * rows, cut, ids[1], k)
        for b in range(blocks):
            out[b, pl.ds(pl.multiple_of(start, 16), rows), :] = part[b]


def join(ids, mine, other, cut):
    blocks, rows, lanes = mine.shape
    return call(
        functools.partial(join_kernel, cut),
        (shape((blocks, 2 * rows, lanes), BF16),),
        [],
        (ids, mine, other),
        [SMEM, VMEM, VMEM],
        "join",
    )[0]


def ride_kernel(
    seqs, level, split, halved, top, jobs, cut, high, last, ids, par, own, kept, sent, other, *refs
):
    count = 1 + max(p for job in jobs for p in job[0])
    parts, refs = refs[:count], refs[count:]
    out = payload = None
    if last:
        keep, kept_out = refs
        halves = ((0, keep),)
    elif cut is None:
        kept_out, out, payload = refs
        halves = ((0, payload),)
    else:
        keep, kept_out, out, payload = refs
        halves = ((0, keep), (1, payload))
    for picks, width, at in jobs:
        chosen = [other if p == -1 else sent if p == -2 else parts[p] for p in picks]
        for k, target in halves:
            start = 0 if cut is None else split_rows(2 * high, cut, ids[1], k)[0]
            add_rows(chosen, start, high, target, 0, 0, width, at)
    chain_hop(
        seqs, level, split, halved, top, ids, par, own, kept, sent, other, out, kept_out, payload,
        high,
    )


def unpack_first(cut, ids, *refs):
    count = 1 << cut[1]
    pieces, refs = refs[:count], refs[count:]
    w_in, w_out = refs[:2]
    outs = refs[2:]
    vb = w_in.shape[1]
    wide = 2 * vb
    each = sum(out.shape[0] for out in outs)
    for k in range(count):
        row, rows = split_rows(D, cut, ids[1], k)
        w_in[pl.ds(row, rows), :] = pieces[k][0, :, :vb].astype(F32)
        for first in range(0, rows, vb):
            w_out[:, pl.ds(pl.multiple_of(row + first, vb), vb)] = pieces[k][
                0, first : first + vb, vb:
            ].astype(F32)
        for b in range(count):

            @pl.when(row == b * rows)
            def _(k=k, b=b, rows=rows):
                for run in range(D // wide):
                    start = run * each
                    for out in outs:
                        end = start + out.shape[0]
                        lo, hi = max(start, b * rows), min(end, (b + 1) * rows)
                        if lo < hi:
                            out[lo - start : hi - start, run * wide : (run + 1) * wide] = pieces[k][
                                1, lo - b * rows : hi - b * rows, :
                            ].astype(F32)
                        start = end


def unpack_sides(cut, ids, *refs):
    count = 1 << cut[1]
    pieces, (left, right) = refs[:count], refs[count:]
    vb = left.shape[1]
    for k in range(count):
        row, rows = split_rows(D, cut, ids[1], k)
        left[pl.ds(row, rows), :] = pieces[k][0, :, :vb].astype(F32)
        right[pl.ds(row, rows), :] = pieces[k][0, :, vb:].astype(F32)


def unpack(body, cut, ids, pieces, dims):
    return call(
        functools.partial(body, cut),
        tuple(shape(d) for d in dims),
        [],
        (ids, *pieces),
        [SMEM] + [VMEM] * len(pieces),
        "unpack",
    )


BOTH = ("seq", "tp")


def swap(value, mask):
    count = lax.axis_size("seq") * lax.axis_size("tp")
    return lax.ppermute(value, BOTH, [(i, i ^ mask) for i in range(count)])


def after(value, *others):
    return lax.optimization_barrier((value, *others))[0]


def bits_of(count):
    return [1 << k for k in range(count.bit_length() - 1)]


def has(index, bit):
    return jnp.bitwise_and(index, bit) > 0


def half_of(value, upper):
    half = value.shape[0] // 2
    return lax.dynamic_slice_in_dim(value, jnp.where(upper, half, 0), half, 0)


def joined(mine, other, upper):
    return jnp.where(
        upper,
        jnp.concatenate([other, mine], axis=0),
        jnp.concatenate([mine, other], axis=0),
    )


def spread_out(own, tp):
    pieces = {0: own}
    for bit in reversed(bits_of(tp // 2)):
        for r in list(pieces):
            pieces[r ^ bit] = [swap(a, bit) for a in pieces[r]]
    return [pieces[r] for r in range(tp // 2)]


def per_device(
    tokens,
    cotangent,
    valid_lengths,
    norm1_gain,
    ema_rate,
    ema_beta,
    ema_eta,
    ema_skip,
    w_shared,
    query_gain,
    key_gain,
    rel_bias,
    w_value,
    w_reset,
    w_update,
    w_hidden,
    u_hidden,
    norm2_gain,
    w_in,
    w_out,
):
    part = lax.axis_index("tp")
    tp = lax.axis_size("tp")
    seq = lax.axis_size("seq")
    all_seqs, local_rows, _ = tokens.shape
    vb = w_value.shape[1]
    nb = D // tp
    ybits = far_shift()
    traded = local_rows < CH
    lower = part % 2 == 0

    def trade(value):
        if not traded:
            return value
        other = swap(jnp.where(lower, value[1], value[0]), 1)
        mine = jnp.where(lower, value[0], value[1])
        return joined(mine, other, ~lower)[None]

    def trade_back(value):
        if not traded:
            return value
        first, second = value[0, :local_rows], value[0, local_rows:]
        other = swap(jnp.where(lower, second, first), 1)
        mine = jnp.where(lower, first, second)
        return jnp.where(lower, jnp.stack([mine, other]), jnp.stack([other, mine]))

    if traded:
        assert all_seqs == 2 and 2 * local_rows == CH
        seqs = 1
    else:
        assert local_rows == CH
        seqs = all_seqs
    rows = seqs * CH
    ids, ids_lengths = Here(seqs, None), Here(seqs, valid_lengths.astype(jnp.int32))
    masks = bits_of(tp * seq)[int(traded) :]
    levels = len(masks)

    tok = trade(tokens)
    cot = trade(cotangent)
    gain1 = norm1_gain[None]
    gain2 = norm2_gain[None]
    skip = ema_skip[None]
    rate, beta = ema_rate.T, ema_beta.T
    qg, kg, rb = query_gain[None], key_gain[None], rel_bias[None]

    top = tp // 2
    weights = (w_value, w_reset, w_hidden, w_update, u_hidden, w_in, w_out)
    rows2 = 2 * nb + vb
    normed, par, before, ends, low = call(
        functools.partial(enter_kernel, seqs),
        (
            shape((rows, D), BF16),
            shape((4, NDIM, D)),
            shape((2, seqs, NDIM, PIECES, D)),
            shape((2 * seqs + 1, NDIM, D)),
            shape((3 * seqs, NDIM, D), BF16),
        ),
        [
            pltpu.VMEM((seqs, CH, D), BF16),
            pltpu.VMEM((1, D), F32),
            pltpu.VMEM((NDIM, D), F32),
            pltpu.VMEM((NDIM, D), F32),
            pltpu.VMEM((NDIM, D), F32),
            pltpu.VMEM((BLOCKS, rows, LANES), F32),
            pltpu.VMEM((6, NDIM, D), F32),
            pltpu.SemaphoreType.DMA((5,)),
        ],
        (tok, gain1, rate, beta, ema_eta.T),
        [ANY] * 5,
        "enter",
        limit=12,
    )
    start = 1 - int(traded)
    groups = [(0, 1)] * start + [(start, 2)] + [(i, 1) for i in range(start + 2, levels)]
    hops = []
    (half1,) = call(
        first_half_kernel,
        (shape((D // 2, 2 * vb), BF16),),
        [pltpu.SemaphoreType.DMA((2,))],
        (w_value, w_reset),
        [ANY] * 2,
        "half",
        limit=60,
        outs=(pl.BlockSpec(),),
    )
    mine1 = swap(half1, top)
    state = ends
    for i, (shift, bits) in enumerate(groups):
        if i == start:
            low = after(low, mine1)
            pack1, pack2, pack3, half2, half3 = call(
                pack_kernel,
                (
                    shape((D, 2 * vb), BF16),
                    shape((rows2, D), BF16),
                    shape((D, 2 * vb), BF16),
                    shape((rows2, D // 2), BF16),
                    shape((D // 2, 2 * vb), BF16),
                ),
                [pltpu.SemaphoreType.DMA((10 + 3 * D // vb // 2,))],
                lax.optimization_barrier((*weights, low))[:-1],
                [ANY] * 7,
                "pack",
                limit=60,
                outs=(pl.BlockSpec(),) * 5,
            )
        if i == start + 1:
            mine2 = swap(after(half2, low), top)
            other1 = swap(after(mine1, low), tp)
            near_gates = spread_out([after(pack1, low), after(pack2, low)], tp)
        if i == start + 2:
            low = after(low, mine2, other1, *near_gates[-1])
            mine3 = swap(after(half3, low), top)
            other2 = swap(after(mine2, low), tp << ybits)
            near_feeds = spread_out([after(pack3, low)], tp)
        got = []
        for k in range(1, 1 << bits):
            got.append(swap(low, k << (shift + int(traded))))
            hops.append((shift, k, got[-1]))
        if i + 1 < len(groups):
            state, low = call(
                functools.partial(hop_kernel, seqs, shift, 1 << bits),
                (shape((2 * seqs + 1, NDIM, D)), shape((3 * seqs, NDIM, D), BF16)),
                [],
                (ids, state, *got),
                [SMEM] + [VMEM] * (1 + len(got)),
                "hop",
            )
    st_in, skip_pre, mixed, shared_pre, prob = call(
        functools.partial(look_kernel, seqs, [h[:2] for h in hops]),
        (
            shape((2, seqs, NDIM, D)),
            shape((rows, D)),
            shape((rows, D), BF16),
            shape((rows, Z)),
            shape((seqs, CH, CH)),
        ),
        [
            pltpu.VMEM((BLOCKS, rows, LANES), F32),
            pltpu.VMEM((BLOCKS, rows, LANES), F32),
            pltpu.VMEM((NDIM, PIECES, D), F32),
        ],
        (
            ids_lengths, after(normed, mine3), par, before, skip, w_shared, qg, kg, rb,
            *[h[2] for h in hops],
        ),
        [SMEM] + [VMEM] * (8 + len(hops)),
        "look",
        limit=10,
    )
    far_gates = spread_out([mine1, after(other1, prob), mine2, after(other2, prob)], tp)
    other3 = swap(mine3, tp)
    gates = [w for group in near_gates + far_gates for w in group]

    values, value_pre, reset_pre, attended, gated, hidden_pre, update_pre, middle = call(
        functools.partial(mix_kernel, seqs, tp),
        (
            shape((tp, rows, vb), BF16),
            shape((tp, rows, vb)),
            shape((tp, rows, vb)),
            shape((tp, rows, vb)),
            shape((tp, rows, vb), BF16),
            shape((rows, D)),
            shape((rows, D)),
            shape((rows, D)),
        ),
        [
            pltpu.VMEM((tp, D, 2 * vb), BF16),
            pltpu.VMEM((tp, rows2, D), BF16),
            pltpu.VMEM((D, 2 * D), BF16),
            pltpu.SemaphoreType.DMA((3 * tp,)),
        ],
        (ids, tok, normed, after(mixed, other3), prob, *gates),
        [SMEM] + [VMEM] * 4 + [ANY] * len(gates),
        "mix",
        limit=10,
    )

    far_feeds = spread_out([mine3, other3], tp)
    feeds = [w for group in near_feeds + far_feeds for w in group]
    out, keep3, send3, grad_hu, resid, grad_gain2 = call(
        functools.partial(ffn_kernel, seqs, tp),
        (
            shape((rows, D), BF16),
            shape((tp // 2, D, 2 * vb), BF16),
            shape((tp // 2, D, 2 * vb), BF16),
            shape((rows, 2 * D), BF16),
            shape((rows, D)),
            shape((1, D)),
        ),
        [
            pltpu.VMEM((tp, D, 2 * vb), BF16),
            pltpu.VMEM((rows, D), BF16),
            pltpu.VMEM((rows, D), BF16),
            pltpu.VMEM((rows, D), F32),
            pltpu.VMEM((rows, D), F32),
            pltpu.SemaphoreType.DMA((3 * tp // 2,)),
        ],
        (ids_lengths, tok, cot, middle, hidden_pre, update_pre, gain2, *feeds),
        [SMEM] + [VMEM] * 6 + [ANY] * len(feeds),
        "ffn",
        limit=10,
    )

    half = tp // 2
    yn = 1 << ybits
    wide = 2 * vb
    runs = D // wide
    cut_of_y = (0, ybits)
    zcuts = [(shift, 1) for shift in range(ybits, seq.bit_length() - 1)]

    def over_tp(pieces):
        return [pieces[0]] + [swap(p, 2 * k) for k, p in enumerate(pieces) if k]

    def over_y(pieces):
        return [pieces[0]] + [swap(p, tp * k) for k, p in enumerate(pieces) if k]

    def over_z(value, cut):
        return swap(value, tp << cut[0])

    def cut_tp(parts, dims):
        n = dims[0]
        return fold(
            ids,
            [(1,) + dims[1:]] * n,
            [(parts, 0, dims[2], "tp", [(k, 0, 0) for k in range(n)])],
        )

    def cut_y(parts, dims):
        return fold(
            ids,
            [(dims[0], dims[1] // yn, dims[2])] * yn,
            [(parts, 0, dims[2], cut_of_y, [(k, 0, 0) for k in range(yn)])],
        )

    last = [None]

    def now(value):
        return value if last[0] is None else after(value, last[0])

    chunk = (half, D, wide)
    got3 = swap(send3, 1)
    keep2, send2 = call(
        functools.partial(gates_kernel, tp),
        (shape(chunk, BF16), shape(chunk, BF16)),
        [pltpu.VMEM((D, 2 * D), F32)],
        (ids, mixed, gated, grad_hu),
        [SMEM] + [VMEM] * 3,
        "gates",
        limit=10,
    )
    got2 = swap(send2, 1)
    g3 = cut_tp([keep3, got3], chunk)
    g3 = over_tp(g3)
    g2 = cut_y([keep2, after(got2, g3[0])], chunk)
    g2 = over_y(g2)

    count = Z + SMALL_ROWS
    count += -count % (16 * tp)
    (
        keep1, send1, grad_skip, grad_normed, behind, back_ends, sums_keep, sums_send,
    ) = call(
        functools.partial(back_kernel, seqs, tp),
        (
            shape(chunk, BF16),
            shape(chunk, BF16),
            shape((BLOCKS, rows, LANES)),
            shape((rows, D)),
            shape((seqs, NDIM, PIECES, D)),
            shape((seqs, NDIM, D)),
            shape((count // 2, D)),
            shape((count // 2, D)),
        ),
        [
            pltpu.VMEM((tp, D, 2 * vb), BF16),
            pltpu.VMEM((tp, rows2, D), BF16),
            pltpu.VMEM((D, 2 * D), BF16),
            pltpu.VMEM((rows, D), F32),
            pltpu.VMEM((seqs, CH, CH), F32),
            pltpu.VMEM((3, NDIM, D), F32),
            pltpu.VMEM((D, Z), F32),
            pltpu.VMEM((1, D), F32),
            pltpu.VMEM((count, D), F32),
            pltpu.VMEM((BLOCKS, rows, LANES), F32),
            pltpu.VMEM((NDIM, PIECES, D), F32),
            pltpu.SemaphoreType.DMA((3 * tp,)),
        ],
        (
            ids, normed, mixed, skip_pre, shared_pre, prob, values, value_pre, reset_pre, attended,
            after(grad_hu, g2[0]), par, w_shared, qg, kg, tok, before, st_in, skip, grad_gain2,
            *gates,
        ),
        [SMEM] + [VMEM] * 19 + [ANY] * len(gates),
        "back",
        limit=12,
    )

    g3 = cut_y([after(g3[0], send1)] + g3[1:], (1, D, wide))
    g2 = cut_tp([after(g2[0], g3[0])] + g2[1:], (half, D // yn, wide))
    (
        keep1, send1, grad_skip, grad_normed, behind, back_ends, sums_keep, sums_send, _,
    ) = lax.optimization_barrier(
        (keep1, send1, grad_skip, grad_normed, behind, back_ends, sums_keep, sums_send, g2[0])
    )
    adjoint = back_ends.reshape(seqs * NDIM, D)
    last[0] = g2[0]
    g3 = over_y(g3)
    g2 = over_tp(g2)
    got1 = swap(send1, 1)
    got_adjoint = adjoint if traded else swap(adjoint, 1)
    got_sums = swap(sums_send, 1)
    done = {}

    def first_chunks():
        high = D // yn
        for i, cut in enumerate(zcuts[:-1] + [None]):
            high = high // 2 if cut else high
            pieces = 2 if cut else 1
            if i:
                jobs = [([now(keep), other], 0, wide, cut, [(k, 0, 0) for k in range(pieces)])]
            else:
                jobs = [
                    ([now(g3[0])] + g3[1:], 0, wide, cut, [(k, 0, 0) for k in range(pieces)]),
                    (g2, 0, wide, cut, [(k, 1, 0) for k in range(pieces)]),
                ]
            keep, *send = fold(ids, [(2, high, wide)] * pieces, jobs)
            other = over_z(*send, cut) if cut else over_z(keep, zcuts[-1])
            yield keep
        (total,) = fold(ids, [keep.shape], [([now(keep), other], 0, wide, None, [(0, 0, 0)])])
        for cut in reversed(zcuts[:-1]):
            other = over_z(total, cut)
            yield total
            total = join(ids, now(total), other, cut)
        pieces = over_y([total] * yn)
        yield total
        done["first"] = unpack(
            unpack_first,
            cut_of_y,
            ids,
            [now(pieces[0])] + pieces[1:],
            [(D, vb), (vb, D), (nb, D), (nb, D), (vb, D)],
        )
        yield done["first"][0]

    def second_chunk():
        small_high = count // 4
        ad_rows = seqs * NDIM

        def payload_rows():
            return (ad_rows + small_high) * runs

        own, kept, payload = call(
            functools.partial(first_back_hop, seqs, not traded),
            (
                shape((ad_rows, D)),
                shape((small_high, D)),
                shape((payload_rows(), wide), BF16),
            ),
            [],
            (ids, par, now(adjoint), got_adjoint, sums_keep, got_sums),
            [SMEM] + [VMEM] * 5,
            "hop",
        )
        got = [] if traded else [(got_adjoint, 0)]
        level = int(not traded)
        halved = True
        other = swap(payload, masks[level])
        yield payload
        parts = fold(
            ids,
            [(1, D, vb)] * half + [(half, D // yn, vb)] * yn,
            [
                ([now(keep1), got1], 0, vb, "tp", [(k, 0, 0) for k in range(half)]),
                ([keep1, got1], vb, vb, cut_of_y, [(half + k, 0, 0) for k in range(yn)]),
            ],
        )
        left, right = over_tp(parts[:half]), over_y(parts[half:])
        yield parts[0]
        crossed = False
        while level + 1 < levels - len(zcuts):
            got.append((other, 0))
            split = 2 * masks[level] if 2 * masks[level] < tp else 0
            small_high = small_high // 2 if split else small_high
            own, kept, payload = call(
                functools.partial(back_hop, seqs, level, split, halved),
                (
                    shape((ad_rows, D)),
                    shape((small_high, D)),
                    shape((payload_rows(), wide), BF16),
                ),
                [],
                (ids, par, now(own), kept, payload, other),
                [SMEM] + [VMEM] * 5,
                "hop",
            )
            halved = bool(split)
            level += 1
            other = swap(payload, masks[level])
            yield payload
            if crossed:
                continue
            crossed = True
            parts = fold(
                ids,
                [(1, D // yn, vb)] * (yn + half),
                [
                    ([now(left[0])] + left[1:], 0, vb, cut_of_y, [(k, 0, 0) for k in range(yn)]),
                    (right, 0, vb, "tp", [(yn + k, 0, 0) for k in range(half)]),
                ],
            )
            left, right = over_y(parts[:yn]), over_tp(parts[yn:])
            yield parts[0]
        high = D // yn
        top = 0
        flat = [p.reshape(p.shape[1:]) for p in left + right]
        jobs = [
            (tuple(range(len(left))), vb, 0),
            (tuple(range(len(left), len(flat))), vb, vb),
        ]
        for cut in zcuts[:-1] + [None]:
            got.append((other, top))
            high = high // 2 if cut else high
            kept_chunk = [shape((high, wide), BF16)] if cut else []
            *flat, kept, own, payload = call(
                functools.partial(
                    ride_kernel, seqs, level, 0, halved, top, jobs, cut, high, False
                ),
                (
                    *kept_chunk,
                    shape((small_high, D)),
                    shape((ad_rows, D)),
                    shape((high + payload_rows(), wide), BF16),
                ),
                [],
                (ids, par, now(own), kept, payload, other, *flat),
                [SMEM] + [VMEM] * (5 + len(flat)),
                "ride",
            )
            halved = False
            level += 1
            top = high
            jobs = [((0 if cut else -2, -1), wide, 0)]
            other = swap(payload, masks[level])
            yield payload
        got.append((other, top))
        total, kept = call(
            functools.partial(ride_kernel, seqs, level, 0, False, top, jobs, None, high, True),
            (shape((high, wide), BF16), shape((small_high, D))),
            [],
            (ids, par, now(own), kept, payload, other, *flat),
            [SMEM] + [VMEM] * (5 + len(flat)),
            "ride",
        )
        bits = list(reversed(bits_of(tp)))
        total = total[None]
        far = swap(kept, bits[0])
        other = over_z(total, zcuts[-2]) if len(zcuts) > 1 else None
        yield total
        (done["tokens"],) = call(
            functools.partial(leave_kernel, seqs, [at for _, at in got]),
            (shape((seqs, CH, D), BF16),),
            [
                pltpu.VMEM((seqs, NDIM, D), F32),
                pltpu.VMEM((NDIM, PIECES, D), F32),
                pltpu.VMEM((BLOCKS, rows, LANES), F32),
            ],
            (
                ids, tok, par, now(grad_skip), grad_normed, behind, resid, gain1, skip,
                *[g for g, _ in got],
            ),
            [SMEM] + [VMEM] * (8 + levels),
            "leave",
            limit=10,
        )
        yield done["tokens"]
        for i in range(len(zcuts) - 2, -1, -1):
            total = join(ids, now(total), other, zcuts[i])
            if i:
                other = over_z(total, zcuts[i - 1])
                yield total
        pieces = over_y([total] * yn)
        yield total
        for i in range(len(bits) - 1):
            (kept,) = call(
                functools.partial(pair_kernel, bits[i]),
                (shape((2 * kept.shape[0], D)),),
                [],
                (ids, now(kept), far),
                [SMEM, VMEM, VMEM],
                "pair",
            )
            far = swap(kept, bits[i + 1])
            yield kept
        done["small"] = call(
            finish_kernel,
            (
                shape((1, D)),
                shape((NDIM, D)),
                shape((NDIM, D)),
                shape((NDIM, D)),
                shape((1, D)),
                shape((D, Z)),
                shape((1, Z)),
                shape((1, Z)),
                shape((1, Z)),
                shape((1, D)),
            ),
            [pltpu.VMEM((count, D), F32)],
            (ids, par, rate, beta, gain1, now(kept), far),
            [SMEM] + [VMEM] * 6,
            "finish",
        )
        yield done["small"][0]
        done["second"] = unpack(
            unpack_sides, cut_of_y, ids, [now(pieces[0])] + pieces[1:], [(D, vb), (D, vb)]
        )
        yield done["second"][0]

    walks = {"f": first_chunks(), "s": second_chunk()}
    order = "sssfsfsfsfsssssfs"

    def advance(name):
        try:
            last[0] = next(walks[name])
        except StopIteration:
            del walks[name]

    for name in order:
        if name in walks:
            advance(name)
    while walks:
        for name in list(walks):
            advance(name)

    grad_w_in, grad_w_out, grad_w_hidden, grad_w_update, grad_u_hidden = done["first"]
    grad_w_value, grad_w_reset = done["second"]
    firsts = [
        small.T if small.shape[0] == NDIM else small[0] if small.shape[0] == 1 else small
        for small in done["small"]
    ]
    grad_norm2_gain = firsts.pop()
    return (
        trade_back(out.reshape(seqs, CH, D)),
        trade_back(done["tokens"]),
        *firsts,
        grad_w_value,
        grad_w_reset,
        grad_w_update,
        grad_w_hidden,
        grad_u_hidden,
        grad_norm2_gain,
        grad_w_in,
        grad_w_out,
    )


def solution(mesh):
    rows = P(None, ("seq", "tp"), None)
    cols = P(None, "tp")
    tall = P("tp", None)
    whole = P()
    return jax.shard_map(
        per_device,
        mesh=mesh,
        in_specs=(rows, rows) + (whole,) * 10 + (cols, cols, tall, tall, tall, whole, cols, tall),
        out_specs=(rows, rows) + (whole,) * 9 + (cols, cols, tall, tall, tall, whole, cols, tall),
        check_vma=False,
    )
```

```python
import functools

import jax
import jax.numpy as jnp
from jax import lax
from jax.experimental import pallas as pl
from jax.experimental.pallas import tpu as pltpu
from jax.sharding import PartitionSpec as P

D = 512
Z = 128
NDIM = 16
CH = 128
PIECE = 16
PIECES = CH // PIECE
LANES = 128
BLOCKS = D // LANES
EPS = 1e-05
F32 = jnp.float32
BF16 = jnp.bfloat16
SMALL_ROWS = 64

VMEM = pl.BlockSpec(memory_space=pltpu.VMEM)
SMEM = pl.BlockSpec(memory_space=pltpu.SMEM)
ANY = pl.BlockSpec(memory_space=pl.ANY)


def sigmoid(v):
    return 0.5 * jnp.tanh(0.5 * v) + 0.5


def silu(v):
    return v * sigmoid(v)


def silu_slope(v):
    s = sigmoid(v)
    return s * (1.0 + v * (1.0 - s))


def mm(a, b):
    return jnp.dot(a, b, preferred_element_type=F32)


def mm_nt(a, b):
    return lax.dot_general(a, b, (((1,), (1,)), ((), ())), preferred_element_type=F32)


def mm_tn(a, b):
    return lax.dot_general(a, b, (((0,), (0,)), ((), ())), preferred_element_type=F32)


def normalized(v):
    center = v - jnp.mean(v, axis=-1, keepdims=True)
    scale = lax.rsqrt(jnp.mean(center * center, axis=-1, keepdims=True) + EPS)
    return center * scale, scale


def norm_back(grad, xhat, scale, gain):
    full = grad * gain
    return scale * (
        full
        - jnp.mean(full, axis=-1, keepdims=True)
        - xhat * jnp.mean(full * xhat, axis=-1, keepdims=True)
    )


def rows_of(s):
    return pl.ds(s * CH, CH)


def lanes_of(i):
    return pl.ds(pl.multiple_of((i % BLOCKS) * LANES, LANES), LANES)


def spread(row):
    return jnp.broadcast_to(row, (PIECES, LANES))


def piece_rows(s, t):
    return pl.ds(s * CH + t, PIECES, stride=PIECE)


def put_rows(ref, rows, value):
    for b in range(BLOCKS):
        ref[b, rows, :] = value[:, b * LANES : (b + 1) * LANES]


def get_rows(ref, rows):
    return jnp.concatenate([ref[b, rows, :] for b in range(BLOCKS)], axis=1)


class Here:
    def __init__(self, seqs, lengths):
        self.seqs, self.lengths = seqs, lengths

    def __getitem__(self, i):
        if i == 0:
            return lax.axis_index("tp")
        if i == 1:
            return lax.axis_index("seq")
        if i == 2:
            index = lax.axis_index("seq") * lax.axis_size("tp") + lax.axis_index("tp")
            return index if self.seqs > 1 else jnp.right_shift(index, 1)
        return self.lengths[i - 3 if self.seqs > 1 else jnp.bitwise_and(lax.axis_index("tp"), 1)]


def call(body, out, scratch, operands, specs, name, limit=2, outs=None):
    place = operands[0]
    if isinstance(place, Here):
        kernel = body
        if place.lengths is None:
            operands, specs = operands[1:], specs[1:]
            body = lambda *refs: kernel(place, *refs)
        else:
            operands = (place.lengths, *operands[1:])
            body = lambda lengths, *refs: kernel(Here(place.seqs, lengths), *refs)
    return pl.pallas_call(
        body,
        out_shape=out,
        in_specs=specs,
        out_specs=outs or jax.tree.map(lambda _: VMEM, out),
        scratch_shapes=scratch,
        name=name,
        compiler_params=pltpu.CompilerParams(vmem_limit_bytes=int(limit * 1024 * 1024)),
    )(*operands)


def shape(dims, dtype=F32):
    return jax.ShapeDtypeStruct(dims, dtype)


def put_low(low, pairs):
    for i in range(0, len(pairs), 2):
        high = pairs[i].astype(BF16)
        low[3 * i // 2] = high
        low[3 * i // 2 + 1] = (pairs[i] - high.astype(F32)).astype(BF16)
        low[3 * i // 2 + 2] = pairs[i + 1].astype(BF16)


def get_low(low, s):
    high, rest, slope = (low[3 * s + i].astype(F32) for i in range(3))
    return high + rest, slope


def enter_kernel(seqs, ids, *refs):
    count = 10
    far, near, sems = refs[:count], refs[count + 5 : 2 * count + 5], refs[-1]
    normed, par, before, ends, low = refs[count : count + 5]
    tok, gain, rate, beta, eta, skip, gain2, qg, kg, rb, nf, tab = refs[count + 5 : -1]
    copies = [pltpu.make_async_copy(a, b, sems.at[i]) for i, (a, b) in enumerate(zip(far, near))]
    for c in copies:
        c.start()
    for c in copies:
        c.wait()
    r = rate[...]
    d = 1.0 - r
    par[0] = d
    par[1] = jnp.log(d)
    par[2] = jnp.sqrt(r * (2.0 - r)) * beta[...]
    par[3] = eta[...]
    for i, row in enumerate((skip, gain2, gain)):
        par[4, i : i + 1, :] = row[...]
    for i, row in enumerate((qg, kg, rb)):
        par[4, 3:4, i * Z : (i + 1) * Z] = row[...]
    for s in range(seqs):
        par[4, 4 + s : 5 + s, :] = jnp.full((1, D), ids[3 + s].astype(F32))
    d2 = d * d
    d4 = d2 * d2
    d8 = d4 * d4
    d15 = d8 * d4 * d2 * d
    q = d8 * d8
    tab[0] = q
    tab[1] = 16.0 * d15
    tab[2] = q * q
    tab[3] = 32.0 * q * d15
    tab[4] = q * q * q * q
    tab[5] = 64.0 * q * q * q * d15
    for s in range(seqs):
        xhat, _ = normalized(tok[s].astype(F32))
        scaled = (xhat * gain[...]).astype(BF16)
        normed[rows_of(s), :] = scaled
        put_rows(nf, rows_of(s), scaled.astype(F32))
    place = lax.broadcasted_iota(jnp.int32, (PIECES, LANES), 0)

    def body(i, carry):
        s = i // BLOCKS
        lane = lanes_of(i)
        xs = [nf[i % BLOCKS, piece_rows(s, t), :] for t in range(PIECE)]
        for j0 in range(0, NDIM, 8):
            ds = [spread(par[0, j0 + j : j0 + j + 1, lane]) for j in range(8)]
            st = [xs[0]] * 8
            ta = [jnp.zeros((PIECES, LANES), F32)] * 8
            for t in range(1, PIECE):
                for j in range(8):
                    ta[j] = ds[j] * ta[j] + st[j]
                    st[j] = ds[j] * st[j] + xs[t]
            for j in range(8):
                a, b = st[j], ta[j]
                for k, step in enumerate((1, 2, 4)):
                    qm = spread(tab[2 * k, j0 + j : j0 + j + 1, lane])
                    rm = spread(tab[2 * k + 1, j0 + j : j0 + j + 1, lane])
                    sa = jnp.where(place >= step, pltpu.roll(a, step, 0), 0.0)
                    sb = jnp.where(place >= step, pltpu.roll(b, step, 0), 0.0)
                    b = b + qm * sb + rm * sa
                    a = a + qm * sa
                before[0, s, j0 + j, :, lane] = jnp.where(place >= 1, pltpu.roll(a, 1, 0), 0.0)
                before[1, s, j0 + j, :, lane] = jnp.where(place >= 1, pltpu.roll(b, 1, 0), 0.0)
                ends[2 * s, j0 + j : j0 + j + 1, lane] = a[PIECES - 1 :]
                ends[2 * s + 1, j0 + j : j0 + j + 1, lane] = b[PIECES - 1 :]
        return carry

    lax.fori_loop(0, seqs * BLOCKS, body, 0)
    ends[2 * seqs] = par[1]
    put_low(low, [ends[i] for i in range(2 * seqs)])


def first_half_kernel(w_value, w_reset, h1, sems):
    vb, cut = w_value.shape[1], D // 2
    at = pl.ds(pl.multiple_of(jnp.bitwise_and(lax.axis_index("seq"), 1) * cut, cut), cut)
    copies = [
        pltpu.make_async_copy(w.at[at, :], h1.at[:, pl.ds(i * vb, vb)], sems.at[i])
        for i, w in enumerate((w_value, w_reset))
    ]
    for c in copies:
        c.start()
    for c in copies:
        c.wait()


def pack_kernel(
    w_value, w_reset, w_hidden, w_update, u_hidden, w_in, w_out, p1, p2, p3, h2, h3, sems
):
    copies = []

    def add(source, target):
        copies.append(pltpu.make_async_copy(source, target, sems.at[len(copies)]))

    vb, cut = w_value.shape[1], D // 2
    upper = jnp.bitwise_and(lax.axis_index("seq"), 1) * cut
    at = pl.ds(pl.multiple_of(upper, cut), cut)
    for i, w in enumerate((w_value, w_reset)):
        add(w, p1.at[:, pl.ds(i * vb, vb)])
    far = jnp.bitwise_and(jnp.right_shift(lax.axis_index("seq"), far_shift()), 1) * cut
    top = 0
    for w in (w_hidden, w_update, u_hidden):
        row = pl.ds(top, w.shape[0])
        add(w.at[:, pl.ds(pl.multiple_of(far, cut), cut)], h2.at[row, :])
        add(w, p2.at[row, :])
        top += w.shape[0]
    add(w_in.at[at, :], h3.at[:, pl.ds(0, vb)])
    add(w_in, p3.at[:, pl.ds(0, vb)])
    for k in range(D // vb):
        row = pl.ds(k * vb, vb)
        add(w_out.at[:, row], p3.at[row, pl.ds(vb, vb)])
        if k < cut // vb:
            lane = pl.ds(pl.multiple_of(upper + k * vb, vb), vb)
            add(w_out.at[:, lane], h3.at[row, pl.ds(vb, vb)])
    for c in copies:
        c.start()
    for c in copies:
        c.wait()


def vectors(par):
    whole = [par.at[4, pl.ds(i, 1), :] for i in range(3)]
    return whole + [par.at[4, pl.ds(3, 1), pl.ds(i * Z, Z)] for i in range(3)]


def piece_powers(par, pw):
    k = lax.broadcasted_iota(jnp.int32, (PIECES, D), 0).astype(F32) * PIECE
    for j in range(NDIM):
        pw[j] = jnp.exp(k * par[1, j : j + 1, :])


def take_weights(refs, tp, first, second):
    top = tp // 2
    near = [refs[r * first : (r + 1) * first] for r in range(top)]
    refs = refs[top * first :]
    far = [refs[r * second : (r + 1) * second] for r in range(top)]
    return near, far, refs[top * second :]


def far_shift():
    return (lax.axis_size("seq").bit_length() - 1) // 2


def gate_copies(tp, ids, near, far, w1, w2, sems):
    top, cut = tp // 2, D // 2
    first = jnp.bitwise_and(ids[1], 1)
    second = jnp.bitwise_and(jnp.right_shift(ids[1], far_shift()), 1)
    copies = [[] for _ in range(tp)]

    def add(r, source, target):
        at = sems.at[sum(len(c) for c in copies)]
        copies[r].append(pltpu.make_async_copy(source, target, at))

    for r in range(top):
        add(r, near[r][0], w1.at[r])
        add(r, near[r][1], w2.at[r])
    for r in range(top):
        mine1, other1, mine2, other2 = far[r]
        for part, at in ((mine1, first), (other1, 1 - first)):
            add(top + r, part, w1.at[top + r, pl.ds(pl.multiple_of(at * cut, cut), cut), :])
        for part, at in ((mine2, second), (other2, 1 - second)):
            add(top + r, part, w2.at[top + r, :, pl.ds(pl.multiple_of(at * cut, cut), cut)])
    for group in copies:
        for c in group:
            c.start()
    return copies


def gate_rows(tp, me, w2, whu):
    nb = D // tp
    for r in range(tp):
        row = pl.ds(pl.multiple_of(jnp.bitwise_xor(me, r) * nb, nb), nb)
        whu[row, pl.ds(0, D)] = w2[r, pl.ds(0, nb), :]
        whu[row, pl.ds(D, D)] = w2[r, pl.ds(nb, nb), :]


def look_kernel(
    seqs, hops, ids, normed, par, before, wsh, *refs
):
    recvs, refs = refs[: len(hops)], refs[len(hops) :]
    st_in, skip_pre, mixed, shared_pre, prob, nf, sm, pw = refs
    skip, _, _, qg, kg, rb = vectors(par)
    place = ids[2]
    put_rows(nf, slice(None), normed[...].astype(F32))
    piece_powers(par, pw)
    logd = par[1]
    dinv = 1.0 / par[0]
    for s in range(seqs):
        a = jnp.zeros((NDIM, D), F32)
        b = jnp.zeros((NDIM, D), F32)
        for (shift, k), got in zip(hops, recvs):
            end = jnp.left_shift(jnp.bitwise_xor(jnp.right_shift(place, shift), k) + 1, shift)
            off = (place - end).astype(F32) * float(CH)
            power = jnp.where(place >= end, jnp.exp(jnp.maximum(off, 0.0) * logd), 0.0)
            oa, ob = (part * power for part in get_low(got, s))
            b = b + ob + off * oa * dinv
            a = a + oa
        st_in[0, s] = a
        st_in[1, s] = b

    def ema(i, carry):
        s = i // BLOCKS
        lane = lanes_of(i)
        row = [pl.ds(j, 1) for j in range(NDIM)]
        ds = [spread(par[0, row[j], lane]) for j in range(NDIM)]
        ws = [spread(par[2, row[j], lane] * par[3, row[j], lane]) for j in range(NDIM)]
        st = [
            before[0, s, j, :, lane] + pw[j, :, lane] * st_in[0, s, row[j], lane]
            for j in range(NDIM)
        ]
        for t in range(PIECE):
            x = nf[i % BLOCKS, piece_rows(s, t), :]
            parts = [None, None]
            for j in range(NDIM):
                st[j] = ds[j] * st[j] + x
                term = ws[j] * st[j]
                parts[j % 2] = term if parts[j % 2] is None else parts[j % 2] + term
            sm[i % BLOCKS, piece_rows(s, t), :] = parts[0] + parts[1]
        return carry

    lax.fori_loop(0, seqs * BLOCKS, ema, 0)
    for s in range(seqs):
        pre = get_rows(sm, rows_of(s)) + skip[...] * get_rows(nf, rows_of(s))
        skip_pre[rows_of(s), :] = pre
        mixed[rows_of(s), :] = silu(pre).astype(BF16)
    sp = mm(mixed[...], wsh[...])
    shared_pre[...] = sp
    shared = silu(sp)
    query = (shared * qg[...]).astype(BF16)
    keys = (shared * kg[...]).astype(BF16)
    t_at = lax.broadcasted_iota(jnp.int32, (CH, CH), 0)
    s_at = lax.broadcasted_iota(jnp.int32, (CH, CH), 1)
    bias_t = jnp.broadcast_to(rb[...], (CH, CH))
    for bit in range(7):
        bias_t = jnp.where(
            jnp.bitwise_and(t_at, 1 << bit) > 0, pltpu.roll(bias_t, 1 << bit, 1), bias_t
        )
    bias = bias_t.T
    for s in range(seqs):
        raw = mm_nt(query[s * CH : (s + 1) * CH], keys[s * CH : (s + 1) * CH]) * Z ** (-0.5)
        live = (place * CH + s_at).astype(F32) < par[4, 4 + s : 5 + s, :CH]
        allowed = (s_at <= t_at) & (live | (s_at == t_at))
        masked = jnp.where(allowed, raw + bias, -1e30)
        top = jnp.max(masked, axis=-1, keepdims=True)
        weights = jnp.where(allowed, jnp.exp(masked - top), 0.0)
        prob[s] = weights / jnp.sum(weights, axis=-1, keepdims=True)


def mix_kernel(seqs, tp, ids, tok, normed, mixed, prob, *refs):
    near, far, refs = take_weights(refs, tp, 2, 4)
    (
        values, value_pre, reset_pre, attended, gated, hidden_pre, update_pre, middle,
        w1, w2, whu, sems,
    ) = refs
    vb = values.shape[2]
    nb = D // tp
    copies = gate_copies(tp, ids, near, far, w1, w2, sems)
    for r in range(tp):
        for c in copies[r]:
            c.wait()
        vp = mm(normed[...], w1[r, :, :vb])
        value_pre[r] = vp
        v = silu(vp).astype(BF16)
        values[r] = v
        rp = mm(mixed[...], w1[r, :, vb:])
        reset_pre[r] = rp
        gate = silu(rp)
        for s in range(seqs):
            att = mm(prob[s].astype(BF16), v[s * CH : (s + 1) * CH])
            attended[r, rows_of(s), :] = att
            gated[r, rows_of(s), :] = (gate[s * CH : (s + 1) * CH] * att).astype(BF16)
        part = mm(gated[r], w2[r, pl.ds(2 * nb, vb), :])
        hidden_pre[...] = hidden_pre[...] + part if r else part
    gate_rows(tp, ids[0], w2, whu)
    hu = mm(mixed[...], whu[...])
    hidden_pre[...] += hu[:, :D]
    update_pre[...] = hu[:, D:]
    for s in range(seqs):
        x = tok[s].astype(F32)
        middle[rows_of(s), :] = x + sigmoid(update_pre[rows_of(s), :]) * (
            silu(hidden_pre[rows_of(s), :]) - x
        )


def ffn_kernel(seqs, tp, ids, tok, cot, middle, hidden_pre, update_pre, par, *refs):
    gain2 = vectors(par)[1]
    near, far, refs = take_weights(refs, tp, 1, 2)
    (
        out, keep, send, grad_hu, resid, grad_gain2,
        w3, n2, lg, acc, gn2, sems,
    ) = refs
    vb = w3.shape[2] // 2
    top, half = tp // 2, D // 2
    cuts = D // vb
    upper = jnp.bitwise_and(ids[1], 1)
    copies = [[] for _ in range(tp)]

    def add(r, source, target):
        at = sems.at[sum(len(c) for c in copies)]
        copies[r].append(pltpu.make_async_copy(source, target, at))

    for r in range(top):
        add(r, near[r][0], w3.at[r])
    for r in range(top):
        for part, at in zip(far[r], (upper, 1 - upper)):
            row = pl.ds(pl.multiple_of(at * half, half), half)
            add(top + r, part, w3.at[top + r, row, :])
    for group in copies:
        for c in group:
            c.start()
    place = ids[2]
    xhat, scale = normalized(middle[...])
    n2[...] = (xhat * gain2[...]).astype(BF16)
    at = (lax.broadcasted_iota(jnp.int32, (CH, D), 0) + place * CH).astype(F32)
    for s in range(seqs):
        lg[rows_of(s), :] = jnp.where(
            at < par[4, 4 + s : 5 + s, :], cot[s].astype(F32), 0.0
        ).astype(BF16)
    acc[...] = jnp.zeros_like(acc)
    gn2[...] = jnp.zeros_like(gn2)
    for h in range(tp // 2):
        for odd in range(2):
            r = 2 * h + odd
            for c in copies[r]:
                c.wait()
            grads = (keep, send)[odd]
            pre = mm(n2[...], w3[r, :, :vb])
            inner = silu(pre).astype(BF16)
            back = None
            for k in range(cuts):
                cols = slice(k * vb, (k + 1) * vb)
                w_out = w3[r, cols, vb:]
                acc[:, cols] += mm(inner, w_out)
                term = mm_nt(lg[:, cols], w_out)
                back = term if back is None else back + term
            gip = (back * silu_slope(pre)).astype(BF16)
            gn2[...] += mm_nt(gip, w3[r, :, :vb])
            grads[h, :, :vb] = mm_tn(n2[...], gip).astype(BF16)
            gwo = mm_tn(inner, lg[...]).astype(BF16)
            for k in range(cuts):
                grads[h, k * vb : (k + 1) * vb, vb:] = gwo[:, k * vb : (k + 1) * vb]
    mid = middle[...]
    out[...] = (mid + acc[...]).astype(BF16)
    grad = gn2[...]
    grad_gain2[...] = jnp.sum(grad * xhat, axis=0, keepdims=True)
    gm = lg[...].astype(F32) + norm_back(grad, xhat, scale, gain2[...])
    for s in range(seqs):
        x = tok[s].astype(F32)
        g = gm[s * CH : (s + 1) * CH]
        hp = hidden_pre[rows_of(s), :]
        update = sigmoid(update_pre[rows_of(s), :])
        grad_hu[rows_of(s), :D] = (g * update * silu_slope(hp)).astype(BF16)
        grad_hu[rows_of(s), D:] = (g * (silu(hp) - x) * update * (1.0 - update)).astype(BF16)
        resid[rows_of(s), :] = g * (1.0 - update)


def gates_kernel(tp, ids, mixed, gated, grad_hu, keep2, send2, ghu):
    nb = D // tp
    vb = gated.shape[2]
    wide = 2 * vb
    me = ids[0]
    ghu[...] = mm_tn(mixed[...], grad_hu[...])

    def block(h, carry):
        for odd in range(2):
            r = 2 * h + odd
            g2 = (keep2, send2)[odd]
            row = pl.ds(pl.multiple_of(jnp.bitwise_xor(me, r) * nb, nb), nb)
            gu = mm_tn(gated[r], grad_hu[:, :D]).astype(BF16)
            for k in range(D // wide):
                top = k * (2 * nb + vb)
                g2[h, pl.ds(top, nb), :] = ghu[row, pl.ds(k * wide, wide)].astype(BF16)
                g2[h, pl.ds(top + nb, nb), :] = ghu[row, pl.ds(D + k * wide, wide)].astype(BF16)
                g2[h, pl.ds(top + 2 * nb, vb), :] = gu[:, k * wide : (k + 1) * wide]
        return carry

    lax.fori_loop(0, tp // 2, block, 0)


def back_kernel(
    seqs, tp,
    ids, normed, mixed, skip_pre, shared_pre, prob, values, value_pre, reset_pre, attended,
    grad_hu, par, wsh, tok, before, st_in, grad_gain2, *refs,
):
    skip, _, _, qg, kg, _ = vectors(par)
    near, far, refs = take_weights(refs, tp, 2, 4)
    (
        keep1, send1, grad_skip, grad_normed, after, ends, sums_keep, sums_send,
        w1, w2, whu, gm, gp, tab, grad_wsh, misc, table, nf, pw, sems,
    ) = refs
    vb = values.shape[2]
    nb = D // tp
    me = ids[0]
    copies = gate_copies(tp, ids, near, far, w1, w2, sems)
    gp[...] = jnp.zeros_like(gp)
    grad_normed[...] = jnp.zeros_like(grad_normed)
    for group in copies:
        for c in group:
            c.wait()
    gate_rows(tp, me, w2, whu)
    gm[...] = mm_nt(grad_hu[...], whu[...])

    def block(h, carry):
        for odd in range(2):
            r = 2 * h + odd
            g1 = (keep1, send1)[odd]
            gg = mm_nt(grad_hu[:, :D], w2[r, pl.ds(2 * nb, vb), :])
            rp = reset_pre[r]
            sig = sigmoid(rp)
            ga = (gg * (rp * sig)).astype(BF16)
            grp = (gg * attended[r] * (sig * (1.0 + rp * (1.0 - sig)))).astype(BF16)
            g1[h, :, vb:] = mm_tn(mixed[...], grp).astype(BF16)
            gm[...] += mm_nt(grp, w1[r, :, vb:])
            gvs = []
            for s in range(seqs):
                part = ga[s * CH : (s + 1) * CH]
                gvs.append(mm_tn(prob[s].astype(BF16), part))
                gp[s] += mm_nt(part, values[r, rows_of(s), :])
            gv = jnp.concatenate(gvs, axis=0) if seqs > 1 else gvs[0]
            gvp = (gv * silu_slope(value_pre[r])).astype(BF16)
            g1[h, :, :vb] = mm_tn(normed[...], gvp).astype(BF16)
            grad_normed[...] += mm_nt(gvp, w1[r, :, :vb])
        return carry

    lax.fori_loop(0, tp // 2, block, 0)
    sp = shared_pre[...]
    shared = silu(sp)
    query = (shared * qg[...]).astype(BF16)
    keys = (shared * kg[...]).astype(BF16)
    total = jnp.zeros((CH, CH), F32)
    gqs = []
    gks = []
    for s in range(seqs):
        pr = prob[s]
        low = (pr * (gp[s] - jnp.sum(pr * gp[s], axis=-1, keepdims=True))).astype(BF16)
        total = total + low.astype(F32)
        gqs.append(mm(low, keys[s * CH : (s + 1) * CH]) * Z ** (-0.5))
        gks.append(mm_tn(low, query[s * CH : (s + 1) * CH]) * Z ** (-0.5))
    gq = jnp.concatenate(gqs, axis=0) if seqs > 1 else gqs[0]
    gk = jnp.concatenate(gks, axis=0) if seqs > 1 else gks[0]
    turned = total.T
    s_at = lax.broadcasted_iota(jnp.int32, (CH, CH), 0)
    for bit in range(7):
        turned = jnp.where(
            jnp.bitwise_and(s_at, 1 << bit) > 0, pltpu.roll(turned, CH - (1 << bit), 1), turned
        )
    misc[...] = jnp.concatenate(
        [
            jnp.sum(gq * shared, axis=0, keepdims=True),
            jnp.sum(gk * shared, axis=0, keepdims=True),
            jnp.sum(turned, axis=0, keepdims=True),
            jnp.zeros((1, D - 3 * Z), F32),
        ],
        axis=1,
    )
    gsp = ((gq * qg[...] + gk * kg[...]) * silu_slope(sp)).astype(BF16)
    grad_wsh[...] = mm_tn(mixed[...], gsp)
    put_rows(
        grad_skip,
        slice(None),
        (gm[...] + mm_nt(gsp, wsh[...])) * silu_slope(skip_pre[...]),
    )
    d = par[0]
    d2 = d * d
    d4 = d2 * d2
    d8 = d4 * d4
    q = d8 * d8
    tab[0] = q
    tab[1] = q * q
    tab[2] = q * q * q * q
    place = lax.broadcasted_iota(jnp.int32, (PIECES, LANES), 0)

    def body(i, carry):
        s = i // BLOCKS
        lane = lanes_of(i)
        ds = [spread(par[0, j : j + 1, lane]) for j in range(NDIM)]
        ad = [grad_skip[i % BLOCKS, piece_rows(s, PIECE - 1), :]] * NDIM
        for t in range(PIECE - 2, -1, -1):
            g = grad_skip[i % BLOCKS, piece_rows(s, t), :]
            for j in range(NDIM):
                ad[j] = ds[j] * ad[j] + g
        for j in range(NDIM):
            a = ad[j]
            for k, step in enumerate((1, 2, 4)):
                qm = spread(tab[k, j : j + 1, lane])
                a = a + qm * jnp.where(place < PIECES - step, pltpu.roll(a, PIECES - step, 0), 0.0)
            after[s, j, :, lane] = jnp.where(
                place < PIECES - 1, pltpu.roll(a, PIECES - 1, 0), 0.0
            )
            ends[s, j : j + 1, lane] = a[:1]
        return carry

    lax.fori_loop(0, seqs * BLOCKS, body, 0)
    small_sums(
        seqs, ids, tok, normed, grad_skip, grad_normed, par, before, st_in, skip, grad_gain2, misc,
        grad_wsh, sums_keep, sums_send, table, nf, pw,
    )


def small_sums(
    seqs, ids, tok, normed, grad_skip, grad_normed, par, before, st_in, skip, gain2_row, misc, grad_wsh,
    keep, send, table, nf, pw,
):
    put_rows(nf, slice(None), normed[...].astype(F32))
    piece_powers(par, pw)
    count = D // (D // Z)
    small = table.at[count:, :]
    small[...] = jnp.zeros_like(small)
    for k in range(D // Z):
        table[:count, k * Z : (k + 1) * Z] = grad_wsh[k * count : (k + 1) * count, :]

    def body(i, carry):
        s = i // BLOCKS
        lane = lanes_of(i)
        k16 = lax.broadcasted_iota(jnp.int32, (PIECES, LANES), 0).astype(F32) * PIECE
        for j0 in range(0, NDIM, 8):
            row = [pl.ds(j0 + j, 1) for j in range(8)]
            ds = [spread(par[0, row[j], lane]) for j in range(8)]
            st, ta, q, r = [], [], [], []
            for j in range(8):
                e = pw[j0 + j, :, lane] * st_in[0, s, row[j], lane]
                st.append(before[0, s, j0 + j, :, lane] + e)
                ta.append(
                    before[1, s, j0 + j, :, lane]
                    + pw[j0 + j, :, lane] * st_in[1, s, row[j], lane]
                    + k16 * e / ds[j]
                )
                q.append(jnp.zeros((PIECES, LANES), F32))
                r.append(jnp.zeros((PIECES, LANES), F32))
            for t in range(PIECE):
                x = nf[i % BLOCKS, piece_rows(s, t), :]
                g = grad_skip[i % BLOCKS, piece_rows(s, t), :]
                for j in range(8):
                    ta[j] = ds[j] * ta[j] + st[j]
                    st[j] = ds[j] * st[j] + x
                    q[j] = q[j] + g * st[j]
                    r[j] = r[j] + g * ta[j]
            for j in range(8):
                small[pl.ds(j0 + j, 1), lane] += jnp.sum(q[j], axis=0, keepdims=True)
                small[pl.ds(NDIM + j0 + j, 1), lane] += jnp.sum(r[j], axis=0, keepdims=True)
        return carry

    lax.fori_loop(0, seqs * BLOCKS, body, 0)
    gsk = jnp.zeros((1, D), F32)
    gn1 = jnp.zeros((1, D), F32)
    for s in range(seqs):
        xhat, _ = normalized(tok[s].astype(F32))
        g = get_rows(grad_skip, rows_of(s))
        direct = g * skip[...] + grad_normed[rows_of(s), :]
        gsk = gsk + jnp.sum(g * get_rows(nf, rows_of(s)), axis=0, keepdims=True)
        gn1 = gn1 + jnp.sum(direct * xhat, axis=0, keepdims=True)
    small[2 * NDIM : 2 * NDIM + 1, :] = gsk
    small[2 * NDIM + 1 : 2 * NDIM + 2, :] = gn1
    small[2 * NDIM + 2 : 2 * NDIM + 3, :] = gain2_row[...]
    small[2 * NDIM + 3 : 2 * NDIM + 4, :] = misc[...]
    half = keep.shape[0]
    mine = jnp.bitwise_and(ids[0], 1) * half
    keep[...] = table[pl.ds(pl.multiple_of(mine, 8), half), :]
    send[...] = table[pl.ds(pl.multiple_of(half - mine, 8), half), :]


def pair_kernel(bit, ids, mine, other, out):
    half = mine.shape[0]
    upper = jnp.where(jnp.bitwise_and(ids[0], bit) > 0, half, 0)
    out[pl.ds(pl.multiple_of(upper, 8), half), :] = mine[...]
    out[pl.ds(pl.multiple_of(half - upper, 8), half), :] = other[...]


def finish_kernel(
    ids, par, rate, beta, mine, other,
    grad_gain, grad_rate, grad_beta, grad_eta, grad_skip, grad_wsh, grad_qg, grad_kg, grad_rb,
    grad_gain2, table,
):
    gain = vectors(par)[2]
    pair_kernel(1, ids, mine, other, table)
    count = D // (D // Z)
    for k in range(D // Z):
        grad_wsh[k * count : (k + 1) * count, :] = table[:count, k * Z : (k + 1) * Z]
    small = table.at[count:, :]
    inflow, eta, r = par[2], par[3], rate[...]
    root = jnp.sqrt(r * (2.0 - r))
    q_sum = small[:NDIM, :]
    grad_inflow = eta * q_sum
    grad_decay = eta * inflow * small[NDIM : 2 * NDIM, :]
    grad_rate[...] = grad_inflow * beta[...] * (1.0 - r) / root - grad_decay
    grad_beta[...] = grad_inflow * root
    grad_eta[...] = inflow * q_sum
    row = [small[2 * NDIM + i : 2 * NDIM + i + 1, :] for i in range(4)]
    grad_skip[...] = row[0]
    grad_gain[...] = row[1] + jnp.sum(inflow * grad_inflow, axis=0, keepdims=True) / gain[...]
    grad_gain2[...] = row[2]
    grad_qg[...] = row[3][:, :Z]
    grad_kg[...] = row[3][:, Z : 2 * Z]
    grad_rb[...] = row[3][:, 2 * Z : 3 * Z]


def leave_kernel(
    seqs, tops, ids, tok, par, grad_skip, grad_normed, behind, resid, *refs
):
    levels = len(tops)
    recvs, refs = refs[:levels], refs[levels:]
    grad_tokens, ad_in, pw, sm = refs
    skip, _, gain = vectors(par)[:3]
    place = ids[2]
    logd = par[1]
    gots = [get_wide(recvs[k], tops[k], seqs * NDIM) for k in range(levels)]
    for s in range(seqs):
        a = jnp.zeros((NDIM, D), F32)
        for k in range(levels):
            low = jnp.bitwise_and(place, 1 << k) == 0
            off = jnp.bitwise_and(place, (1 << k) - 1)
            away = ((1 << k) - 1 - off).astype(F32) * float(CH)
            got = gots[k][s * NDIM : (s + 1) * NDIM]
            a = a + got * jnp.where(low, jnp.exp(away * logd), 0.0)
        ad_in[s] = a
    k = (PIECES - 1 - lax.broadcasted_iota(jnp.int32, (PIECES, D), 0)).astype(F32) * PIECE
    for j in range(NDIM):
        pw[j] = jnp.exp(k * par[1, j : j + 1, :])

    def body(i, carry):
        s = i // BLOCKS
        lane = lanes_of(i)
        row = [pl.ds(j, 1) for j in range(NDIM)]
        ds = [spread(par[0, row[j], lane]) for j in range(NDIM)]
        ws = [spread(par[2, row[j], lane] * par[3, row[j], lane]) for j in range(NDIM)]
        ad = [
            behind[s, j, :, lane] + pw[j, :, lane] * ad_in[s, row[j], lane] for j in range(NDIM)
        ]
        for t in range(PIECE - 1, -1, -1):
            g = grad_skip[i % BLOCKS, piece_rows(s, t), :]
            parts = [None, None]
            for j in range(NDIM):
                ad[j] = ds[j] * ad[j] + g
                term = ws[j] * ad[j]
                parts[j % 2] = term if parts[j % 2] is None else parts[j % 2] + term
            sm[i % BLOCKS, piece_rows(s, t), :] = parts[0] + parts[1]
        return carry

    lax.fori_loop(0, seqs * BLOCKS, body, 0)
    for s in range(seqs):
        xhat, scale = normalized(tok[s].astype(F32))
        grad = (
            get_rows(sm, rows_of(s))
            + get_rows(grad_skip, rows_of(s)) * skip[...]
            + grad_normed[rows_of(s), :]
        )
        grad_tokens[s] = (
            resid[rows_of(s), :] + norm_back(grad, xhat, scale, gain[...])
        ).astype(BF16)


def hop_kernel(seqs, shift, count, ids, state, *refs):
    others, (total, low) = refs[: count - 1], refs[count - 1 :]
    mine = jnp.bitwise_and(jnp.right_shift(ids[2], shift), count - 1)
    logd = state[2 * seqs]
    total[2 * seqs] = logd
    sums = [None] * (2 * seqs)
    for k in range(count):
        after = (count - 1 - jnp.bitwise_xor(mine, k)).astype(F32) * float(CH << shift)
        power = jnp.exp(after * logd)
        slope = after * jnp.exp((after - 1.0) * logd)
        for s in range(seqs):
            part = get_low(others[k - 1], s) if k else (state[2 * s], state[2 * s + 1])
            a, b = power * part[0], power * part[1] + slope * part[0]
            sums[2 * s : 2 * s + 2] = [sums[2 * s] + a, sums[2 * s + 1] + b] if k else [a, b]
    for i in range(2 * seqs):
        total[i] = sums[i]
    put_low(low, sums)


def put_wide(ref, top, value):
    wide = ref.shape[1]
    count = value.shape[0]
    for k in range(D // wide):
        ref[pl.ds(top + k * count, count), :] = value[:, k * wide : (k + 1) * wide].astype(ref.dtype)


def get_wide(ref, top, count):
    wide = ref.shape[1]
    runs = [ref[pl.ds(top + k * count, count), :].astype(F32) for k in range(D // wide)]
    return jnp.concatenate(runs, axis=1) if len(runs) > 1 else runs[0]


def first_back_hop(seqs, joins, ids, par, own, other, sums, got, out, keep, payload):
    rows = seqs * NDIM
    fold_lanes = D // payload.shape[1]
    if joins:
        join_adjoint(seqs, 0, ids, par, own, other[...], out)
    else:
        out[...] = own[...]
    put_wide(payload, 0, out[...])
    half = keep.shape[0]
    upper = jnp.where(jnp.bitwise_and(ids[0], 2) > 0, half, 0)
    mine = pl.ds(pl.multiple_of(upper, 8), half)
    theirs = pl.ds(pl.multiple_of(half - upper, 8), half)
    keep[...] = sums[mine, :] + got[mine, :]
    put_wide(payload, rows * fold_lanes, sums[theirs, :] + got[theirs, :])


def join_adjoint(seqs, level, ids, par, own, got, out):
    upper = jnp.bitwise_and(ids[2], 1 << level) > 0
    power = jnp.exp(float(CH << level) * par[1])
    for s in range(seqs):
        row = slice(s * NDIM, (s + 1) * NDIM)
        early = jnp.where(upper, got[row], own[row, :])
        late = jnp.where(upper, own[row, :], got[row])
        out[row, :] = early + power * late


def chain_hop(seqs, level, split, halved, top, ids, par, own, kept, sent, other, out, keep, payload, base):
    rows = seqs * NDIM
    lanes = D // other.shape[1]
    small_base = 0 if payload is None else base + rows * (D // payload.shape[1])
    if out is not None:
        join_adjoint(seqs, level, ids, par, own, get_wide(other, top, rows), out)
        put_wide(payload, base, out[...])
    half = keep.shape[0]
    if split:
        upper = jnp.bitwise_and(ids[0], split) > 0
        got = get_wide(other, top + rows * lanes, 2 * half)
        first, second = kept[:half, :] + got[:half], kept[half:, :] + got[half:]
        keep[...] = jnp.where(upper, second, first)
        put_wide(payload, small_base, jnp.where(upper, first, second))
    else:
        mine = kept[...] if halved else get_wide(sent, top + rows * lanes, half)
        total = mine + get_wide(other, top + rows * lanes, half)
        keep[...] = total
        if payload is not None:
            put_wide(payload, small_base, total)


def back_hop(seqs, level, split, halved, ids, par, own, kept, sent, other, out, keep, payload):
    chain_hop(
        seqs, level, split, halved, 0, ids, par, own, kept, sent, other, out, keep, payload, 0
    )


def split_rows(count, cut, place, k):
    shift, bits = cut
    rows = count >> bits
    sub = jnp.bitwise_and(jnp.right_shift(place, shift), (1 << bits) - 1)
    return pl.multiple_of(jnp.bitwise_xor(sub, k) * rows, rows), rows


def add_rows(parts, start, high, out, top, lane, width, at):
    step = min(64, high)

    def body(i, carry):
        row = pl.ds(pl.multiple_of(start + i * step, step), step)
        total = parts[0][row, lane : lane + width].astype(F32)
        for other in parts[1:]:
            total = total + other[row, lane : lane + width].astype(F32)
        out[pl.ds(pl.multiple_of(top + i * step, 16), step), at : at + width] = total.astype(BF16)
        return carry

    lax.fori_loop(0, high // step, body, 0)


def fold_kernel(jobs, inputs, ids, *refs):
    parts, outs = refs[:inputs], refs[inputs:]
    at = 0
    for count, lane, width, cut, targets in jobs:
        own = parts[at : at + count]
        at += count
        blocks, rows, _ = own[0].shape
        for k, (target, block, offset) in enumerate(targets):
            if cut == "tp":
                ranges, start, high = (k,), 0, rows
            elif cut is None:
                ranges, start, high = range(blocks), 0, rows
            else:
                start, high = split_rows(rows, cut, ids[1], k)
                ranges = range(blocks)
            for to, b in enumerate(ranges):
                add_rows(
                    [p.at[b] for p in own], start, high, outs[target].at[block + to], 0, lane,
                    width, offset,
                )


def fold(ids, shapes, jobs):
    arrays = [a for job in jobs for a in job[0]]
    plan = [(len(job[0]),) + tuple(job[1:]) for job in jobs]
    return call(
        functools.partial(fold_kernel, plan, len(arrays)),
        tuple(shape(dims, BF16) for dims in shapes),
        [],
        (ids, *arrays),
        [SMEM] + [VMEM] * len(arrays),
        "fold",
    )


def join_kernel(cut, ids, mine, other, out):
    blocks, rows, _ = mine.shape
    for k, part in enumerate((mine, other)):
        start, _ = split_rows(2 * rows, cut, ids[1], k)
        for b in range(blocks):
            out[b, pl.ds(pl.multiple_of(start, 16), rows), :] = part[b]


def join(ids, mine, other, cut):
    blocks, rows, lanes = mine.shape
    return call(
        functools.partial(join_kernel, cut),
        (shape((blocks, 2 * rows, lanes), BF16),),
        [],
        (ids, mine, other),
        [SMEM, VMEM, VMEM],
        "join",
    )[0]


def start_kernel(
    seqs, bits, ids, par, own, other, sums, got, keep1, got1, out, keep, left, payload, right, send
):
    vb = keep1.shape[2] // 2
    for b, target in enumerate((left, payload)):
        add_rows([keep1.at[b], got1.at[b]], 0, D, target, 0, 0, vb, 0)
    for k, target in enumerate((right, send)):
        start, high = split_rows(D, (0, bits), ids[1], k)
        for b in range(2):
            add_rows([keep1.at[b], got1.at[b]], start, high, target.at[b], 0, vb, vb, 0)
    join_adjoint(seqs, 0, ids, par, own, other[...], out)
    rows, half = seqs * NDIM, keep.shape[0]
    put_wide(payload, D, out[...])
    upper = jnp.where(jnp.bitwise_and(ids[0], 2) > 0, half, 0)
    mine = pl.ds(pl.multiple_of(upper, 8), half)
    theirs = pl.ds(pl.multiple_of(half - upper, 8), half)
    keep[...] = sums[mine, :] + got[mine, :]
    put_wide(payload, D + rows * (D // vb), sums[theirs, :] + got[theirs, :])


def cross_kernel(
    seqs, bits, ids, par, own, kept, sent, other, left, right, got, out, keep, left_out, payload,
    right_out, send,
):
    vb = left.shape[1]
    for k, target in enumerate((left_out, payload)):
        start, high = split_rows(D, (0, bits), ids[1], k)
        add_rows([left, other], start, high, target, 0, 0, vb, 0)
    for b, target in enumerate((right_out, send)):
        add_rows([right.at[b], got.at[b]], 0, high, target, 0, 0, vb, 0)
    chain_hop(
        seqs, 1, 0, True, D, ids, par, own, kept, sent, other, out, keep, payload, high
    )


def ride_kernel(
    seqs, level, split, halved, top, jobs, cut, high, last, ids, par, own, kept, sent, other, *refs
):
    count = 1 + max(p for job in jobs for p in job[0])
    parts, refs = refs[:count], refs[count:]
    out = payload = None
    if last:
        keep, kept_out = refs
        halves = ((0, keep),)
    elif cut is None:
        kept_out, out, payload = refs
        halves = ((0, payload),)
    else:
        keep, kept_out, out, payload = refs
        halves = ((0, keep), (1, payload))
    for picks, width, at in jobs:
        chosen = [other if p == -1 else sent if p == -2 else parts[p] for p in picks]
        for k, target in halves:
            start = 0 if cut is None else split_rows(2 * high, cut, ids[1], k)[0]
            add_rows(chosen, start, high, target, 0, 0, width, at)
    chain_hop(
        seqs, level, split, halved, top, ids, par, own, kept, sent, other, out, kept_out, payload,
        high,
    )


def unpack_first(cut, ids, *refs):
    count = 1 << cut[1]
    pieces, refs = refs[:count], refs[count:]
    w_in, w_out = refs[:2]
    outs = refs[2:]
    vb = w_in.shape[1]
    wide = 2 * vb
    each = sum(out.shape[0] for out in outs)
    for k in range(count):
        row, rows = split_rows(D, cut, ids[1], k)
        w_in[pl.ds(row, rows), :] = pieces[k][0, :, :vb].astype(F32)
        for first in range(0, rows, vb):
            w_out[:, pl.ds(pl.multiple_of(row + first, vb), vb)] = pieces[k][
                0, first : first + vb, vb:
            ].astype(F32)
        for b in range(count):

            @pl.when(row == b * rows)
            def _(k=k, b=b, rows=rows):
                for run in range(D // wide):
                    start = run * each
                    for out in outs:
                        end = start + out.shape[0]
                        lo, hi = max(start, b * rows), min(end, (b + 1) * rows)
                        if lo < hi:
                            out[lo - start : hi - start, run * wide : (run + 1) * wide] = pieces[k][
                                1, lo - b * rows : hi - b * rows, :
                            ].astype(F32)
                        start = end


def unpack_sides(cut, ids, *refs):
    count = 1 << cut[1]
    pieces, (left, right) = refs[:count], refs[count:]
    vb = left.shape[1]
    for k in range(count):
        row, rows = split_rows(D, cut, ids[1], k)
        left[pl.ds(row, rows), :] = pieces[k][0, :, :vb].astype(F32)
        right[pl.ds(row, rows), :] = pieces[k][0, :, vb:].astype(F32)


def unpack(body, cut, ids, pieces, dims):
    return call(
        functools.partial(body, cut),
        tuple(shape(d) for d in dims),
        [],
        (ids, *pieces),
        [SMEM] + [VMEM] * len(pieces),
        "unpack",
    )


BOTH = ("seq", "tp")


def swap(value, mask):
    count = lax.axis_size("seq") * lax.axis_size("tp")
    return lax.ppermute(value, BOTH, [(i, i ^ mask) for i in range(count)])


def after(value, *others):
    return lax.optimization_barrier((value, *others))[0]


def bits_of(count):
    return [1 << k for k in range(count.bit_length() - 1)]


def has(index, bit):
    return jnp.bitwise_and(index, bit) > 0


def half_of(value, upper):
    half = value.shape[0] // 2
    return lax.dynamic_slice_in_dim(value, jnp.where(upper, half, 0), half, 0)


def joined(mine, other, upper):
    return jnp.where(
        upper,
        jnp.concatenate([other, mine], axis=0),
        jnp.concatenate([mine, other], axis=0),
    )


def spread_out(own, tp):
    pieces = {0: own}
    for bit in reversed(bits_of(tp // 2)):
        for r in list(pieces):
            pieces[r ^ bit] = [swap(a, bit) for a in pieces[r]]
    return [pieces[r] for r in range(tp // 2)]


def per_device(
    tokens,
    cotangent,
    valid_lengths,
    norm1_gain,
    ema_rate,
    ema_beta,
    ema_eta,
    ema_skip,
    w_shared,
    query_gain,
    key_gain,
    rel_bias,
    w_value,
    w_reset,
    w_update,
    w_hidden,
    u_hidden,
    norm2_gain,
    w_in,
    w_out,
):
    part = lax.axis_index("tp")
    tp = lax.axis_size("tp")
    seq = lax.axis_size("seq")
    all_seqs, local_rows, _ = tokens.shape
    vb = w_value.shape[1]
    nb = D // tp
    ybits = far_shift()
    traded = local_rows < CH
    lower = part % 2 == 0

    def trade(value):
        if not traded:
            return value
        other = swap(jnp.where(lower, value[1], value[0]), 1)
        mine = jnp.where(lower, value[0], value[1])
        return joined(mine, other, ~lower)[None]

    def trade_back(value):
        if not traded:
            return value
        first, second = value[0, :local_rows], value[0, local_rows:]
        other = swap(jnp.where(lower, second, first), 1)
        mine = jnp.where(lower, first, second)
        return jnp.where(lower, jnp.stack([mine, other]), jnp.stack([other, mine]))

    if traded:
        assert all_seqs == 2 and 2 * local_rows == CH
        seqs = 1
    else:
        assert local_rows == CH
        seqs = all_seqs
    rows = seqs * CH
    ids, ids_lengths = Here(seqs, None), Here(seqs, valid_lengths.astype(jnp.int32))
    masks = bits_of(tp * seq)[int(traded) :]
    levels = len(masks)

    tok = trade(tokens)
    cot = trade(cotangent)
    gain1 = norm1_gain[None]
    gain2 = norm2_gain[None]
    skip = ema_skip[None]
    rate, beta = ema_rate.T, ema_beta.T
    qg, kg, rb = query_gain[None], key_gain[None], rel_bias[None]

    top = tp // 2
    weights = (w_value, w_reset, w_hidden, w_update, u_hidden, w_in, w_out)
    rows2 = 2 * nb + vb
    normed, par, before, ends, low = call(
        functools.partial(enter_kernel, seqs),
        (
            shape((rows, D), BF16),
            shape((5, NDIM, D)),
            shape((2, seqs, NDIM, PIECES, D)),
            shape((2 * seqs + 1, NDIM, D)),
            shape((3 * seqs, NDIM, D), BF16),
        ),
        [
            pltpu.VMEM((seqs, CH, D), BF16),
            pltpu.VMEM((1, D), F32),
            pltpu.VMEM((NDIM, D), F32),
            pltpu.VMEM((NDIM, D), F32),
            pltpu.VMEM((NDIM, D), F32),
            pltpu.VMEM((1, D), F32),
            pltpu.VMEM((1, D), F32),
            pltpu.VMEM((1, Z), F32),
            pltpu.VMEM((1, Z), F32),
            pltpu.VMEM((1, Z), F32),
            pltpu.VMEM((BLOCKS, rows, LANES), F32),
            pltpu.VMEM((6, NDIM, D), F32),
            pltpu.SemaphoreType.DMA((10,)),
        ],
        (ids_lengths, tok, gain1, rate, beta, ema_eta.T, skip, gain2, qg, kg, rb),
        [SMEM] + [ANY] * 10,
        "enter",
        limit=12,
    )
    start = 1 - int(traded)
    groups = [(0, 1)] * start + [(start, 2)] + [(i, 1) for i in range(start + 2, levels)]
    hops = []
    (half1,) = call(
        first_half_kernel,
        (shape((D // 2, 2 * vb), BF16),),
        [pltpu.SemaphoreType.DMA((2,))],
        (w_value, w_reset),
        [ANY] * 2,
        "half",
        limit=60,
        outs=(pl.BlockSpec(),),
    )
    mine1 = swap(half1, top)
    state = ends
    for i, (shift, bits) in enumerate(groups):
        if i == start:
            low = after(low, mine1)
            pack1, pack2, pack3, half2, half3 = call(
                pack_kernel,
                (
                    shape((D, 2 * vb), BF16),
                    shape((rows2, D), BF16),
                    shape((D, 2 * vb), BF16),
                    shape((rows2, D // 2), BF16),
                    shape((D // 2, 2 * vb), BF16),
                ),
                [pltpu.SemaphoreType.DMA((10 + 3 * D // vb // 2,))],
                lax.optimization_barrier((*weights, low))[:-1],
                [ANY] * 7,
                "pack",
                limit=60,
                outs=(pl.BlockSpec(),) * 5,
            )
        if i == start + 1:
            mine2 = swap(after(half2, low), top)
            other1 = swap(after(mine1, low), tp)
            near_gates = spread_out([after(pack1, low), after(pack2, low)], tp)
        if i == start + 2:
            low = after(low, mine2, other1, *near_gates[-1])
            mine3 = swap(after(half3, low), top)
            other2 = swap(after(mine2, low), tp << ybits)
            near_feeds = spread_out([after(pack3, low)], tp)
        got = []
        for k in range(1, 1 << bits):
            got.append(swap(low, k << (shift + int(traded))))
            hops.append((shift, k, got[-1]))
        if i + 1 < len(groups):
            state, low = call(
                functools.partial(hop_kernel, seqs, shift, 1 << bits),
                (shape((2 * seqs + 1, NDIM, D)), shape((3 * seqs, NDIM, D), BF16)),
                [],
                (ids, state, *got),
                [SMEM] + [VMEM] * (1 + len(got)),
                "hop",
            )
    st_in, skip_pre, mixed, shared_pre, prob = call(
        functools.partial(look_kernel, seqs, [h[:2] for h in hops]),
        (
            shape((2, seqs, NDIM, D)),
            shape((rows, D)),
            shape((rows, D), BF16),
            shape((rows, Z)),
            shape((seqs, CH, CH)),
        ),
        [
            pltpu.VMEM((BLOCKS, rows, LANES), F32),
            pltpu.VMEM((BLOCKS, rows, LANES), F32),
            pltpu.VMEM((NDIM, PIECES, D), F32),
        ],
        (
            ids, after(normed, mine3), par, before, w_shared,
            *[h[2] for h in hops],
        ),
        [SMEM] + [VMEM] * (4 + len(hops)),
        "look",
        limit=10,
    )
    far_gates = spread_out([mine1, after(other1, prob), mine2, after(other2, prob)], tp)
    other3 = swap(mine3, tp)
    gates = [w for group in near_gates + far_gates for w in group]

    values, value_pre, reset_pre, attended, gated, hidden_pre, update_pre, middle = call(
        functools.partial(mix_kernel, seqs, tp),
        (
            shape((tp, rows, vb), BF16),
            shape((tp, rows, vb)),
            shape((tp, rows, vb)),
            shape((tp, rows, vb)),
            shape((tp, rows, vb), BF16),
            shape((rows, D)),
            shape((rows, D)),
            shape((rows, D)),
        ),
        [
            pltpu.VMEM((tp, D, 2 * vb), BF16),
            pltpu.VMEM((tp, rows2, D), BF16),
            pltpu.VMEM((D, 2 * D), BF16),
            pltpu.SemaphoreType.DMA((3 * tp,)),
        ],
        (ids, tok, normed, after(mixed, other3), prob, *gates),
        [SMEM] + [VMEM] * 4 + [ANY] * len(gates),
        "mix",
        limit=10,
    )

    far_feeds = spread_out([mine3, other3], tp)
    feeds = [w for group in near_feeds + far_feeds for w in group]
    out, keep3, send3, grad_hu, resid, grad_gain2 = call(
        functools.partial(ffn_kernel, seqs, tp),
        (
            shape((rows, D), BF16),
            shape((tp // 2, D, 2 * vb), BF16),
            shape((tp // 2, D, 2 * vb), BF16),
            shape((rows, 2 * D), BF16),
            shape((rows, D)),
            shape((1, D)),
        ),
        [
            pltpu.VMEM((tp, D, 2 * vb), BF16),
            pltpu.VMEM((rows, D), BF16),
            pltpu.VMEM((rows, D), BF16),
            pltpu.VMEM((rows, D), F32),
            pltpu.VMEM((rows, D), F32),
            pltpu.SemaphoreType.DMA((3 * tp // 2,)),
        ],
        (ids, tok, cot, middle, hidden_pre, update_pre, par, *feeds),
        [SMEM] + [VMEM] * 6 + [ANY] * len(feeds),
        "ffn",
        limit=10,
    )

    half = tp // 2
    yn = 1 << ybits
    wide = 2 * vb
    runs = D // wide
    cut_of_y = (0, ybits)
    zcuts = [(shift, 1) for shift in range(ybits, seq.bit_length() - 1)]

    def over_tp(pieces):
        return [pieces[0]] + [swap(p, 2 * k) for k, p in enumerate(pieces) if k]

    def over_y(pieces):
        return [pieces[0]] + [swap(p, tp * k) for k, p in enumerate(pieces) if k]

    def over_z(value, cut):
        return swap(value, tp << cut[0])

    def cut_tp(parts, dims):
        n = dims[0]
        return fold(
            ids,
            [(1,) + dims[1:]] * n,
            [(parts, 0, dims[2], "tp", [(k, 0, 0) for k in range(n)])],
        )

    def cut_y(parts, dims):
        return fold(
            ids,
            [(dims[0], dims[1] // yn, dims[2])] * yn,
            [(parts, 0, dims[2], cut_of_y, [(k, 0, 0) for k in range(yn)])],
        )

    last = [None]

    def now(value):
        return value if last[0] is None else after(value, last[0])

    chunk = (half, D, wide)
    got3 = swap(send3, 1)
    keep2, send2 = call(
        functools.partial(gates_kernel, tp),
        (shape(chunk, BF16), shape(chunk, BF16)),
        [pltpu.VMEM((D, 2 * D), F32)],
        (ids, mixed, gated, grad_hu),
        [SMEM] + [VMEM] * 3,
        "gates",
        limit=10,
    )
    got2 = swap(send2, 1)
    g3 = cut_tp([keep3, got3], chunk)
    g3 = over_tp(g3)
    g2 = cut_y([keep2, after(got2, g3[0])], chunk)
    g2 = over_y(g2)

    count = Z + SMALL_ROWS
    count += -count % (16 * tp)
    (
        keep1, send1, grad_skip, grad_normed, behind, back_ends, sums_keep, sums_send,
    ) = call(
        functools.partial(back_kernel, seqs, tp),
        (
            shape(chunk, BF16),
            shape(chunk, BF16),
            shape((BLOCKS, rows, LANES)),
            shape((rows, D)),
            shape((seqs, NDIM, PIECES, D)),
            shape((seqs, NDIM, D)),
            shape((count // 2, D)),
            shape((count // 2, D)),
        ),
        [
            pltpu.VMEM((tp, D, 2 * vb), BF16),
            pltpu.VMEM((tp, rows2, D), BF16),
            pltpu.VMEM((D, 2 * D), BF16),
            pltpu.VMEM((rows, D), F32),
            pltpu.VMEM((seqs, CH, CH), F32),
            pltpu.VMEM((3, NDIM, D), F32),
            pltpu.VMEM((D, Z), F32),
            pltpu.VMEM((1, D), F32),
            pltpu.VMEM((count, D), F32),
            pltpu.VMEM((BLOCKS, rows, LANES), F32),
            pltpu.VMEM((NDIM, PIECES, D), F32),
            pltpu.SemaphoreType.DMA((3 * tp,)),
        ],
        (
            ids, normed, mixed, skip_pre, shared_pre, prob, values, value_pre, reset_pre, attended,
            after(grad_hu, g2[0]), par, w_shared, tok, before, st_in, grad_gain2,
            *gates,
        ),
        [SMEM] + [VMEM] * 16 + [ANY] * len(gates),
        "back",
        limit=12,
    )

    g3 = cut_y([after(g3[0], send1)] + g3[1:], (1, D, wide))
    g2 = cut_tp([after(g2[0], g3[0])] + g2[1:], (half, D // yn, wide))
    (
        keep1, send1, grad_skip, grad_normed, behind, back_ends, sums_keep, sums_send, _,
    ) = lax.optimization_barrier(
        (keep1, send1, grad_skip, grad_normed, behind, back_ends, sums_keep, sums_send, g2[0])
    )
    adjoint = back_ends.reshape(seqs * NDIM, D)
    last[0] = g2[0]
    g3 = over_y(g3)
    g2 = over_tp(g2)
    got1 = swap(send1, 1)
    got_adjoint = adjoint if traded else swap(adjoint, 1)
    got_sums = swap(sums_send, 1)
    done = {}

    def first_chunks():
        high = D // yn
        for i, cut in enumerate(zcuts[:-1] + [None]):
            high = high // 2 if cut else high
            pieces = 2 if cut else 1
            if i:
                jobs = [([now(keep), other], 0, wide, cut, [(k, 0, 0) for k in range(pieces)])]
            else:
                jobs = [
                    ([now(g3[0])] + g3[1:], 0, wide, cut, [(k, 0, 0) for k in range(pieces)]),
                    (g2, 0, wide, cut, [(k, 1, 0) for k in range(pieces)]),
                ]
            keep, *send = fold(ids, [(2, high, wide)] * pieces, jobs)
            other = over_z(*send, cut) if cut else over_z(keep, zcuts[-1])
            yield keep
        (total,) = fold(ids, [keep.shape], [([now(keep), other], 0, wide, None, [(0, 0, 0)])])
        for cut in reversed(zcuts[:-1]):
            other = over_z(total, cut)
            yield total
            total = join(ids, now(total), other, cut)
        pieces = over_y([total] * yn)
        yield total
        done["first"] = unpack(
            unpack_first,
            cut_of_y,
            ids,
            [now(pieces[0])] + pieces[1:],
            [(D, vb), (vb, D), (nb, D), (nb, D), (vb, D)],
        )
        yield done["first"][0]

    def second_chunk():
        small_high = count // 4
        ad_rows = seqs * NDIM

        def payload_rows():
            return (ad_rows + small_high) * runs

        together = half == 2 and yn == 2 and not traded
        if together:
            lanes = D // vb
            own, kept, left, payload, right, send = call(
                functools.partial(start_kernel, seqs, ybits),
                (
                    shape((ad_rows, D)),
                    shape((small_high, D)),
                    shape((D, vb), BF16),
                    shape((D + (ad_rows + small_high) * lanes, vb), BF16),
                    shape((2, D // 2, vb), BF16),
                    shape((2, D // 2, vb), BF16),
                ),
                [],
                (ids, par, now(adjoint), got_adjoint, sums_keep, got_sums, keep1, got1),
                [SMEM] + [VMEM] * 7,
                "start",
            )
            other, got_right = swap(payload, 2), swap(send, tp)
            got = [(got_adjoint, 0), (other, D)]
            yield payload
            own, kept, left, payload, right, send = call(
                functools.partial(cross_kernel, seqs, ybits),
                (
                    shape((ad_rows, D)),
                    shape((small_high, D)),
                    shape((D // 2, vb), BF16),
                    shape((D // 2 + (ad_rows + small_high) * lanes, vb), BF16),
                    shape((D // 2, vb), BF16),
                    shape((D // 2, vb), BF16),
                ),
                [],
                (ids, par, now(own), kept, payload, other, left, right, got_right),
                [SMEM] + [VMEM] * 8,
                "cross",
            )
            other, got_right = swap(payload, tp), swap(send, 2)
            level, top, halved = 2, D // 2, False
            flat = [left, right, got_right]
            jobs = [((0, -1), vb, 0), ((1, 2), vb, vb)]
            yield payload
        else:
            own, kept, payload = call(
                functools.partial(first_back_hop, seqs, not traded),
                (
                    shape((ad_rows, D)),
                    shape((small_high, D)),
                    shape((payload_rows(), wide), BF16),
                ),
                [],
                (ids, par, now(adjoint), got_adjoint, sums_keep, got_sums),
                [SMEM] + [VMEM] * 5,
                "hop",
            )
            got = [] if traded else [(got_adjoint, 0)]
            level = int(not traded)
            halved = True
            other = swap(payload, masks[level])
            yield payload
            parts = fold(
                ids,
                [(1, D, vb)] * half + [(half, D // yn, vb)] * yn,
                [
                    ([now(keep1), got1], 0, vb, "tp", [(k, 0, 0) for k in range(half)]),
                    ([keep1, got1], vb, vb, cut_of_y, [(half + k, 0, 0) for k in range(yn)]),
                ],
            )
            left, right = over_tp(parts[:half]), over_y(parts[half:])
            yield parts[0]
            crossed = False
            while level + 1 < levels - len(zcuts):
                got.append((other, 0))
                split = 2 * masks[level] if 2 * masks[level] < tp else 0
                small_high = small_high // 2 if split else small_high
                own, kept, payload = call(
                    functools.partial(back_hop, seqs, level, split, halved),
                    (
                        shape((ad_rows, D)),
                        shape((small_high, D)),
                        shape((payload_rows(), wide), BF16),
                    ),
                    [],
                    (ids, par, now(own), kept, payload, other),
                    [SMEM] + [VMEM] * 5,
                    "hop",
                )
                halved = bool(split)
                level += 1
                other = swap(payload, masks[level])
                yield payload
                if crossed:
                    continue
                crossed = True
                parts = fold(
                    ids,
                    [(1, D // yn, vb)] * (yn + half),
                    [
                        ([now(left[0])] + left[1:], 0, vb, cut_of_y, [(k, 0, 0) for k in range(yn)]),
                        (right, 0, vb, "tp", [(yn + k, 0, 0) for k in range(half)]),
                    ],
                )
                left, right = over_y(parts[:yn]), over_tp(parts[yn:])
                yield parts[0]
            top = 0
            flat = [p.reshape(p.shape[1:]) for p in left + right]
            jobs = [
                (tuple(range(len(left))), vb, 0),
                (tuple(range(len(left), len(flat))), vb, vb),
            ]
        high = D // yn
        for cut in zcuts[:-1] + [None]:
            got.append((other, top))
            high = high // 2 if cut else high
            kept_chunk = [shape((high, wide), BF16)] if cut else []
            *flat, kept, own, payload = call(
                functools.partial(
                    ride_kernel, seqs, level, 0, halved, top, jobs, cut, high, False
                ),
                (
                    *kept_chunk,
                    shape((small_high, D)),
                    shape((ad_rows, D)),
                    shape((high + payload_rows(), wide), BF16),
                ),
                [],
                (ids, par, now(own), kept, payload, other, *flat),
                [SMEM] + [VMEM] * (5 + len(flat)),
                "ride",
            )
            halved = False
            level += 1
            top = high
            jobs = [((0 if cut else -2, -1), wide, 0)]
            other = swap(payload, masks[level])
            yield payload
        got.append((other, top))
        total, kept = call(
            functools.partial(ride_kernel, seqs, level, 0, False, top, jobs, None, high, True),
            (shape((high, wide), BF16), shape((small_high, D))),
            [],
            (ids, par, now(own), kept, payload, other, *flat),
            [SMEM] + [VMEM] * (5 + len(flat)),
            "ride",
        )
        bits = list(reversed(bits_of(tp)))
        total = total[None]
        far = swap(kept, bits[0])
        other = over_z(total, zcuts[-2]) if len(zcuts) > 1 else None
        yield total
        (done["tokens"],) = call(
            functools.partial(leave_kernel, seqs, [at for _, at in got]),
            (shape((seqs, CH, D), BF16),),
            [
                pltpu.VMEM((seqs, NDIM, D), F32),
                pltpu.VMEM((NDIM, PIECES, D), F32),
                pltpu.VMEM((BLOCKS, rows, LANES), F32),
            ],
            (
                ids, tok, par, now(grad_skip), grad_normed, behind, resid,
                *[g for g, _ in got],
            ),
            [SMEM] + [VMEM] * (6 + levels),
            "leave",
            limit=10,
        )
        yield done["tokens"]
        for i in range(len(zcuts) - 2, -1, -1):
            total = join(ids, now(total), other, zcuts[i])
            if i:
                other = over_z(total, zcuts[i - 1])
                yield total
        pieces = over_y([total] * yn)
        yield total
        for i in range(len(bits) - 1):
            (kept,) = call(
                functools.partial(pair_kernel, bits[i]),
                (shape((2 * kept.shape[0], D)),),
                [],
                (ids, now(kept), far),
                [SMEM, VMEM, VMEM],
                "pair",
            )
            far = swap(kept, bits[i + 1])
            yield kept
        done["small"] = call(
            finish_kernel,
            (
                shape((1, D)),
                shape((NDIM, D)),
                shape((NDIM, D)),
                shape((NDIM, D)),
                shape((1, D)),
                shape((D, Z)),
                shape((1, Z)),
                shape((1, Z)),
                shape((1, Z)),
                shape((1, D)),
            ),
            [pltpu.VMEM((count, D), F32)],
            (ids, par, rate, beta, now(kept), far),
            [SMEM] + [VMEM] * 5,
            "finish",
        )
        yield done["small"][0]
        done["second"] = unpack(
            unpack_sides, cut_of_y, ids, [now(pieces[0])] + pieces[1:], [(D, vb), (D, vb)]
        )
        yield done["second"][0]

    walks = {"f": first_chunks(), "s": second_chunk()}
    order = "sfsfssffssssfss"

    def advance(name):
        try:
            last[0] = next(walks[name])
        except StopIteration:
            del walks[name]

    for name in order:
        if name in walks:
            advance(name)
    while walks:
        for name in list(walks):
            advance(name)

    grad_w_in, grad_w_out, grad_w_hidden, grad_w_update, grad_u_hidden = done["first"]
    grad_w_value, grad_w_reset = done["second"]
    firsts = [
        small.T if small.shape[0] == NDIM else small[0] if small.shape[0] == 1 else small
        for small in done["small"]
    ]
    grad_norm2_gain = firsts.pop()
    return (
        trade_back(out.reshape(seqs, CH, D)),
        trade_back(done["tokens"]),
        *firsts,
        grad_w_value,
        grad_w_reset,
        grad_w_update,
        grad_w_hidden,
        grad_u_hidden,
        grad_norm2_gain,
        grad_w_in,
        grad_w_out,
    )


def solution(mesh):
    rows = P(None, ("seq", "tp"), None)
    cols = P(None, "tp")
    tall = P("tp", None)
    whole = P()
    return jax.shard_map(
        per_device,
        mesh=mesh,
        in_specs=(rows, rows) + (whole,) * 10 + (cols, cols, tall, tall, tall, whole, cols, tall),
        out_specs=(rows, rows) + (whole,) * 9 + (cols, cols, tall, tall, tall, whole, cols, tall),
        check_vma=False,
    )
```

```python
import functools

import jax
import jax.numpy as jnp
from jax import lax
from jax.experimental import pallas as pl
from jax.experimental.pallas import tpu as pltpu
from jax.sharding import PartitionSpec as P

D = 512
Z = 128
NDIM = 16
CH = 128
PIECE = 16
PIECES = CH // PIECE
LANES = 128
BLOCKS = D // LANES
EPS = 1e-05
F32 = jnp.float32
BF16 = jnp.bfloat16
SMALL_ROWS = 64

VMEM = pl.BlockSpec(memory_space=pltpu.VMEM)
SMEM = pl.BlockSpec(memory_space=pltpu.SMEM)
ANY = pl.BlockSpec(memory_space=pl.ANY)


def sigmoid(v):
    return 0.5 * jnp.tanh(0.5 * v) + 0.5


def silu(v):
    return v * sigmoid(v)


def silu_slope(v):
    s = sigmoid(v)
    return s * (1.0 + v * (1.0 - s))


def mm(a, b):
    return jnp.dot(a, b, preferred_element_type=F32)


def mm_nt(a, b):
    return lax.dot_general(a, b, (((1,), (1,)), ((), ())), preferred_element_type=F32)


def mm_tn(a, b):
    return lax.dot_general(a, b, (((0,), (0,)), ((), ())), preferred_element_type=F32)


def normalized(v):
    center = v - jnp.mean(v, axis=-1, keepdims=True)
    scale = lax.rsqrt(jnp.mean(center * center, axis=-1, keepdims=True) + EPS)
    return center * scale, scale


def norm_back(grad, xhat, scale, gain):
    full = grad * gain
    return scale * (
        full
        - jnp.mean(full, axis=-1, keepdims=True)
        - xhat * jnp.mean(full * xhat, axis=-1, keepdims=True)
    )


def rows_of(s):
    return pl.ds(s * CH, CH)


def lanes_of(i):
    return pl.ds(pl.multiple_of((i % BLOCKS) * LANES, LANES), LANES)


def spread(row):
    return jnp.broadcast_to(row, (PIECES, LANES))


def piece_rows(s, t):
    return pl.ds(s * CH + t, PIECES, stride=PIECE)


def put_rows(ref, rows, value):
    for b in range(BLOCKS):
        ref[b, rows, :] = value[:, b * LANES : (b + 1) * LANES]


def get_rows(ref, rows):
    return jnp.concatenate([ref[b, rows, :] for b in range(BLOCKS)], axis=1)


class Here:
    def __init__(self, seqs, lengths):
        self.seqs, self.lengths = seqs, lengths

    def __getitem__(self, i):
        if i == 0:
            return lax.axis_index("tp")
        if i == 1:
            return lax.axis_index("seq")
        if i == 2:
            index = lax.axis_index("seq") * lax.axis_size("tp") + lax.axis_index("tp")
            return index if self.seqs > 1 else jnp.right_shift(index, 1)
        return self.lengths[i - 3 if self.seqs > 1 else jnp.bitwise_and(lax.axis_index("tp"), 1)]


def call(body, out, scratch, operands, specs, name, limit=2, outs=None):
    place = operands[0]
    if isinstance(place, Here):
        kernel = body
        if place.lengths is None:
            operands, specs = operands[1:], specs[1:]
            body = lambda *refs: kernel(place, *refs)
        else:
            operands = (place.lengths, *operands[1:])
            body = lambda lengths, *refs: kernel(Here(place.seqs, lengths), *refs)
    return pl.pallas_call(
        body,
        out_shape=out,
        in_specs=specs,
        out_specs=outs or jax.tree.map(lambda _: VMEM, out),
        scratch_shapes=scratch,
        name=name,
        compiler_params=pltpu.CompilerParams(vmem_limit_bytes=int(limit * 1024 * 1024)),
    )(*operands)


def shape(dims, dtype=F32):
    return jax.ShapeDtypeStruct(dims, dtype)


def put_low(low, pairs):
    for i in range(0, len(pairs), 2):
        high = pairs[i].astype(BF16)
        low[3 * i // 2] = high
        low[3 * i // 2 + 1] = (pairs[i] - high.astype(F32)).astype(BF16)
        low[3 * i // 2 + 2] = pairs[i + 1].astype(BF16)


def get_low(low, s):
    high, rest, slope = (low[3 * s + i].astype(F32) for i in range(3))
    return high + rest, slope


def enter_kernel(seqs, ids, *refs):
    count = 10
    far, near, sems = refs[:count], refs[count + 5 : 2 * count + 5], refs[-1]
    normed, par, before, ends, low = refs[count : count + 5]
    tok, gain, rate, beta, eta, skip, gain2, qg, kg, rb, nf, tab = refs[count + 5 : -1]
    copies = [pltpu.make_async_copy(a, b, sems.at[i]) for i, (a, b) in enumerate(zip(far, near))]
    for c in copies:
        c.start()
    for c in copies:
        c.wait()
    r = rate[...]
    d = 1.0 - r
    par[0] = d
    par[1] = jnp.log(d)
    par[2] = jnp.sqrt(r * (2.0 - r)) * beta[...]
    par[3] = eta[...]
    for i, row in enumerate((skip, gain2, gain)):
        par[4, i : i + 1, :] = row[...]
    for i, row in enumerate((qg, kg, rb)):
        par[4, 3:4, i * Z : (i + 1) * Z] = row[...]
    for s in range(seqs):
        par[4, 4 + s : 5 + s, :] = jnp.full((1, D), ids[3 + s].astype(F32))
    d2 = d * d
    d4 = d2 * d2
    d8 = d4 * d4
    d15 = d8 * d4 * d2 * d
    q = d8 * d8
    tab[0] = q
    tab[1] = 16.0 * d15
    tab[2] = q * q
    tab[3] = 32.0 * q * d15
    tab[4] = q * q * q * q
    tab[5] = 64.0 * q * q * q * d15
    for s in range(seqs):
        xhat, _ = normalized(tok[s].astype(F32))
        scaled = (xhat * gain[...]).astype(BF16)
        normed[rows_of(s), :] = scaled
        put_rows(nf, rows_of(s), scaled.astype(F32))
    place = lax.broadcasted_iota(jnp.int32, (PIECES, LANES), 0)

    def body(i, carry):
        s = i // BLOCKS
        lane = lanes_of(i)
        xs = [nf[i % BLOCKS, piece_rows(s, t), :] for t in range(PIECE)]
        for j0 in range(0, NDIM, 8):
            ds = [spread(par[0, j0 + j : j0 + j + 1, lane]) for j in range(8)]
            st = [xs[0]] * 8
            ta = [jnp.zeros((PIECES, LANES), F32)] * 8
            for t in range(1, PIECE):
                for j in range(8):
                    ta[j] = ds[j] * ta[j] + st[j]
                    st[j] = ds[j] * st[j] + xs[t]
            for j in range(8):
                a, b = st[j], ta[j]
                for k, step in enumerate((1, 2, 4)):
                    qm = spread(tab[2 * k, j0 + j : j0 + j + 1, lane])
                    rm = spread(tab[2 * k + 1, j0 + j : j0 + j + 1, lane])
                    sa = jnp.where(place >= step, pltpu.roll(a, step, 0), 0.0)
                    sb = jnp.where(place >= step, pltpu.roll(b, step, 0), 0.0)
                    b = b + qm * sb + rm * sa
                    a = a + qm * sa
                before[0, s, j0 + j, :, lane] = jnp.where(place >= 1, pltpu.roll(a, 1, 0), 0.0)
                before[1, s, j0 + j, :, lane] = jnp.where(place >= 1, pltpu.roll(b, 1, 0), 0.0)
                ends[2 * s, j0 + j : j0 + j + 1, lane] = a[PIECES - 1 :]
                ends[2 * s + 1, j0 + j : j0 + j + 1, lane] = b[PIECES - 1 :]
        return carry

    lax.fori_loop(0, seqs * BLOCKS, body, 0)
    ends[2 * seqs] = par[1]
    put_low(low, [ends[i] for i in range(2 * seqs)])


def first_half_kernel(w_value, w_reset, h1, sems):
    vb, cut = w_value.shape[1], D // 2
    at = pl.ds(pl.multiple_of(jnp.bitwise_and(lax.axis_index("seq"), 1) * cut, cut), cut)
    copies = [
        pltpu.make_async_copy(w.at[at, :], h1.at[:, pl.ds(i * vb, vb)], sems.at[i])
        for i, w in enumerate((w_value, w_reset))
    ]
    for c in copies:
        c.start()
    for c in copies:
        c.wait()


def pack_kernel(
    w_value, w_reset, w_hidden, w_update, u_hidden, w_in, w_out, p1, p2, p3, h2, h3, sems
):
    copies = []

    def add(source, target):
        copies.append(pltpu.make_async_copy(source, target, sems.at[len(copies)]))

    vb, cut = w_value.shape[1], D // 2
    upper = jnp.bitwise_and(lax.axis_index("seq"), 1) * cut
    at = pl.ds(pl.multiple_of(upper, cut), cut)
    for i, w in enumerate((w_value, w_reset)):
        add(w, p1.at[:, pl.ds(i * vb, vb)])
    far = jnp.bitwise_and(jnp.right_shift(lax.axis_index("seq"), far_shift()), 1) * cut
    top = 0
    for w in (w_hidden, w_update, u_hidden):
        row = pl.ds(top, w.shape[0])
        add(w.at[:, pl.ds(pl.multiple_of(far, cut), cut)], h2.at[row, :])
        add(w, p2.at[row, :])
        top += w.shape[0]
    add(w_in.at[at, :], h3.at[:, pl.ds(0, vb)])
    add(w_in, p3.at[:, pl.ds(0, vb)])
    for k in range(D // vb):
        row = pl.ds(k * vb, vb)
        add(w_out.at[:, row], p3.at[row, pl.ds(vb, vb)])
        if k < cut // vb:
            lane = pl.ds(pl.multiple_of(upper + k * vb, vb), vb)
            add(w_out.at[:, lane], h3.at[row, pl.ds(vb, vb)])
    for c in copies:
        c.start()
    for c in copies:
        c.wait()


def vectors(par):
    whole = [par.at[4, pl.ds(i, 1), :] for i in range(3)]
    return whole + [par.at[4, pl.ds(3, 1), pl.ds(i * Z, Z)] for i in range(3)]


def piece_powers(par, pw):
    k = lax.broadcasted_iota(jnp.int32, (PIECES, D), 0).astype(F32) * PIECE
    for j in range(NDIM):
        pw[j] = jnp.exp(k * par[1, j : j + 1, :])


def take_weights(refs, tp, first, second):
    top = tp // 2
    near = [refs[r * first : (r + 1) * first] for r in range(top)]
    refs = refs[top * first :]
    far = [refs[r * second : (r + 1) * second] for r in range(top)]
    return near, far, refs[top * second :]


def far_shift():
    return (lax.axis_size("seq").bit_length() - 1) // 2


def gate_copies(tp, ids, near, far, w1, w2, sems):
    top, cut = tp // 2, D // 2
    first = jnp.bitwise_and(ids[1], 1)
    second = jnp.bitwise_and(jnp.right_shift(ids[1], far_shift()), 1)
    copies = [[] for _ in range(tp)]

    def add(r, source, target):
        at = sems.at[sum(len(c) for c in copies)]
        copies[r].append(pltpu.make_async_copy(source, target, at))

    for r in range(top):
        add(r, near[r][0], w1.at[r])
        add(r, near[r][1], w2.at[r])
    for r in range(top):
        mine1, other1, mine2, other2 = far[r]
        for part, at in ((mine1, first), (other1, 1 - first)):
            add(top + r, part, w1.at[top + r, pl.ds(pl.multiple_of(at * cut, cut), cut), :])
        for part, at in ((mine2, second), (other2, 1 - second)):
            add(top + r, part, w2.at[top + r, :, pl.ds(pl.multiple_of(at * cut, cut), cut)])
    for group in copies:
        for c in group:
            c.start()
    return copies


def gate_rows(tp, me, w2, whu):
    nb = D // tp
    for r in range(tp):
        row = pl.ds(pl.multiple_of(jnp.bitwise_xor(me, r) * nb, nb), nb)
        whu[row, pl.ds(0, D)] = w2[r, pl.ds(0, nb), :]
        whu[row, pl.ds(D, D)] = w2[r, pl.ds(nb, nb), :]


def look_kernel(
    seqs, hops, ids, normed, par, before, wsh, *refs
):
    recvs, refs = refs[: len(hops)], refs[len(hops) :]
    st_in, skip_pre, mixed, shared_pre, prob, nf, sm, pw = refs
    skip, _, _, qg, kg, rb = vectors(par)
    place = ids[2]
    put_rows(nf, slice(None), normed[...].astype(F32))
    piece_powers(par, pw)
    logd = par[1]
    dinv = 1.0 / par[0]
    for s in range(seqs):
        a = jnp.zeros((NDIM, D), F32)
        b = jnp.zeros((NDIM, D), F32)
        for (shift, k), got in zip(hops, recvs):
            end = jnp.left_shift(jnp.bitwise_xor(jnp.right_shift(place, shift), k) + 1, shift)
            off = (place - end).astype(F32) * float(CH)
            power = jnp.where(place >= end, jnp.exp(jnp.maximum(off, 0.0) * logd), 0.0)
            oa, ob = (part * power for part in get_low(got, s))
            b = b + ob + off * oa * dinv
            a = a + oa
        st_in[0, s] = a
        st_in[1, s] = b

    def ema(i, carry):
        s = i // BLOCKS
        lane = lanes_of(i)
        row = [pl.ds(j, 1) for j in range(NDIM)]
        ds = [spread(par[0, row[j], lane]) for j in range(NDIM)]
        ws = [spread(par[2, row[j], lane] * par[3, row[j], lane]) for j in range(NDIM)]
        st = [
            before[0, s, j, :, lane] + pw[j, :, lane] * st_in[0, s, row[j], lane]
            for j in range(NDIM)
        ]
        for t in range(PIECE):
            x = nf[i % BLOCKS, piece_rows(s, t), :]
            parts = [None, None]
            for j in range(NDIM):
                st[j] = ds[j] * st[j] + x
                term = ws[j] * st[j]
                parts[j % 2] = term if parts[j % 2] is None else parts[j % 2] + term
            sm[i % BLOCKS, piece_rows(s, t), :] = parts[0] + parts[1]
        return carry

    lax.fori_loop(0, seqs * BLOCKS, ema, 0)
    for s in range(seqs):
        pre = get_rows(sm, rows_of(s)) + skip[...] * get_rows(nf, rows_of(s))
        skip_pre[rows_of(s), :] = pre
        mixed[rows_of(s), :] = silu(pre).astype(BF16)
    sp = mm(mixed[...], wsh[...])
    shared_pre[...] = sp
    shared = silu(sp)
    query = (shared * qg[...]).astype(BF16)
    keys = (shared * kg[...]).astype(BF16)
    t_at = lax.broadcasted_iota(jnp.int32, (CH, CH), 0)
    s_at = lax.broadcasted_iota(jnp.int32, (CH, CH), 1)
    bias_t = jnp.broadcast_to(rb[...], (CH, CH))
    for bit in range(7):
        bias_t = jnp.where(
            jnp.bitwise_and(t_at, 1 << bit) > 0, pltpu.roll(bias_t, 1 << bit, 1), bias_t
        )
    bias = bias_t.T
    for s in range(seqs):
        raw = mm_nt(query[s * CH : (s + 1) * CH], keys[s * CH : (s + 1) * CH]) * Z ** (-0.5)
        live = (place * CH + s_at).astype(F32) < par[4, 4 + s : 5 + s, :CH]
        allowed = (s_at <= t_at) & (live | (s_at == t_at))
        masked = jnp.where(allowed, raw + bias, -1e30)
        top = jnp.max(masked, axis=-1, keepdims=True)
        weights = jnp.where(allowed, jnp.exp(masked - top), 0.0)
        prob[s] = weights / jnp.sum(weights, axis=-1, keepdims=True)


def mix_kernel(seqs, tp, ids, tok, normed, mixed, prob, *refs):
    near, far, refs = take_weights(refs, tp, 2, 4)
    (
        values, value_pre, reset_pre, attended, gated, hidden_pre, update_pre, middle,
        w1, w2, whu, sems,
    ) = refs
    vb = values.shape[2]
    nb = D // tp
    copies = gate_copies(tp, ids, near, far, w1, w2, sems)
    for r in range(tp):
        for c in copies[r]:
            c.wait()
        vp = mm(normed[...], w1[r, :, :vb])
        value_pre[r] = vp
        v = silu(vp).astype(BF16)
        values[r] = v
        rp = mm(mixed[...], w1[r, :, vb:])
        reset_pre[r] = rp
        gate = silu(rp)
        for s in range(seqs):
            att = mm(prob[s].astype(BF16), v[s * CH : (s + 1) * CH])
            attended[r, rows_of(s), :] = att
            gated[r, rows_of(s), :] = (gate[s * CH : (s + 1) * CH] * att).astype(BF16)
        part = mm(gated[r], w2[r, pl.ds(2 * nb, vb), :])
        hidden_pre[...] = hidden_pre[...] + part if r else part
    gate_rows(tp, ids[0], w2, whu)
    hu = mm(mixed[...], whu[...])
    hidden_pre[...] += hu[:, :D]
    update_pre[...] = hu[:, D:]
    for s in range(seqs):
        x = tok[s].astype(F32)
        middle[rows_of(s), :] = x + sigmoid(update_pre[rows_of(s), :]) * (
            silu(hidden_pre[rows_of(s), :]) - x
        )


def ffn_kernel(seqs, tp, ids, tok, cot, middle, hidden_pre, update_pre, par, *refs):
    gain2 = vectors(par)[1]
    near, far, refs = take_weights(refs, tp, 1, 2)
    (
        out, keep, send, grad_hu, resid, grad_gain2,
        w3, n2, lg, acc, gn2, sems,
    ) = refs
    vb = w3.shape[2] // 2
    top, half = tp // 2, D // 2
    cuts = D // vb
    upper = jnp.bitwise_and(ids[1], 1)
    copies = [[] for _ in range(tp)]

    def add(r, source, target):
        at = sems.at[sum(len(c) for c in copies)]
        copies[r].append(pltpu.make_async_copy(source, target, at))

    for r in range(top):
        add(r, near[r][0], w3.at[r])
    for r in range(top):
        for part, at in zip(far[r], (upper, 1 - upper)):
            row = pl.ds(pl.multiple_of(at * half, half), half)
            add(top + r, part, w3.at[top + r, row, :])
    for group in copies:
        for c in group:
            c.start()
    place = ids[2]
    xhat, scale = normalized(middle[...])
    n2[...] = (xhat * gain2[...]).astype(BF16)
    at = (lax.broadcasted_iota(jnp.int32, (CH, D), 0) + place * CH).astype(F32)
    for s in range(seqs):
        lg[rows_of(s), :] = jnp.where(
            at < par[4, 4 + s : 5 + s, :], cot[s].astype(F32), 0.0
        ).astype(BF16)
    acc[...] = jnp.zeros_like(acc)
    gn2[...] = jnp.zeros_like(gn2)
    for h in range(tp // 2):
        for odd in range(2):
            r = 2 * h + odd
            for c in copies[r]:
                c.wait()
            grads = (keep, send)[odd]
            pre = mm(n2[...], w3[r, :, :vb])
            inner = silu(pre).astype(BF16)
            back = None
            for k in range(cuts):
                cols = slice(k * vb, (k + 1) * vb)
                w_out = w3[r, cols, vb:]
                acc[:, cols] += mm(inner, w_out)
                term = mm_nt(lg[:, cols], w_out)
                back = term if back is None else back + term
            gip = (back * silu_slope(pre)).astype(BF16)
            gn2[...] += mm_nt(gip, w3[r, :, :vb])
            grads[h, :, :vb] = mm_tn(n2[...], gip).astype(BF16)
            gwo = mm_tn(inner, lg[...]).astype(BF16)
            for k in range(cuts):
                grads[h, k * vb : (k + 1) * vb, vb:] = gwo[:, k * vb : (k + 1) * vb]
    mid = middle[...]
    out[...] = (mid + acc[...]).astype(BF16)
    grad = gn2[...]
    grad_gain2[...] = jnp.sum(grad * xhat, axis=0, keepdims=True)
    gm = lg[...].astype(F32) + norm_back(grad, xhat, scale, gain2[...])
    for s in range(seqs):
        x = tok[s].astype(F32)
        g = gm[s * CH : (s + 1) * CH]
        hp = hidden_pre[rows_of(s), :]
        update = sigmoid(update_pre[rows_of(s), :])
        grad_hu[rows_of(s), :D] = (g * update * silu_slope(hp)).astype(BF16)
        grad_hu[rows_of(s), D:] = (g * (silu(hp) - x) * update * (1.0 - update)).astype(BF16)
        resid[rows_of(s), :] = g * (1.0 - update)


def gates_kernel(tp, ids, mixed, gated, grad_hu, keep2, send2, ghu):
    nb = D // tp
    vb = gated.shape[2]
    wide = 2 * vb
    me = ids[0]
    ghu[...] = mm_tn(mixed[...], grad_hu[...])

    def block(h, carry):
        for odd in range(2):
            r = 2 * h + odd
            g2 = (keep2, send2)[odd]
            row = pl.ds(pl.multiple_of(jnp.bitwise_xor(me, r) * nb, nb), nb)
            gu = mm_tn(gated[r], grad_hu[:, :D]).astype(BF16)
            for k in range(D // wide):
                top = k * (2 * nb + vb)
                g2[h, pl.ds(top, nb), :] = ghu[row, pl.ds(k * wide, wide)].astype(BF16)
                g2[h, pl.ds(top + nb, nb), :] = ghu[row, pl.ds(D + k * wide, wide)].astype(BF16)
                g2[h, pl.ds(top + 2 * nb, vb), :] = gu[:, k * wide : (k + 1) * wide]
        return carry

    lax.fori_loop(0, tp // 2, block, 0)


def back_kernel(
    seqs, tp,
    ids, normed, mixed, skip_pre, shared_pre, prob, values, value_pre, reset_pre, attended,
    grad_hu, par, wsh, tok, before, st_in, grad_gain2, *refs,
):
    skip, _, _, qg, kg, _ = vectors(par)
    near, far, refs = take_weights(refs, tp, 2, 4)
    (
        keep1, send1, grad_skip, grad_normed, after, ends, sums_keep, sums_send,
        w1, w2, whu, gm, gp, tab, grad_wsh, misc, table, nf, pw, sems,
    ) = refs
    vb = values.shape[2]
    nb = D // tp
    me = ids[0]
    copies = gate_copies(tp, ids, near, far, w1, w2, sems)
    gp[...] = jnp.zeros_like(gp)
    grad_normed[...] = jnp.zeros_like(grad_normed)
    for group in copies:
        for c in group:
            c.wait()
    gate_rows(tp, me, w2, whu)
    gm[...] = mm_nt(grad_hu[...], whu[...])

    def block(h, carry):
        for odd in range(2):
            r = 2 * h + odd
            g1 = (keep1, send1)[odd]
            gg = mm_nt(grad_hu[:, :D], w2[r, pl.ds(2 * nb, vb), :])
            rp = reset_pre[r]
            sig = sigmoid(rp)
            ga = (gg * (rp * sig)).astype(BF16)
            grp = (gg * attended[r] * (sig * (1.0 + rp * (1.0 - sig)))).astype(BF16)
            g1[h, :, vb:] = mm_tn(mixed[...], grp).astype(BF16)
            gm[...] += mm_nt(grp, w1[r, :, vb:])
            gvs = []
            for s in range(seqs):
                part = ga[s * CH : (s + 1) * CH]
                gvs.append(mm_tn(prob[s].astype(BF16), part))
                gp[s] += mm_nt(part, values[r, rows_of(s), :])
            gv = jnp.concatenate(gvs, axis=0) if seqs > 1 else gvs[0]
            gvp = (gv * silu_slope(value_pre[r])).astype(BF16)
            g1[h, :, :vb] = mm_tn(normed[...], gvp).astype(BF16)
            grad_normed[...] += mm_nt(gvp, w1[r, :, :vb])
        return carry

    lax.fori_loop(0, tp // 2, block, 0)
    sp = shared_pre[...]
    shared = silu(sp)
    query = (shared * qg[...]).astype(BF16)
    keys = (shared * kg[...]).astype(BF16)
    total = jnp.zeros((CH, CH), F32)
    gqs = []
    gks = []
    for s in range(seqs):
        pr = prob[s]
        low = (pr * (gp[s] - jnp.sum(pr * gp[s], axis=-1, keepdims=True))).astype(BF16)
        total = total + low.astype(F32)
        gqs.append(mm(low, keys[s * CH : (s + 1) * CH]) * Z ** (-0.5))
        gks.append(mm_tn(low, query[s * CH : (s + 1) * CH]) * Z ** (-0.5))
    gq = jnp.concatenate(gqs, axis=0) if seqs > 1 else gqs[0]
    gk = jnp.concatenate(gks, axis=0) if seqs > 1 else gks[0]
    turned = total.T
    s_at = lax.broadcasted_iota(jnp.int32, (CH, CH), 0)
    for bit in range(7):
        turned = jnp.where(
            jnp.bitwise_and(s_at, 1 << bit) > 0, pltpu.roll(turned, CH - (1 << bit), 1), turned
        )
    misc[...] = jnp.concatenate(
        [
            jnp.sum(gq * shared, axis=0, keepdims=True),
            jnp.sum(gk * shared, axis=0, keepdims=True),
            jnp.sum(turned, axis=0, keepdims=True),
            jnp.zeros((1, D - 3 * Z), F32),
        ],
        axis=1,
    )
    gsp = ((gq * qg[...] + gk * kg[...]) * silu_slope(sp)).astype(BF16)
    grad_wsh[...] = mm_tn(mixed[...], gsp)
    put_rows(
        grad_skip,
        slice(None),
        (gm[...] + mm_nt(gsp, wsh[...])) * silu_slope(skip_pre[...]),
    )
    d = par[0]
    d2 = d * d
    d4 = d2 * d2
    d8 = d4 * d4
    q = d8 * d8
    tab[0] = q
    tab[1] = q * q
    tab[2] = q * q * q * q
    place = lax.broadcasted_iota(jnp.int32, (PIECES, LANES), 0)

    def body(i, carry):
        s = i // BLOCKS
        lane = lanes_of(i)
        ds = [spread(par[0, j : j + 1, lane]) for j in range(NDIM)]
        ad = [grad_skip[i % BLOCKS, piece_rows(s, PIECE - 1), :]] * NDIM
        for t in range(PIECE - 2, -1, -1):
            g = grad_skip[i % BLOCKS, piece_rows(s, t), :]
            for j in range(NDIM):
                ad[j] = ds[j] * ad[j] + g
        for j in range(NDIM):
            a = ad[j]
            for k, step in enumerate((1, 2, 4)):
                qm = spread(tab[k, j : j + 1, lane])
                a = a + qm * jnp.where(place < PIECES - step, pltpu.roll(a, PIECES - step, 0), 0.0)
            after[s, j, :, lane] = jnp.where(
                place < PIECES - 1, pltpu.roll(a, PIECES - 1, 0), 0.0
            )
            ends[s, j : j + 1, lane] = a[:1]
        return carry

    lax.fori_loop(0, seqs * BLOCKS, body, 0)
    small_sums(
        seqs, ids, tok, normed, grad_skip, grad_normed, par, before, st_in, skip, grad_gain2, misc,
        grad_wsh, sums_keep, sums_send, table, nf, pw,
    )
    for s in range(seqs):
        sums_send[pl.ds(sums_keep.shape[0] + s * NDIM, NDIM), :] = ends[s]


def small_sums(
    seqs, ids, tok, normed, grad_skip, grad_normed, par, before, st_in, skip, gain2_row, misc, grad_wsh,
    keep, send, table, nf, pw,
):
    put_rows(nf, slice(None), normed[...].astype(F32))
    piece_powers(par, pw)
    count = D // (D // Z)
    small = table.at[count:, :]
    small[...] = jnp.zeros_like(small)
    for k in range(D // Z):
        table[:count, k * Z : (k + 1) * Z] = grad_wsh[k * count : (k + 1) * count, :]

    def body(i, carry):
        s = i // BLOCKS
        lane = lanes_of(i)
        k16 = lax.broadcasted_iota(jnp.int32, (PIECES, LANES), 0).astype(F32) * PIECE
        for j0 in range(0, NDIM, 8):
            row = [pl.ds(j0 + j, 1) for j in range(8)]
            ds = [spread(par[0, row[j], lane]) for j in range(8)]
            st, ta, q, r = [], [], [], []
            for j in range(8):
                e = pw[j0 + j, :, lane] * st_in[0, s, row[j], lane]
                st.append(before[0, s, j0 + j, :, lane] + e)
                ta.append(
                    before[1, s, j0 + j, :, lane]
                    + pw[j0 + j, :, lane] * st_in[1, s, row[j], lane]
                    + k16 * e / ds[j]
                )
                q.append(jnp.zeros((PIECES, LANES), F32))
                r.append(jnp.zeros((PIECES, LANES), F32))
            for t in range(PIECE):
                x = nf[i % BLOCKS, piece_rows(s, t), :]
                g = grad_skip[i % BLOCKS, piece_rows(s, t), :]
                for j in range(8):
                    ta[j] = ds[j] * ta[j] + st[j]
                    st[j] = ds[j] * st[j] + x
                    q[j] = q[j] + g * st[j]
                    r[j] = r[j] + g * ta[j]
            for j in range(8):
                small[pl.ds(j0 + j, 1), lane] += jnp.sum(q[j], axis=0, keepdims=True)
                small[pl.ds(NDIM + j0 + j, 1), lane] += jnp.sum(r[j], axis=0, keepdims=True)
        return carry

    lax.fori_loop(0, seqs * BLOCKS, body, 0)
    gsk = jnp.zeros((1, D), F32)
    gn1 = jnp.zeros((1, D), F32)
    for s in range(seqs):
        xhat, _ = normalized(tok[s].astype(F32))
        g = get_rows(grad_skip, rows_of(s))
        direct = g * skip[...] + grad_normed[rows_of(s), :]
        gsk = gsk + jnp.sum(g * get_rows(nf, rows_of(s)), axis=0, keepdims=True)
        gn1 = gn1 + jnp.sum(direct * xhat, axis=0, keepdims=True)
    small[2 * NDIM : 2 * NDIM + 1, :] = gsk
    small[2 * NDIM + 1 : 2 * NDIM + 2, :] = gn1
    small[2 * NDIM + 2 : 2 * NDIM + 3, :] = gain2_row[...]
    small[2 * NDIM + 3 : 2 * NDIM + 4, :] = misc[...]
    half = keep.shape[0]
    mine = jnp.bitwise_and(ids[0], 1) * half
    keep[...] = table[pl.ds(pl.multiple_of(mine, 8), half), :]
    send[pl.ds(0, half), :] = table[pl.ds(pl.multiple_of(half - mine, 8), half), :]


def pair_kernel(bit, ids, mine, other, out):
    half = mine.shape[0]
    upper = jnp.where(jnp.bitwise_and(ids[0], bit) > 0, half, 0)
    out[pl.ds(pl.multiple_of(upper, 8), half), :] = mine[...]
    out[pl.ds(pl.multiple_of(half - upper, 8), half), :] = other[...]


def finish_kernel(
    ids, par, rate, beta, mine, other,
    grad_gain, grad_rate, grad_beta, grad_eta, grad_skip, grad_wsh, grad_qg, grad_kg, grad_rb,
    grad_gain2, table,
):
    gain = vectors(par)[2]
    pair_kernel(1, ids, mine, other, table)
    count = D // (D // Z)
    for k in range(D // Z):
        grad_wsh[k * count : (k + 1) * count, :] = table[:count, k * Z : (k + 1) * Z]
    small = table.at[count:, :]
    inflow, eta, r = par[2], par[3], rate[...]
    root = jnp.sqrt(r * (2.0 - r))
    q_sum = small[:NDIM, :]
    grad_inflow = eta * q_sum
    grad_decay = eta * inflow * small[NDIM : 2 * NDIM, :]
    grad_rate[...] = grad_inflow * beta[...] * (1.0 - r) / root - grad_decay
    grad_beta[...] = grad_inflow * root
    grad_eta[...] = inflow * q_sum
    row = [small[2 * NDIM + i : 2 * NDIM + i + 1, :] for i in range(4)]
    grad_skip[...] = row[0]
    grad_gain[...] = row[1] + jnp.sum(inflow * grad_inflow, axis=0, keepdims=True) / gain[...]
    grad_gain2[...] = row[2]
    grad_qg[...] = row[3][:, :Z]
    grad_kg[...] = row[3][:, Z : 2 * Z]
    grad_rb[...] = row[3][:, 2 * Z : 3 * Z]


def leave_kernel(
    seqs, tops, ids, tok, par, grad_skip, grad_normed, behind, resid, *refs
):
    levels = len(tops)
    recvs, refs = refs[:levels], refs[levels:]
    grad_tokens, ad_in, pw, sm = refs
    skip, _, gain = vectors(par)[:3]
    place = ids[2]
    logd = par[1]
    gots = [get_wide(recvs[k], tops[k], seqs * NDIM) for k in range(levels)]
    for s in range(seqs):
        a = jnp.zeros((NDIM, D), F32)
        for k in range(levels):
            low = jnp.bitwise_and(place, 1 << k) == 0
            off = jnp.bitwise_and(place, (1 << k) - 1)
            away = ((1 << k) - 1 - off).astype(F32) * float(CH)
            got = gots[k][s * NDIM : (s + 1) * NDIM]
            a = a + got * jnp.where(low, jnp.exp(away * logd), 0.0)
        ad_in[s] = a
    k = (PIECES - 1 - lax.broadcasted_iota(jnp.int32, (PIECES, D), 0)).astype(F32) * PIECE
    for j in range(NDIM):
        pw[j] = jnp.exp(k * par[1, j : j + 1, :])

    def body(i, carry):
        s = i // BLOCKS
        lane = lanes_of(i)
        row = [pl.ds(j, 1) for j in range(NDIM)]
        ds = [spread(par[0, row[j], lane]) for j in range(NDIM)]
        ws = [spread(par[2, row[j], lane] * par[3, row[j], lane]) for j in range(NDIM)]
        ad = [
            behind[s, j, :, lane] + pw[j, :, lane] * ad_in[s, row[j], lane] for j in range(NDIM)
        ]
        for t in range(PIECE - 1, -1, -1):
            g = grad_skip[i % BLOCKS, piece_rows(s, t), :]
            parts = [None, None]
            for j in range(NDIM):
                ad[j] = ds[j] * ad[j] + g
                term = ws[j] * ad[j]
                parts[j % 2] = term if parts[j % 2] is None else parts[j % 2] + term
            sm[i % BLOCKS, piece_rows(s, t), :] = parts[0] + parts[1]
        return carry

    lax.fori_loop(0, seqs * BLOCKS, body, 0)
    for s in range(seqs):
        xhat, scale = normalized(tok[s].astype(F32))
        grad = (
            get_rows(sm, rows_of(s))
            + get_rows(grad_skip, rows_of(s)) * skip[...]
            + grad_normed[rows_of(s), :]
        )
        grad_tokens[s] = (
            resid[rows_of(s), :] + norm_back(grad, xhat, scale, gain[...])
        ).astype(BF16)


def hop_kernel(seqs, shift, count, ids, state, *refs):
    others, (total, low) = refs[: count - 1], refs[count - 1 :]
    mine = jnp.bitwise_and(jnp.right_shift(ids[2], shift), count - 1)
    logd = state[2 * seqs]
    total[2 * seqs] = logd
    sums = [None] * (2 * seqs)
    for k in range(count):
        after = (count - 1 - jnp.bitwise_xor(mine, k)).astype(F32) * float(CH << shift)
        power = jnp.exp(after * logd)
        slope = after * jnp.exp((after - 1.0) * logd)
        for s in range(seqs):
            part = get_low(others[k - 1], s) if k else (state[2 * s], state[2 * s + 1])
            a, b = power * part[0], power * part[1] + slope * part[0]
            sums[2 * s : 2 * s + 2] = [sums[2 * s] + a, sums[2 * s + 1] + b] if k else [a, b]
    for i in range(2 * seqs):
        total[i] = sums[i]
    put_low(low, sums)


def put_wide(ref, top, value):
    wide = ref.shape[1]
    count = value.shape[0]
    for k in range(D // wide):
        ref[pl.ds(top + k * count, count), :] = value[:, k * wide : (k + 1) * wide].astype(ref.dtype)


def get_wide(ref, top, count):
    wide = ref.shape[1]
    runs = [ref[pl.ds(top + k * count, count), :].astype(F32) for k in range(D // wide)]
    return jnp.concatenate(runs, axis=1) if len(runs) > 1 else runs[0]


def first_back_hop(seqs, joins, ids, par, own, sums, got, out, keep, payload):
    rows = seqs * NDIM
    fold_lanes = D // payload.shape[1]
    if joins:
        join_adjoint(seqs, 0, ids, par, own, got[pl.ds(sums.shape[0], rows), :], out)
    else:
        out[...] = own[...]
    put_wide(payload, 0, out[...])
    half = keep.shape[0]
    upper = jnp.where(jnp.bitwise_and(ids[0], 2) > 0, half, 0)
    mine = pl.ds(pl.multiple_of(upper, 8), half)
    theirs = pl.ds(pl.multiple_of(half - upper, 8), half)
    keep[...] = sums[mine, :] + got[mine, :]
    put_wide(payload, rows * fold_lanes, sums[theirs, :] + got[theirs, :])


def join_adjoint(seqs, level, ids, par, own, got, out):
    upper = jnp.bitwise_and(ids[2], 1 << level) > 0
    power = jnp.exp(float(CH << level) * par[1])
    for s in range(seqs):
        row = slice(s * NDIM, (s + 1) * NDIM)
        early = jnp.where(upper, got[row], own[row, :])
        late = jnp.where(upper, own[row, :], got[row])
        out[row, :] = early + power * late


def chain_hop(seqs, level, split, halved, top, ids, par, own, kept, sent, other, out, keep, payload, base):
    rows = seqs * NDIM
    lanes = D // other.shape[1]
    small_base = 0 if payload is None else base + rows * (D // payload.shape[1])
    if out is not None:
        join_adjoint(seqs, level, ids, par, own, get_wide(other, top, rows), out)
        put_wide(payload, base, out[...])
    half = keep.shape[0]
    if split:
        upper = jnp.bitwise_and(ids[0], split) > 0
        got = get_wide(other, top + rows * lanes, 2 * half)
        first, second = kept[:half, :] + got[:half], kept[half:, :] + got[half:]
        keep[...] = jnp.where(upper, second, first)
        put_wide(payload, small_base, jnp.where(upper, first, second))
    else:
        mine = kept[...] if halved else get_wide(sent, top + rows * lanes, half)
        total = mine + get_wide(other, top + rows * lanes, half)
        keep[...] = total
        if payload is not None:
            put_wide(payload, small_base, total)


def back_hop(seqs, level, split, halved, ids, par, own, kept, sent, other, out, keep, payload):
    chain_hop(
        seqs, level, split, halved, 0, ids, par, own, kept, sent, other, out, keep, payload, 0
    )


def split_rows(count, cut, place, k):
    shift, bits = cut
    rows = count >> bits
    sub = jnp.bitwise_and(jnp.right_shift(place, shift), (1 << bits) - 1)
    return pl.multiple_of(jnp.bitwise_xor(sub, k) * rows, rows), rows


def add_rows(parts, start, high, out, top, lane, width, at):
    step = min(64, high)

    def body(i, carry):
        row = pl.ds(pl.multiple_of(start + i * step, step), step)
        total = parts[0][row, lane : lane + width].astype(F32)
        for other in parts[1:]:
            total = total + other[row, lane : lane + width].astype(F32)
        out[pl.ds(pl.multiple_of(top + i * step, 16), step), at : at + width] = total.astype(BF16)
        return carry

    lax.fori_loop(0, high // step, body, 0)


def fold_kernel(jobs, inputs, ids, *refs):
    parts, outs = refs[:inputs], refs[inputs:]
    at = 0
    for count, lane, width, cut, targets in jobs:
        own = parts[at : at + count]
        at += count
        blocks, rows, _ = own[0].shape
        for k, (target, block, offset) in enumerate(targets):
            if cut == "tp":
                ranges, start, high = (k,), 0, rows
            elif cut is None:
                ranges, start, high = range(blocks), 0, rows
            else:
                start, high = split_rows(rows, cut, ids[1], k)
                ranges = range(blocks)
            for to, b in enumerate(ranges):
                add_rows(
                    [p.at[b] for p in own], start, high, outs[target].at[block + to], 0, lane,
                    width, offset,
                )


def fold(ids, shapes, jobs):
    arrays = [a for job in jobs for a in job[0]]
    plan = [(len(job[0]),) + tuple(job[1:]) for job in jobs]
    return call(
        functools.partial(fold_kernel, plan, len(arrays)),
        tuple(shape(dims, BF16) for dims in shapes),
        [],
        (ids, *arrays),
        [SMEM] + [VMEM] * len(arrays),
        "fold",
    )


def join_kernel(cut, ids, mine, other, out):
    blocks, rows, _ = mine.shape
    for k, part in enumerate((mine, other)):
        start, _ = split_rows(2 * rows, cut, ids[1], k)
        for b in range(blocks):
            out[b, pl.ds(pl.multiple_of(start, 16), rows), :] = part[b]


def join(ids, mine, other, cut):
    blocks, rows, lanes = mine.shape
    return call(
        functools.partial(join_kernel, cut),
        (shape((blocks, 2 * rows, lanes), BF16),),
        [],
        (ids, mine, other),
        [SMEM, VMEM, VMEM],
        "join",
    )[0]


def start_kernel(
    seqs, bits, ids, par, own, sums, got, keep1, got1, out, keep, left, payload, right, send
):
    vb = keep1.shape[2] // 2
    for b, target in enumerate((left, payload)):
        add_rows([keep1.at[b], got1.at[b]], 0, D, target, 0, 0, vb, 0)
    for k, target in enumerate((right, send)):
        start, high = split_rows(D, (0, bits), ids[1], k)
        for b in range(2):
            add_rows([keep1.at[b], got1.at[b]], start, high, target.at[b], 0, vb, vb, 0)
    rows, half = seqs * NDIM, keep.shape[0]
    join_adjoint(seqs, 0, ids, par, own, got[pl.ds(2 * half, rows), :], out)
    put_wide(payload, D, out[...])
    upper = jnp.where(jnp.bitwise_and(ids[0], 2) > 0, half, 0)
    mine = pl.ds(pl.multiple_of(upper, 8), half)
    theirs = pl.ds(pl.multiple_of(half - upper, 8), half)
    keep[...] = sums[mine, :] + got[mine, :]
    put_wide(payload, D + rows * (D // vb), sums[theirs, :] + got[theirs, :])


def cross_kernel(
    seqs, bits, ids, par, own, kept, sent, other, left, right, got, out, keep, left_out, payload,
    right_out, send,
):
    vb = left.shape[1]
    for k, target in enumerate((left_out, payload)):
        start, high = split_rows(D, (0, bits), ids[1], k)
        add_rows([left, other], start, high, target, 0, 0, vb, 0)
    for b, target in enumerate((right_out, send)):
        add_rows([right.at[b], got.at[b]], 0, high, target, 0, 0, vb, 0)
    chain_hop(
        seqs, 1, 0, True, D, ids, par, own, kept, sent, other, out, keep, payload, high
    )


def ride_kernel(
    seqs, level, split, halved, top, jobs, cut, high, last, ids, par, own, kept, sent, other, *refs
):
    count = 1 + max(p for job in jobs for p in job[0])
    parts, refs = refs[:count], refs[count:]
    out = payload = None
    if last:
        keep, kept_out = refs
        halves = ((0, keep),)
    elif cut is None:
        kept_out, out, payload = refs
        halves = ((0, payload),)
    else:
        keep, kept_out, out, payload = refs
        halves = ((0, keep), (1, payload))
    for picks, width, at in jobs:
        chosen = [other if p == -1 else sent if p == -2 else parts[p] for p in picks]
        for k, target in halves:
            start = 0 if cut is None else split_rows(2 * high, cut, ids[1], k)[0]
            add_rows(chosen, start, high, target, 0, 0, width, at)
    chain_hop(
        seqs, level, split, halved, top, ids, par, own, kept, sent, other, out, kept_out, payload,
        high,
    )


def unpack_first(cut, ids, *refs):
    count = 1 << cut[1]
    pieces, refs = refs[:count], refs[count:]
    w_in, w_out = refs[:2]
    outs = refs[2:]
    vb = w_in.shape[1]
    wide = 2 * vb
    each = sum(out.shape[0] for out in outs)
    for k in range(count):
        row, rows = split_rows(D, cut, ids[1], k)
        w_in[pl.ds(row, rows), :] = pieces[k][0, :, :vb].astype(F32)
        for first in range(0, rows, vb):
            w_out[:, pl.ds(pl.multiple_of(row + first, vb), vb)] = pieces[k][
                0, first : first + vb, vb:
            ].astype(F32)
        for b in range(count):

            @pl.when(row == b * rows)
            def _(k=k, b=b, rows=rows):
                for run in range(D // wide):
                    start = run * each
                    for out in outs:
                        end = start + out.shape[0]
                        lo, hi = max(start, b * rows), min(end, (b + 1) * rows)
                        if lo < hi:
                            out[lo - start : hi - start, run * wide : (run + 1) * wide] = pieces[k][
                                1, lo - b * rows : hi - b * rows, :
                            ].astype(F32)
                        start = end


def unpack_sides(cut, ids, *refs):
    count = 1 << cut[1]
    pieces, (left, right) = refs[:count], refs[count:]
    vb = left.shape[1]
    for k in range(count):
        row, rows = split_rows(D, cut, ids[1], k)
        left[pl.ds(row, rows), :] = pieces[k][0, :, :vb].astype(F32)
        right[pl.ds(row, rows), :] = pieces[k][0, :, vb:].astype(F32)


def unpack(body, cut, ids, pieces, dims):
    return call(
        functools.partial(body, cut),
        tuple(shape(d) for d in dims),
        [],
        (ids, *pieces),
        [SMEM] + [VMEM] * len(pieces),
        "unpack",
    )


BOTH = ("seq", "tp")


def swap(value, mask):
    count = lax.axis_size("seq") * lax.axis_size("tp")
    return lax.ppermute(value, BOTH, [(i, i ^ mask) for i in range(count)])


def after(value, *others):
    return lax.optimization_barrier((value, *others))[0]


def bits_of(count):
    return [1 << k for k in range(count.bit_length() - 1)]


def has(index, bit):
    return jnp.bitwise_and(index, bit) > 0


def half_of(value, upper):
    half = value.shape[0] // 2
    return lax.dynamic_slice_in_dim(value, jnp.where(upper, half, 0), half, 0)


def joined(mine, other, upper):
    return jnp.where(
        upper,
        jnp.concatenate([other, mine], axis=0),
        jnp.concatenate([mine, other], axis=0),
    )


def spread_out(own, tp):
    pieces = {0: own}
    for bit in reversed(bits_of(tp // 2)):
        for r in list(pieces):
            pieces[r ^ bit] = [swap(a, bit) for a in pieces[r]]
    return [pieces[r] for r in range(tp // 2)]


def per_device(
    tokens,
    cotangent,
    valid_lengths,
    norm1_gain,
    ema_rate,
    ema_beta,
    ema_eta,
    ema_skip,
    w_shared,
    query_gain,
    key_gain,
    rel_bias,
    w_value,
    w_reset,
    w_update,
    w_hidden,
    u_hidden,
    norm2_gain,
    w_in,
    w_out,
):
    part = lax.axis_index("tp")
    tp = lax.axis_size("tp")
    seq = lax.axis_size("seq")
    all_seqs, local_rows, _ = tokens.shape
    vb = w_value.shape[1]
    nb = D // tp
    ybits = far_shift()
    traded = local_rows < CH
    lower = part % 2 == 0

    def trade(value):
        if not traded:
            return value
        other = swap(jnp.where(lower, value[1], value[0]), 1)
        mine = jnp.where(lower, value[0], value[1])
        return joined(mine, other, ~lower)[None]

    def trade_back(value):
        if not traded:
            return value
        first, second = value[0, :local_rows], value[0, local_rows:]
        other = swap(jnp.where(lower, second, first), 1)
        mine = jnp.where(lower, first, second)
        return jnp.where(lower, jnp.stack([mine, other]), jnp.stack([other, mine]))

    if traded:
        assert all_seqs == 2 and 2 * local_rows == CH
        seqs = 1
    else:
        assert local_rows == CH
        seqs = all_seqs
    rows = seqs * CH
    ids, ids_lengths = Here(seqs, None), Here(seqs, valid_lengths.astype(jnp.int32))
    masks = bits_of(tp * seq)[int(traded) :]
    levels = len(masks)

    tok = trade(tokens)
    cot = trade(cotangent)
    gain1 = norm1_gain[None]
    gain2 = norm2_gain[None]
    skip = ema_skip[None]
    rate, beta = ema_rate.T, ema_beta.T
    qg, kg, rb = query_gain[None], key_gain[None], rel_bias[None]

    top = tp // 2
    weights = (w_value, w_reset, w_hidden, w_update, u_hidden, w_in, w_out)
    rows2 = 2 * nb + vb
    normed, par, before, ends, low = call(
        functools.partial(enter_kernel, seqs),
        (
            shape((rows, D), BF16),
            shape((5, NDIM, D)),
            shape((2, seqs, NDIM, PIECES, D)),
            shape((2 * seqs + 1, NDIM, D)),
            shape((3 * seqs, NDIM, D), BF16),
        ),
        [
            pltpu.VMEM((seqs, CH, D), BF16),
            pltpu.VMEM((1, D), F32),
            pltpu.VMEM((NDIM, D), F32),
            pltpu.VMEM((NDIM, D), F32),
            pltpu.VMEM((NDIM, D), F32),
            pltpu.VMEM((1, D), F32),
            pltpu.VMEM((1, D), F32),
            pltpu.VMEM((1, Z), F32),
            pltpu.VMEM((1, Z), F32),
            pltpu.VMEM((1, Z), F32),
            pltpu.VMEM((BLOCKS, rows, LANES), F32),
            pltpu.VMEM((6, NDIM, D), F32),
            pltpu.SemaphoreType.DMA((10,)),
        ],
        (ids_lengths, tok, gain1, rate, beta, ema_eta.T, skip, gain2, qg, kg, rb),
        [SMEM] + [ANY] * 10,
        "enter",
        limit=12,
    )
    start = 1 - int(traded)
    groups = [(0, 1)] * start + [(start, 2)] + [(i, 1) for i in range(start + 2, levels)]
    hops = []
    (half1,) = call(
        first_half_kernel,
        (shape((D // 2, 2 * vb), BF16),),
        [pltpu.SemaphoreType.DMA((2,))],
        (w_value, w_reset),
        [ANY] * 2,
        "half",
        limit=60,
        outs=(pl.BlockSpec(),),
    )
    mine1 = swap(half1, top)
    state = ends
    for i, (shift, bits) in enumerate(groups):
        if i == start:
            low = after(low, mine1)
            pack1, pack2, pack3, half2, half3 = call(
                pack_kernel,
                (
                    shape((D, 2 * vb), BF16),
                    shape((rows2, D), BF16),
                    shape((D, 2 * vb), BF16),
                    shape((rows2, D // 2), BF16),
                    shape((D // 2, 2 * vb), BF16),
                ),
                [pltpu.SemaphoreType.DMA((10 + 3 * D // vb // 2,))],
                lax.optimization_barrier((*weights, low))[:-1],
                [ANY] * 7,
                "pack",
                limit=60,
                outs=(pl.BlockSpec(),) * 5,
            )
        if i == start + 1:
            mine2 = swap(after(half2, low), top)
            other1 = swap(after(mine1, low), tp)
            near_gates = spread_out([after(pack1, low), after(pack2, low)], tp)
        if i == start + 2:
            low = after(low, mine2, other1, *near_gates[-1])
            mine3 = swap(after(half3, low), top)
            other2 = swap(after(mine2, low), tp << ybits)
            near_feeds = spread_out([after(pack3, low)], tp)
        got = []
        for k in range(1, 1 << bits):
            got.append(swap(low, k << (shift + int(traded))))
            hops.append((shift, k, got[-1]))
        if i + 1 < len(groups):
            state, low = call(
                functools.partial(hop_kernel, seqs, shift, 1 << bits),
                (shape((2 * seqs + 1, NDIM, D)), shape((3 * seqs, NDIM, D), BF16)),
                [],
                (ids, state, *got),
                [SMEM] + [VMEM] * (1 + len(got)),
                "hop",
            )
    st_in, skip_pre, mixed, shared_pre, prob = call(
        functools.partial(look_kernel, seqs, [h[:2] for h in hops]),
        (
            shape((2, seqs, NDIM, D)),
            shape((rows, D)),
            shape((rows, D), BF16),
            shape((rows, Z)),
            shape((seqs, CH, CH)),
        ),
        [
            pltpu.VMEM((BLOCKS, rows, LANES), F32),
            pltpu.VMEM((BLOCKS, rows, LANES), F32),
            pltpu.VMEM((NDIM, PIECES, D), F32),
        ],
        (
            ids, after(normed, mine3), par, before, w_shared,
            *[h[2] for h in hops],
        ),
        [SMEM] + [VMEM] * (4 + len(hops)),
        "look",
        limit=10,
    )
    far_gates = spread_out([mine1, after(other1, prob), mine2, after(other2, prob)], tp)
    other3 = swap(mine3, tp)
    gates = [w for group in near_gates + far_gates for w in group]

    values, value_pre, reset_pre, attended, gated, hidden_pre, update_pre, middle = call(
        functools.partial(mix_kernel, seqs, tp),
        (
            shape((tp, rows, vb), BF16),
            shape((tp, rows, vb)),
            shape((tp, rows, vb)),
            shape((tp, rows, vb)),
            shape((tp, rows, vb), BF16),
            shape((rows, D)),
            shape((rows, D)),
            shape((rows, D)),
        ),
        [
            pltpu.VMEM((tp, D, 2 * vb), BF16),
            pltpu.VMEM((tp, rows2, D), BF16),
            pltpu.VMEM((D, 2 * D), BF16),
            pltpu.SemaphoreType.DMA((3 * tp,)),
        ],
        (ids, tok, normed, after(mixed, other3), prob, *gates),
        [SMEM] + [VMEM] * 4 + [ANY] * len(gates),
        "mix",
        limit=10,
    )

    far_feeds = spread_out([mine3, other3], tp)
    feeds = [w for group in near_feeds + far_feeds for w in group]
    out, keep3, send3, grad_hu, resid, grad_gain2 = call(
        functools.partial(ffn_kernel, seqs, tp),
        (
            shape((rows, D), BF16),
            shape((tp // 2, D, 2 * vb), BF16),
            shape((tp // 2, D, 2 * vb), BF16),
            shape((rows, 2 * D), BF16),
            shape((rows, D)),
            shape((1, D)),
        ),
        [
            pltpu.VMEM((tp, D, 2 * vb), BF16),
            pltpu.VMEM((rows, D), BF16),
            pltpu.VMEM((rows, D), BF16),
            pltpu.VMEM((rows, D), F32),
            pltpu.VMEM((rows, D), F32),
            pltpu.SemaphoreType.DMA((3 * tp // 2,)),
        ],
        (ids, tok, cot, middle, hidden_pre, update_pre, par, *feeds),
        [SMEM] + [VMEM] * 6 + [ANY] * len(feeds),
        "ffn",
        limit=10,
    )

    half = tp // 2
    yn = 1 << ybits
    wide = 2 * vb
    runs = D // wide
    cut_of_y = (0, ybits)
    zcuts = [(shift, 1) for shift in range(ybits, seq.bit_length() - 1)]

    def over_tp(pieces):
        return [pieces[0]] + [swap(p, 2 * k) for k, p in enumerate(pieces) if k]

    def over_y(pieces):
        return [pieces[0]] + [swap(p, tp * k) for k, p in enumerate(pieces) if k]

    def over_z(value, cut):
        return swap(value, tp << cut[0])

    def cut_tp(parts, dims):
        n = dims[0]
        return fold(
            ids,
            [(1,) + dims[1:]] * n,
            [(parts, 0, dims[2], "tp", [(k, 0, 0) for k in range(n)])],
        )

    def cut_y(parts, dims):
        return fold(
            ids,
            [(dims[0], dims[1] // yn, dims[2])] * yn,
            [(parts, 0, dims[2], cut_of_y, [(k, 0, 0) for k in range(yn)])],
        )

    last = [None]

    def now(value):
        return value if last[0] is None else after(value, last[0])

    chunk = (half, D, wide)
    got3 = swap(send3, 1)
    keep2, send2 = call(
        functools.partial(gates_kernel, tp),
        (shape(chunk, BF16), shape(chunk, BF16)),
        [pltpu.VMEM((D, 2 * D), F32)],
        (ids, mixed, gated, grad_hu),
        [SMEM] + [VMEM] * 3,
        "gates",
        limit=10,
    )
    got2 = swap(send2, 1)
    g3 = cut_tp([keep3, got3], chunk)
    g3 = over_tp(g3)
    g2 = cut_y([keep2, after(got2, g3[0])], chunk)
    g2 = over_y(g2)

    count = Z + SMALL_ROWS
    count += -count % (16 * tp)
    (
        keep1, send1, grad_skip, grad_normed, behind, back_ends, sums_keep, sums_send,
    ) = call(
        functools.partial(back_kernel, seqs, tp),
        (
            shape(chunk, BF16),
            shape(chunk, BF16),
            shape((BLOCKS, rows, LANES)),
            shape((rows, D)),
            shape((seqs, NDIM, PIECES, D)),
            shape((seqs, NDIM, D)),
            shape((count // 2, D)),
            shape((count // 2 + seqs * NDIM, D)),
        ),
        [
            pltpu.VMEM((tp, D, 2 * vb), BF16),
            pltpu.VMEM((tp, rows2, D), BF16),
            pltpu.VMEM((D, 2 * D), BF16),
            pltpu.VMEM((rows, D), F32),
            pltpu.VMEM((seqs, CH, CH), F32),
            pltpu.VMEM((3, NDIM, D), F32),
            pltpu.VMEM((D, Z), F32),
            pltpu.VMEM((1, D), F32),
            pltpu.VMEM((count, D), F32),
            pltpu.VMEM((BLOCKS, rows, LANES), F32),
            pltpu.VMEM((NDIM, PIECES, D), F32),
            pltpu.SemaphoreType.DMA((3 * tp,)),
        ],
        (
            ids, normed, mixed, skip_pre, shared_pre, prob, values, value_pre, reset_pre, attended,
            after(grad_hu, g2[0]), par, w_shared, tok, before, st_in, grad_gain2,
            *gates,
        ),
        [SMEM] + [VMEM] * 16 + [ANY] * len(gates),
        "back",
        limit=12,
    )

    g3 = cut_y([after(g3[0], send1)] + g3[1:], (1, D, wide))
    g2 = cut_tp([after(g2[0], g3[0])] + g2[1:], (half, D // yn, wide))
    (
        keep1, send1, grad_skip, grad_normed, behind, back_ends, sums_keep, sums_send, _,
    ) = lax.optimization_barrier(
        (keep1, send1, grad_skip, grad_normed, behind, back_ends, sums_keep, sums_send, g2[0])
    )
    adjoint = back_ends.reshape(seqs * NDIM, D)
    last[0] = g2[0]
    g3 = over_y(g3)
    g2 = over_tp(g2)
    got1 = swap(send1, 1)
    got_sums = swap(sums_send, 1)
    done = {}

    def first_chunks():
        high = D // yn
        for i, cut in enumerate(zcuts[:-1] + [None]):
            high = high // 2 if cut else high
            pieces = 2 if cut else 1
            if i:
                jobs = [([now(keep), other], 0, wide, cut, [(k, 0, 0) for k in range(pieces)])]
            else:
                jobs = [
                    ([now(g3[0])] + g3[1:], 0, wide, cut, [(k, 0, 0) for k in range(pieces)]),
                    (g2, 0, wide, cut, [(k, 1, 0) for k in range(pieces)]),
                ]
            keep, *send = fold(ids, [(2, high, wide)] * pieces, jobs)
            other = over_z(*send, cut) if cut else over_z(keep, zcuts[-1])
            yield keep
        (total,) = fold(ids, [keep.shape], [([now(keep), other], 0, wide, None, [(0, 0, 0)])])
        for cut in reversed(zcuts[:-1]):
            other = over_z(total, cut)
            yield total
            total = join(ids, now(total), other, cut)
        pieces = over_y([total] * yn)
        yield total
        done["first"] = unpack(
            unpack_first,
            cut_of_y,
            ids,
            [now(pieces[0])] + pieces[1:],
            [(D, vb), (vb, D), (nb, D), (nb, D), (vb, D)],
        )
        yield done["first"][0]

    def second_chunk():
        small_high = count // 4
        ad_rows = seqs * NDIM

        def payload_rows():
            return (ad_rows + small_high) * runs

        together = half == 2 and yn == 2 and not traded
        if together:
            lanes = D // vb
            own, kept, left, payload, right, send = call(
                functools.partial(start_kernel, seqs, ybits),
                (
                    shape((ad_rows, D)),
                    shape((small_high, D)),
                    shape((D, vb), BF16),
                    shape((D + (ad_rows + small_high) * lanes, vb), BF16),
                    shape((2, D // 2, vb), BF16),
                    shape((2, D // 2, vb), BF16),
                ),
                [],
                (ids, par, now(adjoint), sums_keep, got_sums, keep1, got1),
                [SMEM] + [VMEM] * 6,
                "start",
            )
            other, got_right = swap(payload, 2), swap(send, tp)
            got = [(got_sums, count // 2), (other, D)]
            yield payload
            own, kept, left, payload, right, send = call(
                functools.partial(cross_kernel, seqs, ybits),
                (
                    shape((ad_rows, D)),
                    shape((small_high, D)),
                    shape((D // 2, vb), BF16),
                    shape((D // 2 + (ad_rows + small_high) * lanes, vb), BF16),
                    shape((D // 2, vb), BF16),
                    shape((D // 2, vb), BF16),
                ),
                [],
                (ids, par, now(own), kept, payload, other, left, right, got_right),
                [SMEM] + [VMEM] * 8,
                "cross",
            )
            other, got_right = swap(payload, tp), swap(send, 2)
            level, top, halved = 2, D // 2, False
            flat = [left, right, got_right]
            jobs = [((0, -1), vb, 0), ((1, 2), vb, vb)]
            yield payload
        else:
            own, kept, payload = call(
                functools.partial(first_back_hop, seqs, not traded),
                (
                    shape((ad_rows, D)),
                    shape((small_high, D)),
                    shape((payload_rows(), wide), BF16),
                ),
                [],
                (ids, par, now(adjoint), sums_keep, got_sums),
                [SMEM] + [VMEM] * 4,
                "hop",
            )
            got = [] if traded else [(got_sums, count // 2)]
            level = int(not traded)
            halved = True
            other = swap(payload, masks[level])
            yield payload
            parts = fold(
                ids,
                [(1, D, vb)] * half + [(half, D // yn, vb)] * yn,
                [
                    ([now(keep1), got1], 0, vb, "tp", [(k, 0, 0) for k in range(half)]),
                    ([keep1, got1], vb, vb, cut_of_y, [(half + k, 0, 0) for k in range(yn)]),
                ],
            )
            left, right = over_tp(parts[:half]), over_y(parts[half:])
            yield parts[0]
            crossed = False
            while level + 1 < levels - len(zcuts):
                got.append((other, 0))
                split = 2 * masks[level] if 2 * masks[level] < tp else 0
                small_high = small_high // 2 if split else small_high
                own, kept, payload = call(
                    functools.partial(back_hop, seqs, level, split, halved),
                    (
                        shape((ad_rows, D)),
                        shape((small_high, D)),
                        shape((payload_rows(), wide), BF16),
                    ),
                    [],
                    (ids, par, now(own), kept, payload, other),
                    [SMEM] + [VMEM] * 5,
                    "hop",
                )
                halved = bool(split)
                level += 1
                other = swap(payload, masks[level])
                yield payload
                if crossed:
                    continue
                crossed = True
                parts = fold(
                    ids,
                    [(1, D // yn, vb)] * (yn + half),
                    [
                        ([now(left[0])] + left[1:], 0, vb, cut_of_y, [(k, 0, 0) for k in range(yn)]),
                        (right, 0, vb, "tp", [(yn + k, 0, 0) for k in range(half)]),
                    ],
                )
                left, right = over_y(parts[:yn]), over_tp(parts[yn:])
                yield parts[0]
            top = 0
            flat = [p.reshape(p.shape[1:]) for p in left + right]
            jobs = [
                (tuple(range(len(left))), vb, 0),
                (tuple(range(len(left), len(flat))), vb, vb),
            ]
        high = D // yn
        for cut in zcuts[:-1] + [None]:
            got.append((other, top))
            high = high // 2 if cut else high
            kept_chunk = [shape((high, wide), BF16)] if cut else []
            *flat, kept, own, payload = call(
                functools.partial(
                    ride_kernel, seqs, level, 0, halved, top, jobs, cut, high, False
                ),
                (
                    *kept_chunk,
                    shape((small_high, D)),
                    shape((ad_rows, D)),
                    shape((high + payload_rows(), wide), BF16),
                ),
                [],
                (ids, par, now(own), kept, payload, other, *flat),
                [SMEM] + [VMEM] * (5 + len(flat)),
                "ride",
            )
            halved = False
            level += 1
            top = high
            jobs = [((0 if cut else -2, -1), wide, 0)]
            other = swap(payload, masks[level])
            yield payload
        got.append((other, top))
        total, kept = call(
            functools.partial(ride_kernel, seqs, level, 0, False, top, jobs, None, high, True),
            (shape((high, wide), BF16), shape((small_high, D))),
            [],
            (ids, par, now(own), kept, payload, other, *flat),
            [SMEM] + [VMEM] * (5 + len(flat)),
            "ride",
        )
        bits = list(reversed(bits_of(tp)))
        total = total[None]
        far = swap(kept, bits[0])
        other = over_z(total, zcuts[-2]) if len(zcuts) > 1 else None
        yield total
        (done["tokens"],) = call(
            functools.partial(leave_kernel, seqs, [at for _, at in got]),
            (shape((seqs, CH, D), BF16),),
            [
                pltpu.VMEM((seqs, NDIM, D), F32),
                pltpu.VMEM((NDIM, PIECES, D), F32),
                pltpu.VMEM((BLOCKS, rows, LANES), F32),
            ],
            (
                ids, tok, par, now(grad_skip), grad_normed, behind, resid,
                *[g for g, _ in got],
            ),
            [SMEM] + [VMEM] * (6 + levels),
            "leave",
            limit=10,
        )
        yield done["tokens"]
        for i in range(len(zcuts) - 2, -1, -1):
            total = join(ids, now(total), other, zcuts[i])
            if i:
                other = over_z(total, zcuts[i - 1])
                yield total
        pieces = over_y([total] * yn)
        yield total
        for i in range(len(bits) - 1):
            (kept,) = call(
                functools.partial(pair_kernel, bits[i]),
                (shape((2 * kept.shape[0], D)),),
                [],
                (ids, now(kept), far),
                [SMEM, VMEM, VMEM],
                "pair",
            )
            far = swap(kept, bits[i + 1])
            yield kept
        done["small"] = call(
            finish_kernel,
            (
                shape((1, D)),
                shape((NDIM, D)),
                shape((NDIM, D)),
                shape((NDIM, D)),
                shape((1, D)),
                shape((D, Z)),
                shape((1, Z)),
                shape((1, Z)),
                shape((1, Z)),
                shape((1, D)),
            ),
            [pltpu.VMEM((count, D), F32)],
            (ids, par, rate, beta, now(kept), far),
            [SMEM] + [VMEM] * 5,
            "finish",
        )
        yield done["small"][0]
        done["second"] = unpack(
            unpack_sides, cut_of_y, ids, [now(pieces[0])] + pieces[1:], [(D, vb), (D, vb)]
        )
        yield done["second"][0]

    walks = {"f": first_chunks(), "s": second_chunk()}
    order = "sfsfssffssssfss"

    def advance(name):
        try:
            last[0] = next(walks[name])
        except StopIteration:
            del walks[name]

    for name in order:
        if name in walks:
            advance(name)
    while walks:
        for name in list(walks):
            advance(name)

    grad_w_in, grad_w_out, grad_w_hidden, grad_w_update, grad_u_hidden = done["first"]
    grad_w_value, grad_w_reset = done["second"]
    firsts = [
        small.T if small.shape[0] == NDIM else small[0] if small.shape[0] == 1 else small
        for small in done["small"]
    ]
    grad_norm2_gain = firsts.pop()
    return (
        trade_back(out.reshape(seqs, CH, D)),
        trade_back(done["tokens"]),
        *firsts,
        grad_w_value,
        grad_w_reset,
        grad_w_update,
        grad_w_hidden,
        grad_u_hidden,
        grad_norm2_gain,
        grad_w_in,
        grad_w_out,
    )


def solution(mesh):
    rows = P(None, ("seq", "tp"), None)
    cols = P(None, "tp")
    tall = P("tp", None)
    whole = P()
    return jax.shard_map(
        per_device,
        mesh=mesh,
        in_specs=(rows, rows) + (whole,) * 10 + (cols, cols, tall, tall, tall, whole, cols, tall),
        out_specs=(rows, rows) + (whole,) * 9 + (cols, cols, tall, tall, tall, whole, cols, tall),
        check_vma=False,
    )
```

```python
import functools

import jax
import jax.numpy as jnp
from jax import lax
from jax.experimental import pallas as pl
from jax.experimental.pallas import tpu as pltpu
from jax.sharding import PartitionSpec as P

D = 512
Z = 128
NDIM = 16
CH = 128
PIECE = 16
PIECES = CH // PIECE
LANES = 128
BLOCKS = D // LANES
EPS = 1e-05
F32 = jnp.float32
BF16 = jnp.bfloat16
SMALL_ROWS = 64

VMEM = pl.BlockSpec(memory_space=pltpu.VMEM)
SMEM = pl.BlockSpec(memory_space=pltpu.SMEM)
ANY = pl.BlockSpec(memory_space=pl.ANY)


def sigmoid(v):
    return 0.5 * jnp.tanh(0.5 * v) + 0.5


def silu(v):
    return v * sigmoid(v)


def silu_slope(v):
    s = sigmoid(v)
    return s * (1.0 + v * (1.0 - s))


def mm(a, b):
    return jnp.dot(a, b, preferred_element_type=F32)


def mm_nt(a, b):
    return lax.dot_general(a, b, (((1,), (1,)), ((), ())), preferred_element_type=F32)


def mm_tn(a, b):
    return lax.dot_general(a, b, (((0,), (0,)), ((), ())), preferred_element_type=F32)


def normalized(v):
    center = v - jnp.mean(v, axis=-1, keepdims=True)
    scale = lax.rsqrt(jnp.mean(center * center, axis=-1, keepdims=True) + EPS)
    return center * scale, scale


def norm_back(grad, xhat, scale, gain):
    full = grad * gain
    return scale * (
        full
        - jnp.mean(full, axis=-1, keepdims=True)
        - xhat * jnp.mean(full * xhat, axis=-1, keepdims=True)
    )


def rows_of(s):
    return pl.ds(s * CH, CH)


def lanes_of(i):
    return pl.ds(pl.multiple_of((i % BLOCKS) * LANES, LANES), LANES)


def spread(row):
    return jnp.broadcast_to(row, (PIECES, LANES))


def piece_rows(s, t):
    return pl.ds(s * CH + t, PIECES, stride=PIECE)


def put_rows(ref, rows, value):
    for b in range(BLOCKS):
        ref[b, rows, :] = value[:, b * LANES : (b + 1) * LANES]


def get_rows(ref, rows):
    return jnp.concatenate([ref[b, rows, :] for b in range(BLOCKS)], axis=1)


class Here:
    def __init__(self, seqs, lengths):
        self.seqs, self.lengths = seqs, lengths

    def __getitem__(self, i):
        if i == 0:
            return lax.axis_index("tp")
        if i == 1:
            return lax.axis_index("seq")
        if i == 2:
            index = lax.axis_index("seq") * lax.axis_size("tp") + lax.axis_index("tp")
            return index if self.seqs > 1 else jnp.right_shift(index, 1)
        return self.lengths[i - 3 if self.seqs > 1 else jnp.bitwise_and(lax.axis_index("tp"), 1)]


def call(body, out, scratch, operands, specs, name, limit=2, outs=None):
    place = operands[0]
    if isinstance(place, Here):
        kernel = body
        if place.lengths is None:
            operands, specs = operands[1:], specs[1:]
            body = lambda *refs: kernel(place, *refs)
        else:
            operands = (place.lengths, *operands[1:])
            body = lambda lengths, *refs: kernel(Here(place.seqs, lengths), *refs)
    return pl.pallas_call(
        body,
        out_shape=out,
        in_specs=specs,
        out_specs=outs or jax.tree.map(lambda _: VMEM, out),
        scratch_shapes=scratch,
        name=name,
        compiler_params=pltpu.CompilerParams(vmem_limit_bytes=int(limit * 1024 * 1024)),
    )(*operands)


def shape(dims, dtype=F32):
    return jax.ShapeDtypeStruct(dims, dtype)


def put_low(low, pairs):
    for i in range(0, len(pairs), 2):
        high = pairs[i].astype(BF16)
        low[3 * i // 2] = high
        low[3 * i // 2 + 1] = (pairs[i] - high.astype(F32)).astype(BF16)
        low[3 * i // 2 + 2] = pairs[i + 1].astype(BF16)


def get_low(low, s):
    high, rest, slope = (low[3 * s + i].astype(F32) for i in range(3))
    return high + rest, slope


def enter_kernel(seqs, ids, *refs):
    count = 10
    far, near, sems = refs[:count], refs[count + 5 : 2 * count + 5], refs[-1]
    normed, par, before, ends, low = refs[count : count + 5]
    tok, gain, rate, beta, eta, skip, gain2, qg, kg, rb, nf, tab = refs[count + 5 : -1]
    copies = [pltpu.make_async_copy(a, b, sems.at[i]) for i, (a, b) in enumerate(zip(far, near))]
    for c in copies:
        c.start()
    for c in copies:
        c.wait()
    r = rate[...]
    d = 1.0 - r
    par[0] = d
    par[1] = jnp.log(d)
    par[2] = jnp.sqrt(r * (2.0 - r)) * beta[...]
    par[3] = eta[...]
    for i, row in enumerate((skip, gain2, gain)):
        par[4, i : i + 1, :] = row[...]
    for i, row in enumerate((qg, kg, rb)):
        par[4, 3:4, i * Z : (i + 1) * Z] = row[...]
    for s in range(seqs):
        par[4, 4 + s : 5 + s, :] = jnp.full((1, D), ids[3 + s].astype(F32))
    d2 = d * d
    d4 = d2 * d2
    d8 = d4 * d4
    d15 = d8 * d4 * d2 * d
    q = d8 * d8
    tab[0] = q
    tab[1] = 16.0 * d15
    tab[2] = q * q
    tab[3] = 32.0 * q * d15
    tab[4] = q * q * q * q
    tab[5] = 64.0 * q * q * q * d15
    for s in range(seqs):
        xhat, _ = normalized(tok[s].astype(F32))
        scaled = (xhat * gain[...]).astype(BF16)
        normed[rows_of(s), :] = scaled
        put_rows(nf, rows_of(s), scaled.astype(F32))
    place = lax.broadcasted_iota(jnp.int32, (PIECES, LANES), 0)

    def body(i, carry):
        s = i // BLOCKS
        lane = lanes_of(i)
        xs = [nf[i % BLOCKS, piece_rows(s, t), :] for t in range(PIECE)]
        for j0 in range(0, NDIM, 8):
            ds = [spread(par[0, j0 + j : j0 + j + 1, lane]) for j in range(8)]
            st = [xs[0]] * 8
            ta = [jnp.zeros((PIECES, LANES), F32)] * 8
            for t in range(1, PIECE):
                for j in range(8):
                    ta[j] = ds[j] * ta[j] + st[j]
                    st[j] = ds[j] * st[j] + xs[t]
            for j in range(8):
                a, b = st[j], ta[j]
                for k, step in enumerate((1, 2, 4)):
                    qm = spread(tab[2 * k, j0 + j : j0 + j + 1, lane])
                    rm = spread(tab[2 * k + 1, j0 + j : j0 + j + 1, lane])
                    sa = jnp.where(place >= step, pltpu.roll(a, step, 0), 0.0)
                    sb = jnp.where(place >= step, pltpu.roll(b, step, 0), 0.0)
                    b = b + qm * sb + rm * sa
                    a = a + qm * sa
                before[0, s, j0 + j, :, lane] = jnp.where(place >= 1, pltpu.roll(a, 1, 0), 0.0)
                before[1, s, j0 + j, :, lane] = jnp.where(place >= 1, pltpu.roll(b, 1, 0), 0.0)
                ends[2 * s, j0 + j : j0 + j + 1, lane] = a[PIECES - 1 :]
                ends[2 * s + 1, j0 + j : j0 + j + 1, lane] = b[PIECES - 1 :]
        return carry

    lax.fori_loop(0, seqs * BLOCKS, body, 0)
    ends[2 * seqs] = par[1]
    put_low(low, [ends[i] for i in range(2 * seqs)])


def pack_kernel(
    w_value, w_reset, w_hidden, w_update, u_hidden, w_in, w_out, p1, p2, p3, h2, h3, sems
):
    copies = []

    def add(source, target):
        copies.append(pltpu.make_async_copy(source, target, sems.at[len(copies)]))

    vb, cut = w_value.shape[1], D // 2
    upper = jnp.bitwise_and(lax.axis_index("seq"), 1) * cut
    at = pl.ds(pl.multiple_of(upper, cut), cut)
    for i, w in enumerate((w_value, w_reset)):
        add(w, p1.at[:, pl.ds(i * vb, vb)])
    far = jnp.bitwise_and(jnp.right_shift(lax.axis_index("seq"), far_shift()), 1) * cut
    top = 0
    for w in (w_hidden, w_update, u_hidden):
        row = pl.ds(top, w.shape[0])
        add(w.at[:, pl.ds(pl.multiple_of(far, cut), cut)], h2.at[row, :])
        add(w, p2.at[row, :])
        top += w.shape[0]
    add(w_in.at[at, :], h3.at[:, pl.ds(0, vb)])
    add(w_in, p3.at[:, pl.ds(0, vb)])
    for k in range(D // vb):
        row = pl.ds(k * vb, vb)
        add(w_out.at[:, row], p3.at[row, pl.ds(vb, vb)])
        if k < cut // vb:
            lane = pl.ds(pl.multiple_of(upper + k * vb, vb), vb)
            add(w_out.at[:, lane], h3.at[row, pl.ds(vb, vb)])
    for c in copies:
        c.start()
    for c in copies:
        c.wait()


def vectors(par):
    whole = [par.at[4, pl.ds(i, 1), :] for i in range(3)]
    return whole + [par.at[4, pl.ds(3, 1), pl.ds(i * Z, Z)] for i in range(3)]


def piece_powers(par, pw):
    k = lax.broadcasted_iota(jnp.int32, (PIECES, D), 0).astype(F32) * PIECE
    for j in range(NDIM):
        pw[j] = jnp.exp(k * par[1, j : j + 1, :])


def take_weights(refs, tp, first, second):
    top = tp // 2
    near = [refs[r * first : (r + 1) * first] for r in range(top)]
    refs = refs[top * first :]
    far = [refs[r * second : (r + 1) * second] for r in range(top)]
    return near, far, refs[top * second :]


def far_shift():
    return (lax.axis_size("seq").bit_length() - 1) // 2


def gate_copies(tp, ids, near, far, w1, w2, sems):
    top, cut = tp // 2, D // 2
    first = jnp.bitwise_and(ids[1], 1)
    second = jnp.bitwise_and(jnp.right_shift(ids[1], far_shift()), 1)
    copies = [[] for _ in range(tp)]

    def add(r, source, target):
        at = sems.at[sum(len(c) for c in copies)]
        copies[r].append(pltpu.make_async_copy(source, target, at))

    for r in range(top):
        add(r, near[r][0], w1.at[r])
        add(r, near[r][1], w2.at[r])
    for r in range(top):
        mine1, other1, mine2, other2 = far[r]
        for part, at in ((mine1, first), (other1, 1 - first)):
            add(top + r, part, w1.at[top + r, pl.ds(pl.multiple_of(at * cut, cut), cut), :])
        for part, at in ((mine2, second), (other2, 1 - second)):
            add(top + r, part, w2.at[top + r, :, pl.ds(pl.multiple_of(at * cut, cut), cut)])
    for group in copies:
        for c in group:
            c.start()
    return copies


def gate_rows(tp, me, w2, whu):
    nb = D // tp
    for r in range(tp):
        row = pl.ds(pl.multiple_of(jnp.bitwise_xor(me, r) * nb, nb), nb)
        whu[row, pl.ds(0, D)] = w2[r, pl.ds(0, nb), :]
        whu[row, pl.ds(D, D)] = w2[r, pl.ds(nb, nb), :]


def look_kernel(
    seqs, hops, ids, normed, par, before, wsh, *refs
):
    recvs, refs = refs[: len(hops)], refs[len(hops) :]
    st_in, skip_pre, mixed, shared_pre, prob, nf, sm, pw = refs
    skip, _, _, qg, kg, rb = vectors(par)
    place = ids[2]
    put_rows(nf, slice(None), normed[...].astype(F32))
    piece_powers(par, pw)
    logd = par[1]
    dinv = 1.0 / par[0]
    for s in range(seqs):
        a = jnp.zeros((NDIM, D), F32)
        b = jnp.zeros((NDIM, D), F32)
        for (shift, k), got in zip(hops, recvs):
            end = jnp.left_shift(jnp.bitwise_xor(jnp.right_shift(place, shift), k) + 1, shift)
            off = (place - end).astype(F32) * float(CH)
            power = jnp.where(place >= end, jnp.exp(jnp.maximum(off, 0.0) * logd), 0.0)
            oa, ob = (part * power for part in get_low(got, s))
            b = b + ob + off * oa * dinv
            a = a + oa
        st_in[0, s] = a
        st_in[1, s] = b

    def ema(i, carry):
        s = i // BLOCKS
        lane = lanes_of(i)
        row = [pl.ds(j, 1) for j in range(NDIM)]
        ds = [spread(par[0, row[j], lane]) for j in range(NDIM)]
        ws = [spread(par[2, row[j], lane] * par[3, row[j], lane]) for j in range(NDIM)]
        st = [
            before[0, s, j, :, lane] + pw[j, :, lane] * st_in[0, s, row[j], lane]
            for j in range(NDIM)
        ]
        for t in range(PIECE):
            x = nf[i % BLOCKS, piece_rows(s, t), :]
            parts = [None, None]
            for j in range(NDIM):
                st[j] = ds[j] * st[j] + x
                term = ws[j] * st[j]
                parts[j % 2] = term if parts[j % 2] is None else parts[j % 2] + term
            sm[i % BLOCKS, piece_rows(s, t), :] = parts[0] + parts[1]
        return carry

    lax.fori_loop(0, seqs * BLOCKS, ema, 0)
    for s in range(seqs):
        pre = get_rows(sm, rows_of(s)) + skip[...] * get_rows(nf, rows_of(s))
        skip_pre[rows_of(s), :] = pre
        mixed[rows_of(s), :] = silu(pre).astype(BF16)
    sp = mm(mixed[...], wsh[...])
    shared_pre[...] = sp
    shared = silu(sp)
    query = (shared * qg[...]).astype(BF16)
    keys = (shared * kg[...]).astype(BF16)
    t_at = lax.broadcasted_iota(jnp.int32, (CH, CH), 0)
    s_at = lax.broadcasted_iota(jnp.int32, (CH, CH), 1)
    bias_t = jnp.broadcast_to(rb[...], (CH, CH))
    for bit in range(7):
        bias_t = jnp.where(
            jnp.bitwise_and(t_at, 1 << bit) > 0, pltpu.roll(bias_t, 1 << bit, 1), bias_t
        )
    bias = bias_t.T
    for s in range(seqs):
        raw = mm_nt(query[s * CH : (s + 1) * CH], keys[s * CH : (s + 1) * CH]) * Z ** (-0.5)
        live = (place * CH + s_at).astype(F32) < par[4, 4 + s : 5 + s, :CH]
        allowed = (s_at <= t_at) & (live | (s_at == t_at))
        masked = jnp.where(allowed, raw + bias, -1e30)
        top = jnp.max(masked, axis=-1, keepdims=True)
        weights = jnp.where(allowed, jnp.exp(masked - top), 0.0)
        prob[s] = weights / jnp.sum(weights, axis=-1, keepdims=True)


def mix_kernel(seqs, tp, ids, tok, normed, mixed, prob, *refs):
    near, far, refs = take_weights(refs, tp, 2, 4)
    (
        values, value_pre, reset_pre, attended, gated, hidden_pre, update_pre, middle,
        w1, w2, whu, sems,
    ) = refs
    vb = values.shape[2]
    nb = D // tp
    copies = gate_copies(tp, ids, near, far, w1, w2, sems)
    for r in range(tp):
        for c in copies[r]:
            c.wait()
        vp = mm(normed[...], w1[r, :, :vb])
        value_pre[r] = vp
        v = silu(vp).astype(BF16)
        values[r] = v
        rp = mm(mixed[...], w1[r, :, vb:])
        reset_pre[r] = rp
        gate = silu(rp)
        for s in range(seqs):
            att = mm(prob[s].astype(BF16), v[s * CH : (s + 1) * CH])
            attended[r, rows_of(s), :] = att
            gated[r, rows_of(s), :] = (gate[s * CH : (s + 1) * CH] * att).astype(BF16)
        part = mm(gated[r], w2[r, pl.ds(2 * nb, vb), :])
        hidden_pre[...] = hidden_pre[...] + part if r else part
    gate_rows(tp, ids[0], w2, whu)
    hu = mm(mixed[...], whu[...])
    hidden_pre[...] += hu[:, :D]
    update_pre[...] = hu[:, D:]
    for s in range(seqs):
        x = tok[s].astype(F32)
        middle[rows_of(s), :] = x + sigmoid(update_pre[rows_of(s), :]) * (
            silu(hidden_pre[rows_of(s), :]) - x
        )


def ffn_kernel(seqs, tp, ids, tok, cot, middle, hidden_pre, update_pre, par, *refs):
    gain2 = vectors(par)[1]
    near, far, refs = take_weights(refs, tp, 1, 2)
    (
        out, keep, send, grad_hu, resid, grad_gain2,
        w3, n2, lg, acc, gn2, sems,
    ) = refs
    vb = w3.shape[2] // 2
    top, half = tp // 2, D // 2
    cuts = D // vb
    upper = jnp.bitwise_and(ids[1], 1)
    copies = [[] for _ in range(tp)]

    def add(r, source, target):
        at = sems.at[sum(len(c) for c in copies)]
        copies[r].append(pltpu.make_async_copy(source, target, at))

    for r in range(top):
        add(r, near[r][0], w3.at[r])
    for r in range(top):
        for part, at in zip(far[r], (upper, 1 - upper)):
            row = pl.ds(pl.multiple_of(at * half, half), half)
            add(top + r, part, w3.at[top + r, row, :])
    for group in copies:
        for c in group:
            c.start()
    place = ids[2]
    xhat, scale = normalized(middle[...])
    n2[...] = (xhat * gain2[...]).astype(BF16)
    at = (lax.broadcasted_iota(jnp.int32, (CH, D), 0) + place * CH).astype(F32)
    for s in range(seqs):
        lg[rows_of(s), :] = jnp.where(
            at < par[4, 4 + s : 5 + s, :], cot[s].astype(F32), 0.0
        ).astype(BF16)
    acc[...] = jnp.zeros_like(acc)
    gn2[...] = jnp.zeros_like(gn2)
    for h in range(tp // 2):
        for odd in range(2):
            r = 2 * h + odd
            for c in copies[r]:
                c.wait()
            grads = (keep, send)[odd]
            pre = mm(n2[...], w3[r, :, :vb])
            inner = silu(pre).astype(BF16)
            back = None
            for k in range(cuts):
                cols = slice(k * vb, (k + 1) * vb)
                w_out = w3[r, cols, vb:]
                acc[:, cols] += mm(inner, w_out)
                term = mm_nt(lg[:, cols], w_out)
                back = term if back is None else back + term
            gip = (back * silu_slope(pre)).astype(BF16)
            gn2[...] += mm_nt(gip, w3[r, :, :vb])
            grads[h, :, :vb] = mm_tn(n2[...], gip).astype(BF16)
            gwo = mm_tn(inner, lg[...]).astype(BF16)
            for k in range(cuts):
                grads[h, k * vb : (k + 1) * vb, vb:] = gwo[:, k * vb : (k + 1) * vb]
    mid = middle[...]
    out[...] = (mid + acc[...]).astype(BF16)
    grad = gn2[...]
    grad_gain2[...] = jnp.sum(grad * xhat, axis=0, keepdims=True)
    gm = lg[...].astype(F32) + norm_back(grad, xhat, scale, gain2[...])
    for s in range(seqs):
        x = tok[s].astype(F32)
        g = gm[s * CH : (s + 1) * CH]
        hp = hidden_pre[rows_of(s), :]
        update = sigmoid(update_pre[rows_of(s), :])
        grad_hu[rows_of(s), :D] = (g * update * silu_slope(hp)).astype(BF16)
        grad_hu[rows_of(s), D:] = (g * (silu(hp) - x) * update * (1.0 - update)).astype(BF16)
        resid[rows_of(s), :] = g * (1.0 - update)


def gates_kernel(tp, ids, mixed, gated, grad_hu, keep2, send2, ghu):
    nb = D // tp
    vb = gated.shape[2]
    wide = 2 * vb
    me = ids[0]
    ghu[...] = mm_tn(mixed[...], grad_hu[...])

    def block(h, carry):
        for odd in range(2):
            r = 2 * h + odd
            g2 = (keep2, send2)[odd]
            row = pl.ds(pl.multiple_of(jnp.bitwise_xor(me, r) * nb, nb), nb)
            gu = mm_tn(gated[r], grad_hu[:, :D]).astype(BF16)
            for k in range(D // wide):
                top = k * (2 * nb + vb)
                g2[h, pl.ds(top, nb), :] = ghu[row, pl.ds(k * wide, wide)].astype(BF16)
                g2[h, pl.ds(top + nb, nb), :] = ghu[row, pl.ds(D + k * wide, wide)].astype(BF16)
                g2[h, pl.ds(top + 2 * nb, vb), :] = gu[:, k * wide : (k + 1) * wide]
        return carry

    lax.fori_loop(0, tp // 2, block, 0)


def back_kernel(
    seqs, tp,
    ids, normed, mixed, skip_pre, shared_pre, prob, values, value_pre, reset_pre, attended,
    grad_hu, par, wsh, tok, before, st_in, grad_gain2, *refs,
):
    skip, _, _, qg, kg, _ = vectors(par)
    near, far, refs = take_weights(refs, tp, 2, 4)
    (
        keep1, send1, grad_skip, grad_normed, after, ends, sums_keep, sums_send,
        w1, w2, whu, gm, gp, tab, grad_wsh, misc, table, nf, pw, sems,
    ) = refs
    vb = values.shape[2]
    nb = D // tp
    me = ids[0]
    copies = gate_copies(tp, ids, near, far, w1, w2, sems)
    gp[...] = jnp.zeros_like(gp)
    grad_normed[...] = jnp.zeros_like(grad_normed)
    for group in copies:
        for c in group:
            c.wait()
    gate_rows(tp, me, w2, whu)
    gm[...] = mm_nt(grad_hu[...], whu[...])

    def block(h, carry):
        for odd in range(2):
            r = 2 * h + odd
            g1 = (keep1, send1)[odd]
            gg = mm_nt(grad_hu[:, :D], w2[r, pl.ds(2 * nb, vb), :])
            rp = reset_pre[r]
            sig = sigmoid(rp)
            ga = (gg * (rp * sig)).astype(BF16)
            grp = (gg * attended[r] * (sig * (1.0 + rp * (1.0 - sig)))).astype(BF16)
            g1[h, :, vb:] = mm_tn(mixed[...], grp).astype(BF16)
            gm[...] += mm_nt(grp, w1[r, :, vb:])
            gvs = []
            for s in range(seqs):
                part = ga[s * CH : (s + 1) * CH]
                gvs.append(mm_tn(prob[s].astype(BF16), part))
                gp[s] += mm_nt(part, values[r, rows_of(s), :])
            gv = jnp.concatenate(gvs, axis=0) if seqs > 1 else gvs[0]
            gvp = (gv * silu_slope(value_pre[r])).astype(BF16)
            g1[h, :, :vb] = mm_tn(normed[...], gvp).astype(BF16)
            grad_normed[...] += mm_nt(gvp, w1[r, :, :vb])
        return carry

    lax.fori_loop(0, tp // 2, block, 0)
    sp = shared_pre[...]
    shared = silu(sp)
    query = (shared * qg[...]).astype(BF16)
    keys = (shared * kg[...]).astype(BF16)
    total = jnp.zeros((CH, CH), F32)
    gqs = []
    gks = []
    for s in range(seqs):
        pr = prob[s]
        low = (pr * (gp[s] - jnp.sum(pr * gp[s], axis=-1, keepdims=True))).astype(BF16)
        total = total + low.astype(F32)
        gqs.append(mm(low, keys[s * CH : (s + 1) * CH]) * Z ** (-0.5))
        gks.append(mm_tn(low, query[s * CH : (s + 1) * CH]) * Z ** (-0.5))
    gq = jnp.concatenate(gqs, axis=0) if seqs > 1 else gqs[0]
    gk = jnp.concatenate(gks, axis=0) if seqs > 1 else gks[0]
    turned = total.T
    s_at = lax.broadcasted_iota(jnp.int32, (CH, CH), 0)
    for bit in range(7):
        turned = jnp.where(
            jnp.bitwise_and(s_at, 1 << bit) > 0, pltpu.roll(turned, CH - (1 << bit), 1), turned
        )
    misc[...] = jnp.concatenate(
        [
            jnp.sum(gq * shared, axis=0, keepdims=True),
            jnp.sum(gk * shared, axis=0, keepdims=True),
            jnp.sum(turned, axis=0, keepdims=True),
            jnp.zeros((1, D - 3 * Z), F32),
        ],
        axis=1,
    )
    gsp = ((gq * qg[...] + gk * kg[...]) * silu_slope(sp)).astype(BF16)
    grad_wsh[...] = mm_tn(mixed[...], gsp)
    put_rows(
        grad_skip,
        slice(None),
        (gm[...] + mm_nt(gsp, wsh[...])) * silu_slope(skip_pre[...]),
    )
    d = par[0]
    d2 = d * d
    d4 = d2 * d2
    d8 = d4 * d4
    q = d8 * d8
    tab[0] = q
    tab[1] = q * q
    tab[2] = q * q * q * q
    place = lax.broadcasted_iota(jnp.int32, (PIECES, LANES), 0)

    def body(i, carry):
        s = i // BLOCKS
        lane = lanes_of(i)
        ds = [spread(par[0, j : j + 1, lane]) for j in range(NDIM)]
        ad = [grad_skip[i % BLOCKS, piece_rows(s, PIECE - 1), :]] * NDIM
        for t in range(PIECE - 2, -1, -1):
            g = grad_skip[i % BLOCKS, piece_rows(s, t), :]
            for j in range(NDIM):
                ad[j] = ds[j] * ad[j] + g
        for j in range(NDIM):
            a = ad[j]
            for k, step in enumerate((1, 2, 4)):
                qm = spread(tab[k, j : j + 1, lane])
                a = a + qm * jnp.where(place < PIECES - step, pltpu.roll(a, PIECES - step, 0), 0.0)
            after[s, j, :, lane] = jnp.where(
                place < PIECES - 1, pltpu.roll(a, PIECES - 1, 0), 0.0
            )
            ends[s, j : j + 1, lane] = a[:1]
        return carry

    lax.fori_loop(0, seqs * BLOCKS, body, 0)
    small_sums(
        seqs, ids, tok, normed, grad_skip, grad_normed, par, before, st_in, skip, grad_gain2, misc,
        grad_wsh, sums_keep, sums_send, table, nf, pw,
    )
    for s in range(seqs):
        sums_send[pl.ds(sums_keep.shape[0] + s * NDIM, NDIM), :] = ends[s]


def small_sums(
    seqs, ids, tok, normed, grad_skip, grad_normed, par, before, st_in, skip, gain2_row, misc, grad_wsh,
    keep, send, table, nf, pw,
):
    put_rows(nf, slice(None), normed[...].astype(F32))
    piece_powers(par, pw)
    count = D // (D // Z)
    small = table.at[count:, :]
    small[...] = jnp.zeros_like(small)
    for k in range(D // Z):
        table[:count, k * Z : (k + 1) * Z] = grad_wsh[k * count : (k + 1) * count, :]

    def body(i, carry):
        s = i // BLOCKS
        lane = lanes_of(i)
        k16 = lax.broadcasted_iota(jnp.int32, (PIECES, LANES), 0).astype(F32) * PIECE
        for j0 in range(0, NDIM, 8):
            row = [pl.ds(j0 + j, 1) for j in range(8)]
            ds = [spread(par[0, row[j], lane]) for j in range(8)]
            st, ta, q, r = [], [], [], []
            for j in range(8):
                e = pw[j0 + j, :, lane] * st_in[0, s, row[j], lane]
                st.append(before[0, s, j0 + j, :, lane] + e)
                ta.append(
                    before[1, s, j0 + j, :, lane]
                    + pw[j0 + j, :, lane] * st_in[1, s, row[j], lane]
                    + k16 * e / ds[j]
                )
                q.append(jnp.zeros((PIECES, LANES), F32))
                r.append(jnp.zeros((PIECES, LANES), F32))
            for t in range(PIECE):
                x = nf[i % BLOCKS, piece_rows(s, t), :]
                g = grad_skip[i % BLOCKS, piece_rows(s, t), :]
                for j in range(8):
                    ta[j] = ds[j] * ta[j] + st[j]
                    st[j] = ds[j] * st[j] + x
                    q[j] = q[j] + g * st[j]
                    r[j] = r[j] + g * ta[j]
            for j in range(8):
                small[pl.ds(j0 + j, 1), lane] += jnp.sum(q[j], axis=0, keepdims=True)
                small[pl.ds(NDIM + j0 + j, 1), lane] += jnp.sum(r[j], axis=0, keepdims=True)
        return carry

    lax.fori_loop(0, seqs * BLOCKS, body, 0)
    gsk = jnp.zeros((1, D), F32)
    gn1 = jnp.zeros((1, D), F32)
    for s in range(seqs):
        xhat, _ = normalized(tok[s].astype(F32))
        g = get_rows(grad_skip, rows_of(s))
        direct = g * skip[...] + grad_normed[rows_of(s), :]
        gsk = gsk + jnp.sum(g * get_rows(nf, rows_of(s)), axis=0, keepdims=True)
        gn1 = gn1 + jnp.sum(direct * xhat, axis=0, keepdims=True)
    small[2 * NDIM : 2 * NDIM + 1, :] = gsk
    small[2 * NDIM + 1 : 2 * NDIM + 2, :] = gn1
    small[2 * NDIM + 2 : 2 * NDIM + 3, :] = gain2_row[...]
    small[2 * NDIM + 3 : 2 * NDIM + 4, :] = misc[...]
    half = keep.shape[0]
    mine = jnp.bitwise_and(ids[0], 1) * half
    keep[...] = table[pl.ds(pl.multiple_of(mine, 8), half), :]
    send[pl.ds(0, half), :] = table[pl.ds(pl.multiple_of(half - mine, 8), half), :]


def pair_kernel(bit, ids, mine, other, out):
    half = mine.shape[0]
    upper = jnp.where(jnp.bitwise_and(ids[0], bit) > 0, half, 0)
    out[pl.ds(pl.multiple_of(upper, 8), half), :] = mine[...]
    out[pl.ds(pl.multiple_of(half - upper, 8), half), :] = other[...]


def finish_kernel(
    ids, par, rate, beta, mine, other,
    grad_gain, grad_rate, grad_beta, grad_eta, grad_skip, grad_wsh, grad_qg, grad_kg, grad_rb,
    grad_gain2, table,
):
    gain = vectors(par)[2]
    pair_kernel(1, ids, mine, other, table)
    count = D // (D // Z)
    for k in range(D // Z):
        grad_wsh[k * count : (k + 1) * count, :] = table[:count, k * Z : (k + 1) * Z]
    small = table.at[count:, :]
    inflow, eta, r = par[2], par[3], rate[...]
    root = jnp.sqrt(r * (2.0 - r))
    q_sum = small[:NDIM, :]
    grad_inflow = eta * q_sum
    grad_decay = eta * inflow * small[NDIM : 2 * NDIM, :]
    grad_rate[...] = grad_inflow * beta[...] * (1.0 - r) / root - grad_decay
    grad_beta[...] = grad_inflow * root
    grad_eta[...] = inflow * q_sum
    row = [small[2 * NDIM + i : 2 * NDIM + i + 1, :] for i in range(4)]
    grad_skip[...] = row[0]
    grad_gain[...] = row[1] + jnp.sum(inflow * grad_inflow, axis=0, keepdims=True) / gain[...]
    grad_gain2[...] = row[2]
    grad_qg[...] = row[3][:, :Z]
    grad_kg[...] = row[3][:, Z : 2 * Z]
    grad_rb[...] = row[3][:, 2 * Z : 3 * Z]


def leave_kernel(
    seqs, tops, ids, tok, par, grad_skip, grad_normed, behind, resid, *refs
):
    levels = len(tops)
    recvs, refs = refs[:levels], refs[levels:]
    grad_tokens, ad_in, pw, sm = refs
    skip, _, gain = vectors(par)[:3]
    place = ids[2]
    logd = par[1]
    gots = [get_wide(recvs[k], tops[k], seqs * NDIM) for k in range(levels)]
    for s in range(seqs):
        a = jnp.zeros((NDIM, D), F32)
        for k in range(levels):
            low = jnp.bitwise_and(place, 1 << k) == 0
            off = jnp.bitwise_and(place, (1 << k) - 1)
            away = ((1 << k) - 1 - off).astype(F32) * float(CH)
            got = gots[k][s * NDIM : (s + 1) * NDIM]
            a = a + got * jnp.where(low, jnp.exp(away * logd), 0.0)
        ad_in[s] = a
    k = (PIECES - 1 - lax.broadcasted_iota(jnp.int32, (PIECES, D), 0)).astype(F32) * PIECE
    for j in range(NDIM):
        pw[j] = jnp.exp(k * par[1, j : j + 1, :])

    def body(i, carry):
        s = i // BLOCKS
        lane = lanes_of(i)
        row = [pl.ds(j, 1) for j in range(NDIM)]
        ds = [spread(par[0, row[j], lane]) for j in range(NDIM)]
        ws = [spread(par[2, row[j], lane] * par[3, row[j], lane]) for j in range(NDIM)]
        ad = [
            behind[s, j, :, lane] + pw[j, :, lane] * ad_in[s, row[j], lane] for j in range(NDIM)
        ]
        for t in range(PIECE - 1, -1, -1):
            g = grad_skip[i % BLOCKS, piece_rows(s, t), :]
            parts = [None, None]
            for j in range(NDIM):
                ad[j] = ds[j] * ad[j] + g
                term = ws[j] * ad[j]
                parts[j % 2] = term if parts[j % 2] is None else parts[j % 2] + term
            sm[i % BLOCKS, piece_rows(s, t), :] = parts[0] + parts[1]
        return carry

    lax.fori_loop(0, seqs * BLOCKS, body, 0)
    for s in range(seqs):
        xhat, scale = normalized(tok[s].astype(F32))
        grad = (
            get_rows(sm, rows_of(s))
            + get_rows(grad_skip, rows_of(s)) * skip[...]
            + grad_normed[rows_of(s), :]
        )
        grad_tokens[s] = (
            resid[rows_of(s), :] + norm_back(grad, xhat, scale, gain[...])
        ).astype(BF16)


def hop_kernel(seqs, shift, count, ids, state, *refs):
    others, (total, low) = refs[: count - 1], refs[count - 1 :]
    mine = jnp.bitwise_and(jnp.right_shift(ids[2], shift), count - 1)
    logd = state[2 * seqs]
    total[2 * seqs] = logd
    sums = [None] * (2 * seqs)
    for k in range(count):
        after = (count - 1 - jnp.bitwise_xor(mine, k)).astype(F32) * float(CH << shift)
        power = jnp.exp(after * logd)
        slope = after * jnp.exp((after - 1.0) * logd)
        for s in range(seqs):
            part = get_low(others[k - 1], s) if k else (state[2 * s], state[2 * s + 1])
            a, b = power * part[0], power * part[1] + slope * part[0]
            sums[2 * s : 2 * s + 2] = [sums[2 * s] + a, sums[2 * s + 1] + b] if k else [a, b]
    for i in range(2 * seqs):
        total[i] = sums[i]
    put_low(low, sums)


def put_wide(ref, top, value):
    wide = ref.shape[1]
    count = value.shape[0]
    for k in range(D // wide):
        ref[pl.ds(top + k * count, count), :] = value[:, k * wide : (k + 1) * wide].astype(ref.dtype)


def get_wide(ref, top, count):
    wide = ref.shape[1]
    runs = [ref[pl.ds(top + k * count, count), :].astype(F32) for k in range(D // wide)]
    return jnp.concatenate(runs, axis=1) if len(runs) > 1 else runs[0]


def first_back_hop(seqs, joins, ids, par, own, sums, got, out, keep, payload):
    rows = seqs * NDIM
    fold_lanes = D // payload.shape[1]
    if joins:
        join_adjoint(seqs, 0, ids, par, own, got[pl.ds(sums.shape[0], rows), :], out)
    else:
        out[...] = own[...]
    put_wide(payload, 0, out[...])
    half = keep.shape[0]
    upper = jnp.where(jnp.bitwise_and(ids[0], 2) > 0, half, 0)
    mine = pl.ds(pl.multiple_of(upper, 8), half)
    theirs = pl.ds(pl.multiple_of(half - upper, 8), half)
    keep[...] = sums[mine, :] + got[mine, :]
    put_wide(payload, rows * fold_lanes, sums[theirs, :] + got[theirs, :])


def join_adjoint(seqs, level, ids, par, own, got, out):
    upper = jnp.bitwise_and(ids[2], 1 << level) > 0
    power = jnp.exp(float(CH << level) * par[1])
    for s in range(seqs):
        row = slice(s * NDIM, (s + 1) * NDIM)
        early = jnp.where(upper, got[row], own[row, :])
        late = jnp.where(upper, own[row, :], got[row])
        out[row, :] = early + power * late


def chain_hop(seqs, level, split, halved, top, ids, par, own, kept, sent, other, out, keep, payload, base):
    rows = seqs * NDIM
    lanes = D // other.shape[1]
    small_base = 0 if payload is None else base + rows * (D // payload.shape[1])
    if out is not None:
        join_adjoint(seqs, level, ids, par, own, get_wide(other, top, rows), out)
        put_wide(payload, base, out[...])
    half = keep.shape[0]
    if split:
        upper = jnp.bitwise_and(ids[0], split) > 0
        got = get_wide(other, top + rows * lanes, 2 * half)
        first, second = kept[:half, :] + got[:half], kept[half:, :] + got[half:]
        keep[...] = jnp.where(upper, second, first)
        put_wide(payload, small_base, jnp.where(upper, first, second))
    else:
        mine = kept[...] if halved else get_wide(sent, top + rows * lanes, half)
        total = mine + get_wide(other, top + rows * lanes, half)
        keep[...] = total
        if payload is not None:
            put_wide(payload, small_base, total)


def back_hop(seqs, level, split, halved, ids, par, own, kept, sent, other, out, keep, payload):
    chain_hop(
        seqs, level, split, halved, 0, ids, par, own, kept, sent, other, out, keep, payload, 0
    )


def split_rows(count, cut, place, k):
    shift, bits = cut
    rows = count >> bits
    sub = jnp.bitwise_and(jnp.right_shift(place, shift), (1 << bits) - 1)
    return pl.multiple_of(jnp.bitwise_xor(sub, k) * rows, rows), rows


def add_rows(parts, start, high, out, top, lane, width, at):
    step = min(64, high)

    def body(i, carry):
        row = pl.ds(pl.multiple_of(start + i * step, step), step)
        total = parts[0][row, lane : lane + width].astype(F32)
        for other in parts[1:]:
            total = total + other[row, lane : lane + width].astype(F32)
        out[pl.ds(pl.multiple_of(top + i * step, 16), step), at : at + width] = total.astype(BF16)
        return carry

    lax.fori_loop(0, high // step, body, 0)


def fold_kernel(jobs, inputs, ids, *refs):
    parts, outs = refs[:inputs], refs[inputs:]
    at = 0
    for count, lane, width, cut, targets in jobs:
        own = parts[at : at + count]
        at += count
        blocks, rows, _ = own[0].shape
        for k, (target, block, offset) in enumerate(targets):
            if cut == "tp":
                ranges, start, high = (k,), 0, rows
            elif cut is None:
                ranges, start, high = range(blocks), 0, rows
            else:
                start, high = split_rows(rows, cut, ids[1], k)
                ranges = range(blocks)
            for to, b in enumerate(ranges):
                add_rows(
                    [p.at[b] for p in own], start, high, outs[target].at[block + to], 0, lane,
                    width, offset,
                )


def fold(ids, shapes, jobs):
    arrays = [a for job in jobs for a in job[0]]
    plan = [(len(job[0]),) + tuple(job[1:]) for job in jobs]
    return call(
        functools.partial(fold_kernel, plan, len(arrays)),
        tuple(shape(dims, BF16) for dims in shapes),
        [],
        (ids, *arrays),
        [SMEM] + [VMEM] * len(arrays),
        "fold",
    )


def join_kernel(cut, ids, mine, other, out):
    blocks, rows, _ = mine.shape
    for k, part in enumerate((mine, other)):
        start, _ = split_rows(2 * rows, cut, ids[1], k)
        for b in range(blocks):
            out[b, pl.ds(pl.multiple_of(start, 16), rows), :] = part[b]


def join(ids, mine, other, cut):
    blocks, rows, lanes = mine.shape
    return call(
        functools.partial(join_kernel, cut),
        (shape((blocks, 2 * rows, lanes), BF16),),
        [],
        (ids, mine, other),
        [SMEM, VMEM, VMEM],
        "join",
    )[0]


def start_kernel(
    seqs, bits, ids, par, own, sums, got, keep1, got1, out, keep, left, payload, right, send
):
    vb = keep1.shape[2] // 2
    for b, target in enumerate((left, payload)):
        add_rows([keep1.at[b], got1.at[b]], 0, D, target, 0, 0, vb, 0)
    for k, target in enumerate((right, send)):
        start, high = split_rows(D, (0, bits), ids[1], k)
        for b in range(2):
            add_rows([keep1.at[b], got1.at[b]], start, high, target.at[b], 0, vb, vb, 0)
    rows, half = seqs * NDIM, keep.shape[0]
    join_adjoint(seqs, 0, ids, par, own, got[pl.ds(2 * half, rows), :], out)
    put_wide(payload, D, out[...])
    upper = jnp.where(jnp.bitwise_and(ids[0], 2) > 0, half, 0)
    mine = pl.ds(pl.multiple_of(upper, 8), half)
    theirs = pl.ds(pl.multiple_of(half - upper, 8), half)
    keep[...] = sums[mine, :] + got[mine, :]
    put_wide(payload, D + rows * (D // vb), sums[theirs, :] + got[theirs, :])


def cross_kernel(
    seqs, bits, ids, par, own, kept, sent, other, left, right, got, out, keep, left_out, payload,
    right_out, send,
):
    vb = left.shape[1]
    for k, target in enumerate((left_out, payload)):
        start, high = split_rows(D, (0, bits), ids[1], k)
        add_rows([left, other], start, high, target, 0, 0, vb, 0)
    for b, target in enumerate((right_out, send)):
        add_rows([right.at[b], got.at[b]], 0, high, target, 0, 0, vb, 0)
    chain_hop(
        seqs, 1, 0, True, D, ids, par, own, kept, sent, other, out, keep, payload, high
    )


def ride_kernel(
    seqs, level, split, halved, top, jobs, cut, high, last, ids, par, own, kept, sent, other, *refs
):
    count = 1 + max(p for job in jobs for p in job[0])
    parts, refs = refs[:count], refs[count:]
    out = payload = None
    if last:
        keep, kept_out = refs
        halves = ((0, keep),)
    elif cut is None:
        kept_out, out, payload = refs
        halves = ((0, payload),)
    else:
        keep, kept_out, out, payload = refs
        halves = ((0, keep), (1, payload))
    for picks, width, at in jobs:
        chosen = [other if p == -1 else sent if p == -2 else parts[p] for p in picks]
        for k, target in halves:
            start = 0 if cut is None else split_rows(2 * high, cut, ids[1], k)[0]
            add_rows(chosen, start, high, target, 0, 0, width, at)
    chain_hop(
        seqs, level, split, halved, top, ids, par, own, kept, sent, other, out, kept_out, payload,
        high,
    )


def unpack_first(cut, ids, *refs):
    count = 1 << cut[1]
    pieces, refs = refs[:count], refs[count:]
    w_in, w_out = refs[:2]
    outs = refs[2:]
    vb = w_in.shape[1]
    wide = 2 * vb
    each = sum(out.shape[0] for out in outs)
    for k in range(count):
        row, rows = split_rows(D, cut, ids[1], k)
        w_in[pl.ds(row, rows), :] = pieces[k][0, :, :vb].astype(F32)
        for first in range(0, rows, vb):
            w_out[:, pl.ds(pl.multiple_of(row + first, vb), vb)] = pieces[k][
                0, first : first + vb, vb:
            ].astype(F32)
        for b in range(count):

            @pl.when(row == b * rows)
            def _(k=k, b=b, rows=rows):
                for run in range(D // wide):
                    start = run * each
                    for out in outs:
                        end = start + out.shape[0]
                        lo, hi = max(start, b * rows), min(end, (b + 1) * rows)
                        if lo < hi:
                            out[lo - start : hi - start, run * wide : (run + 1) * wide] = pieces[k][
                                1, lo - b * rows : hi - b * rows, :
                            ].astype(F32)
                        start = end


def unpack_sides(cut, ids, *refs):
    count = 1 << cut[1]
    pieces, (left, right) = refs[:count], refs[count:]
    vb = left.shape[1]
    for k in range(count):
        row, rows = split_rows(D, cut, ids[1], k)
        left[pl.ds(row, rows), :] = pieces[k][0, :, :vb].astype(F32)
        right[pl.ds(row, rows), :] = pieces[k][0, :, vb:].astype(F32)


def unpack(body, cut, ids, pieces, dims):
    return call(
        functools.partial(body, cut),
        tuple(shape(d) for d in dims),
        [],
        (ids, *pieces),
        [SMEM] + [VMEM] * len(pieces),
        "unpack",
    )


BOTH = ("seq", "tp")


def swap(value, mask):
    count = lax.axis_size("seq") * lax.axis_size("tp")
    return lax.ppermute(value, BOTH, [(i, i ^ mask) for i in range(count)])


def after(value, *others):
    return lax.optimization_barrier((value, *others))[0]


def bits_of(count):
    return [1 << k for k in range(count.bit_length() - 1)]


def has(index, bit):
    return jnp.bitwise_and(index, bit) > 0


def half_of(value, upper):
    half = value.shape[0] // 2
    return lax.dynamic_slice_in_dim(value, jnp.where(upper, half, 0), half, 0)


def joined(mine, other, upper):
    return jnp.where(
        upper,
        jnp.concatenate([other, mine], axis=0),
        jnp.concatenate([mine, other], axis=0),
    )


def spread_out(own, tp):
    pieces = {0: own}
    for bit in reversed(bits_of(tp // 2)):
        for r in list(pieces):
            pieces[r ^ bit] = [swap(a, bit) for a in pieces[r]]
    return [pieces[r] for r in range(tp // 2)]


def per_device(
    tokens,
    cotangent,
    valid_lengths,
    norm1_gain,
    ema_rate,
    ema_beta,
    ema_eta,
    ema_skip,
    w_shared,
    query_gain,
    key_gain,
    rel_bias,
    w_value,
    w_reset,
    w_update,
    w_hidden,
    u_hidden,
    norm2_gain,
    w_in,
    w_out,
):
    part = lax.axis_index("tp")
    tp = lax.axis_size("tp")
    seq = lax.axis_size("seq")
    all_seqs, local_rows, _ = tokens.shape
    vb = w_value.shape[1]
    nb = D // tp
    ybits = far_shift()
    traded = local_rows < CH
    lower = part % 2 == 0

    def trade(value):
        if not traded:
            return value
        other = swap(jnp.where(lower, value[1], value[0]), 1)
        mine = jnp.where(lower, value[0], value[1])
        return joined(mine, other, ~lower)[None]

    def trade_back(value):
        if not traded:
            return value
        first, second = value[0, :local_rows], value[0, local_rows:]
        other = swap(jnp.where(lower, second, first), 1)
        mine = jnp.where(lower, first, second)
        return jnp.where(lower, jnp.stack([mine, other]), jnp.stack([other, mine]))

    if traded:
        assert all_seqs == 2 and 2 * local_rows == CH
        seqs = 1
    else:
        assert local_rows == CH
        seqs = all_seqs
    rows = seqs * CH
    ids, ids_lengths = Here(seqs, None), Here(seqs, valid_lengths.astype(jnp.int32))
    masks = bits_of(tp * seq)[int(traded) :]
    levels = len(masks)

    tok = trade(tokens)
    cot = trade(cotangent)
    gain1 = norm1_gain[None]
    gain2 = norm2_gain[None]
    skip = ema_skip[None]
    rate, beta = ema_rate.T, ema_beta.T
    qg, kg, rb = query_gain[None], key_gain[None], rel_bias[None]

    top = tp // 2
    weights = (w_value, w_reset, w_hidden, w_update, u_hidden, w_in, w_out)
    rows2 = 2 * nb + vb
    normed, par, before, ends, low = call(
        functools.partial(enter_kernel, seqs),
        (
            shape((rows, D), BF16),
            shape((5, NDIM, D)),
            shape((2, seqs, NDIM, PIECES, D)),
            shape((2 * seqs + 1, NDIM, D)),
            shape((3 * seqs, NDIM, D), BF16),
        ),
        [
            pltpu.VMEM((seqs, CH, D), BF16),
            pltpu.VMEM((1, D), F32),
            pltpu.VMEM((NDIM, D), F32),
            pltpu.VMEM((NDIM, D), F32),
            pltpu.VMEM((NDIM, D), F32),
            pltpu.VMEM((1, D), F32),
            pltpu.VMEM((1, D), F32),
            pltpu.VMEM((1, Z), F32),
            pltpu.VMEM((1, Z), F32),
            pltpu.VMEM((1, Z), F32),
            pltpu.VMEM((BLOCKS, rows, LANES), F32),
            pltpu.VMEM((6, NDIM, D), F32),
            pltpu.SemaphoreType.DMA((10,)),
        ],
        (ids_lengths, tok, gain1, rate, beta, ema_eta.T, skip, gain2, qg, kg, rb),
        [SMEM] + [ANY] * 10,
        "enter",
        limit=12,
    )
    start = 1 - int(traded)
    groups = [(0, 1)] * start + [(start, 2)] + [(i, 1) for i in range(start + 2, levels)]
    hops = []
    first_half = has(lax.axis_index("seq"), 1)
    half1 = jnp.concatenate([half_of(w, first_half) for w in (w_value, w_reset)], axis=1)
    mine1 = swap(half1, top)
    state = ends
    for i, (shift, bits) in enumerate(groups):
        if i == start:
            low = after(low, mine1)
            pack1, pack2, pack3, half2, half3 = call(
                pack_kernel,
                (
                    shape((D, 2 * vb), BF16),
                    shape((rows2, D), BF16),
                    shape((D, 2 * vb), BF16),
                    shape((rows2, D // 2), BF16),
                    shape((D // 2, 2 * vb), BF16),
                ),
                [pltpu.SemaphoreType.DMA((10 + 3 * D // vb // 2,))],
                lax.optimization_barrier((*weights, low))[:-1],
                [ANY] * 7,
                "pack",
                limit=60,
                outs=(pl.BlockSpec(),) * 5,
            )
        if i == start + 1:
            mine2 = swap(after(half2, low), top)
            other1 = swap(after(mine1, low), tp)
            near_gates = spread_out([after(pack1, low), after(pack2, low)], tp)
        if i == start + 2:
            low = after(low, mine2, other1, *near_gates[-1])
            mine3 = swap(after(half3, low), top)
            other2 = swap(after(mine2, low), tp << ybits)
            near_feeds = spread_out([after(pack3, low)], tp)
        got = []
        for k in range(1, 1 << bits):
            got.append(swap(low, k << (shift + int(traded))))
            hops.append((shift, k, got[-1]))
        if i + 1 < len(groups):
            state, low = call(
                functools.partial(hop_kernel, seqs, shift, 1 << bits),
                (shape((2 * seqs + 1, NDIM, D)), shape((3 * seqs, NDIM, D), BF16)),
                [],
                (ids, state, *got),
                [SMEM] + [VMEM] * (1 + len(got)),
                "hop",
            )
    st_in, skip_pre, mixed, shared_pre, prob = call(
        functools.partial(look_kernel, seqs, [h[:2] for h in hops]),
        (
            shape((2, seqs, NDIM, D)),
            shape((rows, D)),
            shape((rows, D), BF16),
            shape((rows, Z)),
            shape((seqs, CH, CH)),
        ),
        [
            pltpu.VMEM((BLOCKS, rows, LANES), F32),
            pltpu.VMEM((BLOCKS, rows, LANES), F32),
            pltpu.VMEM((NDIM, PIECES, D), F32),
        ],
        (
            ids, after(normed, mine3), par, before, w_shared,
            *[h[2] for h in hops],
        ),
        [SMEM] + [VMEM] * (4 + len(hops)),
        "look",
        limit=10,
    )
    far_gates = spread_out([mine1, after(other1, prob), mine2, after(other2, prob)], tp)
    other3 = swap(mine3, tp)
    gates = [w for group in near_gates + far_gates for w in group]

    values, value_pre, reset_pre, attended, gated, hidden_pre, update_pre, middle = call(
        functools.partial(mix_kernel, seqs, tp),
        (
            shape((tp, rows, vb), BF16),
            shape((tp, rows, vb)),
            shape((tp, rows, vb)),
            shape((tp, rows, vb)),
            shape((tp, rows, vb), BF16),
            shape((rows, D)),
            shape((rows, D)),
            shape((rows, D)),
        ),
        [
            pltpu.VMEM((tp, D, 2 * vb), BF16),
            pltpu.VMEM((tp, rows2, D), BF16),
            pltpu.VMEM((D, 2 * D), BF16),
            pltpu.SemaphoreType.DMA((3 * tp,)),
        ],
        (ids, tok, normed, after(mixed, other3), prob, *gates),
        [SMEM] + [VMEM] * 4 + [ANY] * len(gates),
        "mix",
        limit=10,
    )

    far_feeds = spread_out([mine3, other3], tp)
    feeds = [w for group in near_feeds + far_feeds for w in group]
    out, keep3, send3, grad_hu, resid, grad_gain2 = call(
        functools.partial(ffn_kernel, seqs, tp),
        (
            shape((rows, D), BF16),
            shape((tp // 2, D, 2 * vb), BF16),
            shape((tp // 2, D, 2 * vb), BF16),
            shape((rows, 2 * D), BF16),
            shape((rows, D)),
            shape((1, D)),
        ),
        [
            pltpu.VMEM((tp, D, 2 * vb), BF16),
            pltpu.VMEM((rows, D), BF16),
            pltpu.VMEM((rows, D), BF16),
            pltpu.VMEM((rows, D), F32),
            pltpu.VMEM((rows, D), F32),
            pltpu.SemaphoreType.DMA((3 * tp // 2,)),
        ],
        (ids, tok, cot, middle, hidden_pre, update_pre, par, *feeds),
        [SMEM] + [VMEM] * 6 + [ANY] * len(feeds),
        "ffn",
        limit=10,
    )

    half = tp // 2
    yn = 1 << ybits
    wide = 2 * vb
    runs = D // wide
    cut_of_y = (0, ybits)
    zcuts = [(shift, 1) for shift in range(ybits, seq.bit_length() - 1)]

    def over_tp(pieces):
        return [pieces[0]] + [swap(p, 2 * k) for k, p in enumerate(pieces) if k]

    def over_y(pieces):
        return [pieces[0]] + [swap(p, tp * k) for k, p in enumerate(pieces) if k]

    def over_z(value, cut):
        return swap(value, tp << cut[0])

    def cut_tp(parts, dims):
        n = dims[0]
        return fold(
            ids,
            [(1,) + dims[1:]] * n,
            [(parts, 0, dims[2], "tp", [(k, 0, 0) for k in range(n)])],
        )

    def cut_y(parts, dims):
        return fold(
            ids,
            [(dims[0], dims[1] // yn, dims[2])] * yn,
            [(parts, 0, dims[2], cut_of_y, [(k, 0, 0) for k in range(yn)])],
        )

    last = [None]

    def now(value):
        return value if last[0] is None else after(value, last[0])

    chunk = (half, D, wide)
    got3 = swap(send3, 1)
    keep2, send2 = call(
        functools.partial(gates_kernel, tp),
        (shape(chunk, BF16), shape(chunk, BF16)),
        [pltpu.VMEM((D, 2 * D), F32)],
        (ids, mixed, gated, grad_hu),
        [SMEM] + [VMEM] * 3,
        "gates",
        limit=10,
    )
    got2 = swap(send2, 1)
    g3 = cut_tp([keep3, got3], chunk)
    g3 = over_tp(g3)
    g2 = cut_y([keep2, after(got2, g3[0])], chunk)
    g2 = over_y(g2)

    count = Z + SMALL_ROWS
    count += -count % (16 * tp)
    (
        keep1, send1, grad_skip, grad_normed, behind, back_ends, sums_keep, sums_send,
    ) = call(
        functools.partial(back_kernel, seqs, tp),
        (
            shape(chunk, BF16),
            shape(chunk, BF16),
            shape((BLOCKS, rows, LANES)),
            shape((rows, D)),
            shape((seqs, NDIM, PIECES, D)),
            shape((seqs, NDIM, D)),
            shape((count // 2, D)),
            shape((count // 2 + seqs * NDIM, D)),
        ),
        [
            pltpu.VMEM((tp, D, 2 * vb), BF16),
            pltpu.VMEM((tp, rows2, D), BF16),
            pltpu.VMEM((D, 2 * D), BF16),
            pltpu.VMEM((rows, D), F32),
            pltpu.VMEM((seqs, CH, CH), F32),
            pltpu.VMEM((3, NDIM, D), F32),
            pltpu.VMEM((D, Z), F32),
            pltpu.VMEM((1, D), F32),
            pltpu.VMEM((count, D), F32),
            pltpu.VMEM((BLOCKS, rows, LANES), F32),
            pltpu.VMEM((NDIM, PIECES, D), F32),
            pltpu.SemaphoreType.DMA((3 * tp,)),
        ],
        (
            ids, normed, mixed, skip_pre, shared_pre, prob, values, value_pre, reset_pre, attended,
            after(grad_hu, g2[0]), par, w_shared, tok, before, st_in, grad_gain2,
            *gates,
        ),
        [SMEM] + [VMEM] * 16 + [ANY] * len(gates),
        "back",
        limit=12,
    )

    g3 = cut_y([after(g3[0], send1)] + g3[1:], (1, D, wide))
    g2 = cut_tp([after(g2[0], g3[0])] + g2[1:], (half, D // yn, wide))
    (
        keep1, send1, grad_skip, grad_normed, behind, back_ends, sums_keep, sums_send, _,
    ) = lax.optimization_barrier(
        (keep1, send1, grad_skip, grad_normed, behind, back_ends, sums_keep, sums_send, g2[0])
    )
    adjoint = back_ends.reshape(seqs * NDIM, D)
    last[0] = g2[0]
    g3 = over_y(g3)
    g2 = over_tp(g2)
    got1 = swap(send1, 1)
    got_sums = swap(sums_send, 1)
    done = {}

    def first_chunks():
        high = D // yn
        for i, cut in enumerate(zcuts[:-1] + [None]):
            high = high // 2 if cut else high
            pieces = 2 if cut else 1
            if i:
                jobs = [([now(keep), other], 0, wide, cut, [(k, 0, 0) for k in range(pieces)])]
            else:
                jobs = [
                    ([now(g3[0])] + g3[1:], 0, wide, cut, [(k, 0, 0) for k in range(pieces)]),
                    (g2, 0, wide, cut, [(k, 1, 0) for k in range(pieces)]),
                ]
            keep, *send = fold(ids, [(2, high, wide)] * pieces, jobs)
            other = over_z(*send, cut) if cut else over_z(keep, zcuts[-1])
            yield keep
        (total,) = fold(ids, [keep.shape], [([now(keep), other], 0, wide, None, [(0, 0, 0)])])
        for cut in reversed(zcuts[:-1]):
            other = over_z(total, cut)
            yield total
            total = join(ids, now(total), other, cut)
        pieces = over_y([total] * yn)
        yield total
        done["first"] = unpack(
            unpack_first,
            cut_of_y,
            ids,
            [now(pieces[0])] + pieces[1:],
            [(D, vb), (vb, D), (nb, D), (nb, D), (vb, D)],
        )
        yield done["first"][0]

    def second_chunk():
        small_high = count // 4
        ad_rows = seqs * NDIM

        def payload_rows():
            return (ad_rows + small_high) * runs

        together = half == 2 and yn == 2 and not traded
        if together:
            lanes = D // vb
            own, kept, left, payload, right, send = call(
                functools.partial(start_kernel, seqs, ybits),
                (
                    shape((ad_rows, D)),
                    shape((small_high, D)),
                    shape((D, vb), BF16),
                    shape((D + (ad_rows + small_high) * lanes, vb), BF16),
                    shape((2, D // 2, vb), BF16),
                    shape((2, D // 2, vb), BF16),
                ),
                [],
                (ids, par, now(adjoint), sums_keep, got_sums, keep1, got1),
                [SMEM] + [VMEM] * 6,
                "start",
            )
            other, got_right = swap(payload, 2), swap(send, tp)
            got = [(got_sums, count // 2), (other, D)]
            yield payload
            own, kept, left, payload, right, send = call(
                functools.partial(cross_kernel, seqs, ybits),
                (
                    shape((ad_rows, D)),
                    shape((small_high, D)),
                    shape((D // 2, vb), BF16),
                    shape((D // 2 + (ad_rows + small_high) * lanes, vb), BF16),
                    shape((D // 2, vb), BF16),
                    shape((D // 2, vb), BF16),
                ),
                [],
                (ids, par, now(own), kept, payload, other, left, right, got_right),
                [SMEM] + [VMEM] * 8,
                "cross",
            )
            other, got_right = swap(payload, tp), swap(send, 2)
            level, top, halved = 2, D // 2, False
            flat = [left, right, got_right]
            jobs = [((0, -1), vb, 0), ((1, 2), vb, vb)]
            yield payload
        else:
            own, kept, payload = call(
                functools.partial(first_back_hop, seqs, not traded),
                (
                    shape((ad_rows, D)),
                    shape((small_high, D)),
                    shape((payload_rows(), wide), BF16),
                ),
                [],
                (ids, par, now(adjoint), sums_keep, got_sums),
                [SMEM] + [VMEM] * 4,
                "hop",
            )
            got = [] if traded else [(got_sums, count // 2)]
            level = int(not traded)
            halved = True
            other = swap(payload, masks[level])
            yield payload
            parts = fold(
                ids,
                [(1, D, vb)] * half + [(half, D // yn, vb)] * yn,
                [
                    ([now(keep1), got1], 0, vb, "tp", [(k, 0, 0) for k in range(half)]),
                    ([keep1, got1], vb, vb, cut_of_y, [(half + k, 0, 0) for k in range(yn)]),
                ],
            )
            left, right = over_tp(parts[:half]), over_y(parts[half:])
            yield parts[0]
            crossed = False
            while level + 1 < levels - len(zcuts):
                got.append((other, 0))
                split = 2 * masks[level] if 2 * masks[level] < tp else 0
                small_high = small_high // 2 if split else small_high
                own, kept, payload = call(
                    functools.partial(back_hop, seqs, level, split, halved),
                    (
                        shape((ad_rows, D)),
                        shape((small_high, D)),
                        shape((payload_rows(), wide), BF16),
                    ),
                    [],
                    (ids, par, now(own), kept, payload, other),
                    [SMEM] + [VMEM] * 5,
                    "hop",
                )
                halved = bool(split)
                level += 1
                other = swap(payload, masks[level])
                yield payload
                if crossed:
                    continue
                crossed = True
                parts = fold(
                    ids,
                    [(1, D // yn, vb)] * (yn + half),
                    [
                        ([now(left[0])] + left[1:], 0, vb, cut_of_y, [(k, 0, 0) for k in range(yn)]),
                        (right, 0, vb, "tp", [(yn + k, 0, 0) for k in range(half)]),
                    ],
                )
                left, right = over_y(parts[:yn]), over_tp(parts[yn:])
                yield parts[0]
            top = 0
            flat = [p.reshape(p.shape[1:]) for p in left + right]
            jobs = [
                (tuple(range(len(left))), vb, 0),
                (tuple(range(len(left), len(flat))), vb, vb),
            ]
        high = D // yn
        for cut in zcuts[:-1] + [None]:
            got.append((other, top))
            high = high // 2 if cut else high
            kept_chunk = [shape((high, wide), BF16)] if cut else []
            *flat, kept, own, payload = call(
                functools.partial(
                    ride_kernel, seqs, level, 0, halved, top, jobs, cut, high, False
                ),
                (
                    *kept_chunk,
                    shape((small_high, D)),
                    shape((ad_rows, D)),
                    shape((high + payload_rows(), wide), BF16),
                ),
                [],
                (ids, par, now(own), kept, payload, other, *flat),
                [SMEM] + [VMEM] * (5 + len(flat)),
                "ride",
            )
            halved = False
            level += 1
            top = high
            jobs = [((0 if cut else -2, -1), wide, 0)]
            other = swap(payload, masks[level])
            yield payload
        got.append((other, top))
        total, kept = call(
            functools.partial(ride_kernel, seqs, level, 0, False, top, jobs, None, high, True),
            (shape((high, wide), BF16), shape((small_high, D))),
            [],
            (ids, par, now(own), kept, payload, other, *flat),
            [SMEM] + [VMEM] * (5 + len(flat)),
            "ride",
        )
        bits = list(reversed(bits_of(tp)))
        total = total[None]
        far = swap(kept, bits[0])
        other = over_z(total, zcuts[-2]) if len(zcuts) > 1 else None
        yield total
        (done["tokens"],) = call(
            functools.partial(leave_kernel, seqs, [at for _, at in got]),
            (shape((seqs, CH, D), BF16),),
            [
                pltpu.VMEM((seqs, NDIM, D), F32),
                pltpu.VMEM((NDIM, PIECES, D), F32),
                pltpu.VMEM((BLOCKS, rows, LANES), F32),
            ],
            (
                ids, tok, par, now(grad_skip), grad_normed, behind, resid,
                *[g for g, _ in got],
            ),
            [SMEM] + [VMEM] * (6 + levels),
            "leave",
            limit=10,
        )
        yield done["tokens"]
        for i in range(len(zcuts) - 2, -1, -1):
            total = join(ids, now(total), other, zcuts[i])
            if i:
                other = over_z(total, zcuts[i - 1])
                yield total
        pieces = over_y([total] * yn)
        yield total
        for i in range(len(bits) - 1):
            (kept,) = call(
                functools.partial(pair_kernel, bits[i]),
                (shape((2 * kept.shape[0], D)),),
                [],
                (ids, now(kept), far),
                [SMEM, VMEM, VMEM],
                "pair",
            )
            far = swap(kept, bits[i + 1])
            yield kept
        done["small"] = call(
            finish_kernel,
            (
                shape((1, D)),
                shape((NDIM, D)),
                shape((NDIM, D)),
                shape((NDIM, D)),
                shape((1, D)),
                shape((D, Z)),
                shape((1, Z)),
                shape((1, Z)),
                shape((1, Z)),
                shape((1, D)),
            ),
            [pltpu.VMEM((count, D), F32)],
            (ids, par, rate, beta, now(kept), far),
            [SMEM] + [VMEM] * 5,
            "finish",
        )
        yield done["small"][0]
        done["second"] = unpack(
            unpack_sides, cut_of_y, ids, [now(pieces[0])] + pieces[1:], [(D, vb), (D, vb)]
        )
        yield done["second"][0]

    walks = {"f": first_chunks(), "s": second_chunk()}
    order = "sfsfssffssssfss"

    def advance(name):
        try:
            last[0] = next(walks[name])
        except StopIteration:
            del walks[name]

    for name in order:
        if name in walks:
            advance(name)
    while walks:
        for name in list(walks):
            advance(name)

    grad_w_in, grad_w_out, grad_w_hidden, grad_w_update, grad_u_hidden = done["first"]
    grad_w_value, grad_w_reset = done["second"]
    firsts = [
        small.T if small.shape[0] == NDIM else small[0] if small.shape[0] == 1 else small
        for small in done["small"]
    ]
    grad_norm2_gain = firsts.pop()
    return (
        trade_back(out.reshape(seqs, CH, D)),
        trade_back(done["tokens"]),
        *firsts,
        grad_w_value,
        grad_w_reset,
        grad_w_update,
        grad_w_hidden,
        grad_u_hidden,
        grad_norm2_gain,
        grad_w_in,
        grad_w_out,
    )


def solution(mesh):
    rows = P(None, ("seq", "tp"), None)
    cols = P(None, "tp")
    tall = P("tp", None)
    whole = P()
    return jax.shard_map(
        per_device,
        mesh=mesh,
        in_specs=(rows, rows) + (whole,) * 10 + (cols, cols, tall, tall, tall, whole, cols, tall),
        out_specs=(rows, rows) + (whole,) * 9 + (cols, cols, tall, tall, tall, whole, cols, tall),
        check_vma=False,
    )
```

```python
import functools

import jax
import jax.numpy as jnp
from jax import lax
from jax.experimental import pallas as pl
from jax.experimental.pallas import tpu as pltpu
from jax.sharding import PartitionSpec as P

D = 512
Z = 128
NDIM = 16
CH = 128
PIECE = 16
PIECES = CH // PIECE
LANES = 128
BLOCKS = D // LANES
EPS = 1e-05
F32 = jnp.float32
BF16 = jnp.bfloat16
SMALL_ROWS = 64

VMEM = pl.BlockSpec(memory_space=pltpu.VMEM)
SMEM = pl.BlockSpec(memory_space=pltpu.SMEM)
ANY = pl.BlockSpec(memory_space=pl.ANY)


def sigmoid(v):
    return 0.5 * jnp.tanh(0.5 * v) + 0.5


def silu(v):
    return v * sigmoid(v)


def silu_slope(v):
    s = sigmoid(v)
    return s * (1.0 + v * (1.0 - s))


def mm(a, b):
    return jnp.dot(a, b, preferred_element_type=F32)


def mm_nt(a, b):
    return lax.dot_general(a, b, (((1,), (1,)), ((), ())), preferred_element_type=F32)


def mm_tn(a, b):
    return lax.dot_general(a, b, (((0,), (0,)), ((), ())), preferred_element_type=F32)


def normalized(v):
    center = v - jnp.mean(v, axis=-1, keepdims=True)
    scale = lax.rsqrt(jnp.mean(center * center, axis=-1, keepdims=True) + EPS)
    return center * scale, scale


def norm_back(grad, xhat, scale, gain):
    full = grad * gain
    return scale * (
        full
        - jnp.mean(full, axis=-1, keepdims=True)
        - xhat * jnp.mean(full * xhat, axis=-1, keepdims=True)
    )


def rows_of(s):
    return pl.ds(s * CH, CH)


def lanes_of(i):
    return pl.ds(pl.multiple_of((i % BLOCKS) * LANES, LANES), LANES)


def spread(row):
    return jnp.broadcast_to(row, (PIECES, LANES))


def piece_rows(s, t):
    return pl.ds(s * CH + t, PIECES, stride=PIECE)


def put_rows(ref, rows, value):
    for b in range(BLOCKS):
        ref[b, rows, :] = value[:, b * LANES : (b + 1) * LANES]


def get_rows(ref, rows):
    return jnp.concatenate([ref[b, rows, :] for b in range(BLOCKS)], axis=1)


class Here:
    def __init__(self, seqs, lengths):
        self.seqs, self.lengths = seqs, lengths

    def __getitem__(self, i):
        if i == 0:
            return lax.axis_index("tp")
        if i == 1:
            return lax.axis_index("seq")
        if i == 2:
            index = lax.axis_index("seq") * lax.axis_size("tp") + lax.axis_index("tp")
            return index if self.seqs > 1 else jnp.right_shift(index, 1)
        return self.lengths[i - 3 if self.seqs > 1 else jnp.bitwise_and(lax.axis_index("tp"), 1)]


def call(body, out, scratch, operands, specs, name, limit=2, outs=None):
    place = operands[0]
    if isinstance(place, Here):
        kernel = body
        if place.lengths is None:
            operands, specs = operands[1:], specs[1:]
            body = lambda *refs: kernel(place, *refs)
        else:
            operands = (place.lengths, *operands[1:])
            body = lambda lengths, *refs: kernel(Here(place.seqs, lengths), *refs)
    return pl.pallas_call(
        body,
        out_shape=out,
        in_specs=specs,
        out_specs=outs or jax.tree.map(lambda _: VMEM, out),
        scratch_shapes=scratch,
        name=name,
        compiler_params=pltpu.CompilerParams(vmem_limit_bytes=int(limit * 1024 * 1024)),
    )(*operands)


def shape(dims, dtype=F32):
    return jax.ShapeDtypeStruct(dims, dtype)


def put_low(low, pairs):
    for i in range(0, len(pairs), 2):
        high = pairs[i].astype(BF16)
        low[3 * i // 2] = high
        low[3 * i // 2 + 1] = (pairs[i] - high.astype(F32)).astype(BF16)
        low[3 * i // 2 + 2] = pairs[i + 1].astype(BF16)


def get_low(low, s):
    high, rest, slope = (low[3 * s + i].astype(F32) for i in range(3))
    return high + rest, slope


def enter_kernel(seqs, ids, *refs):
    count = 10
    far, near, sems = refs[:count], refs[count + 5 : 2 * count + 5], refs[-1]
    normed, par, before, ends, low = refs[count : count + 5]
    tok, gain, rate, beta, eta, skip, gain2, qg, kg, rb, nf, tab = refs[count + 5 : -1]
    copies = [pltpu.make_async_copy(a, b, sems.at[i]) for i, (a, b) in enumerate(zip(far, near))]
    for c in copies:
        c.start()
    for c in copies:
        c.wait()
    r = rate[...]
    d = 1.0 - r
    par[0] = d
    par[1] = jnp.log(d)
    par[2] = jnp.sqrt(r * (2.0 - r)) * beta[...]
    par[3] = eta[...]
    for i, row in enumerate((skip, gain2, gain)):
        par[4, i : i + 1, :] = row[...]
    for i, row in enumerate((qg, kg, rb)):
        par[4, 3:4, i * Z : (i + 1) * Z] = row[...]
    for s in range(seqs):
        par[4, 4 + s : 5 + s, :] = jnp.full((1, D), ids[3 + s].astype(F32))
    d2 = d * d
    d4 = d2 * d2
    d8 = d4 * d4
    d15 = d8 * d4 * d2 * d
    q = d8 * d8
    tab[0] = q
    tab[1] = 16.0 * d15
    tab[2] = q * q
    tab[3] = 32.0 * q * d15
    tab[4] = q * q * q * q
    tab[5] = 64.0 * q * q * q * d15
    for s in range(seqs):
        xhat, _ = normalized(tok[s].astype(F32))
        scaled = (xhat * gain[...]).astype(BF16)
        normed[rows_of(s), :] = scaled
        put_rows(nf, rows_of(s), scaled.astype(F32))
    place = lax.broadcasted_iota(jnp.int32, (PIECES, LANES), 0)

    def body(i, carry):
        s = i // BLOCKS
        lane = lanes_of(i)
        xs = [nf[i % BLOCKS, piece_rows(s, t), :] for t in range(PIECE)]
        for j0 in range(0, NDIM, 8):
            ds = [spread(par[0, j0 + j : j0 + j + 1, lane]) for j in range(8)]
            st = [xs[0]] * 8
            ta = [jnp.zeros((PIECES, LANES), F32)] * 8
            for t in range(1, PIECE):
                for j in range(8):
                    ta[j] = ds[j] * ta[j] + st[j]
                    st[j] = ds[j] * st[j] + xs[t]
            for j in range(8):
                a, b = st[j], ta[j]
                for k, step in enumerate((1, 2, 4)):
                    qm = spread(tab[2 * k, j0 + j : j0 + j + 1, lane])
                    rm = spread(tab[2 * k + 1, j0 + j : j0 + j + 1, lane])
                    sa = jnp.where(place >= step, pltpu.roll(a, step, 0), 0.0)
                    sb = jnp.where(place >= step, pltpu.roll(b, step, 0), 0.0)
                    b = b + qm * sb + rm * sa
                    a = a + qm * sa
                before[0, s, j0 + j, :, lane] = jnp.where(place >= 1, pltpu.roll(a, 1, 0), 0.0)
                before[1, s, j0 + j, :, lane] = jnp.where(place >= 1, pltpu.roll(b, 1, 0), 0.0)
                ends[2 * s, j0 + j : j0 + j + 1, lane] = a[PIECES - 1 :]
                ends[2 * s + 1, j0 + j : j0 + j + 1, lane] = b[PIECES - 1 :]
        return carry

    lax.fori_loop(0, seqs * BLOCKS, body, 0)
    ends[2 * seqs] = par[1]
    put_low(low, [ends[i] for i in range(2 * seqs)])


def pack_kernel(
    w_value, w_reset, w_hidden, w_update, u_hidden, w_in, w_out, p1, p2, p3, h2, h3, sems
):
    copies = []

    def add(source, target):
        copies.append(pltpu.make_async_copy(source, target, sems.at[len(copies)]))

    vb, cut = w_value.shape[1], D // 2
    upper = jnp.bitwise_and(lax.axis_index("seq"), 1) * cut
    at = pl.ds(pl.multiple_of(upper, cut), cut)
    for i, w in enumerate((w_value, w_reset)):
        add(w, p1.at[:, pl.ds(i * vb, vb)])
    far = jnp.bitwise_and(jnp.right_shift(lax.axis_index("seq"), far_shift()), 1) * cut
    top = 0
    for w in (w_hidden, w_update, u_hidden):
        row = pl.ds(top, w.shape[0])
        add(w.at[:, pl.ds(pl.multiple_of(far, cut), cut)], h2.at[row, :])
        add(w, p2.at[row, :])
        top += w.shape[0]
    add(w_in.at[at, :], h3.at[:, pl.ds(0, vb)])
    add(w_in, p3.at[:, pl.ds(0, vb)])
    for k in range(D // vb):
        row = pl.ds(k * vb, vb)
        add(w_out.at[:, row], p3.at[row, pl.ds(vb, vb)])
        if k < cut // vb:
            lane = pl.ds(pl.multiple_of(upper + k * vb, vb), vb)
            add(w_out.at[:, lane], h3.at[row, pl.ds(vb, vb)])
    for c in copies:
        c.start()
    for c in copies:
        c.wait()


def vectors(par):
    whole = [par.at[4, pl.ds(i, 1), :] for i in range(3)]
    return whole + [par.at[4, pl.ds(3, 1), pl.ds(i * Z, Z)] for i in range(3)]


def piece_powers(par, pw):
    k = lax.broadcasted_iota(jnp.int32, (PIECES, D), 0).astype(F32) * PIECE
    for j in range(NDIM):
        pw[j] = jnp.exp(k * par[1, j : j + 1, :])


def take_weights(refs, tp, first, second):
    top = tp // 2
    near = [refs[r * first : (r + 1) * first] for r in range(top)]
    refs = refs[top * first :]
    far = [refs[r * second : (r + 1) * second] for r in range(top)]
    return near, far, refs[top * second :]


def far_shift():
    return (lax.axis_size("seq").bit_length() - 1) // 2


def gate_copies(tp, ids, near, far, w1, w2, sems):
    top, cut = tp // 2, D // 2
    first = jnp.bitwise_and(ids[1], 1)
    second = jnp.bitwise_and(jnp.right_shift(ids[1], far_shift()), 1)
    copies = [[] for _ in range(tp)]

    def add(r, source, target):
        at = sems.at[sum(len(c) for c in copies)]
        copies[r].append(pltpu.make_async_copy(source, target, at))

    for r in range(top):
        add(r, near[r][0], w1.at[r])
        add(r, near[r][1], w2.at[r])
    for r in range(top):
        mine1, other1, mine2, other2 = far[r]
        for part, at in ((mine1, first), (other1, 1 - first)):
            add(top + r, part, w1.at[top + r, pl.ds(pl.multiple_of(at * cut, cut), cut), :])
        for part, at in ((mine2, second), (other2, 1 - second)):
            add(top + r, part, w2.at[top + r, :, pl.ds(pl.multiple_of(at * cut, cut), cut)])
    for group in copies:
        for c in group:
            c.start()
    return copies


def gate_rows(tp, me, w2, whu):
    nb = D // tp
    for r in range(tp):
        row = pl.ds(pl.multiple_of(jnp.bitwise_xor(me, r) * nb, nb), nb)
        whu[row, pl.ds(0, D)] = w2[r, pl.ds(0, nb), :]
        whu[row, pl.ds(D, D)] = w2[r, pl.ds(nb, nb), :]


def look_kernel(
    seqs, hops, ids, normed, par, before, wsh, *refs
):
    recvs, refs = refs[: len(hops)], refs[len(hops) :]
    st_in, skip_pre, mixed, shared_pre, prob, nf, sm, pw = refs
    skip, _, _, qg, kg, rb = vectors(par)
    place = ids[2]
    put_rows(nf, slice(None), normed[...].astype(F32))
    piece_powers(par, pw)
    logd = par[1]
    dinv = 1.0 / par[0]
    for s in range(seqs):
        a = jnp.zeros((NDIM, D), F32)
        b = jnp.zeros((NDIM, D), F32)
        for (shift, k), got in zip(hops, recvs):
            end = jnp.left_shift(jnp.bitwise_xor(jnp.right_shift(place, shift), k) + 1, shift)
            off = (place - end).astype(F32) * float(CH)
            power = jnp.where(place >= end, jnp.exp(jnp.maximum(off, 0.0) * logd), 0.0)
            oa, ob = (part * power for part in get_low(got, s))
            b = b + ob + off * oa * dinv
            a = a + oa
        st_in[0, s] = a
        st_in[1, s] = b

    def ema(i, carry):
        s = i // BLOCKS
        lane = lanes_of(i)
        row = [pl.ds(j, 1) for j in range(NDIM)]
        ds = [spread(par[0, row[j], lane]) for j in range(NDIM)]
        ws = [spread(par[2, row[j], lane] * par[3, row[j], lane]) for j in range(NDIM)]
        st = [
            before[0, s, j, :, lane] + pw[j, :, lane] * st_in[0, s, row[j], lane]
            for j in range(NDIM)
        ]
        for t in range(PIECE):
            x = nf[i % BLOCKS, piece_rows(s, t), :]
            parts = [None, None]
            for j in range(NDIM):
                st[j] = ds[j] * st[j] + x
                term = ws[j] * st[j]
                parts[j % 2] = term if parts[j % 2] is None else parts[j % 2] + term
            sm[i % BLOCKS, piece_rows(s, t), :] = parts[0] + parts[1]
        return carry

    lax.fori_loop(0, seqs * BLOCKS, ema, 0)
    for s in range(seqs):
        pre = get_rows(sm, rows_of(s)) + skip[...] * get_rows(nf, rows_of(s))
        skip_pre[rows_of(s), :] = pre
        mixed[rows_of(s), :] = silu(pre).astype(BF16)
    sp = mm(mixed[...], wsh[...])
    shared_pre[...] = sp
    shared = silu(sp)
    query = (shared * qg[...]).astype(BF16)
    keys = (shared * kg[...]).astype(BF16)
    t_at = lax.broadcasted_iota(jnp.int32, (CH, CH), 0)
    s_at = lax.broadcasted_iota(jnp.int32, (CH, CH), 1)
    bias_t = jnp.broadcast_to(rb[...], (CH, CH))
    for bit in range(7):
        bias_t = jnp.where(
            jnp.bitwise_and(t_at, 1 << bit) > 0, pltpu.roll(bias_t, 1 << bit, 1), bias_t
        )
    bias = bias_t.T
    for s in range(seqs):
        raw = mm_nt(query[s * CH : (s + 1) * CH], keys[s * CH : (s + 1) * CH]) * Z ** (-0.5)
        live = (place * CH + s_at).astype(F32) < par[4, 4 + s : 5 + s, :CH]
        allowed = (s_at <= t_at) & (live | (s_at == t_at))
        masked = jnp.where(allowed, raw + bias, -1e30)
        top = jnp.max(masked, axis=-1, keepdims=True)
        weights = jnp.where(allowed, jnp.exp(masked - top), 0.0)
        prob[s] = weights / jnp.sum(weights, axis=-1, keepdims=True)


def mix_kernel(seqs, tp, ids, tok, normed, mixed, prob, *refs):
    near, far, refs = take_weights(refs, tp, 2, 4)
    (
        values, value_pre, reset_pre, attended, gated, hidden_pre, update_pre, middle,
        w1, w2, whu, sems,
    ) = refs
    vb = values.shape[2]
    nb = D // tp
    copies = gate_copies(tp, ids, near, far, w1, w2, sems)
    for r in range(tp):
        for c in copies[r]:
            c.wait()
        vp = mm(normed[...], w1[r, :, :vb])
        value_pre[r] = vp
        v = silu(vp).astype(BF16)
        values[r] = v
        rp = mm(mixed[...], w1[r, :, vb:])
        reset_pre[r] = rp
        gate = silu(rp)
        for s in range(seqs):
            att = mm(prob[s].astype(BF16), v[s * CH : (s + 1) * CH])
            attended[r, rows_of(s), :] = att
            gated[r, rows_of(s), :] = (gate[s * CH : (s + 1) * CH] * att).astype(BF16)
        part = mm(gated[r], w2[r, pl.ds(2 * nb, vb), :])
        hidden_pre[...] = hidden_pre[...] + part if r else part
    gate_rows(tp, ids[0], w2, whu)
    hu = mm(mixed[...], whu[...])
    hidden_pre[...] += hu[:, :D]
    update_pre[...] = hu[:, D:]
    for s in range(seqs):
        x = tok[s].astype(F32)
        middle[rows_of(s), :] = x + sigmoid(update_pre[rows_of(s), :]) * (
            silu(hidden_pre[rows_of(s), :]) - x
        )


def ffn_kernel(seqs, tp, ids, tok, cot, middle, hidden_pre, update_pre, par, *refs):
    gain2 = vectors(par)[1]
    near, far, refs = take_weights(refs, tp, 1, 2)
    (
        out, keep, send, grad_hu, resid, grad_gain2,
        w3, n2, lg, acc, gn2, sems,
    ) = refs
    vb = w3.shape[2] // 2
    top, half = tp // 2, D // 2
    cuts = D // vb
    upper = jnp.bitwise_and(ids[1], 1)
    copies = [[] for _ in range(tp)]

    def add(r, source, target):
        at = sems.at[sum(len(c) for c in copies)]
        copies[r].append(pltpu.make_async_copy(source, target, at))

    for r in range(top):
        add(r, near[r][0], w3.at[r])
    for r in range(top):
        for part, at in zip(far[r], (upper, 1 - upper)):
            row = pl.ds(pl.multiple_of(at * half, half), half)
            add(top + r, part, w3.at[top + r, row, :])
    for group in copies:
        for c in group:
            c.start()
    place = ids[2]
    xhat, scale = normalized(middle[...])
    n2[...] = (xhat * gain2[...]).astype(BF16)
    at = (lax.broadcasted_iota(jnp.int32, (CH, D), 0) + place * CH).astype(F32)
    for s in range(seqs):
        lg[rows_of(s), :] = jnp.where(
            at < par[4, 4 + s : 5 + s, :], cot[s].astype(F32), 0.0
        ).astype(BF16)
    acc[...] = jnp.zeros_like(acc)
    gn2[...] = jnp.zeros_like(gn2)
    for h in range(tp // 2):
        for odd in range(2):
            r = 2 * h + odd
            for c in copies[r]:
                c.wait()
            grads = (keep, send)[odd]
            pre = mm(n2[...], w3[r, :, :vb])
            inner = silu(pre).astype(BF16)
            back = None
            for k in range(cuts):
                cols = slice(k * vb, (k + 1) * vb)
                w_out = w3[r, cols, vb:]
                acc[:, cols] += mm(inner, w_out)
                term = mm_nt(lg[:, cols], w_out)
                back = term if back is None else back + term
            gip = (back * silu_slope(pre)).astype(BF16)
            gn2[...] += mm_nt(gip, w3[r, :, :vb])
            grads[h, :, :vb] = mm_tn(n2[...], gip).astype(BF16)
            gwo = mm_tn(inner, lg[...]).astype(BF16)
            for k in range(cuts):
                grads[h, k * vb : (k + 1) * vb, vb:] = gwo[:, k * vb : (k + 1) * vb]
    mid = middle[...]
    out[...] = (mid + acc[...]).astype(BF16)
    grad = gn2[...]
    grad_gain2[...] = jnp.sum(grad * xhat, axis=0, keepdims=True)
    gm = lg[...].astype(F32) + norm_back(grad, xhat, scale, gain2[...])
    for s in range(seqs):
        x = tok[s].astype(F32)
        g = gm[s * CH : (s + 1) * CH]
        hp = hidden_pre[rows_of(s), :]
        update = sigmoid(update_pre[rows_of(s), :])
        grad_hu[rows_of(s), :D] = (g * update * silu_slope(hp)).astype(BF16)
        grad_hu[rows_of(s), D:] = (g * (silu(hp) - x) * update * (1.0 - update)).astype(BF16)
        resid[rows_of(s), :] = g * (1.0 - update)


def gates_kernel(tp, ids, mixed, gated, grad_hu, keep2, send2, ghu):
    nb = D // tp
    vb = gated.shape[2]
    wide = 2 * vb
    me = ids[0]
    ghu[...] = mm_tn(mixed[...], grad_hu[...])

    def block(h, carry):
        for odd in range(2):
            r = 2 * h + odd
            g2 = (keep2, send2)[odd]
            row = pl.ds(pl.multiple_of(jnp.bitwise_xor(me, r) * nb, nb), nb)
            gu = mm_tn(gated[r], grad_hu[:, :D]).astype(BF16)
            for k in range(D // wide):
                top = k * (2 * nb + vb)
                g2[h, pl.ds(top, nb), :] = ghu[row, pl.ds(k * wide, wide)].astype(BF16)
                g2[h, pl.ds(top + nb, nb), :] = ghu[row, pl.ds(D + k * wide, wide)].astype(BF16)
                g2[h, pl.ds(top + 2 * nb, vb), :] = gu[:, k * wide : (k + 1) * wide]
        return carry

    lax.fori_loop(0, tp // 2, block, 0)


def back_kernel(
    seqs, tp,
    ids, normed, mixed, skip_pre, shared_pre, prob, values, value_pre, reset_pre, attended,
    grad_hu, par, wsh, tok, before, st_in, grad_gain2, *refs,
):
    skip, _, _, qg, kg, _ = vectors(par)
    near, far, refs = take_weights(refs, tp, 2, 4)
    (
        keep1, send1, grad_skip, grad_normed, after, ends, sums_keep, sums_send,
        w1, w2, whu, gm, gp, tab, grad_wsh, misc, table, nf, pw, sems,
    ) = refs
    vb = values.shape[2]
    nb = D // tp
    me = ids[0]
    copies = gate_copies(tp, ids, near, far, w1, w2, sems)
    gp[...] = jnp.zeros_like(gp)
    grad_normed[...] = jnp.zeros_like(grad_normed)
    for group in copies:
        for c in group:
            c.wait()
    gate_rows(tp, me, w2, whu)
    gm[...] = mm_nt(grad_hu[...], whu[...])

    def block(h, carry):
        for odd in range(2):
            r = 2 * h + odd
            g1 = (keep1, send1)[odd]
            gg = mm_nt(grad_hu[:, :D], w2[r, pl.ds(2 * nb, vb), :])
            rp = reset_pre[r]
            sig = sigmoid(rp)
            ga = (gg * (rp * sig)).astype(BF16)
            grp = (gg * attended[r] * (sig * (1.0 + rp * (1.0 - sig)))).astype(BF16)
            g1[h, :, vb:] = mm_tn(mixed[...], grp).astype(BF16)
            gm[...] += mm_nt(grp, w1[r, :, vb:])
            gvs = []
            for s in range(seqs):
                part = ga[s * CH : (s + 1) * CH]
                gvs.append(mm_tn(prob[s].astype(BF16), part))
                gp[s] += mm_nt(part, values[r, rows_of(s), :])
            gv = jnp.concatenate(gvs, axis=0) if seqs > 1 else gvs[0]
            gvp = (gv * silu_slope(value_pre[r])).astype(BF16)
            g1[h, :, :vb] = mm_tn(normed[...], gvp).astype(BF16)
            grad_normed[...] += mm_nt(gvp, w1[r, :, :vb])
        return carry

    lax.fori_loop(0, tp // 2, block, 0)
    sp = shared_pre[...]
    shared = silu(sp)
    query = (shared * qg[...]).astype(BF16)
    keys = (shared * kg[...]).astype(BF16)
    total = jnp.zeros((CH, CH), F32)
    gqs = []
    gks = []
    for s in range(seqs):
        pr = prob[s]
        low = (pr * (gp[s] - jnp.sum(pr * gp[s], axis=-1, keepdims=True))).astype(BF16)
        total = total + low.astype(F32)
        gqs.append(mm(low, keys[s * CH : (s + 1) * CH]) * Z ** (-0.5))
        gks.append(mm_tn(low, query[s * CH : (s + 1) * CH]) * Z ** (-0.5))
    gq = jnp.concatenate(gqs, axis=0) if seqs > 1 else gqs[0]
    gk = jnp.concatenate(gks, axis=0) if seqs > 1 else gks[0]
    turned = total.T
    s_at = lax.broadcasted_iota(jnp.int32, (CH, CH), 0)
    for bit in range(7):
        turned = jnp.where(
            jnp.bitwise_and(s_at, 1 << bit) > 0, pltpu.roll(turned, CH - (1 << bit), 1), turned
        )
    misc[...] = jnp.concatenate(
        [
            jnp.sum(gq * shared, axis=0, keepdims=True),
            jnp.sum(gk * shared, axis=0, keepdims=True),
            jnp.sum(turned, axis=0, keepdims=True),
            jnp.zeros((1, D - 3 * Z), F32),
        ],
        axis=1,
    )
    gsp = ((gq * qg[...] + gk * kg[...]) * silu_slope(sp)).astype(BF16)
    grad_wsh[...] = mm_tn(mixed[...], gsp)
    put_rows(
        grad_skip,
        slice(None),
        (gm[...] + mm_nt(gsp, wsh[...])) * silu_slope(skip_pre[...]),
    )
    d = par[0]
    d2 = d * d
    d4 = d2 * d2
    d8 = d4 * d4
    q = d8 * d8
    tab[0] = q
    tab[1] = q * q
    tab[2] = q * q * q * q
    place = lax.broadcasted_iota(jnp.int32, (PIECES, LANES), 0)

    def body(i, carry):
        s = i // BLOCKS
        lane = lanes_of(i)
        ds = [spread(par[0, j : j + 1, lane]) for j in range(NDIM)]
        ad = [grad_skip[i % BLOCKS, piece_rows(s, PIECE - 1), :]] * NDIM
        for t in range(PIECE - 2, -1, -1):
            g = grad_skip[i % BLOCKS, piece_rows(s, t), :]
            for j in range(NDIM):
                ad[j] = ds[j] * ad[j] + g
        for j in range(NDIM):
            a = ad[j]
            for k, step in enumerate((1, 2, 4)):
                qm = spread(tab[k, j : j + 1, lane])
                a = a + qm * jnp.where(place < PIECES - step, pltpu.roll(a, PIECES - step, 0), 0.0)
            after[s, j, :, lane] = jnp.where(
                place < PIECES - 1, pltpu.roll(a, PIECES - 1, 0), 0.0
            )
            ends[s, j : j + 1, lane] = a[:1]
        return carry

    lax.fori_loop(0, seqs * BLOCKS, body, 0)
    small_sums(
        seqs, ids, tok, normed, grad_skip, grad_normed, par, before, st_in, skip, grad_gain2, misc,
        grad_wsh, sums_keep, sums_send, table, nf, pw,
    )
    for s in range(seqs):
        sums_send[pl.ds(sums_keep.shape[0] + s * NDIM, NDIM), :] = ends[s]


def small_sums(
    seqs, ids, tok, normed, grad_skip, grad_normed, par, before, st_in, skip, gain2_row, misc, grad_wsh,
    keep, send, table, nf, pw,
):
    put_rows(nf, slice(None), normed[...].astype(F32))
    piece_powers(par, pw)
    count = D // (D // Z)
    small = table.at[count:, :]
    small[...] = jnp.zeros_like(small)
    for k in range(D // Z):
        table[:count, k * Z : (k + 1) * Z] = grad_wsh[k * count : (k + 1) * count, :]

    def body(i, carry):
        s = i // BLOCKS
        lane = lanes_of(i)
        k16 = lax.broadcasted_iota(jnp.int32, (PIECES, LANES), 0).astype(F32) * PIECE
        for j0 in range(0, NDIM, 8):
            row = [pl.ds(j0 + j, 1) for j in range(8)]
            ds = [spread(par[0, row[j], lane]) for j in range(8)]
            st, ta, q, r = [], [], [], []
            for j in range(8):
                e = pw[j0 + j, :, lane] * st_in[0, s, row[j], lane]
                st.append(before[0, s, j0 + j, :, lane] + e)
                ta.append(
                    before[1, s, j0 + j, :, lane]
                    + pw[j0 + j, :, lane] * st_in[1, s, row[j], lane]
                    + k16 * e / ds[j]
                )
                q.append(jnp.zeros((PIECES, LANES), F32))
                r.append(jnp.zeros((PIECES, LANES), F32))
            for t in range(PIECE):
                x = nf[i % BLOCKS, piece_rows(s, t), :]
                g = grad_skip[i % BLOCKS, piece_rows(s, t), :]
                for j in range(8):
                    ta[j] = ds[j] * ta[j] + st[j]
                    st[j] = ds[j] * st[j] + x
                    q[j] = q[j] + g * st[j]
                    r[j] = r[j] + g * ta[j]
            for j in range(8):
                small[pl.ds(j0 + j, 1), lane] += jnp.sum(q[j], axis=0, keepdims=True)
                small[pl.ds(NDIM + j0 + j, 1), lane] += jnp.sum(r[j], axis=0, keepdims=True)
        return carry

    lax.fori_loop(0, seqs * BLOCKS, body, 0)
    gsk = jnp.zeros((1, D), F32)
    gn1 = jnp.zeros((1, D), F32)
    for s in range(seqs):
        xhat, _ = normalized(tok[s].astype(F32))
        g = get_rows(grad_skip, rows_of(s))
        direct = g * skip[...] + grad_normed[rows_of(s), :]
        gsk = gsk + jnp.sum(g * get_rows(nf, rows_of(s)), axis=0, keepdims=True)
        gn1 = gn1 + jnp.sum(direct * xhat, axis=0, keepdims=True)
    small[2 * NDIM : 2 * NDIM + 1, :] = gsk
    small[2 * NDIM + 1 : 2 * NDIM + 2, :] = gn1
    small[2 * NDIM + 2 : 2 * NDIM + 3, :] = gain2_row[...]
    small[2 * NDIM + 3 : 2 * NDIM + 4, :] = misc[...]
    half = keep.shape[0]
    mine = jnp.bitwise_and(ids[0], 1) * half
    keep[...] = table[pl.ds(pl.multiple_of(mine, 8), half), :]
    send[pl.ds(0, half), :] = table[pl.ds(pl.multiple_of(half - mine, 8), half), :]


def pair_kernel(bit, ids, mine, other, out):
    half = mine.shape[0]
    upper = jnp.where(jnp.bitwise_and(ids[0], bit) > 0, half, 0)
    out[pl.ds(pl.multiple_of(upper, 8), half), :] = mine[...]
    out[pl.ds(pl.multiple_of(half - upper, 8), half), :] = other[...]


def finish_kernel(
    ids, par, rate, beta, mine, other,
    grad_gain, grad_rate, grad_beta, grad_eta, grad_skip, grad_wsh, grad_qg, grad_kg, grad_rb,
    grad_gain2, table,
):
    gain = vectors(par)[2]
    pair_kernel(1, ids, mine, other, table)
    count = D // (D // Z)
    for k in range(D // Z):
        grad_wsh[k * count : (k + 1) * count, :] = table[:count, k * Z : (k + 1) * Z]
    small = table.at[count:, :]
    inflow, eta, r = par[2], par[3], rate[...]
    root = jnp.sqrt(r * (2.0 - r))
    q_sum = small[:NDIM, :]
    grad_inflow = eta * q_sum
    grad_decay = eta * inflow * small[NDIM : 2 * NDIM, :]
    grad_rate[...] = grad_inflow * beta[...] * (1.0 - r) / root - grad_decay
    grad_beta[...] = grad_inflow * root
    grad_eta[...] = inflow * q_sum
    row = [small[2 * NDIM + i : 2 * NDIM + i + 1, :] for i in range(4)]
    grad_skip[...] = row[0]
    grad_gain[...] = row[1] + jnp.sum(inflow * grad_inflow, axis=0, keepdims=True) / gain[...]
    grad_gain2[...] = row[2]
    grad_qg[...] = row[3][:, :Z]
    grad_kg[...] = row[3][:, Z : 2 * Z]
    grad_rb[...] = row[3][:, 2 * Z : 3 * Z]


def leave_kernel(
    seqs, tops, ids, tok, par, grad_skip, grad_normed, behind, resid, *refs
):
    levels = len(tops)
    recvs, refs = refs[:levels], refs[levels:]
    grad_tokens, ad_in, pw, sm = refs
    skip, _, gain = vectors(par)[:3]
    place = ids[2]
    logd = par[1]
    gots = [get_wide(recvs[k], tops[k], seqs * NDIM) for k in range(levels)]
    for s in range(seqs):
        a = jnp.zeros((NDIM, D), F32)
        for k in range(levels):
            low = jnp.bitwise_and(place, 1 << k) == 0
            off = jnp.bitwise_and(place, (1 << k) - 1)
            away = ((1 << k) - 1 - off).astype(F32) * float(CH)
            got = gots[k][s * NDIM : (s + 1) * NDIM]
            a = a + got * jnp.where(low, jnp.exp(away * logd), 0.0)
        ad_in[s] = a
    k = (PIECES - 1 - lax.broadcasted_iota(jnp.int32, (PIECES, D), 0)).astype(F32) * PIECE
    for j in range(NDIM):
        pw[j] = jnp.exp(k * par[1, j : j + 1, :])

    def body(i, carry):
        s = i // BLOCKS
        lane = lanes_of(i)
        row = [pl.ds(j, 1) for j in range(NDIM)]
        ds = [spread(par[0, row[j], lane]) for j in range(NDIM)]
        ws = [spread(par[2, row[j], lane] * par[3, row[j], lane]) for j in range(NDIM)]
        ad = [
            behind[s, j, :, lane] + pw[j, :, lane] * ad_in[s, row[j], lane] for j in range(NDIM)
        ]
        for t in range(PIECE - 1, -1, -1):
            g = grad_skip[i % BLOCKS, piece_rows(s, t), :]
            parts = [None, None]
            for j in range(NDIM):
                ad[j] = ds[j] * ad[j] + g
                term = ws[j] * ad[j]
                parts[j % 2] = term if parts[j % 2] is None else parts[j % 2] + term
            sm[i % BLOCKS, piece_rows(s, t), :] = parts[0] + parts[1]
        return carry

    lax.fori_loop(0, seqs * BLOCKS, body, 0)
    for s in range(seqs):
        xhat, scale = normalized(tok[s].astype(F32))
        grad = (
            get_rows(sm, rows_of(s))
            + get_rows(grad_skip, rows_of(s)) * skip[...]
            + grad_normed[rows_of(s), :]
        )
        grad_tokens[s] = (
            resid[rows_of(s), :] + norm_back(grad, xhat, scale, gain[...])
        ).astype(BF16)


def hop_kernel(seqs, shift, count, ids, state, *refs):
    others, (total, low) = refs[: count - 1], refs[count - 1 :]
    mine = jnp.bitwise_and(jnp.right_shift(ids[2], shift), count - 1)
    logd = state[2 * seqs]
    total[2 * seqs] = logd
    sums = [None] * (2 * seqs)
    for k in range(count):
        after = (count - 1 - jnp.bitwise_xor(mine, k)).astype(F32) * float(CH << shift)
        power = jnp.exp(after * logd)
        slope = after * jnp.exp((after - 1.0) * logd)
        for s in range(seqs):
            part = get_low(others[k - 1], s) if k else (state[2 * s], state[2 * s + 1])
            a, b = power * part[0], power * part[1] + slope * part[0]
            sums[2 * s : 2 * s + 2] = [sums[2 * s] + a, sums[2 * s + 1] + b] if k else [a, b]
    for i in range(2 * seqs):
        total[i] = sums[i]
    put_low(low, sums)


def put_wide(ref, top, value):
    wide = ref.shape[1]
    count = value.shape[0]
    for k in range(D // wide):
        ref[pl.ds(top + k * count, count), :] = value[:, k * wide : (k + 1) * wide].astype(ref.dtype)


def get_wide(ref, top, count):
    wide = ref.shape[1]
    runs = [ref[pl.ds(top + k * count, count), :].astype(F32) for k in range(D // wide)]
    return jnp.concatenate(runs, axis=1) if len(runs) > 1 else runs[0]


def first_back_hop(seqs, joins, ids, par, own, sums, got, out, keep, payload):
    rows = seqs * NDIM
    fold_lanes = D // payload.shape[1]
    if joins:
        join_adjoint(seqs, 0, ids, par, own, got[pl.ds(sums.shape[0], rows), :], out)
    else:
        out[...] = own[...]
    put_wide(payload, 0, out[...])
    half = keep.shape[0]
    upper = jnp.where(jnp.bitwise_and(ids[0], 2) > 0, half, 0)
    mine = pl.ds(pl.multiple_of(upper, 8), half)
    theirs = pl.ds(pl.multiple_of(half - upper, 8), half)
    keep[...] = sums[mine, :] + got[mine, :]
    put_wide(payload, rows * fold_lanes, sums[theirs, :] + got[theirs, :])


def join_adjoint(seqs, level, ids, par, own, got, out):
    upper = jnp.bitwise_and(ids[2], 1 << level) > 0
    power = jnp.exp(float(CH << level) * par[1])
    for s in range(seqs):
        row = slice(s * NDIM, (s + 1) * NDIM)
        early = jnp.where(upper, got[row], own[row, :])
        late = jnp.where(upper, own[row, :], got[row])
        out[row, :] = early + power * late


def chain_hop(seqs, level, split, halved, top, ids, par, own, kept, sent, other, out, keep, payload, base):
    rows = seqs * NDIM
    lanes = D // other.shape[1]
    small_base = 0 if payload is None else base + rows * (D // payload.shape[1])
    if out is not None:
        join_adjoint(seqs, level, ids, par, own, get_wide(other, top, rows), out)
        put_wide(payload, base, out[...])
    half = keep.shape[0]
    if split:
        upper = jnp.bitwise_and(ids[0], split) > 0
        got = get_wide(other, top + rows * lanes, 2 * half)
        first, second = kept[:half, :] + got[:half], kept[half:, :] + got[half:]
        keep[...] = jnp.where(upper, second, first)
        put_wide(payload, small_base, jnp.where(upper, first, second))
    else:
        mine = kept[...] if halved else get_wide(sent, top + rows * lanes, half)
        total = mine + get_wide(other, top + rows * lanes, half)
        keep[...] = total
        if payload is not None:
            put_wide(payload, small_base, total)


def back_hop(seqs, level, split, halved, ids, par, own, kept, sent, other, out, keep, payload):
    chain_hop(
        seqs, level, split, halved, 0, ids, par, own, kept, sent, other, out, keep, payload, 0
    )


def split_rows(count, cut, place, k):
    shift, bits = cut
    rows = count >> bits
    sub = jnp.bitwise_and(jnp.right_shift(place, shift), (1 << bits) - 1)
    return pl.multiple_of(jnp.bitwise_xor(sub, k) * rows, rows), rows


def add_rows(parts, start, high, out, top, lane, width, at):
    step = min(64, high)

    def body(i, carry):
        row = pl.ds(pl.multiple_of(start + i * step, step), step)
        total = parts[0][row, lane : lane + width].astype(F32)
        for other in parts[1:]:
            total = total + other[row, lane : lane + width].astype(F32)
        out[pl.ds(pl.multiple_of(top + i * step, 16), step), at : at + width] = total.astype(BF16)
        return carry

    lax.fori_loop(0, high // step, body, 0)


def fold_kernel(jobs, inputs, ids, *refs):
    parts, outs = refs[:inputs], refs[inputs:]
    at = 0
    for count, lane, width, cut, targets in jobs:
        own = parts[at : at + count]
        at += count
        blocks, rows, _ = own[0].shape
        for k, (target, block, offset) in enumerate(targets):
            if cut == "tp":
                ranges, start, high = (k,), 0, rows
            elif cut is None:
                ranges, start, high = range(blocks), 0, rows
            else:
                start, high = split_rows(rows, cut, ids[1], k)
                ranges = range(blocks)
            for to, b in enumerate(ranges):
                add_rows(
                    [p.at[b] for p in own], start, high, outs[target].at[block + to], 0, lane,
                    width, offset,
                )


def fold(ids, shapes, jobs):
    arrays = [a for job in jobs for a in job[0]]
    plan = [(len(job[0]),) + tuple(job[1:]) for job in jobs]
    return call(
        functools.partial(fold_kernel, plan, len(arrays)),
        tuple(shape(dims, BF16) for dims in shapes),
        [],
        (ids, *arrays),
        [SMEM] + [VMEM] * len(arrays),
        "fold",
    )


def join_kernel(cut, ids, mine, other, out):
    blocks, rows, _ = mine.shape
    for k, part in enumerate((mine, other)):
        start, _ = split_rows(2 * rows, cut, ids[1], k)
        for b in range(blocks):
            out[b, pl.ds(pl.multiple_of(start, 16), rows), :] = part[b]


def join(ids, mine, other, cut):
    blocks, rows, lanes = mine.shape
    return call(
        functools.partial(join_kernel, cut),
        (shape((blocks, 2 * rows, lanes), BF16),),
        [],
        (ids, mine, other),
        [SMEM, VMEM, VMEM],
        "join",
    )[0]


def start_kernel(
    seqs, bits, ids, par, own, sums, got, keep1, got1, out, keep, left, payload, right, send
):
    vb = keep1.shape[2] // 2
    for b, target in enumerate((left, payload)):
        add_rows([keep1.at[b], got1.at[b]], 0, D, target, 0, 0, vb, 0)
    for k, target in enumerate((right, send)):
        start, high = split_rows(D, (0, bits), ids[1], k)
        for b in range(2):
            add_rows([keep1.at[b], got1.at[b]], start, high, target.at[b], 0, vb, vb, 0)
    rows, half = seqs * NDIM, keep.shape[0]
    join_adjoint(seqs, 0, ids, par, own, got[pl.ds(2 * half, rows), :], out)
    put_wide(payload, D, out[...])
    upper = jnp.where(jnp.bitwise_and(ids[0], 2) > 0, half, 0)
    mine = pl.ds(pl.multiple_of(upper, 8), half)
    theirs = pl.ds(pl.multiple_of(half - upper, 8), half)
    keep[...] = sums[mine, :] + got[mine, :]
    put_wide(payload, D + rows * (D // vb), sums[theirs, :] + got[theirs, :])


def cross_kernel(
    seqs, bits, ids, par, own, kept, sent, other, left, right, got, out, keep, left_out, payload,
    right_out, send,
):
    vb = left.shape[1]
    for k, target in enumerate((left_out, payload)):
        start, high = split_rows(D, (0, bits), ids[1], k)
        add_rows([left, other], start, high, target, 0, 0, vb, 0)
    for b, target in enumerate((right_out, send)):
        add_rows([right.at[b], got.at[b]], 0, high, target, 0, 0, vb, 0)
    chain_hop(
        seqs, 1, 0, True, D, ids, par, own, kept, sent, other, out, keep, payload, high
    )


def ride_kernel(
    seqs, level, split, halved, top, jobs, cut, high, last, ids, par, own, kept, sent, other, *refs
):
    count = 1 + max(p for job in jobs for p in job[0])
    parts, refs = refs[:count], refs[count:]
    out = payload = None
    if last:
        keep, kept_out = refs
        halves = ((0, keep),)
    elif cut is None:
        kept_out, out, payload = refs
        halves = ((0, payload),)
    else:
        keep, kept_out, out, payload = refs
        halves = ((0, keep), (1, payload))
    for picks, width, at in jobs:
        chosen = [other if p == -1 else sent if p == -2 else parts[p] for p in picks]
        for k, target in halves:
            start = 0 if cut is None else split_rows(2 * high, cut, ids[1], k)[0]
            add_rows(chosen, start, high, target, 0, 0, width, at)
    chain_hop(
        seqs, level, split, halved, top, ids, par, own, kept, sent, other, out, kept_out, payload,
        high,
    )


def unpack_first(cut, ids, *refs):
    count = 1 << cut[1]
    pieces, refs = refs[:count], refs[count:]
    w_in, w_out = refs[:2]
    outs = refs[2:]
    vb = w_in.shape[1]
    wide = 2 * vb
    each = sum(out.shape[0] for out in outs)
    for k in range(count):
        row, rows = split_rows(D, cut, ids[1], k)
        w_in[pl.ds(row, rows), :] = pieces[k][0, :, :vb].astype(F32)
        for first in range(0, rows, vb):
            w_out[:, pl.ds(pl.multiple_of(row + first, vb), vb)] = pieces[k][
                0, first : first + vb, vb:
            ].astype(F32)
        for b in range(count):

            @pl.when(row == b * rows)
            def _(k=k, b=b, rows=rows):
                for run in range(D // wide):
                    start = run * each
                    for out in outs:
                        end = start + out.shape[0]
                        lo, hi = max(start, b * rows), min(end, (b + 1) * rows)
                        if lo < hi:
                            out[lo - start : hi - start, run * wide : (run + 1) * wide] = pieces[k][
                                1, lo - b * rows : hi - b * rows, :
                            ].astype(F32)
                        start = end


def unpack_sides(cut, ids, *refs):
    count = 1 << cut[1]
    pieces, (left, right) = refs[:count], refs[count:]
    vb = left.shape[1]
    for k in range(count):
        row, rows = split_rows(D, cut, ids[1], k)
        left[pl.ds(row, rows), :] = pieces[k][0, :, :vb].astype(F32)
        right[pl.ds(row, rows), :] = pieces[k][0, :, vb:].astype(F32)


def unpack(body, cut, ids, pieces, dims):
    return call(
        functools.partial(body, cut),
        tuple(shape(d) for d in dims),
        [],
        (ids, *pieces),
        [SMEM] + [VMEM] * len(pieces),
        "unpack",
    )


BOTH = ("seq", "tp")


def swap(value, mask):
    count = lax.axis_size("seq") * lax.axis_size("tp")
    return lax.ppermute(value, BOTH, [(i, i ^ mask) for i in range(count)])


def after(value, *others):
    return lax.optimization_barrier((value, *others))[0]


def bits_of(count):
    return [1 << k for k in range(count.bit_length() - 1)]


def has(index, bit):
    return jnp.bitwise_and(index, bit) > 0


def half_of(value, upper):
    half = value.shape[0] // 2
    return lax.dynamic_slice_in_dim(value, jnp.where(upper, half, 0), half, 0)


def joined(mine, other, upper):
    return jnp.where(
        upper,
        jnp.concatenate([other, mine], axis=0),
        jnp.concatenate([mine, other], axis=0),
    )


def spread_out(own, tp):
    pieces = {0: own}
    for bit in reversed(bits_of(tp // 2)):
        for r in list(pieces):
            pieces[r ^ bit] = [swap(a, bit) for a in pieces[r]]
    return [pieces[r] for r in range(tp // 2)]


def per_device(
    tokens,
    cotangent,
    valid_lengths,
    norm1_gain,
    ema_rate,
    ema_beta,
    ema_eta,
    ema_skip,
    w_shared,
    query_gain,
    key_gain,
    rel_bias,
    w_value,
    w_reset,
    w_update,
    w_hidden,
    u_hidden,
    norm2_gain,
    w_in,
    w_out,
):
    part = lax.axis_index("tp")
    tp = lax.axis_size("tp")
    seq = lax.axis_size("seq")
    all_seqs, local_rows, _ = tokens.shape
    vb = w_value.shape[1]
    nb = D // tp
    ybits = far_shift()
    traded = local_rows < CH
    lower = part % 2 == 0

    def trade(value):
        if not traded:
            return value
        other = swap(jnp.where(lower, value[1], value[0]), 1)
        mine = jnp.where(lower, value[0], value[1])
        return joined(mine, other, ~lower)[None]

    def trade_back(value):
        if not traded:
            return value
        first, second = value[0, :local_rows], value[0, local_rows:]
        other = swap(jnp.where(lower, second, first), 1)
        mine = jnp.where(lower, first, second)
        return jnp.where(lower, jnp.stack([mine, other]), jnp.stack([other, mine]))

    if traded:
        assert all_seqs == 2 and 2 * local_rows == CH
        seqs = 1
    else:
        assert local_rows == CH
        seqs = all_seqs
    rows = seqs * CH
    ids, ids_lengths = Here(seqs, None), Here(seqs, valid_lengths.astype(jnp.int32))
    masks = bits_of(tp * seq)[int(traded) :]
    levels = len(masks)

    tok = trade(tokens)
    cot = trade(cotangent)
    gain1 = norm1_gain[None]
    gain2 = norm2_gain[None]
    skip = ema_skip[None]
    rate, beta = ema_rate.T, ema_beta.T
    qg, kg, rb = query_gain[None], key_gain[None], rel_bias[None]

    top = tp // 2
    weights = (w_value, w_reset, w_hidden, w_update, u_hidden, w_in, w_out)
    rows2 = 2 * nb + vb
    normed, par, before, ends, low = call(
        functools.partial(enter_kernel, seqs),
        (
            shape((rows, D), BF16),
            shape((5, NDIM, D)),
            shape((2, seqs, NDIM, PIECES, D)),
            shape((2 * seqs + 1, NDIM, D)),
            shape((3 * seqs, NDIM, D), BF16),
        ),
        [
            pltpu.VMEM((seqs, CH, D), BF16),
            pltpu.VMEM((1, D), F32),
            pltpu.VMEM((NDIM, D), F32),
            pltpu.VMEM((NDIM, D), F32),
            pltpu.VMEM((NDIM, D), F32),
            pltpu.VMEM((1, D), F32),
            pltpu.VMEM((1, D), F32),
            pltpu.VMEM((1, Z), F32),
            pltpu.VMEM((1, Z), F32),
            pltpu.VMEM((1, Z), F32),
            pltpu.VMEM((BLOCKS, rows, LANES), F32),
            pltpu.VMEM((6, NDIM, D), F32),
            pltpu.SemaphoreType.DMA((10,)),
        ],
        (ids_lengths, tok, gain1, rate, beta, ema_eta.T, skip, gain2, qg, kg, rb),
        [SMEM] + [ANY] * 10,
        "enter",
        limit=12,
    )
    start = 1 - int(traded)
    groups = [(0, 1)] * start + [(start, 2)] + [(i, 1) for i in range(start + 2, levels)]
    hops = []
    first_half = has(lax.axis_index("seq"), 1)
    half1 = jnp.concatenate([half_of(w, first_half) for w in (w_value, w_reset)], axis=1)
    mine1 = swap(half1, top)
    state = ends
    for i, (shift, bits) in enumerate(groups):
        if i == start:
            low = after(low, mine1)
            pack1, pack2, pack3, half2, half3 = call(
                pack_kernel,
                (
                    shape((D, 2 * vb), BF16),
                    shape((rows2, D), BF16),
                    shape((D, 2 * vb), BF16),
                    shape((rows2, D // 2), BF16),
                    shape((D // 2, 2 * vb), BF16),
                ),
                [pltpu.SemaphoreType.DMA((10 + 3 * D // vb // 2,))],
                lax.optimization_barrier((*weights, low))[:-1],
                [ANY] * 7,
                "pack",
                limit=60,
                outs=(pl.BlockSpec(),) * 5,
            )
        if i == start + 1:
            mine2 = swap(after(half2, low), top)
            other1 = swap(after(mine1, low), tp)
            near_gates = spread_out([after(pack1, low), after(pack2, low)], tp)
        if i == start + 2:
            low = after(low, mine2, other1, *near_gates[-1])
            mine3 = swap(after(half3, low), top)
            other2 = swap(after(mine2, low), tp << ybits)
            near_feeds = spread_out([after(pack3, low)], tp)
        got = []
        for k in range(1, 1 << bits):
            got.append(swap(low, k << (shift + int(traded))))
            hops.append((shift, k, got[-1]))
        if i + 1 < len(groups):
            state, low = call(
                functools.partial(hop_kernel, seqs, shift, 1 << bits),
                (shape((2 * seqs + 1, NDIM, D)), shape((3 * seqs, NDIM, D), BF16)),
                [],
                (ids, state, *got),
                [SMEM] + [VMEM] * (1 + len(got)),
                "hop",
            )
    st_in, skip_pre, mixed, shared_pre, prob = call(
        functools.partial(look_kernel, seqs, [h[:2] for h in hops]),
        (
            shape((2, seqs, NDIM, D)),
            shape((rows, D)),
            shape((rows, D), BF16),
            shape((rows, Z)),
            shape((seqs, CH, CH)),
        ),
        [
            pltpu.VMEM((BLOCKS, rows, LANES), F32),
            pltpu.VMEM((BLOCKS, rows, LANES), F32),
            pltpu.VMEM((NDIM, PIECES, D), F32),
        ],
        (
            ids, after(normed, mine3), par, before, w_shared,
            *[h[2] for h in hops],
        ),
        [SMEM] + [VMEM] * (4 + len(hops)),
        "look",
        limit=10,
    )
    far_gates = spread_out([mine1, after(other1, prob), mine2, after(other2, prob)], tp)
    other3 = swap(mine3, tp)
    gates = [w for group in near_gates + far_gates for w in group]

    values, value_pre, reset_pre, attended, gated, hidden_pre, update_pre, middle = call(
        functools.partial(mix_kernel, seqs, tp),
        (
            shape((tp, rows, vb), BF16),
            shape((tp, rows, vb)),
            shape((tp, rows, vb)),
            shape((tp, rows, vb)),
            shape((tp, rows, vb), BF16),
            shape((rows, D)),
            shape((rows, D)),
            shape((rows, D)),
        ),
        [
            pltpu.VMEM((tp, D, 2 * vb), BF16),
            pltpu.VMEM((tp, rows2, D), BF16),
            pltpu.VMEM((D, 2 * D), BF16),
            pltpu.SemaphoreType.DMA((3 * tp,)),
        ],
        (ids, tok, normed, after(mixed, other3), prob, *gates),
        [SMEM] + [VMEM] * 4 + [ANY] * len(gates),
        "mix",
        limit=10,
    )

    far_feeds = spread_out([mine3, other3], tp)
    feeds = [w for group in near_feeds + far_feeds for w in group]
    out, keep3, send3, grad_hu, resid, grad_gain2 = call(
        functools.partial(ffn_kernel, seqs, tp),
        (
            shape((rows, D), BF16),
            shape((tp // 2, D, 2 * vb), BF16),
            shape((tp // 2, D, 2 * vb), BF16),
            shape((rows, 2 * D), BF16),
            shape((rows, D)),
            shape((1, D)),
        ),
        [
            pltpu.VMEM((tp, D, 2 * vb), BF16),
            pltpu.VMEM((rows, D), BF16),
            pltpu.VMEM((rows, D), BF16),
            pltpu.VMEM((rows, D), F32),
            pltpu.VMEM((rows, D), F32),
            pltpu.SemaphoreType.DMA((3 * tp // 2,)),
        ],
        (ids, tok, cot, middle, hidden_pre, update_pre, par, *feeds),
        [SMEM] + [VMEM] * 6 + [ANY] * len(feeds),
        "ffn",
        limit=10,
    )

    half = tp // 2
    yn = 1 << ybits
    wide = 2 * vb
    runs = D // wide
    cut_of_y = (0, ybits)
    zcuts = [(shift, 1) for shift in range(ybits, seq.bit_length() - 1)]

    def over_tp(pieces):
        return [pieces[0]] + [swap(p, 2 * k) for k, p in enumerate(pieces) if k]

    def over_y(pieces):
        return [pieces[0]] + [swap(p, tp * k) for k, p in enumerate(pieces) if k]

    def over_z(value, cut):
        return swap(value, tp << cut[0])

    def cut_tp(parts, dims):
        n = dims[0]
        return fold(
            ids,
            [(1,) + dims[1:]] * n,
            [(parts, 0, dims[2], "tp", [(k, 0, 0) for k in range(n)])],
        )

    def cut_y(parts, dims):
        return fold(
            ids,
            [(dims[0], dims[1] // yn, dims[2])] * yn,
            [(parts, 0, dims[2], cut_of_y, [(k, 0, 0) for k in range(yn)])],
        )

    last = [None]

    def now(value):
        return value if last[0] is None else after(value, last[0])

    chunk = (half, D, wide)
    got3 = swap(send3, 1)
    keep2, send2 = call(
        functools.partial(gates_kernel, tp),
        (shape(chunk, BF16), shape(chunk, BF16)),
        [pltpu.VMEM((D, 2 * D), F32)],
        (ids, mixed, gated, grad_hu),
        [SMEM] + [VMEM] * 3,
        "gates",
        limit=10,
    )
    got2 = swap(send2, 1)
    g3 = cut_tp([keep3, got3], chunk)
    g3 = over_tp(g3)
    g2 = cut_y([keep2, after(got2, g3[0])], chunk)
    g2 = over_y(g2)

    count = Z + SMALL_ROWS
    count += -count % (16 * tp)
    (
        keep1, send1, grad_skip, grad_normed, behind, back_ends, sums_keep, sums_send,
    ) = call(
        functools.partial(back_kernel, seqs, tp),
        (
            shape(chunk, BF16),
            shape(chunk, BF16),
            shape((BLOCKS, rows, LANES)),
            shape((rows, D)),
            shape((seqs, NDIM, PIECES, D)),
            shape((seqs, NDIM, D)),
            shape((count // 2, D)),
            shape((count // 2 + seqs * NDIM, D)),
        ),
        [
            pltpu.VMEM((tp, D, 2 * vb), BF16),
            pltpu.VMEM((tp, rows2, D), BF16),
            pltpu.VMEM((D, 2 * D), BF16),
            pltpu.VMEM((rows, D), F32),
            pltpu.VMEM((seqs, CH, CH), F32),
            pltpu.VMEM((3, NDIM, D), F32),
            pltpu.VMEM((D, Z), F32),
            pltpu.VMEM((1, D), F32),
            pltpu.VMEM((count, D), F32),
            pltpu.VMEM((BLOCKS, rows, LANES), F32),
            pltpu.VMEM((NDIM, PIECES, D), F32),
            pltpu.SemaphoreType.DMA((3 * tp,)),
        ],
        (
            ids, normed, mixed, skip_pre, shared_pre, prob, values, value_pre, reset_pre, attended,
            after(grad_hu, g2[0]), par, w_shared, tok, before, st_in, grad_gain2,
            *gates,
        ),
        [SMEM] + [VMEM] * 16 + [ANY] * len(gates),
        "back",
        limit=12,
    )

    g3 = cut_y([after(g3[0], send1)] + g3[1:], (1, D, wide))
    g2 = cut_tp([after(g2[0], g3[0])] + g2[1:], (half, D // yn, wide))
    (
        keep1, send1, grad_skip, grad_normed, behind, back_ends, sums_keep, sums_send, _,
    ) = lax.optimization_barrier(
        (keep1, send1, grad_skip, grad_normed, behind, back_ends, sums_keep, sums_send, g2[0])
    )
    adjoint = back_ends.reshape(seqs * NDIM, D)
    last[0] = g2[0]
    g3 = over_y(g3)
    g2 = over_tp(g2)
    got1 = swap(send1, 1)
    got_sums = swap(sums_send, 1)
    done = {}

    def first_chunks():
        high = D // yn
        for i, cut in enumerate(zcuts[:-1] + [None]):
            high = high // 2 if cut else high
            pieces = 2 if cut else 1
            if i:
                jobs = [([now(keep), other], 0, wide, cut, [(k, 0, 0) for k in range(pieces)])]
            else:
                jobs = [
                    ([now(g3[0])] + g3[1:], 0, wide, cut, [(k, 0, 0) for k in range(pieces)]),
                    (g2, 0, wide, cut, [(k, 1, 0) for k in range(pieces)]),
                ]
            keep, *send = fold(ids, [(2, high, wide)] * pieces, jobs)
            other = over_z(*send, cut) if cut else over_z(keep, zcuts[-1])
            yield keep
        (total,) = fold(ids, [keep.shape], [([now(keep), other], 0, wide, None, [(0, 0, 0)])])
        for cut in reversed(zcuts[:-1]):
            other = over_z(total, cut)
            yield total
            total = join(ids, now(total), other, cut)
        pieces = over_y([total] * yn)
        yield total
        done["first"] = unpack(
            unpack_first,
            cut_of_y,
            ids,
            [now(pieces[0])] + pieces[1:],
            [(D, vb), (vb, D), (nb, D), (nb, D), (vb, D)],
        )
        yield done["first"][0]

    def second_chunk():
        small_high = count // 4
        ad_rows = seqs * NDIM

        def payload_rows():
            return (ad_rows + small_high) * runs

        together = half == 2 and yn == 2 and not traded
        if together:
            lanes = D // vb
            own, kept, left, payload, right, send = call(
                functools.partial(start_kernel, seqs, ybits),
                (
                    shape((ad_rows, D)),
                    shape((small_high, D)),
                    shape((D, vb), BF16),
                    shape((D + (ad_rows + small_high) * lanes, vb), BF16),
                    shape((2, D // 2, vb), BF16),
                    shape((2, D // 2, vb), BF16),
                ),
                [],
                (ids, par, now(adjoint), sums_keep, got_sums, keep1, got1),
                [SMEM] + [VMEM] * 6,
                "start",
            )
            other, got_right = swap(payload, 2), swap(send, tp)
            got = [(got_sums, count // 2), (other, D)]
            yield payload
            own, kept, left, payload, right, send = call(
                functools.partial(cross_kernel, seqs, ybits),
                (
                    shape((ad_rows, D)),
                    shape((small_high, D)),
                    shape((D // 2, vb), BF16),
                    shape((D // 2 + (ad_rows + small_high) * lanes, vb), BF16),
                    shape((D // 2, vb), BF16),
                    shape((D // 2, vb), BF16),
                ),
                [],
                (ids, par, now(own), kept, payload, other, left, right, got_right),
                [SMEM] + [VMEM] * 8,
                "cross",
            )
            other, got_right = swap(payload, tp), swap(send, 2)
            level, top, halved = 2, D // 2, False
            flat = [left, right, got_right]
            jobs = [((0, -1), vb, 0), ((1, 2), vb, vb)]
            yield payload
        else:
            own, kept, payload = call(
                functools.partial(first_back_hop, seqs, not traded),
                (
                    shape((ad_rows, D)),
                    shape((small_high, D)),
                    shape((payload_rows(), wide), BF16),
                ),
                [],
                (ids, par, now(adjoint), sums_keep, got_sums),
                [SMEM] + [VMEM] * 4,
                "hop",
            )
            got = [] if traded else [(got_sums, count // 2)]
            level = int(not traded)
            halved = True
            other = swap(payload, masks[level])
            yield payload
            parts = fold(
                ids,
                [(1, D, vb)] * half + [(half, D // yn, vb)] * yn,
                [
                    ([now(keep1), got1], 0, vb, "tp", [(k, 0, 0) for k in range(half)]),
                    ([keep1, got1], vb, vb, cut_of_y, [(half + k, 0, 0) for k in range(yn)]),
                ],
            )
            left, right = over_tp(parts[:half]), over_y(parts[half:])
            yield parts[0]
            crossed = False
            while level + 1 < levels - len(zcuts):
                got.append((other, 0))
                split = 2 * masks[level] if 2 * masks[level] < tp else 0
                small_high = small_high // 2 if split else small_high
                own, kept, payload = call(
                    functools.partial(back_hop, seqs, level, split, halved),
                    (
                        shape((ad_rows, D)),
                        shape((small_high, D)),
                        shape((payload_rows(), wide), BF16),
                    ),
                    [],
                    (ids, par, now(own), kept, payload, other),
                    [SMEM] + [VMEM] * 5,
                    "hop",
                )
                halved = bool(split)
                level += 1
                other = swap(payload, masks[level])
                yield payload
                if crossed:
                    continue
                crossed = True
                parts = fold(
                    ids,
                    [(1, D // yn, vb)] * (yn + half),
                    [
                        ([now(left[0])] + left[1:], 0, vb, cut_of_y, [(k, 0, 0) for k in range(yn)]),
                        (right, 0, vb, "tp", [(yn + k, 0, 0) for k in range(half)]),
                    ],
                )
                left, right = over_y(parts[:yn]), over_tp(parts[yn:])
                yield parts[0]
            top = 0
            flat = [p.reshape(p.shape[1:]) for p in left + right]
            jobs = [
                (tuple(range(len(left))), vb, 0),
                (tuple(range(len(left), len(flat))), vb, vb),
            ]
        high = D // yn
        for cut in zcuts[:-1] + [None]:
            got.append((other, top))
            high = high // 2 if cut else high
            kept_chunk = [shape((high, wide), BF16)] if cut else []
            *flat, kept, own, payload = call(
                functools.partial(
                    ride_kernel, seqs, level, 0, halved, top, jobs, cut, high, False
                ),
                (
                    *kept_chunk,
                    shape((small_high, D)),
                    shape((ad_rows, D)),
                    shape((high + payload_rows(), wide), BF16),
                ),
                [],
                (ids, par, now(own), kept, payload, other, *flat),
                [SMEM] + [VMEM] * (5 + len(flat)),
                "ride",
            )
            halved = False
            level += 1
            top = high
            jobs = [((0 if cut else -2, -1), wide, 0)]
            other = swap(payload, masks[level])
            yield payload
        got.append((other, top))
        total, kept = call(
            functools.partial(ride_kernel, seqs, level, 0, False, top, jobs, None, high, True),
            (shape((high, wide), BF16), shape((small_high, D))),
            [],
            (ids, par, now(own), kept, payload, other, *flat),
            [SMEM] + [VMEM] * (5 + len(flat)),
            "ride",
        )
        bits = list(reversed(bits_of(tp)))
        total = total[None]
        far = swap(kept, bits[0])
        other = over_z(total, zcuts[-2]) if len(zcuts) > 1 else None
        yield total
        (done["tokens"],) = call(
            functools.partial(leave_kernel, seqs, [at for _, at in got]),
            (shape((seqs, CH, D), BF16),),
            [
                pltpu.VMEM((seqs, NDIM, D), F32),
                pltpu.VMEM((NDIM, PIECES, D), F32),
                pltpu.VMEM((BLOCKS, rows, LANES), F32),
            ],
            (
                ids, tok, par, now(grad_skip), grad_normed, behind, resid,
                *[g for g, _ in got],
            ),
            [SMEM] + [VMEM] * (6 + levels),
            "leave",
            limit=10,
        )
        yield done["tokens"]
        for i in range(len(zcuts) - 2, -1, -1):
            total = join(ids, now(total), other, zcuts[i])
            if i:
                other = over_z(total, zcuts[i - 1])
                yield total
        pieces = over_y([total] * yn)
        yield total
        for i in range(len(bits) - 1):
            (kept,) = call(
                functools.partial(pair_kernel, bits[i]),
                (shape((2 * kept.shape[0], D)),),
                [],
                (ids, now(kept), far),
                [SMEM, VMEM, VMEM],
                "pair",
            )
            far = swap(kept, bits[i + 1])
            yield kept
        done["small"] = call(
            finish_kernel,
            (
                shape((1, D)),
                shape((NDIM, D)),
                shape((NDIM, D)),
                shape((NDIM, D)),
                shape((1, D)),
                shape((D, Z)),
                shape((1, Z)),
                shape((1, Z)),
                shape((1, Z)),
                shape((1, D)),
            ),
            [pltpu.VMEM((count, D), F32)],
            (ids, par, rate, beta, now(kept), far),
            [SMEM] + [VMEM] * 5,
            "finish",
        )
        yield done["small"][0]
        done["second"] = unpack(
            unpack_sides, cut_of_y, ids, [now(pieces[0])] + pieces[1:], [(D, vb), (D, vb)]
        )
        yield done["second"][0]

    walks = {"f": first_chunks(), "s": second_chunk()}
    order = "sfsfssffsssssfs"

    def advance(name):
        try:
            last[0] = next(walks[name])
        except StopIteration:
            del walks[name]

    for name in order:
        if name in walks:
            advance(name)
    while walks:
        for name in list(walks):
            advance(name)

    grad_w_in, grad_w_out, grad_w_hidden, grad_w_update, grad_u_hidden = done["first"]
    grad_w_value, grad_w_reset = done["second"]
    firsts = [
        small.T if small.shape[0] == NDIM else small[0] if small.shape[0] == 1 else small
        for small in done["small"]
    ]
    grad_norm2_gain = firsts.pop()
    return (
        trade_back(out.reshape(seqs, CH, D)),
        trade_back(done["tokens"]),
        *firsts,
        grad_w_value,
        grad_w_reset,
        grad_w_update,
        grad_w_hidden,
        grad_u_hidden,
        grad_norm2_gain,
        grad_w_in,
        grad_w_out,
    )


def solution(mesh):
    rows = P(None, ("seq", "tp"), None)
    cols = P(None, "tp")
    tall = P("tp", None)
    whole = P()
    return jax.shard_map(
        per_device,
        mesh=mesh,
        in_specs=(rows, rows) + (whole,) * 10 + (cols, cols, tall, tall, tall, whole, cols, tall),
        out_specs=(rows, rows) + (whole,) * 9 + (cols, cols, tall, tall, tall, whole, cols, tall),
        check_vma=False,
    )
```
